32 devices in a mesh: section: 2 (over x), dp: 4 (over y, core), tensor: 4 (over z).
Axes of the slice: x: 2, y: 2, z: 4, core: 2. Of those that a mesh axis runs over, the one named last changes fastest.
Arguments:
- tokens: bfloat16 [8, 1024, 768], P('dp', 'tensor'), may hold values from -6 to 6
- cotangent: bfloat16 [8, 1024, 768], P('dp', 'tensor'), may hold values from -6 to 6
- lengths: int32 [8, 8], P('dp'), may hold values from 1 to 896, 1024 in all within a row
- w_qkv: bfloat16 [2, 768, 3, 768], P('section', 'dp', None, 'tensor'), may hold values from -0.21875 to 0.21875
- w_out: bfloat16 [2, 768, 768], P('section', 'tensor', 'dp'), may hold values from -0.625 to 0.625
- w_gate_up: bfloat16 [2, 768, 2, 3072], P('section', 'dp', None, 'tensor'), may hold values from -0.21875 to 0.21875
- w_down: bfloat16 [2, 3072, 768], P('section', 'tensor', 'dp'), may hold values from -0.109375 to 0.109375
- norm_gains: bfloat16 [2, 1536], P('section', 'dp'), may hold values from 0.5 to 1.5
- norm_biases: bfloat16 [2, 1536], P('section', 'dp'), may hold values from -1.796875 to 1.796875
Outputs:
- ends: bfloat16 [2, 8, 1024, 768], P('section', 'dp', 'tensor')
- grad_qkv: float32 [2, 768, 3, 768], P('section', 'dp', None, 'tensor')
- grad_out: float32 [2, 768, 768], P('section', 'tensor', 'dp')
- grad_gate_up: float32 [2, 768, 2, 3072], P('section', 'dp', None, 'tensor')
- grad_down: float32 [2, 3072, 768], P('section', 'tensor', 'dp')
- grad_gains: float32 [2, 1536], P('section', ('dp', 'tensor'))
- grad_biases: float32 [2, 1536], P('section', ('dp', 'tensor'))
The draws below stay inside these ranges and needn't reach their ends.
Inputs may be any that keep to these rules, and one draw needn't show every extreme that they name: `lengths`: each row sums to 1024 and its largest length is exactly 896.
All inputs are finite; a program needn't handle non-finite values.
Results may differ from the reference program's by a relative error of at most 0.02.
Values may be sent and summed in bfloat16 or wider, within the bound.
A program may use at most 256 MiB of HBM per device.

```python
import math
import jax
import jax.numpy as jnp
import numpy as np
from jax import lax

D = 768
HEADS = 12
HD = 64
FF = 3072
SEQ_LEN = 1024
DOCS = 8
LONGEST = 896
SEQS = 8


def block_scale(own_key, extent, pieces, low, top_value):
    def one(position, shards_of):
        draws = jax.random.uniform(jax.random.fold_in(jax.random.fold_in(own_key, 6), position), (shards_of,), jnp.float32, low / len(pieces), top_value / len(pieces))
        return jnp.repeat(jnp.exp(draws), extent[position] // shards_of).reshape((-1,) + (1,) * (len(extent) - position - 1))

    level = one(*pieces[0])
    for cut in pieces[1:]:
        level = level * one(*cut)
    return level


def split_up(number_of, total, bound, lean):
    portions = [(1 << 20) // math.isqrt(grade ** lean) + 1 for grade in range(2, number_of + 1)]
    rest, given = total - bound - (number_of - 1), [1] * (number_of - 1)
    while rest > 0:
        candidates = [i for i in range(number_of - 1) if given[i] < bound]
        mass, budget = sum([portions[i] for i in candidates]), rest
        for i in candidates:
            more = min(bound - given[i], max(1, budget * portions[i] // mass), rest)
            given[i] = given[i] + more
            rest = rest - more
    return np.array([bound] + given)


def uneven_parts(stream_key, number_of, total, reach, skew):
    if number_of == 2:
        one = jax.random.randint(stream_key, (), max(1, total - reach), min(reach, total - 1) + 1)
        return jnp.stack([one, total - one])
    sizes = jnp.asarray(split_up(number_of, total, reach, skew), jnp.int32)
    pairs = (number_of - 1) // 2
    donor, receiver = sizes[1:1 + 2 * pairs:2], sizes[2:2 + 2 * pairs:2]
    margin = jnp.minimum(donor - 1, reach - receiver)
    moved = jax.random.randint(jax.random.fold_in(stream_key, 1), (pairs,), 0, 1 << 20) % (margin + 1)
    sizes = sizes.at[1:1 + 2 * pairs:2].set(donor - moved).at[2:2 + 2 * pairs:2].set(receiver + moved)
    return sizes[jax.random.permutation(jax.random.fold_in(stream_key, 2), number_of)]


def noise(key, dims, deviation, reach, pieces=(), kind=jnp.bfloat16):
    values = deviation * jax.random.normal(key, dims, jnp.float32)
    if pieces:
        values = values * block_scale(key, dims, pieces, -0.22, 0.18)
    return jnp.clip(values, -reach, reach).astype(kind)


def setup_inputs(seed: int = 0) -> dict:
    arg_keys = jax.random.split(jax.random.key(seed), 10)
    tokens = noise(arg_keys[0], (SEQS, SEQ_LEN, D), 1.0, 6.0, ((0, 4), (1, 4)))
    cotangent = noise(arg_keys[1], (SEQS, SEQ_LEN, D), 1.0, 6.0, ((0, 4), (1, 4)))
    lengths = jax.vmap(lambda own: uneven_parts(own, DOCS, SEQ_LEN, LONGEST, 2))(jax.random.split(arg_keys[2], SEQS)).reshape((SEQS, DOCS)).astype(jnp.int32)
    w_qkv = noise(arg_keys[3], (2, D, 3, D), D ** -0.5, 0.21875, ((0, 2), (1, 4), (3, 4)))
    w_out = noise(arg_keys[4], (2, D, D), (max(D // 8, 1)) ** -0.5, 0.625, ((0, 2), (1, 4), (2, 4)))
    w_gate_up = noise(arg_keys[5], (2, D, 2, FF), D ** -0.5, 0.21875, ((0, 2), (1, 4), (3, 4)))
    w_down = noise(arg_keys[6], (2, FF, D), FF ** -0.5, 0.109375, ((0, 2), (1, 4), (2, 4)))
    norm_gains = jnp.clip(1.0 + 0.1 * jax.random.normal(arg_keys[7], (2, 2 * D), jnp.float32), 0.5, 1.5).astype(jnp.bfloat16)
    norm_biases = noise(arg_keys[8], (2, 2 * D), 0.3, 1.796875, ((0, 2), (1, 4)))
    return dict(tokens=tokens, cotangent=cotangent, lengths=lengths, w_qkv=w_qkv, w_out=w_out, w_gate_up=w_gate_up, w_down=w_down, norm_gains=norm_gains, norm_biases=norm_biases)


@jax.custom_vjp
def low(v):
    return lax.optimization_barrier(v.astype(jnp.bfloat16)).astype(jnp.float32)

@jax.custom_vjp
def low_back(v):
    return v

def low_keep(v):
    return (low(v), None)

def low_pass(kept, grad):
    return (grad,)

def back_keep(v):
    return (v, None)

def back_low(kept, grad):
    return (low(grad),)
low.defvjp(low_keep, low_pass)
low_back.defvjp(back_keep, back_low)
eps = 1e-05
neg_fill = -1e+30

def layer_norm(resid, gain, shift):
    center = resid - lax.optimization_barrier(jnp.mean(resid, axis=-1, keepdims=True))
    spread = lax.optimization_barrier(jnp.mean(center * center, axis=-1, keepdims=True))
    return center * lax.rsqrt(spread + eps) * gain + shift

def rope_tables(length, head_size):
    halfway = head_size // 2
    freqs = 1000.0 ** (-jnp.arange(halfway, dtype=jnp.float32) / halfway)
    angles = jnp.arange(length, dtype=jnp.float32)[:, None] * freqs[None, :]
    return (jnp.cos(angles), jnp.sin(angles))

def rotate(values, cosine, sine):
    halfway = values.shape[-1] // 2
    leading = values[..., :halfway]
    trailing = values[..., halfway:]
    cos_table = cosine[None, :, None, :]
    sin_table = sine[None, :, None, :]
    return jnp.concatenate([leading * cos_table - trailing * sin_table, trailing * cos_table + leading * sin_table], axis=-1)

def attention(queries, keys, values, segment):
    group_size, length, heads, head_size = queries.shape
    block_rows = min(512, length)
    block_count = length // block_rows
    scale = head_size ** (-0.5)

    def one_block(block_inputs):
        query_rows, query_seg = block_inputs
        scores = low_back(jnp.einsum('gqhd,gkhd->ghqk', query_rows, keys, precision=lax.Precision.HIGHEST) * scale)
        allowed = query_seg[:, :, None] == segment[:, None, :]
        scores = jnp.where(allowed[:, None], scores, neg_fill)
        probs = jax.nn.softmax(scores, axis=-1)
        return jnp.einsum('ghqk,gkhd->gqhd', low(probs), values, precision=lax.Precision.HIGHEST)
    query_blocks = queries.reshape(group_size, block_count, block_rows, heads, head_size).transpose(1, 0, 2, 3, 4)
    seg_blocks = segment.reshape(group_size, block_count, block_rows).transpose(1, 0, 2)
    outputs = lax.map(jax.checkpoint(one_block), (query_blocks, seg_blocks))
    return outputs.transpose(1, 0, 2, 3, 4).reshape(group_size, length, heads * head_size)

def layer(inputs, w_joint, w_mix, w_pair, w_back, gains, shifts, segment, tables):
    group_size, length, width = inputs.shape
    joined = low_back(jnp.einsum('gld,dcn->glcn', inputs, w_joint, precision=lax.Precision.HIGHEST))
    joined = joined.reshape(group_size, length, 3, HEADS, HD)
    queries = low(rotate(joined[:, :, 0], tables[0], tables[1]))
    keys = low(rotate(joined[:, :, 1], tables[0], tables[1]))
    values = low(joined[:, :, 2])
    mixed = low_back(low(attention(queries, keys, values, segment)))
    attn = low_back(jnp.einsum('gld,de->gle', mixed, w_mix, precision=lax.Precision.HIGHEST))
    hidden = layer_norm(inputs + attn, gains[:width], shifts[:width])
    gate_up = low_back(jnp.einsum('gld,dcf->glcf', low(hidden), w_pair, precision=lax.Precision.HIGHEST))
    active = low(jax.nn.silu(gate_up[:, :, 0]) * gate_up[:, :, 1])
    ffn = low_back(jnp.einsum('glf,fd->gld', active, w_back, precision=lax.Precision.HIGHEST))
    return layer_norm(hidden + ffn, gains[width:], shifts[width:])

def reference(tokens, cotangent, lengths, w_qkv, w_out, w_gate_up, w_down, norm_gains, norm_biases):
    seq_count, length, width = tokens.shape
    positions = jnp.arange(length, dtype=jnp.int32)
    doc_ends = jnp.cumsum(lengths, axis=1).astype(jnp.int32)
    segments = lax.optimization_barrier(jnp.sum((doc_ends[:, None, :] <= positions[None, :, None]).astype(jnp.int32), axis=-1)).astype(jnp.int32)
    tables = rope_tables(length, HD)
    group_size = math.gcd(seq_count, 4)

    def model(inputs, w_joint, w_mix, w_pair, w_back, gains, shifts):

        def step(carried, step_inputs):
            seq_rows, segment = step_inputs
            first_out = layer(seq_rows, w_joint[0], w_mix[0], w_pair[0], w_back[0], gains[0], shifts[0], segment, tables)
            second_in = low(first_out)
            second_out = layer(second_in, w_joint[1], w_mix[1], w_pair[1], w_back[1], gains[1], shifts[1], segment, tables)
            return (carried, second_out)
        row_blocks = inputs.reshape(seq_count // group_size, group_size, length, width)
        seg_blocks = segments.reshape(seq_count // group_size, group_size, length)
        unused, outputs = lax.scan(jax.checkpoint(step), jnp.zeros((), jnp.float32), (row_blocks, seg_blocks))
        return outputs.reshape(seq_count, length, width)
    result, back_fn = jax.vjp(model, tokens.astype(jnp.float32), w_qkv.astype(jnp.float32), w_out.astype(jnp.float32), w_gate_up.astype(jnp.float32), w_down.astype(jnp.float32), norm_gains.astype(jnp.float32), norm_biases.astype(jnp.float32))
    grads = back_fn(cotangent.astype(jnp.float32))
    ends = jnp.stack([grads[0], result]).astype(jnp.bfloat16)
    return (ends, grads[1], grads[2], grads[3], grads[4], grads[5], grads[6])
```

```python
import functools

import jax
import jax.numpy as jnp
from jax import lax
from jax.sharding import Mesh, PartitionSpec as P

HD = 64
eps = 1e-05
neg_fill = -1e30
ALL = ("y", "core", "tensor")
BF = jnp.bfloat16
F32 = jnp.float32


def layer_norm(resid, gain, shift):
    center = resid - jnp.mean(resid, axis=-1, keepdims=True)
    spread = jnp.mean(center * center, axis=-1, keepdims=True)
    return center * lax.rsqrt(spread + eps) * gain + shift


def gate_act(joined):
    return jax.nn.silu(joined[:, 0]) * joined[:, 1]


def rope_tables(positions, head_size):
    halfway = head_size // 2
    freqs = 1000.0 ** (-jnp.arange(halfway, dtype=F32) / halfway)
    angles = positions.astype(F32)[:, None] * freqs[None, :]
    return (jnp.cos(angles), jnp.sin(angles))


def rotate(values, tables, direction):
    halfway = values.shape[-1] // 2
    leading = values[..., :halfway]
    trailing = values[..., halfway:]
    cos_table = tables[0][:, None, :]
    sin_table = tables[1][:, None, :] * direction
    return jnp.concatenate(
        [leading * cos_table - trailing * sin_table, trailing * cos_table + leading * sin_table],
        axis=-1,
    )


def dot(a, b, dims=((1,), (0,))):
    return lax.dot_general(a, b, (dims, ((), ())), preferred_element_type=F32)


def gather_weights(w_qkv, w_out, w_gate_up, w_down, gains, biases, dp, tp):
    def whole(shard):
        return lax.all_gather(shard, ALL, axis=0, tiled=False).reshape((dp, tp) + shard.shape)

    joint = whole(w_qkv).transpose(0, 2, 3, 1, 4)
    joint = joint.reshape(joint.shape[0] * joint.shape[1], 3, -1)
    mix = whole(w_out).transpose(1, 2, 0, 3)
    mix = mix.reshape(mix.shape[0] * mix.shape[1], -1)
    pair = whole(w_gate_up).transpose(0, 2, 3, 1, 4)
    pair = pair.reshape(pair.shape[0] * pair.shape[1], 2, -1)
    back = whole(w_down).transpose(1, 2, 0, 3)
    back = back.reshape(back.shape[0] * back.shape[1], -1)
    gains = lax.all_gather(gains, ("y", "core"), axis=0, tiled=True).astype(F32).reshape(2, -1)
    biases = lax.all_gather(biases, ("y", "core"), axis=0, tiled=True).astype(F32).reshape(2, -1)
    return (joint, mix, pair, back, gains, biases)


def spread_grads(grads, dp, tp):
    joint, mix, pair, back, gains, biases = grads
    width = joint.shape[0]
    joint = joint.reshape(dp, width // dp, 3, tp, -1).transpose(0, 3, 1, 2, 4)
    mix = mix.reshape(tp, -1, dp, width // dp).transpose(2, 0, 1, 3)
    pair = pair.reshape(dp, width // dp, 2, tp, -1).transpose(0, 3, 1, 2, 4)
    back = back.reshape(tp, -1, dp, width // dp).transpose(2, 0, 1, 3)

    def scatter(parts, kind):
        shape = parts.shape[2:]
        flat = parts.reshape((dp * tp,) + shape).astype(kind)
        return lax.psum_scatter(flat, ALL, scatter_dimension=0, tiled=True).reshape(shape).astype(F32)

    def norm(parts):
        return lax.psum_scatter(parts, ALL, scatter_dimension=0, tiled=True)

    return (
        scatter(joint, BF),
        scatter(mix, BF),
        scatter(pair, BF),
        scatter(back, BF),
        norm(gains),
        norm(biases),
    )


def attend(queries, keys, values, allowed):
    scale = HD ** (-0.5)
    scores = jnp.einsum("qhd,khd->hqk", queries, keys, preferred_element_type=F32) * scale
    scores = jnp.where(allowed[None], scores, neg_fill)
    exps = jnp.exp(scores - jnp.max(scores, axis=-1, keepdims=True))
    probs = exps / jnp.sum(exps, axis=-1, keepdims=True)
    probs_low = probs.astype(BF)
    mixed = jnp.einsum("hqk,khd->qhd", probs_low, values, preferred_element_type=F32)
    return mixed.reshape(mixed.shape[0], -1).astype(BF), probs_low


def attend_back(queries, keys, values, probs, grad_mixed):
    scale = HD ** (-0.5)
    grad_mixed = grad_mixed.reshape(queries.shape)
    grad_probs = jnp.einsum("qhd,khd->hqk", grad_mixed, values, preferred_element_type=F32)
    wide = probs.astype(F32)
    inner = jnp.sum(wide * grad_probs, axis=-1, keepdims=True)
    grad_scores = (wide * (grad_probs - inner) * scale).astype(BF)
    grad_queries = jnp.einsum("hqk,khd->qhd", grad_scores, keys, preferred_element_type=F32)
    grad_keys = jnp.einsum("hqk,qhd->khd", grad_scores, queries, preferred_element_type=F32)
    grad_values = jnp.einsum("hqk,qhd->khd", probs, grad_mixed, preferred_element_type=F32)
    return (grad_queries, grad_keys, grad_values)


def layer_forward(inputs_low, weights, allowed, tables):
    w_joint, w_mix, w_pair, w_back, gains, shifts = weights
    rows, width = inputs_low.shape
    joined = dot(inputs_low, w_joint.reshape(width, -1)).reshape(rows, 3, -1, HD)
    queries = rotate(joined[:, 0], tables, 1.0).astype(BF)
    keys = rotate(joined[:, 1], tables, 1.0).astype(BF)
    values = joined[:, 2].astype(BF)
    keys, values = lax.all_gather(jnp.stack([keys, values]), "core", axis=1, tiled=True)
    mixed_low, probs = attend(queries, keys, values, allowed)
    first_sum = inputs_low.astype(F32) + dot(mixed_low, w_mix)
    hidden = layer_norm(first_sum, gains[0], shifts[0])
    hidden_low = hidden.astype(BF)
    gate_up = dot(hidden_low, w_pair.reshape(width, -1)).reshape(rows, 2, -1)
    active_low = gate_act(gate_up).astype(BF)
    second_sum = hidden + dot(active_low, w_back)
    result = layer_norm(second_sum, gains[1], shifts[1])
    kept = (
        inputs_low,
        queries,
        keys,
        values,
        mixed_low,
        probs,
        first_sum,
        hidden_low,
        gate_up,
        active_low,
        second_sum,
    )
    return (result, kept)


def layer_backward(grad_result, kept, weights, tables):
    w_joint, w_mix, w_pair, w_back, gains, shifts = weights
    inputs_low, queries, keys, values, mixed_low, probs, first_sum, hidden_low, gate_up, active_low, second_sum = kept
    rows, width = inputs_low.shape
    unused_out, norm_second = jax.vjp(layer_norm, second_sum, gains[1], shifts[1])
    grad_second, grad_gain_two, grad_shift_two = norm_second(grad_result)
    grad_ffn_low = grad_second.astype(BF)
    grad_active = dot(grad_ffn_low, w_back, ((1,), (1,)))
    grad_w_back = dot(active_low, grad_ffn_low, ((0,), (0,)))
    unused_act, act_back = jax.vjp(gate_act, gate_up)
    grad_pair_low = act_back(grad_active)[0].astype(BF).reshape(rows, -1)
    grad_hidden = grad_second + dot(grad_pair_low, w_pair.reshape(width, -1), ((1,), (1,)))
    grad_w_pair = dot(hidden_low, grad_pair_low, ((0,), (0,)))
    unused_first, norm_first = jax.vjp(layer_norm, first_sum, gains[0], shifts[0])
    grad_first, grad_gain_one, grad_shift_one = norm_first(grad_hidden)
    grad_attn_low = grad_first.astype(BF)
    grad_mixed = dot(grad_attn_low, w_mix, ((1,), (1,))).astype(BF)
    grad_w_mix = dot(mixed_low, grad_attn_low, ((0,), (0,)))
    grad_queries, grad_keys, grad_values = attend_back(queries, keys, values, probs, grad_mixed)
    both = jnp.stack([grad_keys, grad_values]).astype(BF)
    grad_keys, grad_values = lax.psum_scatter(both, "core", scatter_dimension=1, tiled=True).astype(F32)
    grad_queries = rotate(grad_queries, tables, -1.0)
    grad_keys = rotate(grad_keys, tables, -1.0)
    grad_joint_low = jnp.stack([grad_queries, grad_keys, grad_values], axis=1).reshape(rows, -1).astype(BF)
    grad_inputs = grad_first + dot(grad_joint_low, w_joint.reshape(width, -1), ((1,), (1,)))
    grad_w_joint = dot(inputs_low, grad_joint_low, ((0,), (0,)))
    grads = (
        grad_w_joint.reshape(w_joint.shape),
        grad_w_mix,
        grad_w_pair.reshape(w_pair.shape),
        grad_w_back,
        jnp.concatenate([grad_gain_one, grad_gain_two]),
        jnp.concatenate([grad_shift_one, grad_shift_two]),
    )
    return (grad_inputs, grads)


def swap_pairs(tp, step, dp_axes):
    pairs = []
    half = tp // 2
    for core in range(2):
        for at in range(tp):
            source = core * tp + at
            target = (at // half) * tp + half * core + (at + step) % half
            pairs.append((source, target))
    return pairs


def to_sequences(rows, tp):
    half = tp // 2
    at = lax.axis_index("tensor")
    pieces = [None] * half
    got = []
    for step in range(half):
        piece = lax.dynamic_index_in_dim(rows, (at + step) % half, 0, keepdims=False)
        got.append(lax.ppermute(piece, ("core", "tensor"), swap_pairs(tp, step, None)))
    stacked = jnp.stack(got)
    order = (at - jnp.arange(half)) % half
    return jnp.take(stacked, order, axis=0).reshape(-1, rows.shape[-1])


def to_positions(rows, tp):
    half = tp // 2
    at = lax.axis_index("tensor")
    parts = rows.reshape(half, -1, rows.shape[-1])
    got = []
    for step in range(half):
        piece = lax.dynamic_index_in_dim(parts, (at - step) % half, 0, keepdims=False)
        back = [(target, source) for source, target in swap_pairs(tp, step, None)]
        got.append(lax.ppermute(piece, ("core", "tensor"), back))
    stacked = jnp.stack(got)
    order = (at + jnp.arange(half)) % half
    return jnp.take(stacked, (jnp.arange(half) - at) % half, axis=0)


def on_device(dp, tp, tokens, cotangent, lengths, w_qkv, w_out, w_gate_up, w_down, norm_gains, norm_biases):
    section = lax.axis_index("section")
    core = lax.axis_index("core")
    at = lax.axis_index("tensor")
    micro, own, width = tokens.shape
    assert micro * 2 == tp
    length = own * tp
    rows = length // 2
    weights = gather_weights(
        w_qkv[0], w_out[0], w_gate_up[0], w_down[0], norm_gains[0], norm_biases[0], dp, tp
    )
    inputs = to_sequences(tokens, tp)
    grad_top = to_sequences(cotangent, tp)
    chip_lengths = lax.all_gather(lengths, "core", axis=0, tiled=True)
    my_lengths = lax.dynamic_index_in_dim(chip_lengths, at, 0, keepdims=False)
    positions = jnp.arange(length, dtype=jnp.int32)
    segment = jnp.sum((jnp.cumsum(my_lengths)[None, :] <= positions[:, None]).astype(jnp.int32), axis=-1)
    own_positions = core * rows + jnp.arange(rows, dtype=jnp.int32)
    own_segment = lax.dynamic_slice_in_dim(segment, core * rows, rows, 0)
    allowed = own_segment[:, None] == segment[None, :]
    tables = rope_tables(own_positions, HD)

    result, kept = layer_forward(inputs, weights, allowed, tables)
    received = lax.ppermute(result.astype(BF), "section", [(0, 1)])
    inputs = jnp.where(section == 0, inputs, received)
    result, kept = layer_forward(inputs, weights, allowed, tables)
    grad_in, grads = layer_backward(grad_top.astype(F32), kept, weights, tables)
    received = lax.ppermute(grad_in, "section", [(1, 0)])
    grad_top = jnp.where(section == 0, received, grad_top.astype(F32))
    grad_in, grads = layer_backward(grad_top, kept, weights, tables)
    ends = to_positions(jnp.where(section == 0, grad_in, result).astype(BF), tp)
    outs = spread_grads(grads, dp, tp)
    return (ends[None],) + tuple(o[None] for o in outs)


def solution(mesh):
    sections, dp, tp = mesh.devices.shape
    fine = Mesh(mesh.devices.reshape(sections, dp // 2, 2, tp), ("section", "y", "core", "tensor"))
    both = ("y", "core")
    in_specs = (
        P(both, "tensor", None),
        P(both, "tensor", None),
        P(both, None),
        P("section", both, None, "tensor"),
        P("section", "tensor", both),
        P("section", both, None, "tensor"),
        P("section", "tensor", both),
        P("section", both),
        P("section", both),
    )
    out_specs = (
        P("section", both, "tensor", None),
        P("section", both, None, "tensor"),
        P("section", "tensor", both),
        P("section", both, None, "tensor"),
        P("section", "tensor", both),
        P("section", ALL),
        P("section", ALL),
    )
    return jax.shard_map(
        functools.partial(on_device, dp, tp), mesh=fine, in_specs=in_specs, out_specs=out_specs, check_vma=False
    )
```

```python
import functools

import jax
import jax.numpy as jnp
from jax import lax
from jax.experimental import pallas as pl
from jax.experimental.pallas import tpu as pltpu
from jax.sharding import Mesh, PartitionSpec as P

HD = 64
eps = 1e-05
neg_fill = -1e30
ALL = ("y", "core", "tensor")
BF = jnp.bfloat16
F32 = jnp.float32


def dg(a, b, dims):
    return lax.dot_general(a, b, (dims, ((), ())), preferred_element_type=F32)


NN = ((1,), (0,))
NT = ((1,), (1,))
TN = ((0,), (0,))


def low_lanes(shape):
    return lax.broadcasted_iota(jnp.int32, shape, 1) < HD


def swap64(v):
    return pltpu.roll(v, HD, axis=1)


def rope_fwd(t, cos, sin):
    lane = lax.broadcasted_iota(jnp.int32, t.shape, 1) % HD
    other = jnp.where(lane < HD // 2, pltpu.roll(t, 128 - HD // 2, axis=1), pltpu.roll(t, HD // 2, axis=1))
    return t * cos + other * sin


def qkv_kernel(x_ref, w_ref, cos_ref, sin_ref, q_ref, k_ref, v_ref):
    x = x_ref[...]
    width = x.shape[1]
    r = [dg(x, w_ref[:, e, :, :640].reshape(width, 640), NN) for e in range(2)]
    c = [[t[:, 128 * i : 128 * i + 128] for i in range(5)] for t in r]
    low = low_lanes(c[0][0].shape)
    qs = [c[0][0], jnp.where(low, c[0][3], swap64(c[1][3])), c[1][0]]
    ks = [c[0][1], jnp.where(low, swap64(c[0][3]), c[1][3]), c[1][1]]
    vs = [c[0][2], jnp.where(low, c[0][4], swap64(c[1][4])), c[1][2]]
    cos, sin = cos_ref[...], sin_ref[...]
    for i in range(3):
        q_ref[i] = (rope_fwd(qs[i], cos, sin) * HD**-0.5).astype(BF)
        k_ref[i] = rope_fwd(ks[i], cos, sin).astype(BF)
        v_ref[i] = vs[i].astype(BF)


def attn_kernel(q_ref, k_ref, v_ref, ko_ref, vo_ref, m_ref, o_ref, e_ref, l_ref):
    q = q_ref[0]
    k = jnp.concatenate([k_ref[0], ko_ref[0]], axis=0)
    v = jnp.concatenate([v_ref[0], vo_ref[0]], axis=0)
    vt = v.astype(F32).T.astype(BF)
    outs = []
    for h in range(2):
        low = low_lanes(q.shape)
        qm = jnp.where(low if h == 0 else jnp.logical_not(low), q, jnp.zeros_like(q))
        s = dg(k, qm, NT) + m_ref[...]
        e = jnp.exp(s - jnp.max(s, axis=0, keepdims=True))
        inv = 1.0 / jnp.sum(e, axis=0, keepdims=True)
        eb = e.astype(BF)
        e_ref[0, h] = eb
        l_ref[0, h] = jnp.broadcast_to(inv, l_ref.shape[2:])
        outs.append(dg(vt[HD * h : HD * h + HD], eb, NN) * inv)
    o_ref[0] = jnp.concatenate(outs, axis=0).T.astype(BF)


def norm_parts(r):
    center = r - jnp.mean(r, axis=-1, keepdims=True)
    inv = lax.rsqrt(jnp.mean(center * center, axis=-1, keepdims=True) + eps)
    return center * inv, inv


def norm_back(dn, n, inv):
    return inv * (dn - jnp.mean(dn, axis=-1, keepdims=True) - n * jnp.mean(dn * n, axis=-1, keepdims=True))


def out_weight(w_ref):
    c = [[w_ref[:, e, :, 128 * i : 128 * i + 128].reshape(-1, 128) for i in range(2)] for e in range(2)]
    low = low_lanes(c[0][0].shape)
    mid = jnp.where(low, swap64(c[0][0].astype(F32)), c[1][0].astype(F32)).astype(BF)
    return [c[0][1], mid, c[1][1]]


def ffn_kernel(x_ref, o_ref, wo_ref, wgu_ref, wd_ref, g_ref, b_ref, y_ref, gu_ref, n1_ref, i1_ref, n2_ref, i2_ref, h_ref, hb_ref, acc_ref):
    z = pl.program_id(0)
    width = x_ref.shape[1]

    @pl.when(z == 0)
    def _():
        r = x_ref[...].astype(F32)
        for p in range(2):
            w = jnp.concatenate(out_weight(wo_ref.at[:, 2 * p : 2 * p + 2]), axis=1)
            o = jnp.concatenate([o_ref[3 * p + i] for i in range(3)], axis=1)
            r = r + dg(o, w, NT)
        n, inv = norm_parts(r)
        n1_ref[...] = n
        i1_ref[...] = jnp.broadcast_to(inv, i1_ref.shape)
        h = n * g_ref[0:1] + b_ref[0:1]
        h_ref[...] = h
        hb_ref[...] = h.astype(BF)

    hb = hb_ref[...]
    w = wgu_ref[:, 0].reshape(width, -1)
    half = w.shape[1] // 2
    gate = dg(hb, w[:, :half], NN)
    up = dg(hb, w[:, half:], NN)
    gu_ref[0, 0] = gate.astype(BF)
    gu_ref[0, 1] = up.astype(BF)
    act = (gate / (1.0 + jnp.exp(-gate)) * up).astype(BF)
    part = dg(act, wd_ref[:, 0].reshape(width, -1), NT)

    @pl.when(z == 0)
    def _():
        acc_ref[...] = h_ref[...] + part

    @pl.when(z > 0)
    def _():
        acc_ref[...] += part

    @pl.when(z == pl.num_programs(0) - 1)
    def _():
        n, inv = norm_parts(acc_ref[...])
        n2_ref[...] = n
        i2_ref[...] = jnp.broadcast_to(inv, i2_ref.shape)
        y_ref[...] = (n * g_ref[1:2] + b_ref[1:2]).astype(BF)


def ffn_back_kernel(dy_ref, n1_ref, i1_ref, n2_ref, i2_ref, gu_ref, wgu_ref, wd_ref, g_ref, b_ref, ggu_ref, gd_ref, dr1_ref, da_ref, ng_ref, hb_ref, df_ref, acc_ref):
    z = pl.program_id(0)
    width = dy_ref.shape[1]

    @pl.when(z == 0)
    def _():
        dy = dy_ref[...].astype(F32)
        n = n2_ref[...]
        ng_ref[1:2] = jnp.sum(dy * n, axis=0, keepdims=True)
        ng_ref[3:4] = jnp.sum(dy, axis=0, keepdims=True)
        dr2 = norm_back(dy * g_ref[1:2], n, i2_ref[:, :1])
        acc_ref[...] = dr2
        df_ref[...] = dr2.astype(BF)
        hb_ref[...] = (n1_ref[...] * g_ref[0:1] + b_ref[0:1]).astype(BF)

    df = df_ref[...]
    gate = gu_ref[0, 0].astype(F32)
    up = gu_ref[0, 1].astype(F32)
    s = 1.0 / (1.0 + jnp.exp(-gate))
    silu = gate * s
    act = (silu * up).astype(BF)
    gd_ref[:, 0] = dg(df, act, TN).astype(BF).reshape(gd_ref.shape[0], -1, act.shape[1])
    d_act = dg(df, wd_ref[:, 0].reshape(width, -1), NN)
    d_gate = (d_act * up * (s * (1.0 + gate * (1.0 - s)))).astype(BF)
    d_up = (d_act * silu).astype(BF)
    half = d_up.shape[1]
    hb = hb_ref[...]
    ggu_ref[:, 0, :, :half] = dg(hb, d_gate, TN).astype(BF).reshape(ggu_ref.shape[0], -1, half)
    ggu_ref[:, 0, :, half:] = dg(hb, d_up, TN).astype(BF).reshape(ggu_ref.shape[0], -1, half)
    w = wgu_ref[:, 0].reshape(width, -1)
    acc_ref[...] += dg(d_gate, w[:, :half], NT) + dg(d_up, w[:, half:], NT)

    @pl.when(z == pl.num_programs(0) - 1)
    def _():
        dh = acc_ref[...]
        n = n1_ref[...]
        ng_ref[0:1] = jnp.sum(dh * n, axis=0, keepdims=True)
        ng_ref[2:3] = jnp.sum(dh, axis=0, keepdims=True)
        dr1 = norm_back(dh * g_ref[0:1], n, i1_ref[:, :1])
        dr1_ref[...] = dr1
        da_ref[...] = dr1.astype(BF)


def attn_back_kernel(da_ref, wo_ref, o_ref, q_ref, k_ref, v_ref, ko_ref, vo_ref, e_ref, l_ref, cos_ref, sin_ref, dq_ref, own_ref, oth_ref, dwo_ref):
    da = da_ref[...]
    rows = da.shape[0]
    w = jnp.concatenate(out_weight(wo_ref), axis=1)
    do3 = dg(da, w, NN).astype(BF)
    o3 = jnp.concatenate([o_ref[i] for i in range(3)], axis=1)
    dwo_ref[0] = dg(da, o3, TN).astype(BF)
    cos, sin = cos_ref[...], sin_ref[...]
    for i in range(3):
        dot = do3[:, 128 * i : 128 * i + 128].astype(F32).T
        ot = o_ref[i].astype(F32).T
        k = jnp.concatenate([k_ref[i], ko_ref[i]], axis=0)
        v = jnp.concatenate([v_ref[i], vo_ref[i]], axis=0)
        kt = k.astype(F32).T.astype(BF)
        qt = q_ref[i].astype(F32).T.astype(BF)
        dqs, dks, dvs = [], [], []
        for h in range(2):
            span = slice(HD * h, HD * h + HD)
            scaled = dot[span] * l_ref[i, h, 0:1]
            inner = jnp.sum(scaled * ot[span], axis=0, keepdims=True)
            sb = scaled.astype(BF)
            zero = jnp.zeros_like(sb)
            padded = jnp.concatenate([sb, zero] if h == 0 else [zero, sb], axis=0)
            dp = dg(v, padded, NN)
            et = e_ref[i, h]
            ds = (et.astype(F32) * (dp - inner)).astype(BF)
            dvs.append(dg(sb, et, NT))
            dks.append(dg(qt[span], ds, NT))
            dqt = dg(kt[span], ds, NN) * HD**-0.5
            d1, d2 = dqt[: HD // 2], dqt[HD // 2 :]
            dqs.append(d1 * cos + d2 * sin)
            dqs.append(d2 * cos - d1 * sin)
        dq_ref[i] = jnp.concatenate(dqs, axis=0).T.astype(BF)
        dk = jnp.concatenate(dks, axis=0)
        dv = jnp.concatenate(dvs, axis=0)
        own_ref[i, 0] = dk[:, :rows]
        own_ref[i, 1] = dv[:, :rows]
        oth_ref[i, 0] = dk[:, rows:].astype(BF)
        oth_ref[i, 1] = dv[:, rows:].astype(BF)


def joint_back_kernel(x_ref, w_ref, dr1_ref, dq_ref, own_ref, got_ref, dwo_ref, cos_ref, sin_ref, g_ref, dz_ref):
    p = pl.program_id(0)
    x = x_ref[...]
    width = x.shape[1]
    cos, sin = cos_ref[...], sin_ref[...]
    dq = [dq_ref[i].astype(F32) for i in range(3)]
    dk, dv = [], []
    for i in range(3):
        t = own_ref[i, 0] + got_ref[i, 0].astype(F32)
        parts = []
        for h in range(2):
            d1 = t[HD * h : HD * h + HD // 2]
            d2 = t[HD * h + HD // 2 : HD * h + HD]
            parts += [d1 * cos + d2 * sin, d2 * cos - d1 * sin]
        dk.append(jnp.concatenate(parts, axis=0).T)
        dv.append((own_ref[i, 1] + got_ref[i, 1].astype(F32)).T)
    low = low_lanes(dq[0].shape)
    zero = jnp.zeros_like(dv[1])
    d = [
        [dq[0], dk[0], dv[0], jnp.where(low, dq[1], swap64(dk[1])), jnp.where(low, dv[1], zero)],
        [dq[2], dk[2], dv[2], jnp.where(low, swap64(dq[1]), dk[1]), jnp.where(low, swap64(dv[1]), zero)],
    ]
    acc = None
    wlow = low_lanes((width, 128))
    mid = dwo_ref[0, :, 128:256].astype(F32)
    sides = [dwo_ref[0, :, 0:128], dwo_ref[0, :, 256:384]]
    mids = [swap64(mid), mid]
    for e in range(2):
        b = jnp.concatenate(d[e], axis=1).astype(BF)
        t = dg(b, w_ref[:, e, :, :640].reshape(width, 640), NT)
        acc = t if acc is None else acc + t
        g = dg(x, b, TN)
        blocks = g_ref.shape[0]
        g_ref[:, e, :, :512] = g[:, :512].astype(BF).reshape(blocks, -1, 512)
        g_ref[:, e, :, 512:640] = jnp.where(wlow, g[:, 512:], mids[e]).astype(BF).reshape(blocks, -1, 128)
        g_ref[:, e, :, 640:] = sides[e].reshape(blocks, -1, 128)

    @pl.when(p == 0)
    def _():
        dz_ref[...] = dr1_ref[...] + acc

    @pl.when(p > 0)
    def _():
        dz_ref[...] += acc


BIG = pltpu.CompilerParams(vmem_limit_bytes=58 << 20)
VM = pltpu.VMEM


def full(shape):
    return pl.BlockSpec(shape, lambda i: (0,) * len(shape))


def lead(shape, at=0):
    return pl.BlockSpec(shape, lambda i: tuple(i if j == at else 0 for j in range(len(shape))))


def sds(shape, kind):
    return jax.ShapeDtypeStruct(shape, kind)


def forward(x, weights, norms, mask, tabs):
    w1, w2, w3 = weights
    gains, biases = norms
    rows, width = x.shape
    heads = width // 128
    blocks, tp, depth = w1.shape[:3]
    steps = tp // 2
    cos, sin, cost, sint = tabs
    q, k, v = pl.pallas_call(
        qkv_kernel,
        grid=(steps,),
        in_specs=[full((rows, width)), lead((blocks, 2, depth, 768), 1), full((rows, 128)), full((rows, 128))],
        out_specs=[lead((3, rows, 128))] * 3,
        out_shape=[sds((heads, rows, 128), BF)] * 3,
        compiler_params=BIG,
        name="qkv",
    )(x, w1, cos, sin)
    ko, vo = lax.ppermute((k, v), "core", [(0, 1), (1, 0)])
    pair = lead((1, rows, 128))
    o, e, l = pl.pallas_call(
        attn_kernel,
        grid=(heads,),
        in_specs=[pair] * 5 + [full((2 * rows, rows))],
        out_specs=[pair, lead((1, 2, 2 * rows, rows)), lead((1, 2, 8, rows))],
        out_shape=[sds((heads, rows, 128), BF), sds((heads, 2, 2 * rows, rows), BF), sds((heads, 2, 8, rows), F32)],
        compiler_params=BIG,
        name="attn",
    )(q, k, v, ko, vo, mask)
    hidden = w2.shape[3] // 2
    y, gu, n1, i1, n2, i2 = pl.pallas_call(
        ffn_kernel,
        grid=(tp,),
        in_specs=[
            full((rows, width)),
            full((heads, rows, 128)),
            pl.BlockSpec((blocks, tp, depth, 256), lambda i: (0, 0, 0, 2)),
            lead((blocks, 1, depth, 2 * hidden), 1),
            lead((blocks, 1, depth, hidden), 1),
            full((2, width)),
            full((2, width)),
        ],
        out_specs=[full((rows, width)), lead((1, 2, rows, hidden))] + [full((rows, width)), full((rows, 128))] * 2,
        out_shape=[sds((rows, width), BF), sds((tp, 2, rows, hidden), BF)] + [sds((rows, width), F32), sds((rows, 128), F32)] * 2,
        scratch_shapes=[VM((rows, width), F32), VM((rows, width), BF), VM((rows, width), F32)],
        compiler_params=BIG,
        name="ffn",
    )(x, o, w1, w2, w3, gains, biases)
    return y, (q, k, v, ko, vo, o, e, l, gu, n1, i1, n2, i2)


def backward(x, dy, kept, weights, norms, tabs):
    w1, w2, w3 = weights
    gains, biases = norms
    q, k, v, ko, vo, o, e, l, gu, n1, i1, n2, i2 = kept
    rows, width = x.shape
    heads = width // 128
    blocks, tp, depth = w1.shape[:3]
    steps = tp // 2
    hidden = w2.shape[3] // 2
    cos, sin, cost, sint = tabs
    whole, stat = full((rows, width)), full((rows, 128))
    g2, g3, dr1, da, ng = pl.pallas_call(
        ffn_back_kernel,
        grid=(tp,),
        in_specs=[
            whole, whole, stat, whole, stat,
            lead((1, 2, rows, hidden)),
            lead((blocks, 1, depth, 2 * hidden), 1),
            lead((blocks, 1, depth, hidden), 1),
            full((2, width)), full((2, width)),
        ],
        out_specs=[
            lead((blocks, 1, depth, 2 * hidden), 1),
            lead((blocks, 1, depth, hidden), 1),
            whole, whole, full((8, width)),
        ],
        out_shape=[sds(w2.shape, BF), sds(w3.shape, BF), sds((rows, width), F32), sds((rows, width), BF), sds((8, width), F32)],
        scratch_shapes=[VM((rows, width), BF), VM((rows, width), BF), VM((rows, width), F32)],
        compiler_params=BIG,
        name="ffn_back",
    )(dy, n1, i1, n2, i2, gu, w2, w3, gains, biases)
    three = lead((3, rows, 128))
    dq, own, oth, dwo = pl.pallas_call(
        attn_back_kernel,
        grid=(steps,),
        in_specs=[
            whole,
            pl.BlockSpec((blocks, 2, depth, 256), lambda i: (0, i, 0, 2)),
            three, three, three, three, three, three,
            lead((3, 2, 2 * rows, rows)),
            lead((3, 2, 8, rows)),
            full((HD // 2, rows)), full((HD // 2, rows)),
        ],
        out_specs=[three, lead((3, 2, 128, rows)), lead((3, 2, 128, rows)), lead((1, width, 384))],
        out_shape=[
            sds((heads, rows, 128), BF),
            sds((heads, 2, 128, rows), F32),
            sds((heads, 2, 128, rows), BF),
            sds((steps, width, 384), BF),
        ],
        compiler_params=BIG,
        name="attn_back",
    )(da, w1, o, q, k, v, ko, vo, e, l, cost, sint)
    got = lax.ppermute(oth, "core", [(0, 1), (1, 0)])
    g1, dz = pl.pallas_call(
        joint_back_kernel,
        grid=(steps,),
        in_specs=[
            whole,
            lead((blocks, 2, depth, 768), 1),
            whole, three,
            lead((3, 2, 128, rows)), lead((3, 2, 128, rows)),
            lead((1, width, 384)),
            full((HD // 2, rows)), full((HD // 2, rows)),
        ],
        out_specs=[lead((blocks, 2, depth, 768), 1), whole],
        out_shape=[sds(w1.shape, BF), sds((rows, width), F32)],
        compiler_params=BIG,
        name="joint_back",
    )(x, w1, dr1, dq, own, got, dwo, cost, sint)
    return dz, (g1, g2, g3, ng)


def swap_pairs(tp, step, dp_axes):
    pairs = []
    half = tp // 2
    for core in range(2):
        for at in range(tp):
            source = core * tp + at
            target = (at // half) * tp + half * core + (at + step) % half
            pairs.append((source, target))
    return pairs


def to_sequences(rows, tp):
    half = tp // 2
    at = lax.axis_index("tensor")
    pieces = [None] * half
    got = []
    for step in range(half):
        piece = lax.dynamic_index_in_dim(rows, (at + step) % half, 0, keepdims=False)
        got.append(lax.ppermute(piece, ("core", "tensor"), swap_pairs(tp, step, None)))
    stacked = jnp.stack(got)
    order = (at - jnp.arange(half)) % half
    return jnp.take(stacked, order, axis=0).reshape(-1, rows.shape[-1])


def to_positions(rows, tp):
    half = tp // 2
    at = lax.axis_index("tensor")
    parts = rows.reshape(half, -1, rows.shape[-1])
    got = []
    for step in range(half):
        piece = lax.dynamic_index_in_dim(parts, (at - step) % half, 0, keepdims=False)
        back = [(target, source) for source, target in swap_pairs(tp, step, None)]
        got.append(lax.ppermute(piece, ("core", "tensor"), back))
    stacked = jnp.stack(got)
    order = (at + jnp.arange(half)) % half
    return jnp.take(stacked, (jnp.arange(half) - at) % half, axis=0)


def rope_tables(positions):
    halfway = HD // 2
    freqs = 1000.0 ** (-jnp.arange(halfway, dtype=F32) / halfway)
    angles = positions.astype(F32)[:, None] * freqs[None, :]
    cos, sin = jnp.cos(angles), jnp.sin(angles)
    wide = jnp.concatenate([cos] * 4, axis=1)
    signed = jnp.concatenate([-sin, sin] * 2, axis=1)
    return wide, signed, cos.T, sin.T


def pack_shard(w_qkv, w_out, w_gate_up, w_down):
    rows = w_qkv.shape[0]
    odd = lax.axis_index("tensor") % 2 == 1
    heads = w_qkv.reshape(rows, 3, 3, HD)
    mine = w_out.T.reshape(rows, 3, HD)
    heads = jnp.where(odd, jnp.roll(heads, -1, axis=2), heads)
    mine = jnp.where(odd, jnp.roll(mine, -1, axis=1), mine)
    first = jnp.concatenate(
        [heads[:, :, :2].reshape(rows, -1), heads[:, :, 2].reshape(rows, -1), mine[:, 2], mine[:, :2].reshape(rows, -1)], axis=1
    )
    return first, w_gate_up.reshape(rows, -1), w_down.T


def unpack_shard(first, pair, down):
    rows = first.shape[0]
    odd = lax.axis_index("tensor") % 2 == 1
    both = first[:, :384].reshape(rows, 3, 2, HD)
    single = first[:, 384:576].reshape(rows, 3, 1, HD)
    heads = jnp.concatenate([both, single], axis=2)
    mine = jnp.concatenate([first[:, 640:].reshape(rows, 2, HD), first[:, 576:640].reshape(rows, 1, HD)], axis=1)
    heads = jnp.where(odd, jnp.roll(heads, 1, axis=2), heads)
    mine = jnp.where(odd, jnp.roll(mine, 1, axis=1), mine)
    return (
        heads.reshape(rows, 3, -1),
        mine.reshape(rows, -1).T,
        pair.reshape(rows, 2, -1),
        down.T,
    )


BLOCKS = 4


def gather_shard(shard, dp, tp):
    rows, columns = shard.shape
    got = lax.all_gather(shard, ALL, axis=0, tiled=False)
    got = got.reshape(BLOCKS, dp // BLOCKS, tp, rows, columns)
    return got.transpose(0, 2, 1, 3, 4).reshape(BLOCKS, tp, -1, columns)


def scatter_sum(whole, dp, tp):
    columns = whole.shape[3]
    parts = whole.reshape(BLOCKS, tp, dp // BLOCKS, -1, columns).transpose(0, 2, 1, 3, 4)
    parts = parts.reshape(dp * tp, -1, columns)
    return lax.psum_scatter(parts, ALL, scatter_dimension=0, tiled=False).astype(F32)


def on_device(dp, tp, tokens, cotangent, lengths, w_qkv, w_out, w_gate_up, w_down, norm_gains, norm_biases):
    section = lax.axis_index("section")
    core = lax.axis_index("core")
    at = lax.axis_index("tensor")
    micro, own, width = tokens.shape
    assert micro * 2 == tp
    length = own * tp
    rows = length // 2
    shards = pack_shard(w_qkv[0], w_out[0], w_gate_up[0], w_down[0])
    weights = tuple(gather_shard(s, dp, tp) for s in shards)
    norms = jnp.concatenate([norm_gains, norm_biases])
    norms = lax.all_gather(norms, ("y", "core"), axis=1, tiled=True).astype(F32)
    norms = (norms[0].reshape(2, width), norms[1].reshape(2, width))
    tokens = to_sequences(tokens, tp)
    grad_top = to_sequences(cotangent, tp)
    chip_lengths = lax.all_gather(lengths, "core", axis=0, tiled=True)
    my_lengths = lax.dynamic_index_in_dim(chip_lengths, at, 0, keepdims=False)
    near = core * rows + jnp.arange(rows, dtype=jnp.int32)
    far = (1 - core) * rows + jnp.arange(rows, dtype=jnp.int32)
    ends_at = jnp.cumsum(my_lengths)

    def segment(positions):
        return jnp.sum((ends_at[None, :] <= positions[:, None]).astype(jnp.int32), axis=-1)

    seg_near = segment(near)
    seg_all = jnp.concatenate([seg_near, segment(far)])
    mask = jnp.where(seg_all[:, None] == seg_near[None, :], 0.0, neg_fill).astype(F32)
    tabs = rope_tables(near)

    y, kept = forward(tokens, weights, norms, mask, tabs)
    received = lax.ppermute(y, "section", [(0, 1)])
    inputs = jnp.where(section == 0, tokens, received)
    y, kept = forward(inputs, weights, norms, mask, tabs)
    dz, grads = backward(inputs, grad_top.astype(F32), kept, weights, norms, tabs)
    received = lax.ppermute(dz, "section", [(1, 0)])
    dy = jnp.where(section == 0, received, grad_top.astype(F32))
    dz, grads = backward(inputs, dy, kept, weights, norms, tabs)
    ends = to_positions(jnp.where(section == 0, dz.astype(BF), y), tp)
    sums = [scatter_sum(g, dp, tp) for g in grads[:3]]
    outs = unpack_shard(*sums)
    ng = grads[3]
    gains = lax.psum_scatter(ng[0:2].reshape(-1), ALL, scatter_dimension=0, tiled=True)
    biases = lax.psum_scatter(ng[2:4].reshape(-1), ALL, scatter_dimension=0, tiled=True)
    return (ends[None],) + tuple(t[None] for t in outs + (gains, biases))


def solution(mesh):
    sections, dp, tp = mesh.devices.shape
    fine = Mesh(mesh.devices.reshape(sections, dp // 2, 2, tp), ("section", "y", "core", "tensor"))
    both = ("y", "core")
    in_specs = (
        P(both, "tensor", None),
        P(both, "tensor", None),
        P(both, None),
        P("section", both, None, "tensor"),
        P("section", "tensor", both),
        P("section", both, None, "tensor"),
        P("section", "tensor", both),
        P("section", both),
        P("section", both),
    )
    out_specs = (
        P("section", both, "tensor", None),
        P("section", both, None, "tensor"),
        P("section", "tensor", both),
        P("section", both, None, "tensor"),
        P("section", "tensor", both),
        P("section", ALL),
        P("section", ALL),
    )
    return jax.shard_map(
        functools.partial(on_device, dp, tp), mesh=fine, in_specs=in_specs, out_specs=out_specs, check_vma=False
    )
```

```python
import functools

import jax
import jax.numpy as jnp
from jax import lax
from jax.experimental import pallas as pl
from jax.experimental.pallas import tpu as pltpu
from jax.sharding import Mesh, PartitionSpec as P

HD = 64
eps = 1e-05
neg_fill = -1e30
ALL = ("y", "core", "tensor")
BF = jnp.bfloat16
F32 = jnp.float32
MESH = pl.DeviceIdType.MESH


def dg(a, b, dims):
    return lax.dot_general(a, b, (dims, ((), ())), preferred_element_type=F32)


NN = ((1,), (0,))
NT = ((1,), (1,))
TN = ((0,), (0,))


def low_lanes(shape):
    return lax.broadcasted_iota(jnp.int32, shape, 1) < HD


def swap64(v):
    return pltpu.roll(v, HD, axis=1)


def rope_fwd(t, cos, sin):
    lane = lax.broadcasted_iota(jnp.int32, t.shape, 1) % HD
    other = jnp.where(lane < HD // 2, pltpu.roll(t, 128 - HD // 2, axis=1), pltpu.roll(t, HD // 2, axis=1))
    return t * cos + other * sin


def qkv_kernel(x_ref, w_ref, cos_ref, sin_ref, q_ref, k_ref, v_ref):
    x = x_ref[...]
    width = x.shape[1]
    r = [dg(x, w_ref[:, e, :, :640].reshape(width, 640), NN) for e in range(2)]
    c = [[t[:, 128 * i : 128 * i + 128] for i in range(5)] for t in r]
    low = low_lanes(c[0][0].shape)
    qs = [c[0][0], jnp.where(low, c[0][3], swap64(c[1][3])), c[1][0]]
    ks = [c[0][1], jnp.where(low, swap64(c[0][3]), c[1][3]), c[1][1]]
    vs = [c[0][2], jnp.where(low, c[0][4], swap64(c[1][4])), c[1][2]]
    cos, sin = cos_ref[...], sin_ref[...]
    for i in range(3):
        q_ref[i] = (rope_fwd(qs[i], cos, sin) * HD**-0.5).astype(BF)
        k_ref[i] = rope_fwd(ks[i], cos, sin).astype(BF)
        v_ref[i] = vs[i].astype(BF)


def attn_kernel(q_ref, k_ref, v_ref, ko_ref, vo_ref, m_ref, o_ref, e_ref, l_ref):
    q = q_ref[0]
    k = jnp.concatenate([k_ref[0], ko_ref[0]], axis=0)
    v = jnp.concatenate([v_ref[0], vo_ref[0]], axis=0)
    vt = v.astype(F32).T.astype(BF)
    outs = []
    for h in range(2):
        low = low_lanes(q.shape)
        qm = jnp.where(low if h == 0 else jnp.logical_not(low), q, jnp.zeros_like(q))
        s = dg(k, qm, NT) + m_ref[...]
        e = jnp.exp(s - jnp.max(s, axis=0, keepdims=True))
        inv = 1.0 / jnp.sum(e, axis=0, keepdims=True)
        eb = e.astype(BF)
        e_ref[0, h] = eb
        l_ref[0, h] = jnp.broadcast_to(inv, l_ref.shape[2:])
        outs.append(dg(vt[HD * h : HD * h + HD], eb, NN) * inv)
    o_ref[0] = jnp.concatenate(outs, axis=0).T.astype(BF)


def norm_parts(r):
    center = r - jnp.mean(r, axis=-1, keepdims=True)
    inv = lax.rsqrt(jnp.mean(center * center, axis=-1, keepdims=True) + eps)
    return center * inv, inv


def norm_back(dn, n, inv):
    return inv * (dn - jnp.mean(dn, axis=-1, keepdims=True) - n * jnp.mean(dn * n, axis=-1, keepdims=True))


def out_weight(w_ref):
    c = [[w_ref[:, e, :, 128 * i : 128 * i + 128].reshape(-1, 128) for i in range(2)] for e in range(2)]
    low = low_lanes(c[0][0].shape)
    mid = jnp.where(low, swap64(c[0][0].astype(F32)), c[1][0].astype(F32)).astype(BF)
    return [c[0][1], mid, c[1][1]]


def ffn_kernel(x_ref, o_ref, wo_ref, wgu_ref, wd_ref, g_ref, b_ref, y_ref, gu_ref, n1_ref, i1_ref, n2_ref, i2_ref, h_ref, hb_ref, acc_ref):
    z = pl.program_id(0)
    width = x_ref.shape[1]

    @pl.when(z == 0)
    def _():
        r = x_ref[...].astype(F32)
        for p in range(2):
            w = jnp.concatenate(out_weight(wo_ref.at[:, 2 * p : 2 * p + 2]), axis=1)
            o = jnp.concatenate([o_ref[3 * p + i] for i in range(3)], axis=1)
            r = r + dg(o, w, NT)
        n, inv = norm_parts(r)
        n1_ref[...] = n
        i1_ref[...] = jnp.broadcast_to(inv, i1_ref.shape)
        h = n * g_ref[0:1] + b_ref[0:1]
        h_ref[...] = h
        hb_ref[...] = h.astype(BF)

    hb = hb_ref[...]
    w = wgu_ref[:, 0].reshape(width, -1)
    half = w.shape[1] // 2
    gate = dg(hb, w[:, :half], NN)
    up = dg(hb, w[:, half:], NN)
    gu_ref[0, 0] = gate.astype(BF)
    gu_ref[0, 1] = up.astype(BF)
    act = (gate / (1.0 + jnp.exp(-gate)) * up).astype(BF)
    part = dg(act, wd_ref[:, 0].reshape(width, -1), NT)

    @pl.when(z == 0)
    def _():
        acc_ref[...] = h_ref[...] + part

    @pl.when(z > 0)
    def _():
        acc_ref[...] += part

    @pl.when(z == pl.num_programs(0) - 1)
    def _():
        n, inv = norm_parts(acc_ref[...])
        n2_ref[...] = n
        i2_ref[...] = jnp.broadcast_to(inv, i2_ref.shape)
        y_ref[...] = (n * g_ref[1:2] + b_ref[1:2]).astype(BF)


def ffn_back_kernel(dy_ref, n1_ref, i1_ref, n2_ref, i2_ref, gu_ref, wgu_ref, wd_ref, g_ref, b_ref, g_out, dr1_ref, da_ref, ng_ref, hb_ref, df_ref, acc_ref):
    z = pl.program_id(0)
    width = dy_ref.shape[1]

    @pl.when(z == 0)
    def _():
        dy = dy_ref[...].astype(F32)
        n = n2_ref[...]
        ng_ref[1:2] = jnp.sum(dy * n, axis=0, keepdims=True)
        ng_ref[3:4] = jnp.sum(dy, axis=0, keepdims=True)
        dr2 = norm_back(dy * g_ref[1:2], n, i2_ref[:, :1])
        acc_ref[...] = dr2
        df_ref[...] = dr2.astype(BF)
        hb_ref[...] = (n1_ref[...] * g_ref[0:1] + b_ref[0:1]).astype(BF)

    df = df_ref[...]
    gate = gu_ref[0, 0].astype(F32)
    up = gu_ref[0, 1].astype(F32)
    s = 1.0 / (1.0 + jnp.exp(-gate))
    silu = gate * s
    act = (silu * up).astype(BF)
    half = act.shape[1]
    blocks = g_out.shape[0]
    g_out[:, 0, :, 3 * half :] = dg(df, act, TN).astype(BF).reshape(blocks, -1, half)
    d_act = dg(df, wd_ref[:, 0].reshape(width, -1), NN)
    d_gate = (d_act * up * (s * (1.0 + gate * (1.0 - s)))).astype(BF)
    d_up = (d_act * silu).astype(BF)
    hb = hb_ref[...]
    g_out[:, 0, :, :half] = dg(hb, d_gate, TN).astype(BF).reshape(blocks, -1, half)
    g_out[:, 0, :, half : 2 * half] = dg(hb, d_up, TN).astype(BF).reshape(blocks, -1, half)
    w = wgu_ref[:, 0].reshape(width, -1)
    acc_ref[...] += dg(d_gate, w[:, :half], NT) + dg(d_up, w[:, half:], NT)

    @pl.when(z == pl.num_programs(0) - 1)
    def _():
        dh = acc_ref[...]
        n = n1_ref[...]
        ng_ref[0:1] = jnp.sum(dh * n, axis=0, keepdims=True)
        ng_ref[2:3] = jnp.sum(dh, axis=0, keepdims=True)
        dr1 = norm_back(dh * g_ref[0:1], n, i1_ref[:, :1])
        dr1_ref[...] = dr1
        da_ref[...] = dr1.astype(BF)


def attn_back_kernel(da_ref, wo_ref, o_ref, q_ref, k_ref, v_ref, ko_ref, vo_ref, e_ref, l_ref, cos_ref, sin_ref, dq_ref, own_ref, oth_ref, dwo_ref):
    da = da_ref[...]
    rows = da.shape[0]
    w = jnp.concatenate(out_weight(wo_ref), axis=1)
    do3 = dg(da, w, NN).astype(BF)
    o3 = jnp.concatenate([o_ref[i] for i in range(3)], axis=1)
    dwo_ref[0] = dg(da, o3, TN).astype(BF)
    cos, sin = cos_ref[...], sin_ref[...]
    for i in range(3):
        dot = do3[:, 128 * i : 128 * i + 128].astype(F32).T
        ot = o_ref[i].astype(F32).T
        k = jnp.concatenate([k_ref[i], ko_ref[i]], axis=0)
        v = jnp.concatenate([v_ref[i], vo_ref[i]], axis=0)
        kt = k.astype(F32).T.astype(BF)
        qt = q_ref[i].astype(F32).T.astype(BF)
        dqs, dks, dvs = [], [], []
        for h in range(2):
            span = slice(HD * h, HD * h + HD)
            scaled = dot[span] * l_ref[i, h, 0:1]
            inner = jnp.sum(scaled * ot[span], axis=0, keepdims=True)
            sb = scaled.astype(BF)
            zero = jnp.zeros_like(sb)
            padded = jnp.concatenate([sb, zero] if h == 0 else [zero, sb], axis=0)
            dp = dg(v, padded, NN)
            et = e_ref[i, h]
            ds = (et.astype(F32) * (dp - inner)).astype(BF)
            dvs.append(dg(sb, et, NT))
            dks.append(dg(qt[span], ds, NT))
            dqt = dg(kt[span], ds, NN) * HD**-0.5
            d1, d2 = dqt[: HD // 2], dqt[HD // 2 :]
            dqs.append(d1 * cos + d2 * sin)
            dqs.append(d2 * cos - d1 * sin)
        dq_ref[i] = jnp.concatenate(dqs, axis=0).T.astype(BF)
        dk = jnp.concatenate(dks, axis=0)
        dv = jnp.concatenate(dvs, axis=0)
        own_ref[i, 0] = dk[:, :rows]
        own_ref[i, 1] = dv[:, :rows]
        oth_ref[i, 0] = dk[:, rows:].astype(BF)
        oth_ref[i, 1] = dv[:, rows:].astype(BF)


def joint_back_kernel(old_ref, x_ref, w_ref, dr1_ref, dq_ref, own_ref, got_ref, dwo_ref, cos_ref, sin_ref, g_ref, dz_ref):
    p = pl.program_id(0)
    x = x_ref[...]
    width = x.shape[1]
    cos, sin = cos_ref[...], sin_ref[...]
    dq = [dq_ref[i].astype(F32) for i in range(3)]
    dk, dv = [], []
    for i in range(3):
        t = own_ref[i, 0] + got_ref[i, 0].astype(F32)
        parts = []
        for h in range(2):
            d1 = t[HD * h : HD * h + HD // 2]
            d2 = t[HD * h + HD // 2 : HD * h + HD]
            parts += [d1 * cos + d2 * sin, d2 * cos - d1 * sin]
        dk.append(jnp.concatenate(parts, axis=0).T)
        dv.append((own_ref[i, 1] + got_ref[i, 1].astype(F32)).T)
    low = low_lanes(dq[0].shape)
    zero = jnp.zeros_like(dv[1])
    d = [
        [dq[0], dk[0], dv[0], jnp.where(low, dq[1], swap64(dk[1])), jnp.where(low, dv[1], zero)],
        [dq[2], dk[2], dv[2], jnp.where(low, swap64(dq[1]), dk[1]), jnp.where(low, swap64(dv[1]), zero)],
    ]
    acc = None
    wlow = low_lanes((width, 128))
    mid = dwo_ref[0, :, 128:256].astype(F32)
    sides = [dwo_ref[0, :, 0:128], dwo_ref[0, :, 256:384]]
    mids = [swap64(mid), mid]
    for e in range(2):
        b = jnp.concatenate(d[e], axis=1).astype(BF)
        t = dg(b, w_ref[:, e, :, :640].reshape(width, 640), NT)
        acc = t if acc is None else acc + t
        g = dg(x, b, TN)
        blocks = g_ref.shape[0]
        g_ref[:, e, :, :512] = g[:, :512].astype(BF).reshape(blocks, -1, 512)
        g_ref[:, e, :, 512:640] = jnp.where(wlow, g[:, 512:], mids[e]).astype(BF).reshape(blocks, -1, 128)
        g_ref[:, e, :, 640:] = sides[e].reshape(blocks, -1, 128)

    @pl.when(p == 0)
    def _():
        dz_ref[...] = dr1_ref[...] + acc

    @pl.when(p > 0)
    def _():
        dz_ref[...] += acc


BIG = pltpu.CompilerParams(vmem_limit_bytes=58 << 20)
VM = pltpu.VMEM


def full(shape):
    return pl.BlockSpec(shape, lambda i: (0,) * len(shape))


def lead(shape, at=0):
    return pl.BlockSpec(shape, lambda i: tuple(i if j == at else 0 for j in range(len(shape))))


def joint_block(w):
    return pl.BlockSpec((w.shape[0], 2, w.shape[2], 768), lambda i: (0, i, 0, 2))


def sds(shape, kind):
    return jax.ShapeDtypeStruct(shape, kind)


def forward(x, weights, norms, mask, tabs):
    w = weights
    gains, biases = norms
    rows, width = x.shape
    heads = width // 128
    blocks, tp, depth, columns = w.shape
    steps = tp // 2
    cos, sin, cost, sint = tabs
    q, k, v = pl.pallas_call(
        qkv_kernel,
        grid=(steps,),
        in_specs=[full((rows, width)), joint_block(w), full((rows, 128)), full((rows, 128))],
        out_specs=[lead((3, rows, 128))] * 3,
        out_shape=[sds((heads, rows, 128), BF)] * 3,
        compiler_params=BIG,
        name="qkv",
    )(x, w, cos, sin)
    ko, vo = lax.ppermute((k, v), "core", [(0, 1), (1, 0)])
    pair = lead((1, rows, 128))
    o, e, l = pl.pallas_call(
        attn_kernel,
        grid=(heads,),
        in_specs=[pair] * 5 + [full((2 * rows, rows))],
        out_specs=[pair, lead((1, 2, 2 * rows, rows)), lead((1, 2, 8, rows))],
        out_shape=[sds((heads, rows, 128), BF), sds((heads, 2, 2 * rows, rows), BF), sds((heads, 2, 8, rows), F32)],
        compiler_params=BIG,
        name="attn",
    )(q, k, v, ko, vo, mask)
    hidden = columns // 4
    y, gu, n1, i1, n2, i2 = pl.pallas_call(
        ffn_kernel,
        grid=(tp,),
        in_specs=[
            full((rows, width)),
            full((heads, rows, 128)),
            pl.BlockSpec((blocks, tp, depth, 256), lambda i: (0, 0, 0, 8)),
            lead((blocks, 1, depth, 2 * hidden), 1),
            pl.BlockSpec((blocks, 1, depth, hidden), lambda i: (0, i, 0, 3)),
            full((2, width)),
            full((2, width)),
        ],
        out_specs=[full((rows, width)), lead((1, 2, rows, hidden))] + [full((rows, width)), full((rows, 128))] * 2,
        out_shape=[sds((rows, width), BF), sds((tp, 2, rows, hidden), BF)] + [sds((rows, width), F32), sds((rows, 128), F32)] * 2,
        scratch_shapes=[VM((rows, width), F32), VM((rows, width), BF), VM((rows, width), F32)],
        compiler_params=BIG,
        name="ffn",
    )(x, o, w, w, w, gains, biases)
    return y, (q, k, v, ko, vo, o, e, l, gu, n1, i1, n2, i2)


def backward(x, dy, kept, weights, norms, tabs):
    w = weights
    gains, biases = norms
    q, k, v, ko, vo, o, e, l, gu, n1, i1, n2, i2 = kept
    rows, width = x.shape
    heads = width // 128
    blocks, tp, depth, columns = w.shape
    steps = tp // 2
    hidden = columns // 4
    cos, sin, cost, sint = tabs
    whole, stat = full((rows, width)), full((rows, 128))
    g, dr1, da, ng = pl.pallas_call(
        ffn_back_kernel,
        grid=(tp,),
        in_specs=[
            whole, whole, stat, whole, stat,
            lead((1, 2, rows, hidden)),
            lead((blocks, 1, depth, 2 * hidden), 1),
            pl.BlockSpec((blocks, 1, depth, hidden), lambda i: (0, i, 0, 3)),
            full((2, width)), full((2, width)),
        ],
        out_specs=[
            lead((blocks, 1, depth, columns), 1),
            whole, whole, full((8, width)),
        ],
        out_shape=[sds(w.shape, BF), sds((rows, width), F32), sds((rows, width), BF), sds((8, width), F32)],
        scratch_shapes=[VM((rows, width), BF), VM((rows, width), BF), VM((rows, width), F32)],
        compiler_params=BIG,
        name="ffn_back",
    )(dy, n1, i1, n2, i2, gu, w, w, gains, biases)
    three = lead((3, rows, 128))
    dq, own, oth, dwo = pl.pallas_call(
        attn_back_kernel,
        grid=(steps,),
        in_specs=[
            whole,
            pl.BlockSpec((blocks, 2, depth, 256), lambda i: (0, i, 0, 8)),
            three, three, three, three, three, three,
            lead((3, 2, 2 * rows, rows)),
            lead((3, 2, 8, rows)),
            full((HD // 2, rows)), full((HD // 2, rows)),
        ],
        out_specs=[three, lead((3, 2, 128, rows)), lead((3, 2, 128, rows)), lead((1, width, 384))],
        out_shape=[
            sds((heads, rows, 128), BF),
            sds((heads, 2, 128, rows), F32),
            sds((heads, 2, 128, rows), BF),
            sds((steps, width, 384), BF),
        ],
        compiler_params=BIG,
        name="attn_back",
    )(da, w, o, q, k, v, ko, vo, e, l, cost, sint)
    got = lax.ppermute(oth, "core", [(0, 1), (1, 0)])
    g, dz = pl.pallas_call(
        joint_back_kernel,
        grid=(steps,),
        in_specs=[
            pl.BlockSpec(memory_space=pl.ANY),
            whole,
            joint_block(w),
            whole, three,
            lead((3, 2, 128, rows)), lead((3, 2, 128, rows)),
            lead((1, width, 384)),
            full((HD // 2, rows)), full((HD // 2, rows)),
        ],
        out_specs=[joint_block(w), whole],
        out_shape=[sds(w.shape, BF), sds((rows, width), F32)],
        input_output_aliases={0: 0},
        compiler_params=BIG,
        name="joint_back",
    )(g, x, w, dr1, dq, own, got, dwo, cost, sint)
    return dz, (g, ng)


WIDE = 128


def sum_kernel(parts, g_ref, ng_ref, out_ref, nout_ref, own, land_c, land_y, land_r, land_l, land_n, own_sem, cs_sem, cr_sem, ys_sem, yr_sem, rs_sem, rr_sem, ls_sem, lr_sem, ns_sem, nr_sem):
    y, c, z = lax.axis_index("y"), lax.axis_index("core"), lax.axis_index("tensor")
    last = 3
    near = {"core": 1 - c}
    across = {"y": 1 - y}
    right, left = {"tensor": jnp.minimum(z + 1, last)}, {"tensor": jnp.maximum(z - 1, 0)}
    pair = {"tensor": z + 1 - 2 * lax.rem(z, 2)}
    far = {"tensor": lax.rem(z + 2, 4)}
    barrier = pltpu.get_barrier_semaphore()

    def greet(device):
        pl.semaphore_signal(barrier, inc=1, device_id=device, device_id_type=MESH)

    greet(near)
    greet(across)
    greet(far)

    @pl.when(z < last)
    def _():
        greet(right)

    @pl.when(z > 0)
    def _():
        greet(left)

    pl.semaphore_wait(barrier, 3 + jnp.where(z < last, 1, 0) + jnp.where(z > 0, 1, 0))

    def columns(j):
        return pl.ds(pl.multiple_of(j * WIDE, WIDE), WIDE)

    def remote(src, dst, send, recv, device):
        return pltpu.make_async_remote_copy(src, dst, send, recv, device_id=device, device_id_type=MESH)

    def load(j):
        return pltpu.make_async_copy(g_ref.at[:, c, :, :, columns(j)], own.at[j], own_sem.at[j])

    def to_core(j):
        return remote(g_ref.at[:, 1 - c, :, :, columns(j)], land_c.at[j], cs_sem.at[j], cr_sem.at[j], near)

    def to_y(j):
        return remote(land_c.at[j, 1 - y], land_y.at[j], ys_sem.at[j], yr_sem.at[j], across)

    def norm_copy(k):
        return remote(land_n.at[2 * k], land_n.at[2 * k + 1], ns_sem.at[k], nr_sem.at[k], (near, across, pair, far)[k])

    def go_right(j, first, src):
        return remote(src, land_r.at[j, pl.ds(first - 1, 4 - first)], rs_sem.at[j], rr_sem.at[j], right)

    def go_left(j, count, src):
        return remote(src, land_l.at[j, pl.ds(0, count)], ls_sem.at[j], lr_sem.at[j], left)

    for j in range(2):
        to_core(j).start()
        load(j).start()
    land_n[0] = ng_ref[...]
    norm_copy(0).start()

    def step(i, carry):
        @pl.when(i + 2 < parts)
        def _():
            to_core(i + 2).start()
            load(i + 2).start()

        @pl.when(i < parts)
        def _():
            load(i).wait()
            to_core(i).wait_recv()
            land_c[i] = land_c[i] + own[i]
            to_y(i).start()

        @pl.when(jnp.logical_and(i >= 4, i - 4 < parts))
        def _():
            j = i - 4

            @pl.when(z == 1)
            def _():
                go_left(j, 2, land_l.at[j, pl.ds(0, 2)]).wait_recv()
                land_l[j, 0] = land_l[j, 0] + land_c[j, y, 0]
                go_left(j, 1, land_l.at[j, pl.ds(0, 1)]).start()

            @pl.when(z == 2)
            def _():
                go_right(j, 2, land_r.at[j, pl.ds(1, 2)]).wait_recv()
                land_r[j, 2] = land_r[j, 2] + land_c[j, y, 3]
                go_right(j, 3, land_r.at[j, pl.ds(2, 1)]).start()

        @pl.when(jnp.logical_and(i >= 3, i - 3 < parts))
        def _():
            j = i - 3

            @pl.when(z == 1)
            def _():
                go_right(j, 1, land_r.at[j]).wait_recv()
                for k in (2, 3):
                    land_r[j, k - 1] = land_r[j, k - 1] + land_c[j, y, k]
                go_right(j, 2, land_r.at[j, pl.ds(1, 2)]).start()

            @pl.when(z == 2)
            def _():
                go_left(j, 3, land_l.at[j]).wait_recv()
                for k in (0, 1):
                    land_l[j, k] = land_l[j, k] + land_c[j, y, k]
                go_left(j, 2, land_l.at[j, pl.ds(0, 2)]).start()

        @pl.when(jnp.logical_and(i >= 2, i - 2 < parts))
        def _():
            j = i - 2
            to_y(j).wait_recv()
            land_c[j, y] = land_c[j, y] + land_y[j]

            @pl.when(z == 0)
            def _():
                go_right(j, 1, land_c.at[j, y, pl.ds(1, 3)]).start()

            @pl.when(z == last)
            def _():
                go_left(j, 3, land_c.at[j, y, pl.ds(0, 3)]).start()

        @pl.when(i >= 5)
        def _():
            j = i - 5
            mine = land_c[j, y, z].astype(F32)

            @pl.when(z == 0)
            def _():
                go_left(j, 1, land_l.at[j, pl.ds(0, 1)]).wait_recv()
                out_ref[:, columns(j)] = mine + land_l[j, 0].astype(F32)

            @pl.when(z == 1)
            def _():
                out_ref[:, columns(j)] = mine + land_r[j, 0].astype(F32) + land_l[j, 1].astype(F32)

            @pl.when(z == 2)
            def _():
                out_ref[:, columns(j)] = mine + land_r[j, 1].astype(F32) + land_l[j, 2].astype(F32)

            @pl.when(z == last)
            def _():
                go_right(j, 3, land_r.at[j, pl.ds(2, 1)]).wait_recv()
                out_ref[:, columns(j)] = mine + land_r[j, 2].astype(F32)

        for k in range(4):

            @pl.when(i == 3 * (k + 1))
            def _():
                norm_copy(k).wait()
                total = land_n[2 * k] + land_n[2 * k + 1]
                if k < 3:
                    land_n[2 * k + 2] = total
                    norm_copy(k + 1).start()
                else:
                    nout_ref[...] = total

        return carry

    lax.fori_loop(0, parts + 5, step, 0)

    def finish(j, carry):
        to_core(j).wait_send()
        to_y(j).wait_send()

        @pl.when(z == 0)
        def _():
            go_right(j, 1, land_c.at[j, y, pl.ds(1, 3)]).wait_send()

        @pl.when(z == 1)
        def _():
            go_right(j, 2, land_r.at[j, pl.ds(1, 2)]).wait_send()
            go_left(j, 1, land_l.at[j, pl.ds(0, 1)]).wait_send()

        @pl.when(z == 2)
        def _():
            go_right(j, 3, land_r.at[j, pl.ds(2, 1)]).wait_send()
            go_left(j, 2, land_l.at[j, pl.ds(0, 2)]).wait_send()

        @pl.when(z == last)
        def _():
            go_left(j, 3, land_c.at[j, y, pl.ds(0, 3)]).wait_send()

        return carry

    lax.fori_loop(0, parts, finish, 0)


def sum_over_section(g, ng):
    rows, columns = g.shape[2:]
    parts = columns // WIDE
    g = g.reshape(2, 2, 4, rows, columns)
    dma = pltpu.SemaphoreType.DMA
    return pl.pallas_call(
        functools.partial(sum_kernel, parts),
        in_specs=[pl.BlockSpec(memory_space=pl.ANY), pl.BlockSpec(memory_space=VM)],
        out_specs=[pl.BlockSpec(memory_space=VM)] * 2,
        out_shape=[sds((rows, columns), F32), sds(ng.shape, F32)],
        scratch_shapes=[
            VM((parts, 2, 4, rows, WIDE), BF),
            VM((parts, 2, 4, rows, WIDE), BF),
            VM((parts, 4, rows, WIDE), BF),
            VM((parts, 3, rows, WIDE), BF),
            VM((parts, 3, rows, WIDE), BF),
            VM((8,) + ng.shape, F32),
        ]
        + [dma((parts,))] * 9
        + [dma((4,))] * 2,
        compiler_params=pltpu.CompilerParams(collective_id=0, has_side_effects=True, vmem_limit_bytes=58 << 20),
        name="grad_sum",
    )(g, ng)


def swap_pairs(tp, step, dp_axes):
    pairs = []
    half = tp // 2
    for core in range(2):
        for at in range(tp):
            source = core * tp + at
            target = (at // half) * tp + half * core + (at + step) % half
            pairs.append((source, target))
    return pairs


def to_sequences(rows, tp):
    half = tp // 2
    at = lax.axis_index("tensor")
    pieces = [None] * half
    got = []
    for step in range(half):
        piece = lax.dynamic_index_in_dim(rows, (at + step) % half, 0, keepdims=False)
        got.append(lax.ppermute(piece, ("core", "tensor"), swap_pairs(tp, step, None)))
    stacked = jnp.stack(got)
    order = (at - jnp.arange(half)) % half
    return jnp.take(stacked, order, axis=0).reshape(-1, rows.shape[-1])


def to_positions(rows, tp):
    half = tp // 2
    at = lax.axis_index("tensor")
    parts = rows.reshape(half, -1, rows.shape[-1])
    got = []
    for step in range(half):
        piece = lax.dynamic_index_in_dim(parts, (at - step) % half, 0, keepdims=False)
        back = [(target, source) for source, target in swap_pairs(tp, step, None)]
        got.append(lax.ppermute(piece, ("core", "tensor"), back))
    stacked = jnp.stack(got)
    order = (at + jnp.arange(half)) % half
    return jnp.take(stacked, (jnp.arange(half) - at) % half, axis=0)


def rope_tables(positions):
    halfway = HD // 2
    freqs = 1000.0 ** (-jnp.arange(halfway, dtype=F32) / halfway)
    angles = positions.astype(F32)[:, None] * freqs[None, :]
    cos, sin = jnp.cos(angles), jnp.sin(angles)
    wide = jnp.concatenate([cos] * 4, axis=1)
    signed = jnp.concatenate([-sin, sin] * 2, axis=1)
    return wide, signed, cos.T, sin.T


def pack_shard(w_qkv, w_out, w_gate_up, w_down):
    rows = w_qkv.shape[0]
    odd = lax.axis_index("tensor") % 2 == 1
    heads = w_qkv.reshape(rows, 3, 3, HD)
    mine = w_out.T.reshape(rows, 3, HD)
    heads = jnp.where(odd, jnp.roll(heads, -1, axis=2), heads)
    mine = jnp.where(odd, jnp.roll(mine, -1, axis=1), mine)
    first = jnp.concatenate(
        [heads[:, :, :2].reshape(rows, -1), heads[:, :, 2].reshape(rows, -1), mine[:, 2], mine[:, :2].reshape(rows, -1)], axis=1
    )
    return jnp.concatenate([w_gate_up.reshape(rows, -1), first, w_down.T], axis=1)


def unpack_shard(packed):
    rows, columns = packed.shape
    half = columns // 2
    pair, first, down = packed[:, :half], packed[:, half : half + 768], packed[:, half + 768 :]
    odd = lax.axis_index("tensor") % 2 == 1
    both = first[:, :384].reshape(rows, 3, 2, HD)
    single = first[:, 384:576].reshape(rows, 3, 1, HD)
    heads = jnp.concatenate([both, single], axis=2)
    mine = jnp.concatenate([first[:, 640:].reshape(rows, 2, HD), first[:, 576:640].reshape(rows, 1, HD)], axis=1)
    heads = jnp.where(odd, jnp.roll(heads, 1, axis=2), heads)
    mine = jnp.where(odd, jnp.roll(mine, 1, axis=1), mine)
    return (
        heads.reshape(rows, 3, -1),
        mine.reshape(rows, -1).T,
        pair.reshape(rows, 2, -1),
        down.T,
    )


BLOCKS = 4


def gather_shard(shard, dp, tp):
    rows, columns = shard.shape
    got = lax.all_gather(shard, ALL, axis=0, tiled=False)
    got = got.reshape(BLOCKS, dp // BLOCKS, tp, rows, columns)
    return got.transpose(0, 2, 1, 3, 4).reshape(BLOCKS, tp, -1, columns)


def scatter_sum(whole, dp, tp):
    columns = whole.shape[3]
    parts = whole.reshape(BLOCKS, tp, dp // BLOCKS, -1, columns).transpose(0, 2, 1, 3, 4)
    parts = parts.reshape(dp * tp, -1, columns)
    return lax.psum_scatter(parts, ALL, scatter_dimension=0, tiled=False).astype(F32)


def on_device(dp, tp, tokens, cotangent, lengths, w_qkv, w_out, w_gate_up, w_down, norm_gains, norm_biases):
    section = lax.axis_index("section")
    core = lax.axis_index("core")
    at = lax.axis_index("tensor")
    micro, own, width = tokens.shape
    assert micro * 2 == tp
    length = own * tp
    rows = length // 2
    weights = gather_shard(pack_shard(w_qkv[0], w_out[0], w_gate_up[0], w_down[0]), dp, tp)
    norms = jnp.concatenate([norm_gains, norm_biases])
    norms = lax.all_gather(norms, ("y", "core"), axis=1, tiled=True).astype(F32)
    norms = (norms[0].reshape(2, width), norms[1].reshape(2, width))
    tokens = to_sequences(tokens, tp)
    grad_top = to_sequences(cotangent, tp)
    chip_lengths = lax.all_gather(lengths, "core", axis=0, tiled=True)
    my_lengths = lax.dynamic_index_in_dim(chip_lengths, at, 0, keepdims=False)
    near = core * rows + jnp.arange(rows, dtype=jnp.int32)
    far = (1 - core) * rows + jnp.arange(rows, dtype=jnp.int32)
    ends_at = jnp.cumsum(my_lengths)

    def segment(positions):
        return jnp.sum((ends_at[None, :] <= positions[:, None]).astype(jnp.int32), axis=-1)

    seg_near = segment(near)
    seg_all = jnp.concatenate([seg_near, segment(far)])
    mask = jnp.where(seg_all[:, None] == seg_near[None, :], 0.0, neg_fill).astype(F32)
    tabs = rope_tables(near)

    y, kept = forward(tokens, weights, norms, mask, tabs)
    received = lax.ppermute(y, "section", [(0, 1)])
    inputs = jnp.where(section == 0, tokens, received)
    y, kept = forward(inputs, weights, norms, mask, tabs)
    dz, grads = backward(inputs, grad_top, kept, weights, norms, tabs)
    received = lax.ppermute(dz.astype(BF), "section", [(1, 0)])
    dy = jnp.where(section == 0, received, grad_top)
    dz, grads = backward(inputs, dy, kept, weights, norms, tabs)
    ends = to_positions(jnp.where(section == 0, dz.astype(BF), y), tp)
    g, ng = grads
    if dp == 4 and tp == 4:
        mine, total = sum_over_section(g, ng)
        index = lax.axis_index(ALL)
        small = lax.dynamic_slice_in_dim(total[:4].reshape(2, dp * tp, -1), index, 1, 1)
        gains, biases = small[0, 0], small[1, 0]
    else:
        mine = scatter_sum(g, dp, tp)
        gains = lax.psum_scatter(ng[0:2].reshape(-1), ALL, scatter_dimension=0, tiled=True)
        biases = lax.psum_scatter(ng[2:4].reshape(-1), ALL, scatter_dimension=0, tiled=True)
    outs = unpack_shard(mine)
    return (ends[None],) + tuple(t[None] for t in outs + (gains, biases))


def solution(mesh):
    sections, dp, tp = mesh.devices.shape
    fine = Mesh(mesh.devices.reshape(sections, dp // 2, 2, tp), ("section", "y", "core", "tensor"))
    both = ("y", "core")
    in_specs = (
        P(both, "tensor", None),
        P(both, "tensor", None),
        P(both, None),
        P("section", both, None, "tensor"),
        P("section", "tensor", both),
        P("section", both, None, "tensor"),
        P("section", "tensor", both),
        P("section", both),
        P("section", both),
    )
    out_specs = (
        P("section", both, "tensor", None),
        P("section", both, None, "tensor"),
        P("section", "tensor", both),
        P("section", both, None, "tensor"),
        P("section", "tensor", both),
        P("section", ALL),
        P("section", ALL),
    )
    return jax.shard_map(
        functools.partial(on_device, dp, tp), mesh=fine, in_specs=in_specs, out_specs=out_specs, check_vma=False
    )
```

```python
import functools

import jax
import jax.numpy as jnp
import numpy as np
from jax import lax
from jax.experimental import pallas as pl
from jax.experimental.pallas import tpu as pltpu
from jax.sharding import Mesh, PartitionSpec as P

HD = 64
eps = 1e-05
neg_fill = -1e30
ALL = ("y", "core", "tensor")
BF = jnp.bfloat16
F32 = jnp.float32
MESH = pl.DeviceIdType.MESH


def dg(a, b, dims):
    return lax.dot_general(a, b, (dims, ((), ())), preferred_element_type=F32)


NN = ((1,), (0,))
NT = ((1,), (1,))
TN = ((0,), (0,))


def low_lanes(shape):
    return lax.broadcasted_iota(jnp.int32, shape, 1) < HD


def swap64(v):
    return pltpu.roll(v, HD, axis=1)


def rope_fwd(t, cos, sin):
    lane = lax.broadcasted_iota(jnp.int32, t.shape, 1) % HD
    other = jnp.where(lane < HD // 2, pltpu.roll(t, 128 - HD // 2, axis=1), pltpu.roll(t, HD // 2, axis=1))
    return t * cos + other * sin


def qkv_kernel(x_ref, w_ref, cos_ref, sin_ref, q_ref, k_ref, v_ref):
    x = x_ref[...]
    width = x.shape[1]
    r = [dg(x, w_ref[:, e, :, :640].reshape(width, 640), NN) for e in range(2)]
    c = [[t[:, 128 * i : 128 * i + 128] for i in range(5)] for t in r]
    low = low_lanes(c[0][0].shape)
    qs = [c[0][0], jnp.where(low, c[0][3], swap64(c[1][3])), c[1][0]]
    ks = [c[0][1], jnp.where(low, swap64(c[0][3]), c[1][3]), c[1][1]]
    vs = [c[0][2], jnp.where(low, c[0][4], swap64(c[1][4])), c[1][2]]
    cos, sin = cos_ref[...], sin_ref[...]
    for i in range(3):
        q_ref[i] = (rope_fwd(qs[i], cos, sin) * HD**-0.5).astype(BF)
        k_ref[i] = rope_fwd(ks[i], cos, sin).astype(BF)
        v_ref[i] = vs[i].astype(BF)


def attn_kernel(q_ref, k_ref, v_ref, ko_ref, vo_ref, m_ref, o_ref, e_ref, l_ref):
    q = q_ref[0]
    k = jnp.concatenate([k_ref[0], ko_ref[0]], axis=0)
    v = jnp.concatenate([v_ref[0], vo_ref[0]], axis=0)
    vt = v.astype(F32).T.astype(BF)
    outs = []
    for h in range(2):
        low = low_lanes(q.shape)
        qm = jnp.where(low if h == 0 else jnp.logical_not(low), q, jnp.zeros_like(q))
        s = dg(k, qm, NT) + m_ref[...]
        e = jnp.exp(s - jnp.max(s, axis=0, keepdims=True))
        inv = 1.0 / jnp.sum(e, axis=0, keepdims=True)
        eb = e.astype(BF)
        e_ref[0, h] = eb
        l_ref[0, h] = jnp.broadcast_to(inv, l_ref.shape[2:])
        outs.append(dg(vt[HD * h : HD * h + HD], eb, NN) * inv)
    o_ref[0] = jnp.concatenate(outs, axis=0).T.astype(BF)


def norm_parts(r):
    center = r - jnp.mean(r, axis=-1, keepdims=True)
    inv = lax.rsqrt(jnp.mean(center * center, axis=-1, keepdims=True) + eps)
    return center * inv, inv


def norm_back(dn, n, inv):
    return inv * (dn - jnp.mean(dn, axis=-1, keepdims=True) - n * jnp.mean(dn * n, axis=-1, keepdims=True))


def out_weight(w_ref):
    c = [[w_ref[:, e, :, 128 * i : 128 * i + 128].reshape(-1, 128) for i in range(2)] for e in range(2)]
    low = low_lanes(c[0][0].shape)
    mid = jnp.where(low, swap64(c[0][0].astype(F32)), c[1][0].astype(F32)).astype(BF)
    return [c[0][1], mid, c[1][1]]


GROUP = 384
WIDE = 128


def unit_weights(load):
    return [jnp.concatenate([load(t, m) for t in range(4)], axis=1) for m in range(3)]


def ffn_kernel(x_ref, o_ref, wo_ref, w_ref, g_ref, b_ref, y_ref, gu_ref, n1_ref, i1_ref, n2_ref, i2_ref, h_ref, hb_ref, acc_ref):
    z = pl.program_id(0)
    width = x_ref.shape[1]

    @pl.when(z == 0)
    def _():
        r = x_ref[...].astype(F32)
        for p in range(2):
            w = jnp.concatenate(out_weight(wo_ref.at[:, 2 * p : 2 * p + 2]), axis=1)
            o = jnp.concatenate([o_ref[3 * p + i] for i in range(3)], axis=1)
            r = r + dg(o, w, NT)
        n, inv = norm_parts(r)
        n1_ref[...] = n
        i1_ref[...] = jnp.broadcast_to(inv, i1_ref.shape)
        h = n * g_ref[0:1] + b_ref[0:1]
        h_ref[...] = h
        hb_ref[...] = h.astype(BF)

    hb = hb_ref[...]
    wg, wu, wd = unit_weights(lambda t, m: w_ref[:, t, :, 128 * m : 128 * m + 128].reshape(width, 128))
    gate = dg(hb, wg, NN)
    up = dg(hb, wu, NN)
    gu_ref[0, 0] = gate.astype(BF)
    gu_ref[0, 1] = up.astype(BF)
    act = (gate / (1.0 + jnp.exp(-gate)) * up).astype(BF)
    part = dg(act, wd, NT)

    @pl.when(z == 0)
    def _():
        acc_ref[...] = h_ref[...] + part

    @pl.when(z > 0)
    def _():
        acc_ref[...] += part

    @pl.when(z == pl.num_programs(0) - 1)
    def _():
        n, inv = norm_parts(acc_ref[...])
        n2_ref[...] = n
        i2_ref[...] = jnp.broadcast_to(inv, i2_ref.shape)
        y_ref[...] = (n * g_ref[1:2] + b_ref[1:2]).astype(BF)


def ffn_back_kernel(dy_ref, n1_ref, i1_ref, n2_ref, i2_ref, gu_ref, w_ref, g_ref, b_ref, g_out, dr1_ref, da_ref, ng_ref, hb_ref, df_ref, acc_ref):
    z = pl.program_id(0)
    width = dy_ref.shape[1]

    @pl.when(z == 0)
    def _():
        dy = dy_ref[...].astype(F32)
        n = n2_ref[...]
        ng_ref[1:2] = jnp.sum(dy * n, axis=0, keepdims=True)
        ng_ref[3:4] = jnp.sum(dy, axis=0, keepdims=True)
        dr2 = norm_back(dy * g_ref[1:2], n, i2_ref[:, :1])
        acc_ref[...] = dr2
        df_ref[...] = dr2.astype(BF)
        hb_ref[...] = (n1_ref[...] * g_ref[0:1] + b_ref[0:1]).astype(BF)

    df = df_ref[...]
    gate = gu_ref[0, 0].astype(F32)
    up = gu_ref[0, 1].astype(F32)
    s = 1.0 / (1.0 + jnp.exp(-gate))
    silu = gate * s
    act = (silu * up).astype(BF)
    wg, wu, wd = unit_weights(lambda t, m: w_ref[:, t, :, 128 * m : 128 * m + 128].reshape(width, 128))

    def keep(m, grad):
        for t in range(g_out.shape[1]):
            g_out[:, t, :, 128 * m : 128 * m + 128] = grad[:, 128 * t : 128 * t + 128].astype(BF).reshape(g_out.shape[0], -1, 128)

    keep(2, dg(df, act, TN))
    d_act = dg(df, wd, NN)
    d_gate = (d_act * up * (s * (1.0 + gate * (1.0 - s)))).astype(BF)
    d_up = (d_act * silu).astype(BF)
    hb = hb_ref[...]
    keep(0, dg(hb, d_gate, TN))
    keep(1, dg(hb, d_up, TN))
    acc_ref[...] += dg(d_gate, wg, NT) + dg(d_up, wu, NT)

    @pl.when(z == pl.num_programs(0) - 1)
    def _():
        dh = acc_ref[...]
        n = n1_ref[...]
        ng_ref[0:1] = jnp.sum(dh * n, axis=0, keepdims=True)
        ng_ref[2:3] = jnp.sum(dh, axis=0, keepdims=True)
        dr1 = norm_back(dh * g_ref[0:1], n, i1_ref[:, :1])
        dr1_ref[...] = dr1
        da_ref[...] = dr1.astype(BF)


def attn_back_kernel(da_ref, wo_ref, o_ref, q_ref, k_ref, v_ref, ko_ref, vo_ref, e_ref, l_ref, cos_ref, sin_ref, dq_ref, own_ref, oth_ref, dwo_ref):
    da = da_ref[...]
    rows = da.shape[0]
    w = jnp.concatenate(out_weight(wo_ref), axis=1)
    do3 = dg(da, w, NN).astype(BF)
    o3 = jnp.concatenate([o_ref[i] for i in range(3)], axis=1)
    dwo_ref[0] = dg(da, o3, TN).astype(BF)
    cos, sin = cos_ref[...], sin_ref[...]
    for i in range(3):
        dot = do3[:, 128 * i : 128 * i + 128].astype(F32).T
        ot = o_ref[i].astype(F32).T
        k = jnp.concatenate([k_ref[i], ko_ref[i]], axis=0)
        v = jnp.concatenate([v_ref[i], vo_ref[i]], axis=0)
        kt = k.astype(F32).T.astype(BF)
        qt = q_ref[i].astype(F32).T.astype(BF)
        dqs, dks, dvs = [], [], []
        for h in range(2):
            span = slice(HD * h, HD * h + HD)
            scaled = dot[span] * l_ref[i, h, 0:1]
            inner = jnp.sum(scaled * ot[span], axis=0, keepdims=True)
            sb = scaled.astype(BF)
            zero = jnp.zeros_like(sb)
            padded = jnp.concatenate([sb, zero] if h == 0 else [zero, sb], axis=0)
            dp = dg(v, padded, NN)
            et = e_ref[i, h]
            ds = (et.astype(F32) * (dp - inner)).astype(BF)
            dvs.append(dg(sb, et, NT))
            dks.append(dg(qt[span], ds, NT))
            dqt = dg(kt[span], ds, NN) * HD**-0.5
            d1, d2 = dqt[: HD // 2], dqt[HD // 2 :]
            dqs.append(d1 * cos + d2 * sin)
            dqs.append(d2 * cos - d1 * sin)
        dq_ref[i] = jnp.concatenate(dqs, axis=0).T.astype(BF)
        dk = jnp.concatenate(dks, axis=0)
        dv = jnp.concatenate(dvs, axis=0)
        own_ref[i, 0] = dk[:, :rows]
        own_ref[i, 1] = dv[:, :rows]
        oth_ref[i, 0] = dk[:, rows:].astype(BF)
        oth_ref[i, 1] = dv[:, rows:].astype(BF)


def joint_back_kernel(old_ref, x_ref, w_ref, dr1_ref, dq_ref, own_ref, got_ref, dwo_ref, cos_ref, sin_ref, g_ref, dz_ref):
    p = pl.program_id(0)
    x = x_ref[...]
    width = x.shape[1]
    cos, sin = cos_ref[...], sin_ref[...]
    dq = [dq_ref[i].astype(F32) for i in range(3)]
    dk, dv = [], []
    for i in range(3):
        t = own_ref[i, 0] + got_ref[i, 0].astype(F32)
        parts = []
        for h in range(2):
            d1 = t[HD * h : HD * h + HD // 2]
            d2 = t[HD * h + HD // 2 : HD * h + HD]
            parts += [d1 * cos + d2 * sin, d2 * cos - d1 * sin]
        dk.append(jnp.concatenate(parts, axis=0).T)
        dv.append((own_ref[i, 1] + got_ref[i, 1].astype(F32)).T)
    low = low_lanes(dq[0].shape)
    zero = jnp.zeros_like(dv[1])
    d = [
        [dq[0], dk[0], dv[0], jnp.where(low, dq[1], swap64(dk[1])), jnp.where(low, dv[1], zero)],
        [dq[2], dk[2], dv[2], jnp.where(low, swap64(dq[1]), dk[1]), jnp.where(low, swap64(dv[1]), zero)],
    ]
    acc = None
    wlow = low_lanes((width, 128))
    mid = dwo_ref[0, :, 128:256].astype(F32)
    sides = [dwo_ref[0, :, 0:128], dwo_ref[0, :, 256:384]]
    mids = [swap64(mid), mid]
    for e in range(2):
        b = jnp.concatenate(d[e], axis=1).astype(BF)
        t = dg(b, w_ref[:, e, :, :640].reshape(width, 640), NT)
        acc = t if acc is None else acc + t
        g = dg(x, b, TN)
        blocks = g_ref.shape[0]
        g_ref[:, e, :, :512] = g[:, :512].astype(BF).reshape(blocks, -1, 512)
        g_ref[:, e, :, 512:640] = jnp.where(wlow, g[:, 512:], mids[e]).astype(BF).reshape(blocks, -1, 128)
        g_ref[:, e, :, 640:] = sides[e].reshape(blocks, -1, 128)

    @pl.when(p == 0)
    def _():
        dz_ref[...] = dr1_ref[...] + acc

    @pl.when(p > 0)
    def _():
        dz_ref[...] += acc


BIG = pltpu.CompilerParams(vmem_limit_bytes=58 << 20)
VM = pltpu.VMEM


def full(shape):
    return pl.BlockSpec(shape, lambda i: (0,) * len(shape))


def lead(shape, at=0):
    return pl.BlockSpec(shape, lambda i: tuple(i if j == at else 0 for j in range(len(shape))))


def joint_block(w):
    return pl.BlockSpec((w.shape[0], 2, w.shape[2], 768), lambda i: (0, i, 0, 0))


def group_block(w):
    return pl.BlockSpec((w.shape[0], w.shape[1], w.shape[2], GROUP), lambda i: (0, 0, 0, 2 + i))


def sds(shape, kind):
    return jax.ShapeDtypeStruct(shape, kind)


def forward(x, weights, norms, mask, tabs):
    w = weights
    gains, biases = norms
    rows, width = x.shape
    heads = width // 128
    blocks, tp, depth, columns = w.shape
    steps = tp // 2
    cos, sin, cost, sint = tabs
    q, k, v = pl.pallas_call(
        qkv_kernel,
        grid=(steps,),
        in_specs=[full((rows, width)), joint_block(w), full((rows, 128)), full((rows, 128))],
        out_specs=[lead((3, rows, 128))] * 3,
        out_shape=[sds((heads, rows, 128), BF)] * 3,
        compiler_params=BIG,
        name="qkv",
    )(x, w, cos, sin)
    ko, vo = lax.ppermute((k, v), "core", [(0, 1), (1, 0)])
    pair = lead((1, rows, 128))
    o, e, l = pl.pallas_call(
        attn_kernel,
        grid=(heads,),
        in_specs=[pair] * 5 + [full((2 * rows, rows))],
        out_specs=[pair, lead((1, 2, 2 * rows, rows)), lead((1, 2, 8, rows))],
        out_shape=[sds((heads, rows, 128), BF), sds((heads, 2, 2 * rows, rows), BF), sds((heads, 2, 8, rows), F32)],
        compiler_params=BIG,
        name="attn",
    )(q, k, v, ko, vo, mask)
    groups = (columns - width) // GROUP
    units = tp * 128
    y, gu, n1, i1, n2, i2 = pl.pallas_call(
        ffn_kernel,
        grid=(groups,),
        in_specs=[
            full((rows, width)),
            full((heads, rows, 128)),
            pl.BlockSpec((blocks, tp, depth, 256), lambda i: (0, 0, 0, 2)),
            group_block(w),
            full((2, width)),
            full((2, width)),
        ],
        out_specs=[full((rows, width)), lead((1, 2, rows, units))] + [full((rows, width)), full((rows, 128))] * 2,
        out_shape=[sds((rows, width), BF), sds((groups, 2, rows, units), BF)] + [sds((rows, width), F32), sds((rows, 128), F32)] * 2,
        scratch_shapes=[VM((rows, width), F32), VM((rows, width), BF), VM((rows, width), F32)],
        compiler_params=BIG,
        name="ffn",
    )(x, o, w, w, gains, biases)
    return y, (q, k, v, ko, vo, o, e, l, gu, n1, i1, n2, i2)


def backward(x, dy, kept, weights, norms, tabs):
    w = weights
    gains, biases = norms
    q, k, v, ko, vo, o, e, l, gu, n1, i1, n2, i2 = kept
    rows, width = x.shape
    heads = width // 128
    blocks, tp, depth, columns = w.shape
    steps = tp // 2
    groups = (columns - width) // GROUP
    units = tp * 128
    cos, sin, cost, sint = tabs
    whole, stat = full((rows, width)), full((rows, 128))
    g, dr1, da, ng = pl.pallas_call(
        ffn_back_kernel,
        grid=(groups,),
        in_specs=[
            whole, whole, stat, whole, stat,
            lead((1, 2, rows, units)),
            group_block(w),
            full((2, width)), full((2, width)),
        ],
        out_specs=[
            group_block(w),
            whole, whole, full((8, width)),
        ],
        out_shape=[sds(w.shape, BF), sds((rows, width), F32), sds((rows, width), BF), sds((8, width), F32)],
        scratch_shapes=[VM((rows, width), BF), VM((rows, width), BF), VM((rows, width), F32)],
        compiler_params=BIG,
        name="ffn_back",
    )(dy, n1, i1, n2, i2, gu, w, gains, biases)
    three = lead((3, rows, 128))
    dq, own, oth, dwo = pl.pallas_call(
        attn_back_kernel,
        grid=(steps,),
        in_specs=[
            whole,
            pl.BlockSpec((blocks, 2, depth, 256), lambda i: (0, i, 0, 2)),
            three, three, three, three, three, three,
            lead((3, 2, 2 * rows, rows)),
            lead((3, 2, 8, rows)),
            full((HD // 2, rows)), full((HD // 2, rows)),
        ],
        out_specs=[three, lead((3, 2, 128, rows)), lead((3, 2, 128, rows)), lead((1, width, 384))],
        out_shape=[
            sds((heads, rows, 128), BF),
            sds((heads, 2, 128, rows), F32),
            sds((heads, 2, 128, rows), BF),
            sds((steps, width, 384), BF),
        ],
        compiler_params=BIG,
        name="attn_back",
    )(da, w, o, q, k, v, ko, vo, e, l, cost, sint)
    got = lax.ppermute(oth, "core", [(0, 1), (1, 0)])
    g, dz = pl.pallas_call(
        joint_back_kernel,
        grid=(steps,),
        in_specs=[
            pl.BlockSpec(memory_space=pl.ANY),
            whole,
            joint_block(w),
            whole, three,
            lead((3, 2, 128, rows)), lead((3, 2, 128, rows)),
            lead((1, width, 384)),
            full((HD // 2, rows)), full((HD // 2, rows)),
        ],
        out_specs=[joint_block(w), whole],
        out_shape=[sds(w.shape, BF), sds((rows, width), F32)],
        input_output_aliases={0: 0},
        compiler_params=BIG,
        name="joint_back",
    )(g, x, w, dr1, dq, own, got, dwo, cost, sint)
    return dz, (g, ng)


def sum_kernel(parts, g_ref, ng_ref, out_ref, nout_ref, own, land_c, land_y, land_r, land_l, land_n, own_sem, cs_sem, cr_sem, ys_sem, yr_sem, rs_sem, rr_sem, ls_sem, lr_sem, ns_sem, nr_sem):
    y, c, z = lax.axis_index("y"), lax.axis_index("core"), lax.axis_index("tensor")
    last = 3
    near = {"core": 1 - c}
    across = {"y": 1 - y}
    right, left = {"tensor": jnp.minimum(z + 1, last)}, {"tensor": jnp.maximum(z - 1, 0)}
    pair = {"tensor": z + 1 - 2 * lax.rem(z, 2)}
    far = {"tensor": lax.rem(z + 2, 4)}
    barrier = pltpu.get_barrier_semaphore()

    def greet(device):
        pl.semaphore_signal(barrier, inc=1, device_id=device, device_id_type=MESH)

    greet(near)
    greet(across)
    greet(far)

    @pl.when(z < last)
    def _():
        greet(right)

    @pl.when(z > 0)
    def _():
        greet(left)

    pl.semaphore_wait(barrier, 3 + jnp.where(z < last, 1, 0) + jnp.where(z > 0, 1, 0))

    def columns(j):
        return pl.ds(pl.multiple_of(j * WIDE, WIDE), WIDE)

    def remote(src, dst, send, recv, device):
        return pltpu.make_async_remote_copy(src, dst, send, recv, device_id=device, device_id_type=MESH)

    def load(j):
        return pltpu.make_async_copy(g_ref.at[:, c, :, :, columns(j)], own.at[j], own_sem.at[j])

    def to_core(j):
        return remote(g_ref.at[:, 1 - c, :, :, columns(j)], land_c.at[j], cs_sem.at[j], cr_sem.at[j], near)

    def to_y(j):
        return remote(land_c.at[j, 1 - y], land_y.at[j], ys_sem.at[j], yr_sem.at[j], across)

    def norm_copy(k):
        return remote(land_n.at[2 * k], land_n.at[2 * k + 1], ns_sem.at[k], nr_sem.at[k], (near, across, pair, far)[k])

    def go_right(j, first, src):
        return remote(src, land_r.at[j, pl.ds(first - 1, 4 - first)], rs_sem.at[j], rr_sem.at[j], right)

    def go_left(j, count, src):
        return remote(src, land_l.at[j, pl.ds(0, count)], ls_sem.at[j], lr_sem.at[j], left)

    for j in range(2):
        to_core(j).start()
        load(j).start()
    land_n[0] = ng_ref[...]
    norm_copy(0).start()

    def step(i, carry):
        @pl.when(i + 2 < parts)
        def _():
            to_core(i + 2).start()
            load(i + 2).start()

        @pl.when(i < parts)
        def _():
            load(i).wait()
            to_core(i).wait_recv()
            land_c[i] = land_c[i] + own[i]
            to_y(i).start()

        @pl.when(jnp.logical_and(i >= 4, i - 4 < parts))
        def _():
            j = i - 4

            @pl.when(z == 1)
            def _():
                go_left(j, 2, land_l.at[j, pl.ds(0, 2)]).wait_recv()
                land_l[j, 0] = land_l[j, 0] + land_c[j, y, 0]
                go_left(j, 1, land_l.at[j, pl.ds(0, 1)]).start()

            @pl.when(z == 2)
            def _():
                go_right(j, 2, land_r.at[j, pl.ds(1, 2)]).wait_recv()
                land_r[j, 2] = land_r[j, 2] + land_c[j, y, 3]
                go_right(j, 3, land_r.at[j, pl.ds(2, 1)]).start()

        @pl.when(jnp.logical_and(i >= 3, i - 3 < parts))
        def _():
            j = i - 3

            @pl.when(z == 1)
            def _():
                go_right(j, 1, land_r.at[j]).wait_recv()
                for k in (2, 3):
                    land_r[j, k - 1] = land_r[j, k - 1] + land_c[j, y, k]
                go_right(j, 2, land_r.at[j, pl.ds(1, 2)]).start()

            @pl.when(z == 2)
            def _():
                go_left(j, 3, land_l.at[j]).wait_recv()
                for k in (0, 1):
                    land_l[j, k] = land_l[j, k] + land_c[j, y, k]
                go_left(j, 2, land_l.at[j, pl.ds(0, 2)]).start()

        @pl.when(jnp.logical_and(i >= 2, i - 2 < parts))
        def _():
            j = i - 2
            to_y(j).wait_recv()
            land_c[j, y] = land_c[j, y] + land_y[j]

            @pl.when(z == 0)
            def _():
                go_right(j, 1, land_c.at[j, y, pl.ds(1, 3)]).start()

            @pl.when(z == last)
            def _():
                go_left(j, 3, land_c.at[j, y, pl.ds(0, 3)]).start()

        @pl.when(i >= 5)
        def _():
            j = i - 5
            mine = land_c[j, y, z].astype(F32)

            @pl.when(z == 0)
            def _():
                go_left(j, 1, land_l.at[j, pl.ds(0, 1)]).wait_recv()
                out_ref[:, columns(j)] = mine + land_l[j, 0].astype(F32)

            @pl.when(z == 1)
            def _():
                out_ref[:, columns(j)] = mine + land_r[j, 0].astype(F32) + land_l[j, 1].astype(F32)

            @pl.when(z == 2)
            def _():
                out_ref[:, columns(j)] = mine + land_r[j, 1].astype(F32) + land_l[j, 2].astype(F32)

            @pl.when(z == last)
            def _():
                go_right(j, 3, land_r.at[j, pl.ds(2, 1)]).wait_recv()
                out_ref[:, columns(j)] = mine + land_r[j, 2].astype(F32)

        for k in range(4):

            @pl.when(i == 3 * (k + 1))
            def _():
                norm_copy(k).wait()
                total = land_n[2 * k] + land_n[2 * k + 1]
                if k < 3:
                    land_n[2 * k + 2] = total
                    norm_copy(k + 1).start()
                else:
                    nout_ref[...] = total

        return carry

    lax.fori_loop(0, parts + 5, step, 0)

    def finish(j, carry):
        to_core(j).wait_send()
        to_y(j).wait_send()

        @pl.when(z == 0)
        def _():
            go_right(j, 1, land_c.at[j, y, pl.ds(1, 3)]).wait_send()

        @pl.when(z == 1)
        def _():
            go_right(j, 2, land_r.at[j, pl.ds(1, 2)]).wait_send()
            go_left(j, 1, land_l.at[j, pl.ds(0, 1)]).wait_send()

        @pl.when(z == 2)
        def _():
            go_right(j, 3, land_r.at[j, pl.ds(2, 1)]).wait_send()
            go_left(j, 2, land_l.at[j, pl.ds(0, 2)]).wait_send()

        @pl.when(z == last)
        def _():
            go_left(j, 3, land_c.at[j, y, pl.ds(0, 3)]).wait_send()

        return carry

    lax.fori_loop(0, parts, finish, 0)


def sum_over_section(g, ng):
    rows, columns = g.shape[2:]
    parts = columns // WIDE
    g = g.reshape(2, 2, 4, rows, columns)
    dma = pltpu.SemaphoreType.DMA
    return pl.pallas_call(
        functools.partial(sum_kernel, parts),
        in_specs=[pl.BlockSpec(memory_space=pl.ANY), pl.BlockSpec(memory_space=VM)],
        out_specs=[pl.BlockSpec(memory_space=VM)] * 2,
        out_shape=[sds((rows, columns), F32), sds(ng.shape, F32)],
        scratch_shapes=[
            VM((parts, 2, 4, rows, WIDE), BF),
            VM((parts, 2, 4, rows, WIDE), BF),
            VM((parts, 4, rows, WIDE), BF),
            VM((parts, 3, rows, WIDE), BF),
            VM((parts, 3, rows, WIDE), BF),
            VM((8,) + ng.shape, F32),
        ]
        + [dma((parts,))] * 9
        + [dma((4,))] * 2,
        compiler_params=pltpu.CompilerParams(collective_id=0, has_side_effects=True, vmem_limit_bytes=58 << 20),
        name="grad_sum",
    )(g, ng)


LAG = 6


def first_kernel(
    parts, tok_ref, shard_ref, extra_ref, len_ref, cos_ref, sin_ref,
    w_out, y_out, x_out, mask_out, norm_out,
    w, xin, q, kv, land_kv, o, h1, hb, acc, ext, lens,
    tok_sem, tok_send, tok_recv, shard_sem, back_sem, kv_send, kv_recv,
    small_send, small_recv, rs_sem, rr_sem, ls_sem, lr_sem, ys_sem, yr_sem, cs_sem, cr_sem,
):
    y, c, z = lax.axis_index("y"), lax.axis_index("core"), lax.axis_index("tensor")
    last = 3
    rows, width = xin.shape[0] * xin.shape[1], xin.shape[2]
    near, across = {"core": 1 - c}, {"y": 1 - y}
    right, left = {"tensor": jnp.minimum(z + 1, last)}, {"tensor": jnp.maximum(z - 1, 0)}
    side = z // 2
    barrier = pltpu.get_barrier_semaphore()

    def greet(device):
        pl.semaphore_signal(barrier, inc=1, device_id=device, device_id_type=MESH)

    def remote(src, dst, send, recv, device):
        return pltpu.make_async_remote_copy(src, dst, send, recv, device_id=device, device_id_type=MESH)

    def target(i):
        return {"core": side, "tensor": 2 * c + i}

    def at_home(i):
        return jnp.logical_and(side == c, 2 * c + i == z)

    def token_copy(i):
        return remote(tok_ref.at[i], xin.at[z % 2], tok_send.at[i], tok_recv.at[z % 2], target(i))

    def token_home(i):
        return pltpu.make_async_copy(tok_ref.at[i], xin.at[z % 2], tok_sem)

    load = pltpu.make_async_copy(shard_ref, w.at[y, c, z], shard_sem)
    load.start()
    greet(near)
    greet(across)

    @pl.when(z < last)
    def _():
        greet(right)

    @pl.when(z > 0)
    def _():
        greet(left)

    for i in range(2):

        @pl.when(jnp.logical_not(at_home(i)))
        def _():
            greet(target(i))

    count = 4 + jnp.where(z < last, 1, 0) + jnp.where(z > 0, 1, 0) - jnp.where(side == c, 1, 0)
    pl.semaphore_wait(barrier, count)

    for i in range(2):

        @pl.when(at_home(i))
        def _():
            token_home(i).start()

        @pl.when(jnp.logical_not(at_home(i)))
        def _():
            token_copy(i).start()

    ext[y, c] = extra_ref[...]
    lens[c] = len_ref[...]

    def small(k):
        if k == 0:
            return remote(lens.at[c], lens.at[c], small_send.at[0], small_recv.at[0], near)
        if k == 1:
            return remote(ext.at[y, c], ext.at[y, c], small_send.at[1], small_recv.at[1], across)
        return remote(ext.at[:, c], ext.at[:, c], small_send.at[2], small_recv.at[2], near)

    small(0).start()
    small(1).start()
    load.wait()

    def columns(j):
        return pl.ds(pl.multiple_of(j * WIDE, WIDE), WIDE)

    def go_right(j, h):
        b = jnp.maximum(z - h, 0)
        return remote(w.at[y, c, b, :, columns(j)], w.at[y, c, b, :, columns(j)], rs_sem.at[j, h], rr_sem.at[j, h], right)

    def go_left(j, h):
        b = jnp.minimum(z + h, last)
        return remote(w.at[y, c, b, :, columns(j)], w.at[y, c, b, :, columns(j)], ls_sem.at[j, h], lr_sem.at[j, h], left)

    def to_y(j):
        return remote(w.at[y, c, :, :, columns(j)], w.at[y, c, :, :, columns(j)], ys_sem.at[j], yr_sem.at[j], across)

    def to_core(j):
        return remote(w.at[:, c, :, :, columns(j)], w.at[:, c, :, :, columns(j)], cs_sem.at[j], cr_sem.at[j], near)

    def write_back(j):
        return pltpu.make_async_copy(w.at[:, :, :, :, columns(j)], w_out.at[:, :, :, :, columns(j)], back_sem.at[j])

    def stage(r, lag, body):
        @pl.when(jnp.logical_and(r >= lag, r - lag < parts))
        def _():
            body(r - lag)

    def send_own(j):
        @pl.when(z < last)
        def _():
            go_right(j, 0).start()

        @pl.when(z > 0)
        def _():
            go_left(j, 0).start()

    def hop(h, j):
        @pl.when(z >= h)
        def _():
            go_right(j, h - 1).wait_recv()

        @pl.when(z + h <= last)
        def _():
            go_left(j, h - 1).wait_recv()

        if h < last:

            @pl.when(jnp.logical_and(z >= h, z < last))
            def _():
                go_right(j, h).start()

            @pl.when(jnp.logical_and(z + h <= last, z > 0))
            def _():
                go_left(j, h).start()

        else:
            to_y(j).start()

    def over_core(j):
        to_y(j).wait_recv()
        to_core(j).start()

    def complete(j):
        to_core(j).wait_recv()
        write_back(j).start()

    def round_(r):
        stage(r, 0, send_own)
        stage(r, 1, functools.partial(hop, 1))
        stage(r, 2, functools.partial(hop, 2))
        stage(r, 3, functools.partial(hop, 3))
        stage(r, 5, over_core)
        stage(r, LAG, complete)

    def rounds(first, end):
        lax.fori_loop(first, end, lambda r, t: (round_(r), t)[1], 0)

    lead_parts = width // WIDE
    rounds(0, 3)
    small(0).wait()
    small(1).wait()
    small(2).start()

    mine = jnp.where(side == 0, lens[0], lens[1])
    mine = jnp.where(z % 2 == 0, mine[0:1], mine[1:2])
    at_q = c * rows + lax.broadcasted_iota(jnp.int32, (1, rows), 1)
    at_k = lax.broadcasted_iota(jnp.int32, (2 * rows, 1), 0)
    at_k = jnp.where(at_k < rows, c * rows + at_k, (1 - c) * rows + at_k - rows)
    seg_q, seg_k = jnp.zeros((1, rows), jnp.int32), jnp.zeros((2 * rows, 1), jnp.int32)
    end = jnp.zeros((1, 1), jnp.int32)
    for n in range(8):
        end = end + mine[:, n : n + 1]
        seg_q = seg_q + jnp.where(end <= at_q, 1, 0)
        seg_k = seg_k + jnp.where(end <= at_k, 1, 0)
    mask_out[...] = jnp.where(seg_k == seg_q, 0.0, neg_fill).astype(F32)
    rounds(3, lead_parts + LAG)

    small(2).wait()
    halves = [ext[i // 2, i % 2].astype(F32) for i in range(4)]
    for k in range(2):
        for half in range(2):
            pieces = [halves[2 * half + i][3 * k + m : 3 * k + m + 1] for i in range(2) for m in range(3)]
            norm_out[2 * k + half : 2 * k + half + 1] = jnp.concatenate(pieces, axis=1)

    for i in range(2):

        @pl.when(at_home(i))
        def _():
            token_home(i).wait()

        @pl.when(jnp.logical_not(at_home(i)))
        def _():
            token_copy(i).wait_send()
            remote(tok_ref.at[i], xin.at[i], tok_send.at[i], tok_recv.at[i], target(i)).wait_recv()

    x = xin[...].reshape(rows, width)
    x_out[...] = x
    cos, sin = cos_ref[pl.ds(c * rows, rows)], sin_ref[pl.ds(c * rows, rows)]
    low = low_lanes((rows, 128))
    for p in range(2):
        r = [dg(x, w[:, :, 2 * p + e, :, :640].reshape(width, 640), NN) for e in range(2)]
        t = [[v[:, 128 * i : 128 * i + 128] for i in range(5)] for v in r]
        qs = [t[0][0], jnp.where(low, t[0][3], swap64(t[1][3])), t[1][0]]
        ks = [t[0][1], jnp.where(low, swap64(t[0][3]), t[1][3]), t[1][1]]
        vs = [t[0][2], jnp.where(low, t[0][4], swap64(t[1][4])), t[1][2]]
        for i in range(3):
            q[3 * p + i] = (rope_fwd(qs[i], cos, sin) * HD**-0.5).astype(BF)
            kv[0, 3 * p + i] = rope_fwd(ks[i], cos, sin).astype(BF)
            kv[1, 3 * p + i] = vs[i].astype(BF)
    share = remote(kv, land_kv, kv_send, kv_recv, near)
    share.start()
    start = lead_parts + LAG
    rounds(start, start + 1)
    share.wait()

    def pair(p, carry):
        k = jnp.concatenate([kv[0, p], land_kv[0, p]], axis=0)
        v = jnp.concatenate([kv[1, p], land_kv[1, p]], axis=0)
        vt = v.astype(F32).T.astype(BF)
        outs = []
        for h in range(2):
            qm = jnp.where(low if h == 0 else jnp.logical_not(low), q[p], jnp.zeros((rows, 128), BF))
            s = dg(k, qm, NT) + mask_out[...]
            e = jnp.exp(s - jnp.max(s, axis=0, keepdims=True))
            inv = 1.0 / jnp.sum(e, axis=0, keepdims=True)
            outs.append(dg(vt[HD * h : HD * h + HD], e.astype(BF), NN) * inv)
        o[p] = jnp.concatenate(outs, axis=0).T.astype(BF)
        round_(start + 1 + p)
        return carry

    lax.fori_loop(0, 6, pair, 0)
    r = x.astype(F32)
    for p in range(2):
        wo = []
        for e in range(2):
            wo.append([w[:, :, 2 * p + e, :, 512 + 128 * i : 640 + 128 * i].reshape(width, 128) for i in range(2)])
        mid = jnp.where(low_lanes((width, 128)), swap64(wo[0][0].astype(F32)), wo[1][0].astype(F32)).astype(BF)
        r = r + dg(
            jnp.concatenate([o[3 * p + i] for i in range(3)], axis=1),
            jnp.concatenate([wo[0][1], mid, wo[1][1]], axis=1),
            NT,
        )
    n, inv = norm_parts(r)
    h = n * norm_out[0:1] + norm_out[2:3]
    hb[...] = h.astype(BF)
    acc[...] = h
    rounds(start + 7, start + 8)

    def units(k, carry):
        lax.fori_loop(
            jnp.maximum(start + 8, lead_parts + 3 * k + LAG),
            lead_parts + 3 * k + LAG + 3,
            lambda i, t: (round_(i), t)[1],
            0,
        )
        wg, wu, wd = unit_weights(
            lambda t, m: w[:, :, t, :, pl.ds(pl.multiple_of(width + GROUP * k + 128 * m, 128), 128)].reshape(width, 128)
        )
        gate = dg(hb[...], wg, NN)
        up = dg(hb[...], wu, NN)
        act = (gate / (1.0 + jnp.exp(-gate)) * up).astype(BF)
        acc[...] += dg(act, wd, NT)
        return carry

    lax.fori_loop(0, 6, units, 0)
    n, inv = norm_parts(acc[...])
    y_out[...] = (n * norm_out[1:2] + norm_out[3:4]).astype(BF)

    def finish(j, carry):
        write_back(j).wait()
        to_y(j).wait_send()
        to_core(j).wait_send()
        for h in range(last):

            @pl.when(jnp.logical_and(z >= h, z < last))
            def _():
                go_right(j, h).wait_send()

            @pl.when(jnp.logical_and(z + h <= last, z > 0))
            def _():
                go_left(j, h).wait_send()

        return carry

    lax.fori_loop(0, parts, finish, 0)


def first_layer(tokens, shard, extra, lengths, cos, sin):
    micro, own, width = tokens.shape
    depth, columns = shard.shape
    rows = 2 * own
    parts = columns // WIDE
    heads = width // 128
    dma = pltpu.SemaphoreType.DMA
    hbm = pl.BlockSpec(memory_space=pl.ANY)
    vm = pl.BlockSpec(memory_space=VM)
    return pl.pallas_call(
        functools.partial(first_kernel, parts),
        in_specs=[hbm, hbm, vm, vm, vm, vm],
        out_specs=[hbm, vm, vm, vm, vm],
        out_shape=[
            sds((2, 2, 4, depth, columns), BF),
            sds((rows, width), BF),
            sds((rows, width), BF),
            sds((2 * rows, rows), F32),
            sds((4, width), F32),
        ],
        scratch_shapes=[
            VM((2, 2, 4, depth, columns), BF),
            VM((2, own, width), BF),
            VM((heads, rows, 128), BF),
            VM((2, heads, rows, 128), BF),
            VM((2, heads, rows, 128), BF),
            VM((heads, rows, 128), BF),
            VM((8, 128), F32),
            VM((rows, width), BF),
            VM((rows, width), F32),
            VM((2, 2) + extra.shape, BF),
            VM((2,) + lengths.shape, jnp.int32),
            dma, dma((2,)), dma((2,)), dma, dma((parts,)), dma, dma,
            dma((3,)), dma((3,)),
            dma((parts, 3)), dma((parts, 3)), dma((parts, 3)), dma((parts, 3)),
            dma((parts,)), dma((parts,)), dma((parts,)), dma((parts,)),
        ],
        compiler_params=pltpu.CompilerParams(collective_id=1, has_side_effects=True, vmem_limit_bytes=60 << 20),
        name="first",
    )(tokens, shard, extra, lengths, cos, sin)


def swap_pairs(tp, step, dp_axes):
    pairs = []
    half = tp // 2
    for core in range(2):
        for at in range(tp):
            source = core * tp + at
            target = (at // half) * tp + half * core + (at + step) % half
            pairs.append((source, target))
    return pairs


def to_sequences(rows, tp):
    half = tp // 2
    at = lax.axis_index("tensor")
    pieces = [None] * half
    got = []
    for step in range(half):
        piece = lax.dynamic_index_in_dim(rows, (at + step) % half, 0, keepdims=False)
        got.append(lax.ppermute(piece, ("core", "tensor"), swap_pairs(tp, step, None)))
    stacked = jnp.stack(got)
    order = (at - jnp.arange(half)) % half
    return jnp.take(stacked, order, axis=0).reshape(-1, rows.shape[-1])


def to_positions(rows, tp):
    half = tp // 2
    at = lax.axis_index("tensor")
    parts = rows.reshape(half, -1, rows.shape[-1])
    got = []
    for step in range(half):
        piece = lax.dynamic_index_in_dim(parts, (at - step) % half, 0, keepdims=False)
        back = [(target, source) for source, target in swap_pairs(tp, step, None)]
        got.append(lax.ppermute(piece, ("core", "tensor"), back))
    stacked = jnp.stack(got)
    order = (at + jnp.arange(half)) % half
    return jnp.take(stacked, (jnp.arange(half) - at) % half, axis=0)


def rope_tables(positions):
    halfway = HD // 2
    freqs = 1000.0 ** (-jnp.arange(halfway, dtype=F32) / halfway)
    angles = positions.astype(F32)[:, None] * freqs[None, :]
    cos, sin = jnp.cos(angles), jnp.sin(angles)
    wide = jnp.concatenate([cos] * 4, axis=1)
    signed = jnp.concatenate([-sin, sin] * 2, axis=1)
    return wide, signed, cos.T, sin.T


def pack_shard(w_qkv, w_out, w_gate_up, w_down):
    rows = w_qkv.shape[0]
    odd = lax.axis_index("tensor") % 2 == 1
    heads = w_qkv.reshape(rows, 3, 3, HD)
    mine = w_out.T.reshape(rows, 3, HD)
    heads = jnp.where(odd, jnp.roll(heads, -1, axis=2), heads)
    mine = jnp.where(odd, jnp.roll(mine, -1, axis=1), mine)
    first = jnp.concatenate(
        [heads[:, :, :2].reshape(rows, -1), heads[:, :, 2].reshape(rows, -1), mine[:, 2], mine[:, :2].reshape(rows, -1)], axis=1
    )
    units = jnp.concatenate([w_gate_up, w_down.T[:, None]], axis=1)
    units = units.reshape(rows, 3, -1, 128).transpose(0, 2, 1, 3)
    return jnp.concatenate([first, units.reshape(rows, -1)], axis=1)


def unpack_shard(packed):
    rows, columns = packed.shape
    first = packed[:, :768]
    units = packed[:, 768:].reshape(rows, -1, 3, 128).transpose(0, 2, 1, 3).reshape(rows, 3, -1)
    pair, down = units[:, :2], units[:, 2]
    odd = lax.axis_index("tensor") % 2 == 1
    both = first[:, :384].reshape(rows, 3, 2, HD)
    single = first[:, 384:576].reshape(rows, 3, 1, HD)
    heads = jnp.concatenate([both, single], axis=2)
    mine = jnp.concatenate([first[:, 640:].reshape(rows, 2, HD), first[:, 576:640].reshape(rows, 1, HD)], axis=1)
    heads = jnp.where(odd, jnp.roll(heads, 1, axis=2), heads)
    mine = jnp.where(odd, jnp.roll(mine, 1, axis=1), mine)
    return (
        heads.reshape(rows, 3, -1),
        mine.reshape(rows, -1).T,
        pair,
        down.T,
    )


def host_tables(length):
    halfway = HD // 2
    freqs = np.float32(1000.0) ** (-np.arange(halfway, dtype=np.float32) / np.float32(halfway))
    angles = np.arange(length, dtype=np.float32)[:, None] * freqs[None, :]
    cos, sin = np.cos(angles), np.sin(angles)
    return np.concatenate([cos] * 4, axis=1), np.concatenate([-sin, sin] * 2, axis=1)


BLOCKS = 4


def gather_shard(shard, dp, tp):
    rows, columns = shard.shape
    got = lax.all_gather(shard, ALL, axis=0, tiled=False)
    got = got.reshape(BLOCKS, dp // BLOCKS, tp, rows, columns)
    return got.transpose(0, 2, 1, 3, 4).reshape(BLOCKS, tp, -1, columns)


def scatter_sum(whole, dp, tp):
    columns = whole.shape[3]
    parts = whole.reshape(BLOCKS, tp, dp // BLOCKS, -1, columns).transpose(0, 2, 1, 3, 4)
    parts = parts.reshape(dp * tp, -1, columns)
    return lax.psum_scatter(parts, ALL, scatter_dimension=0, tiled=False).astype(F32)


def on_device(dp, tp, tokens, cotangent, lengths, w_qkv, w_out, w_gate_up, w_down, norm_gains, norm_biases):
    section = lax.axis_index("section")
    core = lax.axis_index("core")
    at = lax.axis_index("tensor")
    micro, own, width = tokens.shape
    assert micro * 2 == tp
    length = own * tp
    rows = length // 2
    shard = pack_shard(w_qkv[0], w_out[0], w_gate_up[0], w_down[0])
    near = core * rows + jnp.arange(rows, dtype=jnp.int32)
    far = (1 - core) * rows + jnp.arange(rows, dtype=jnp.int32)
    tabs = rope_tables(near)
    grad_top = to_sequences(cotangent, tp)
    if dp == 4 and tp == 4:
        extra = jnp.concatenate([norm_gains.reshape(-1, 128), norm_biases.reshape(-1, 128)])
        extra = jnp.pad(extra, ((0, 16 - extra.shape[0]), (0, 0)))
        padded = jnp.pad(lengths, ((0, 8 - lengths.shape[0]), (0, 128 - lengths.shape[1])))
        wide, signed = host_tables(length)
        weights, y, tokens, mask, small = first_layer(tokens, shard, extra, padded, wide, signed)
        weights = weights.reshape((BLOCKS,) + weights.shape[2:])
        norms = (small[:2], small[2:])
    else:
        weights = gather_shard(shard, dp, tp)
        norms = jnp.concatenate([norm_gains, norm_biases])
        norms = lax.all_gather(norms, ("y", "core"), axis=1, tiled=True).astype(F32)
        norms = (norms[0].reshape(2, width), norms[1].reshape(2, width))
        tokens = to_sequences(tokens, tp)
        chip_lengths = lax.all_gather(lengths, "core", axis=0, tiled=True)
        my_lengths = lax.dynamic_index_in_dim(chip_lengths, at, 0, keepdims=False)
        ends_at = jnp.cumsum(my_lengths)

        def segment(positions):
            return jnp.sum((ends_at[None, :] <= positions[:, None]).astype(jnp.int32), axis=-1)

        seg_near = segment(near)
        seg_all = jnp.concatenate([seg_near, segment(far)])
        mask = jnp.where(seg_all[:, None] == seg_near[None, :], 0.0, neg_fill).astype(F32)
        y, unused = forward(tokens, weights, norms, mask, tabs)
    received = lax.ppermute(y, "section", [(0, 1)])
    inputs = jnp.where(section == 0, tokens, received)
    y, kept = forward(inputs, weights, norms, mask, tabs)
    dz, grads = backward(inputs, grad_top, kept, weights, norms, tabs)
    received = lax.ppermute(dz.astype(BF), "section", [(1, 0)])
    dy = jnp.where(section == 0, received, grad_top)
    dz, grads = backward(inputs, dy, kept, weights, norms, tabs)
    ends = to_positions(jnp.where(section == 0, dz.astype(BF), y), tp)
    g, ng = grads
    if dp == 4 and tp == 4:
        mine, total = sum_over_section(g, ng)
        index = lax.axis_index(ALL)
        small = lax.dynamic_slice_in_dim(total[:4].reshape(2, dp * tp, -1), index, 1, 1)
        gains, biases = small[0, 0], small[1, 0]
    else:
        mine = scatter_sum(g, dp, tp)
        gains = lax.psum_scatter(ng[0:2].reshape(-1), ALL, scatter_dimension=0, tiled=True)
        biases = lax.psum_scatter(ng[2:4].reshape(-1), ALL, scatter_dimension=0, tiled=True)
    outs = unpack_shard(mine)
    return (ends[None],) + tuple(t[None] for t in outs + (gains, biases))


def solution(mesh):
    sections, dp, tp = mesh.devices.shape
    fine = Mesh(mesh.devices.reshape(sections, dp // 2, 2, tp), ("section", "y", "core", "tensor"))
    both = ("y", "core")
    in_specs = (
        P(both, "tensor", None),
        P(both, "tensor", None),
        P(both, None),
        P("section", both, None, "tensor"),
        P("section", "tensor", both),
        P("section", both, None, "tensor"),
        P("section", "tensor", both),
        P("section", both),
        P("section", both),
    )
    out_specs = (
        P("section", both, "tensor", None),
        P("section", both, None, "tensor"),
        P("section", "tensor", both),
        P("section", both, None, "tensor"),
        P("section", "tensor", both),
        P("section", ALL),
        P("section", ALL),
    )
    return jax.shard_map(
        functools.partial(on_device, dp, tp), mesh=fine, in_specs=in_specs, out_specs=out_specs, check_vma=False
    )
```

```python
import functools

import jax
import jax.numpy as jnp
import numpy as np
from jax import lax
from jax.experimental import pallas as pl
from jax.experimental.pallas import tpu as pltpu
from jax.sharding import Mesh, PartitionSpec as P

HD = 64
eps = 1e-05
neg_fill = -1e30
ALL = ("y", "core", "tensor")
BF = jnp.bfloat16
F32 = jnp.float32
MESH = pl.DeviceIdType.MESH


def dg(a, b, dims):
    return lax.dot_general(a, b, (dims, ((), ())), preferred_element_type=F32)


NN = ((1,), (0,))
NT = ((1,), (1,))
TN = ((0,), (0,))


def low_lanes(shape):
    return lax.broadcasted_iota(jnp.int32, shape, 1) < HD


def swap64(v):
    return pltpu.roll(v, HD, axis=1)


def rope_fwd(t, cos, sin):
    lane = lax.broadcasted_iota(jnp.int32, t.shape, 1) % HD
    other = jnp.where(lane < HD // 2, pltpu.roll(t, 128 - HD // 2, axis=1), pltpu.roll(t, HD // 2, axis=1))
    return t * cos + other * sin


def qkv_kernel(x_ref, w_ref, cos_ref, sin_ref, q_ref, k_ref, v_ref):
    x = x_ref[...]
    width = x.shape[1]
    r = [dg(x, w_ref[:, e, :, :640].reshape(width, 640), NN) for e in range(2)]
    c = [[t[:, 128 * i : 128 * i + 128] for i in range(5)] for t in r]
    low = low_lanes(c[0][0].shape)
    qs = [c[0][0], jnp.where(low, c[0][3], swap64(c[1][3])), c[1][0]]
    ks = [c[0][1], jnp.where(low, swap64(c[0][3]), c[1][3]), c[1][1]]
    vs = [c[0][2], jnp.where(low, c[0][4], swap64(c[1][4])), c[1][2]]
    cos, sin = cos_ref[...], sin_ref[...]
    for i in range(3):
        q_ref[i] = (rope_fwd(qs[i], cos, sin) * HD**-0.5).astype(BF)
        k_ref[i] = rope_fwd(ks[i], cos, sin).astype(BF)
        v_ref[i] = vs[i].astype(BF)


def attn_kernel(q_ref, k_ref, v_ref, ko_ref, vo_ref, m_ref, o_ref, e_ref, l_ref):
    q = q_ref[0]
    k = jnp.concatenate([k_ref[0], ko_ref[0]], axis=0)
    v = jnp.concatenate([v_ref[0], vo_ref[0]], axis=0)
    vt = v.astype(F32).T.astype(BF)
    outs = []
    for h in range(2):
        low = low_lanes(q.shape)
        qm = jnp.where(low if h == 0 else jnp.logical_not(low), q, jnp.zeros_like(q))
        s = dg(k, qm, NT) + m_ref[...]
        e = jnp.exp(s - jnp.max(s, axis=0, keepdims=True))
        inv = 1.0 / jnp.sum(e, axis=0, keepdims=True)
        eb = e.astype(BF)
        e_ref[0, h] = eb
        l_ref[0, h] = jnp.broadcast_to(inv, l_ref.shape[2:])
        outs.append(dg(vt[HD * h : HD * h + HD], eb, NN) * inv)
    o_ref[0] = jnp.concatenate(outs, axis=0).T.astype(BF)


def norm_parts(r):
    center = r - jnp.mean(r, axis=-1, keepdims=True)
    inv = lax.rsqrt(jnp.mean(center * center, axis=-1, keepdims=True) + eps)
    return center * inv, inv


def norm_back(dn, n, inv):
    return inv * (dn - jnp.mean(dn, axis=-1, keepdims=True) - n * jnp.mean(dn * n, axis=-1, keepdims=True))


def out_weight(w_ref):
    c = [[w_ref[:, e, :, 128 * i : 128 * i + 128].reshape(-1, 128) for i in range(2)] for e in range(2)]
    low = low_lanes(c[0][0].shape)
    mid = jnp.where(low, swap64(c[0][0].astype(F32)), c[1][0].astype(F32)).astype(BF)
    return [c[0][1], mid, c[1][1]]


GROUP = 384
WIDE = 128


def unit_weights(load):
    return [jnp.concatenate([load(t, m) for t in range(4)], axis=1) for m in range(3)]


def ffn_kernel(x_ref, o_ref, wo_ref, w_ref, g_ref, b_ref, y_ref, gu_ref, n1_ref, i1_ref, n2_ref, i2_ref, h_ref, hb_ref, acc_ref):
    z = pl.program_id(0)
    width = x_ref.shape[1]

    @pl.when(z == 0)
    def _():
        r = x_ref[...].astype(F32)
        for p in range(2):
            w = jnp.concatenate(out_weight(wo_ref.at[:, 2 * p : 2 * p + 2]), axis=1)
            o = jnp.concatenate([o_ref[3 * p + i] for i in range(3)], axis=1)
            r = r + dg(o, w, NT)
        n, inv = norm_parts(r)
        n1_ref[...] = n
        i1_ref[...] = jnp.broadcast_to(inv, i1_ref.shape)
        h = n * g_ref[0:1] + b_ref[0:1]
        h_ref[...] = h
        hb_ref[...] = h.astype(BF)

    hb = hb_ref[...]
    wg, wu, wd = unit_weights(lambda t, m: w_ref[:, t, :, 128 * m : 128 * m + 128].reshape(width, 128))
    gate = dg(hb, wg, NN)
    up = dg(hb, wu, NN)
    gu_ref[0, 0] = gate.astype(BF)
    gu_ref[0, 1] = up.astype(BF)
    act = (gate / (1.0 + jnp.exp(-gate)) * up).astype(BF)
    part = dg(act, wd, NT)

    @pl.when(z == 0)
    def _():
        acc_ref[...] = h_ref[...] + part

    @pl.when(z > 0)
    def _():
        acc_ref[...] += part

    @pl.when(z == pl.num_programs(0) - 1)
    def _():
        n, inv = norm_parts(acc_ref[...])
        n2_ref[...] = n
        i2_ref[...] = jnp.broadcast_to(inv, i2_ref.shape)
        y_ref[...] = (n * g_ref[1:2] + b_ref[1:2]).astype(BF)


def ffn_back_kernel(grads, dy_ref, n1_ref, i1_ref, n2_ref, i2_ref, gu_ref, w_ref, g_ref, b_ref, *refs):
    if grads:
        g_out, dr1_ref, da_ref, ng_ref, hb_ref, df_ref, acc_ref = refs
    else:
        dr1_ref, da_ref, df_ref, acc_ref = refs
    z = pl.program_id(0)
    width = dy_ref.shape[1]

    @pl.when(z == 0)
    def _():
        dy = dy_ref[...].astype(F32)
        n = n2_ref[...]
        if grads:
            ng_ref[1:2] = jnp.sum(dy * n, axis=0, keepdims=True)
            ng_ref[3:4] = jnp.sum(dy, axis=0, keepdims=True)
            hb_ref[...] = (n1_ref[...] * g_ref[0:1] + b_ref[0:1]).astype(BF)
        dr2 = norm_back(dy * g_ref[1:2], n, i2_ref[:, :1])
        acc_ref[...] = dr2
        df_ref[...] = dr2.astype(BF)

    df = df_ref[...]
    gate = gu_ref[0, 0].astype(F32)
    up = gu_ref[0, 1].astype(F32)
    s = 1.0 / (1.0 + jnp.exp(-gate))
    silu = gate * s
    wg, wu, wd = unit_weights(lambda t, m: w_ref[:, t, :, 128 * m : 128 * m + 128].reshape(width, 128))

    def keep(m, grad):
        for t in range(g_out.shape[1]):
            g_out[:, t, :, 128 * m : 128 * m + 128] = grad[:, 128 * t : 128 * t + 128].astype(BF).reshape(g_out.shape[0], -1, 128)

    if grads:
        keep(2, dg(df, (silu * up).astype(BF), TN))
    d_act = dg(df, wd, NN)
    d_gate = (d_act * up * (s * (1.0 + gate * (1.0 - s)))).astype(BF)
    d_up = (d_act * silu).astype(BF)
    if grads:
        hb = hb_ref[...]
        keep(0, dg(hb, d_gate, TN))
        keep(1, dg(hb, d_up, TN))
    acc_ref[...] += dg(d_gate, wg, NT) + dg(d_up, wu, NT)

    @pl.when(z == pl.num_programs(0) - 1)
    def _():
        dh = acc_ref[...]
        n = n1_ref[...]
        if grads:
            ng_ref[0:1] = jnp.sum(dh * n, axis=0, keepdims=True)
            ng_ref[2:3] = jnp.sum(dh, axis=0, keepdims=True)
        dr1 = norm_back(dh * g_ref[0:1], n, i1_ref[:, :1])
        dr1_ref[...] = dr1
        da_ref[...] = dr1.astype(BF)


def pair_back(do, o, q, k, v, ko, vo, e, l, cos, sin):
    dot = do.astype(F32).T
    ot = o.astype(F32).T
    k = jnp.concatenate([k, ko], axis=0)
    v = jnp.concatenate([v, vo], axis=0)
    kt = k.astype(F32).T.astype(BF)
    qt = q.astype(F32).T.astype(BF)
    dqs, dks, dvs = [], [], []
    for h in range(2):
        span = slice(HD * h, HD * h + HD)
        scaled = dot[span] * l[h]
        inner = jnp.sum(scaled * ot[span], axis=0, keepdims=True)
        sb = scaled.astype(BF)
        zero = jnp.zeros_like(sb)
        padded = jnp.concatenate([sb, zero] if h == 0 else [zero, sb], axis=0)
        dp = dg(v, padded, NN)
        et = e[h]
        ds = (et.astype(F32) * (dp - inner)).astype(BF)
        dvs.append(dg(sb, et, NT))
        dks.append(dg(qt[span], ds, NT))
        dqt = dg(kt[span], ds, NN) * HD**-0.5
        d1, d2 = dqt[: HD // 2], dqt[HD // 2 :]
        dqs.append(d1 * cos + d2 * sin)
        dqs.append(d2 * cos - d1 * sin)
    return [jnp.concatenate(t, axis=0) for t in (dqs, dks, dvs)]


def joint_parts(dq, dkt, dvt, cos, sin):
    dk = []
    for t in dkt:
        parts = []
        for h in range(2):
            d1 = t[HD * h : HD * h + HD // 2]
            d2 = t[HD * h + HD // 2 : HD * h + HD]
            parts += [d1 * cos + d2 * sin, d2 * cos - d1 * sin]
        dk.append(jnp.concatenate(parts, axis=0).T)
    dv = [t.T for t in dvt]
    low = low_lanes(dq[0].shape)
    zero = jnp.zeros_like(dv[1])
    d = [
        [dq[0], dk[0], dv[0], jnp.where(low, dq[1], swap64(dk[1])), jnp.where(low, dv[1], zero)],
        [dq[2], dk[2], dv[2], jnp.where(low, swap64(dq[1]), dk[1]), jnp.where(low, swap64(dv[1]), zero)],
    ]
    return [jnp.concatenate(t, axis=1).astype(BF) for t in d]


def attn_back_kernel(grads, da_ref, wo_ref, o_ref, q_ref, k_ref, v_ref, ko_ref, vo_ref, e_ref, l_ref, cos_ref, sin_ref, dq_ref, own_ref, oth_ref, *dwo_ref):
    da = da_ref[...]
    rows = da.shape[0]
    w = jnp.concatenate(out_weight(wo_ref), axis=1)
    do3 = dg(da, w, NN).astype(BF)
    if grads:
        o3 = jnp.concatenate([o_ref[i] for i in range(3)], axis=1)
        dwo_ref[0][0] = dg(da, o3, TN).astype(BF)
    cos, sin = cos_ref[...], sin_ref[...]
    for i in range(3):
        dqt, dk, dv = pair_back(
            do3[:, 128 * i : 128 * i + 128], o_ref[i], q_ref[i], k_ref[i], v_ref[i], ko_ref[i], vo_ref[i],
            [e_ref[i, h] for h in range(2)], [l_ref[i, h, 0:1] for h in range(2)], cos, sin,
        )
        dq_ref[i] = dqt.T.astype(BF)
        own_ref[i, 0] = dk[:, :rows]
        own_ref[i, 1] = dv[:, :rows]
        oth_ref[i, 0] = dk[:, rows:].astype(BF)
        oth_ref[i, 1] = dv[:, rows:].astype(BF)


def joint_back_kernel(grads, *refs):
    if grads:
        old_ref, x_ref, w_ref, dr1_ref, dq_ref, own_ref, got_ref, dwo_ref, cos_ref, sin_ref, g_ref, dz_ref = refs
    else:
        w_ref, dr1_ref, dq_ref, own_ref, got_ref, cos_ref, sin_ref, dz_ref, dzb_ref = refs
    p = pl.program_id(0)
    width = dr1_ref.shape[1]
    d = joint_parts(
        [dq_ref[i].astype(F32) for i in range(3)],
        [own_ref[i, 0] + got_ref[i, 0].astype(F32) for i in range(3)],
        [own_ref[i, 1] + got_ref[i, 1].astype(F32) for i in range(3)],
        cos_ref[...],
        sin_ref[...],
    )
    acc = None
    for e in range(2):
        t = dg(d[e], w_ref[:, e, :, :640].reshape(width, 640), NT)
        acc = t if acc is None else acc + t
    if grads:
        x = x_ref[...]
        wlow = low_lanes((width, 128))
        mid = dwo_ref[0, :, 128:256].astype(F32)
        sides = [dwo_ref[0, :, 0:128], dwo_ref[0, :, 256:384]]
        mids = [swap64(mid), mid]
        for e in range(2):
            g = dg(x, d[e], TN)
            blocks = g_ref.shape[0]
            g_ref[:, e, :, :512] = g[:, :512].astype(BF).reshape(blocks, -1, 512)
            g_ref[:, e, :, 512:640] = jnp.where(wlow, g[:, 512:], mids[e]).astype(BF).reshape(blocks, -1, 128)
            g_ref[:, e, :, 640:] = sides[e].reshape(blocks, -1, 128)

    @pl.when(p == 0)
    def _():
        dz_ref[...] = dr1_ref[...] + acc

    @pl.when(p > 0)
    def _():
        total = dz_ref[...] + acc
        dz_ref[...] = total
        if not grads:
            dzb_ref[...] = total.astype(BF)


BIG = pltpu.CompilerParams(vmem_limit_bytes=58 << 20)
VM = pltpu.VMEM


def full(shape):
    return pl.BlockSpec(shape, lambda i: (0,) * len(shape))


def lead(shape, at=0):
    return pl.BlockSpec(shape, lambda i: tuple(i if j == at else 0 for j in range(len(shape))))


def joint_block(w):
    return pl.BlockSpec((w.shape[0], 2, w.shape[2], 768), lambda i: (0, i, 0, 0))


def group_block(w):
    return pl.BlockSpec((w.shape[0], w.shape[1], w.shape[2], GROUP), lambda i: (0, 0, 0, 2 + i))


def sds(shape, kind):
    return jax.ShapeDtypeStruct(shape, kind)


def forward(x, weights, norms, mask, tabs):
    w = weights
    gains, biases = norms
    rows, width = x.shape
    heads = width // 128
    blocks, tp, depth, columns = w.shape
    steps = tp // 2
    cos, sin, cost, sint = tabs
    q, k, v = pl.pallas_call(
        qkv_kernel,
        grid=(steps,),
        in_specs=[full((rows, width)), joint_block(w), full((rows, 128)), full((rows, 128))],
        out_specs=[lead((3, rows, 128))] * 3,
        out_shape=[sds((heads, rows, 128), BF)] * 3,
        compiler_params=BIG,
        name="qkv",
    )(x, w, cos, sin)
    ko, vo = lax.ppermute((k, v), "core", [(0, 1), (1, 0)])
    pair = lead((1, rows, 128))
    o, e, l = pl.pallas_call(
        attn_kernel,
        grid=(heads,),
        in_specs=[pair] * 5 + [full((2 * rows, rows))],
        out_specs=[pair, lead((1, 2, 2 * rows, rows)), lead((1, 2, 8, rows))],
        out_shape=[sds((heads, rows, 128), BF), sds((heads, 2, 2 * rows, rows), BF), sds((heads, 2, 8, rows), F32)],
        compiler_params=BIG,
        name="attn",
    )(q, k, v, ko, vo, mask)
    groups = (columns - width) // GROUP
    units = tp * 128
    y, gu, n1, i1, n2, i2 = pl.pallas_call(
        ffn_kernel,
        grid=(groups,),
        in_specs=[
            full((rows, width)),
            full((heads, rows, 128)),
            pl.BlockSpec((blocks, tp, depth, 256), lambda i: (0, 0, 0, 2)),
            group_block(w),
            full((2, width)),
            full((2, width)),
        ],
        out_specs=[full((rows, width)), lead((1, 2, rows, units))] + [full((rows, width)), full((rows, 128))] * 2,
        out_shape=[sds((rows, width), BF), sds((groups, 2, rows, units), BF)] + [sds((rows, width), F32), sds((rows, 128), F32)] * 2,
        scratch_shapes=[VM((rows, width), F32), VM((rows, width), BF), VM((rows, width), F32)],
        compiler_params=BIG,
        name="ffn",
    )(x, o, w, w, gains, biases)
    return y, (q, k, v, ko, vo, o, e, l, gu, n1, i1, n2, i2)


def ffn_backward(dy, kept, w, norms, grads):
    gains, biases = norms
    gu, n1, i1, n2, i2 = kept[8:]
    rows, width = dy.shape
    blocks, tp, depth, columns = w.shape
    groups = (columns - width) // GROUP
    whole, stat = full((rows, width)), full((rows, 128))
    outs = [whole, whole]
    shapes = [sds((rows, width), F32), sds((rows, width), BF)]
    scratch = [VM((rows, width), BF), VM((rows, width), F32)]
    if grads:
        outs = [group_block(w)] + outs + [full((8, width))]
        shapes = [sds(w.shape, BF)] + shapes + [sds((8, width), F32)]
        scratch = [VM((rows, width), BF)] + scratch
    return pl.pallas_call(
        functools.partial(ffn_back_kernel, grads),
        grid=(groups,),
        in_specs=[
            whole, whole, stat, whole, stat,
            lead((1, 2, rows, tp * 128)),
            group_block(w),
            full((2, width)), full((2, width)),
        ],
        out_specs=outs,
        out_shape=shapes,
        scratch_shapes=scratch,
        compiler_params=BIG,
        name="ffn_back" if grads else "ffn_back_light",
    )(dy, n1, i1, n2, i2, gu, w, gains, biases)


def attn_backward(x, da, dr1, g, kept, w, tabs):
    grads = g is not None
    q, k, v, ko, vo, o, e, l = kept[:8]
    rows, width = da.shape
    heads = width // 128
    blocks, tp, depth, columns = w.shape
    steps = tp // 2
    cos, sin, cost, sint = tabs
    whole = full((rows, width))
    three = lead((3, rows, 128))
    side = lead((3, 2, 128, rows))
    table = full((HD // 2, rows))
    extra = [lead((1, width, 384))] if grads else []
    dq, own, oth, *dwo = pl.pallas_call(
        functools.partial(attn_back_kernel, grads),
        grid=(steps,),
        in_specs=[
            whole,
            pl.BlockSpec((blocks, 2, depth, 256), lambda i: (0, i, 0, 2)),
            three, three, three, three, three, three,
            lead((3, 2, 2 * rows, rows)),
            lead((3, 2, 8, rows)),
            table, table,
        ],
        out_specs=[three, side, side] + extra,
        out_shape=[
            sds((heads, rows, 128), BF),
            sds((heads, 2, 128, rows), F32),
            sds((heads, 2, 128, rows), BF),
        ]
        + ([sds((steps, width, 384), BF)] if grads else []),
        compiler_params=BIG,
        name="attn_back",
    )(da, w, o, q, k, v, ko, vo, e, l, cost, sint)
    got = lax.ppermute(oth, "core", [(0, 1), (1, 0)])
    if grads:
        specs = [pl.BlockSpec(memory_space=pl.ANY), whole, joint_block(w), whole, three, side, side] + extra
        args = (g, x, w, dr1, dq, own, got, *dwo)
        outs, shapes = [joint_block(w), whole], [sds(w.shape, BF), sds((rows, width), F32)]
    else:
        specs = [joint_block(w), whole, three, side, side]
        args = (w, dr1, dq, own, got)
        outs, shapes = [whole, whole], [sds((rows, width), F32), sds((rows, width), BF)]
    return pl.pallas_call(
        functools.partial(joint_back_kernel, grads),
        grid=(steps,),
        in_specs=specs + [table, table],
        out_specs=outs,
        out_shape=shapes,
        input_output_aliases={0: 0} if grads else {},
        compiler_params=BIG,
        name="joint_back",
    )(*args, cost, sint)


def last_kernel(
    parts, da_ref, wo_ref, o_ref, q_ref, k_ref, v_ref, ko_ref, vo_ref, e_ref, l_ref, cos_ref, sin_ref,
    x_ref, w_ref, dr1_ref, y_ref, g_ref, ng_ref,
    first_out, pair_out, down_out, ends_out, norm_out,
    do3, dwo, dq, keep, oth, got, dz, g1, e_send, e_land, tmp, own, land_c, land_y, land_r, land_l, land_n,
    oth_send, oth_recv, end_sem, end_send, end_recv,
    own_sem, cs_sem, cr_sem, ys_sem, yr_sem, rs_sem, rr_sem, ls_sem, lr_sem, ns_sem, nr_sem,
):
    step = pl.program_id(0)
    section = lax.axis_index("section")
    y, c, z = lax.axis_index("y"), lax.axis_index("core"), lax.axis_index("tensor")
    last = 3
    rows, width = da_ref.shape
    early = parts - width // WIDE
    near, across = {"core": 1 - c}, {"y": 1 - y}
    right, left = {"tensor": jnp.minimum(z + 1, last)}, {"tensor": jnp.maximum(z - 1, 0)}
    pair = {"tensor": z + 1 - 2 * lax.rem(z, 2)}
    far = {"tensor": lax.rem(z + 2, 4)}
    side = z // 2
    barrier = pltpu.get_barrier_semaphore()

    def greet(device):
        pl.semaphore_signal(barrier, inc=1, device_id=device, device_id_type=MESH)

    def remote(src, dst, send, recv, device):
        return pltpu.make_async_remote_copy(src, dst, send, recv, device_id=device, device_id_type=MESH)

    def target(i):
        return {"core": side, "tensor": 2 * c + i}

    def at_home(i):
        return jnp.logical_and(side == c, 2 * c + i == z)

    def end_copy(i):
        return remote(e_send.at[i], e_land.at[z % 2], end_send.at[i], end_recv.at[z % 2], target(i))

    def end_home(i):
        return pltpu.make_async_copy(e_send.at[i], e_land.at[z % 2], end_sem)

    def oth_copy(p):
        return remote(oth.at[p], got.at[p], oth_send.at[p], oth_recv.at[p], near)

    def columns(j):
        return pl.ds(pl.multiple_of(j * WIDE, WIDE), WIDE)

    def late(j):
        return columns(j - early)

    def load(j):
        return pltpu.make_async_copy(g_ref.at[:, c, :, :, columns(j + parts - early)], own.at[j % 4], own_sem.at[j])

    def to_core(j, kept=False):
        src = g1.at[:, 1 - c, :, :, late(j)] if kept else g_ref.at[:, 1 - c, :, :, columns(j + parts - early)]
        return remote(src, land_c.at[j], cs_sem.at[j], cr_sem.at[j], near)

    def from_core(j):
        return remote(land_c.at[j], land_c.at[j], cs_sem.at[j], cr_sem.at[j], near)

    def to_y(j):
        return remote(land_c.at[j, 1 - y], land_y.at[j], ys_sem.at[j], yr_sem.at[j], across)

    def norm_copy(k):
        return remote(land_n.at[2 * k], land_n.at[2 * k + 1], ns_sem.at[k], nr_sem.at[k], (near, across, pair, far)[k])

    def go_right(j, first, src):
        return remote(src, land_r.at[j, pl.ds(first - 1, 4 - first)], rs_sem.at[j], rr_sem.at[j], right)

    def go_left(j, count, src):
        return remote(src, land_l.at[j, pl.ds(0, count)], ls_sem.at[j], lr_sem.at[j], left)

    def prepare(j):
        @pl.when(j < early)
        def _():
            to_core(j).start()
            load(j).start()

        @pl.when(jnp.logical_and(j >= early, j < parts))
        def _():
            to_core(j, True).start()

    def stage(i, lag, body):
        @pl.when(jnp.logical_and(i >= lag, i - lag < parts))
        def _():
            body(i - lag)

    def first_sum(j):
        from_core(j).wait_recv()

        @pl.when(j < early)
        def _():
            load(j).wait()
            land_c[j] = land_c[j] + own[j % 4]

        @pl.when(j >= early)
        def _():
            land_c[j] = land_c[j] + g1[:, c, :, :, late(j)]

        to_y(j).start()

    def last_hop(j):
        @pl.when(z == 1)
        def _():
            go_left(j, 2, land_l.at[j, pl.ds(0, 2)]).wait_recv()
            land_l[j, 0] = land_l[j, 0] + land_c[j, y, 0]
            go_left(j, 1, land_l.at[j, pl.ds(0, 1)]).start()

        @pl.when(z == 2)
        def _():
            go_right(j, 2, land_r.at[j, pl.ds(1, 2)]).wait_recv()
            land_r[j, 2] = land_r[j, 2] + land_c[j, y, 3]
            go_right(j, 3, land_r.at[j, pl.ds(2, 1)]).start()

    def next_hop(j):
        @pl.when(z == 1)
        def _():
            go_right(j, 1, land_r.at[j]).wait_recv()
            for k in (2, 3):
                land_r[j, k - 1] = land_r[j, k - 1] + land_c[j, y, k]
            go_right(j, 2, land_r.at[j, pl.ds(1, 2)]).start()

        @pl.when(z == 2)
        def _():
            go_left(j, 3, land_l.at[j]).wait_recv()
            for k in (0, 1):
                land_l[j, k] = land_l[j, k] + land_c[j, y, k]
            go_left(j, 2, land_l.at[j, pl.ds(0, 2)]).start()

    def first_hop(j):
        to_y(j).wait_recv()
        land_c[j, y] = land_c[j, y] + land_y[j]

        @pl.when(z == 0)
        def _():
            go_right(j, 1, land_c.at[j, y, pl.ds(1, 3)]).start()

        @pl.when(z == last)
        def _():
            go_left(j, 3, land_c.at[j, y, pl.ds(0, 3)]).start()

    def result(j):
        mine = land_c[j, y, z].astype(F32)

        @pl.when(z == 0)
        def _():
            go_left(j, 1, land_l.at[j, pl.ds(0, 1)]).wait_recv()
            tmp[...] = mine + land_l[j, 0].astype(F32)

        @pl.when(z == 1)
        def _():
            tmp[...] = mine + land_r[j, 0].astype(F32) + land_l[j, 1].astype(F32)

        @pl.when(z == 2)
        def _():
            tmp[...] = mine + land_r[j, 1].astype(F32) + land_l[j, 2].astype(F32)

        @pl.when(z == last)
        def _():
            go_right(j, 3, land_r.at[j, pl.ds(2, 1)]).wait_recv()
            tmp[...] = mine + land_r[j, 2].astype(F32)

        group = j // 3

        @pl.when(j >= early)
        def _():
            first_out[:, late(j)] = tmp[...]

        for m in range(2):

            @pl.when(jnp.logical_and(j < early, j % 3 == m))
            def _():
                pair_out[:, columns(group + m * (early // 3))] = tmp[...]

        @pl.when(jnp.logical_and(j < early, j % 3 == 2))
        def _():
            down_out[columns(group), :] = tmp[...].T

    def round_(i):
        prepare(i + 2)
        stage(i, 0, first_sum)
        stage(i, 4, last_hop)
        stage(i, 3, next_hop)
        stage(i, 2, first_hop)
        stage(i, 5, result)
        for k in range(4):

            @pl.when(i == 3 * (k + 1))
            def _():
                norm_copy(k).wait()
                total = land_n[2 * k] + land_n[2 * k + 1]
                if k < 3:
                    land_n[2 * k + 2] = total
                    norm_copy(k + 1).start()
                else:
                    norm_out[...] = total

    @pl.when(step == 0)
    def _():
        greet(near)
        greet(across)
        greet(far)

        @pl.when(z < last)
        def _():
            greet(right)

        @pl.when(z > 0)
        def _():
            greet(left)

        for i in range(2):

            @pl.when(jnp.logical_not(at_home(i)))
            def _():
                greet(target(i))

        count = 5 + jnp.where(z < last, 1, 0) + jnp.where(z > 0, 1, 0) - jnp.where(side == c, 1, 0)
        pl.semaphore_wait(barrier, count)
        prepare(0)
        prepare(1)
        land_n[0] = ng_ref[...]
        norm_copy(0).start()

    cos, sin = cos_ref[...], sin_ref[...]

    @pl.when(jnp.logical_and(step < 6, step % 3 == 0))
    def _():
        w = jnp.concatenate(out_weight(wo_ref), axis=1)
        t = dg(da_ref[...], w, NN).astype(BF)
        for i in range(3):
            do3[i] = t[:, 128 * i : 128 * i + 128]
        o3 = jnp.concatenate([o_ref[step + i] for i in range(3)], axis=1)
        dwo[step // 3] = dg(da_ref[...], o3, TN).astype(BF)

    @pl.when(step < 6)
    def _():
        dqt, dk, dv = pair_back(
            do3[step % 3], o_ref[step], q_ref[0], k_ref[0], v_ref[0], ko_ref[0], vo_ref[0],
            [e_ref[0, h] for h in range(2)], [l_ref[0, h, 0:1] for h in range(2)], cos, sin,
        )
        dq[step] = dqt.T.astype(BF)
        keep[step, 0] = dk[:, :rows]
        keep[step, 1] = dv[:, :rows]
        oth[step, 0] = dk[:, rows:].astype(BF)
        oth[step, 1] = dv[:, rows:].astype(BF)
        oth_copy(step).start()

    @pl.when(step >= 6)
    def _():
        p = step - 6
        for i in range(3):
            oth_copy(3 * p + i).wait()
        d = joint_parts(
            [dq[3 * p + i].astype(F32) for i in range(3)],
            [keep[3 * p + i, 0] + got[3 * p + i, 0].astype(F32) for i in range(3)],
            [keep[3 * p + i, 1] + got[3 * p + i, 1].astype(F32) for i in range(3)],
            cos, sin,
        )
        acc = None
        wlow = low_lanes((width, 128))
        mid = dwo[p, :, 128:256].astype(F32)
        sides = [dwo[p, :, 0:128], dwo[p, :, 256:384]]
        mids = [swap64(mid), mid]
        for e in range(2):
            t = dg(d[e], w_ref[:, e, :, :640].reshape(width, 640), NT)
            acc = t if acc is None else acc + t
            g = dg(x_ref[...], d[e], TN)
            shape = (2, 2, width // 4)
            g1[:, :, 2 * p + e, :, :512] = g[:, :512].astype(BF).reshape(shape + (512,))
            g1[:, :, 2 * p + e, :, 512:640] = jnp.where(wlow, g[:, 512:], mids[e]).astype(BF).reshape(shape + (128,))
            g1[:, :, 2 * p + e, :, 640:] = sides[e].reshape(shape + (128,))

        @pl.when(p == 0)
        def _():
            dz[...] = dr1_ref[...] + acc

        @pl.when(p > 0)
        def _():
            value = jnp.where(section == 0, (dz[...] + acc).astype(BF), y_ref[...])
            e_send[...] = value.reshape(e_send.shape)
            for i in range(2):

                @pl.when(at_home(i))
                def _():
                    end_home(i).start()

                @pl.when(jnp.logical_not(at_home(i)))
                def _():
                    end_copy(i).start()

    round_(step)

    @pl.when(step == 7)
    def _():
        lax.fori_loop(8, parts + 5, lambda i, t: (round_(i), t)[1], 0)
        for i in range(2):

            @pl.when(at_home(i))
            def _():
                end_home(i).wait()

            @pl.when(jnp.logical_not(at_home(i)))
            def _():
                end_copy(i).wait_send()
                remote(e_send.at[i], e_land.at[i], end_send.at[i], end_recv.at[i], target(i)).wait_recv()

        ends_out[...] = e_land[...]

        def finish(j, carry):
            from_core(j).wait_send()
            to_y(j).wait_send()

            @pl.when(z == 0)
            def _():
                go_right(j, 1, land_c.at[j, y, pl.ds(1, 3)]).wait_send()

            @pl.when(z == 1)
            def _():
                go_right(j, 2, land_r.at[j, pl.ds(1, 2)]).wait_send()
                go_left(j, 1, land_l.at[j, pl.ds(0, 1)]).wait_send()

            @pl.when(z == 2)
            def _():
                go_right(j, 3, land_r.at[j, pl.ds(2, 1)]).wait_send()
                go_left(j, 2, land_l.at[j, pl.ds(0, 2)]).wait_send()

            @pl.when(z == last)
            def _():
                go_left(j, 3, land_c.at[j, y, pl.ds(0, 3)]).wait_send()

            return carry

        lax.fori_loop(0, parts, finish, 0)


def last_back(x, y, da, dr1, g, ng, kept, w, tabs):
    q, k, v, ko, vo, o, e, l = kept[:8]
    rows, width = x.shape
    heads = width // 128
    depth, columns = w.shape[2:]
    parts = columns // WIDE
    units = (columns - width) // 3
    cos, sin, cost, sint = tabs
    dma = pltpu.SemaphoreType.DMA

    def once(shape):
        return pl.BlockSpec(shape, lambda i: (0,) * len(shape), pipeline_mode=pl.Buffered(1))

    def by_pair(shape):
        return pl.BlockSpec(shape, lambda i: (jnp.minimum(i, 5),) + (0,) * (len(shape) - 1))

    pair = by_pair((1, rows, 128))
    return pl.pallas_call(
        functools.partial(last_kernel, parts),
        grid=(8,),
        in_specs=[
            once((rows, width)),
            pl.BlockSpec((4, 2, depth, 256), lambda i: (0, jnp.minimum(i // 3, 1), 0, 2), pipeline_mode=pl.Buffered(1)),
            once((heads, rows, 128)),
            pair, pair, pair, pair, pair,
            by_pair((1, 2, 2 * rows, rows)),
            by_pair((1, 2, 8, rows)),
            once((HD // 2, rows)), once((HD // 2, rows)),
            once((rows, width)),
            pl.BlockSpec((4, 2, depth, 768), lambda i: (0, jnp.maximum(i - 6, 0), 0, 0), pipeline_mode=pl.Buffered(1)),
            once((rows, width)), once((rows, width)),
            pl.BlockSpec(memory_space=pl.ANY),
            once(ng.shape),
        ],
        out_specs=[
            once((depth, width)), once((depth, 2 * units)), once((units, depth)), once((2, rows // 2, width)), once(ng.shape),
        ],
        out_shape=[
            sds((depth, width), F32), sds((depth, 2 * units), F32), sds((units, depth), F32),
            sds((2, rows // 2, width), BF), sds(ng.shape, F32),
        ],
        scratch_shapes=[
            VM((3, rows, 128), BF),
            VM((2, width, 384), BF),
            VM((heads, rows, 128), BF),
            VM((heads, 2, 128, rows), F32),
            VM((heads, 2, 128, rows), BF),
            VM((heads, 2, 128, rows), BF),
            VM((rows, width), F32),
            VM((2, 2, 4, depth, width), BF),
            VM((2, rows // 2, width), BF),
            VM((2, rows // 2, width), BF),
            VM((depth, WIDE), F32),
            VM((4, 2, 4, depth, WIDE), BF),
            VM((parts, 2, 4, depth, WIDE), BF),
            VM((parts, 4, depth, WIDE), BF),
            VM((parts, 3, depth, WIDE), BF),
            VM((parts, 3, depth, WIDE), BF),
            VM((8,) + ng.shape, F32),
            dma((6,)), dma((6,)), dma, dma((2,)), dma((2,)),
        ]
        + [dma((parts,))] * 9
        + [dma((4,))] * 2,
        compiler_params=pltpu.CompilerParams(collective_id=0, has_side_effects=True, vmem_limit_bytes=62 << 20),
        name="last",
    )(da, w, o, q, k, v, ko, vo, e, l, cost, sint, x, w, dr1, y, g.reshape(2, 2, 4, depth, columns), ng)


LAG = 6


def first_kernel(
    parts, tok_ref, shard_ref, extra_ref, len_ref, cos_ref, sin_ref,
    w_out, y_out, x_out, mask_out, norm_out,
    w, xin, q, kv, land_kv, o, h1, hb, acc, ext, lens,
    tok_sem, tok_send, tok_recv, shard_sem, back_sem, kv_send, kv_recv,
    small_send, small_recv, rs_sem, rr_sem, ls_sem, lr_sem, ys_sem, yr_sem, cs_sem, cr_sem,
):
    y, c, z = lax.axis_index("y"), lax.axis_index("core"), lax.axis_index("tensor")
    last = 3
    rows, width = xin.shape[0] * xin.shape[1], xin.shape[2]
    near, across = {"core": 1 - c}, {"y": 1 - y}
    right, left = {"tensor": jnp.minimum(z + 1, last)}, {"tensor": jnp.maximum(z - 1, 0)}
    side = z // 2
    barrier = pltpu.get_barrier_semaphore()

    def greet(device):
        pl.semaphore_signal(barrier, inc=1, device_id=device, device_id_type=MESH)

    def remote(src, dst, send, recv, device):
        return pltpu.make_async_remote_copy(src, dst, send, recv, device_id=device, device_id_type=MESH)

    def target(i):
        return {"core": side, "tensor": 2 * c + i}

    def at_home(i):
        return jnp.logical_and(side == c, 2 * c + i == z)

    def token_copy(i, part):
        return remote(tok_ref.at[i, part], xin.at[z % 2, part], tok_send.at[i], tok_recv.at[z % 2], target(i))

    def token_home(i):
        return pltpu.make_async_copy(tok_ref.at[i], xin.at[z % 2], tok_sem)

    load = pltpu.make_async_copy(shard_ref, w.at[y, c, z], shard_sem)
    load.start()
    greet(near)
    greet(across)

    @pl.when(z < last)
    def _():
        greet(right)

    @pl.when(z > 0)
    def _():
        greet(left)

    for i in range(2):

        @pl.when(jnp.logical_not(at_home(i)))
        def _():
            greet(target(i))

    count = 4 + jnp.where(z < last, 1, 0) + jnp.where(z > 0, 1, 0) - jnp.where(side == c, 1, 0)
    pl.semaphore_wait(barrier, count)

    ext[y, c] = extra_ref[...]
    lens[c] = len_ref[...]

    def small(k):
        if k == 0:
            return remote(lens.at[c], lens.at[c], small_send.at[0], small_recv.at[0], near)
        if k == 1:
            return remote(ext.at[y, c], ext.at[y, c], small_send.at[1], small_recv.at[1], across)
        return remote(ext.at[:, c], ext.at[:, c], small_send.at[2], small_recv.at[2], near)

    small(0).start()
    small(1).start()
    load.wait()

    def columns(j):
        return pl.ds(pl.multiple_of(j * WIDE, WIDE), WIDE)

    def go_right(j, h):
        b = jnp.maximum(z - h, 0)
        return remote(w.at[y, c, b, :, columns(j)], w.at[y, c, b, :, columns(j)], rs_sem.at[j, h], rr_sem.at[j, h], right)

    def go_left(j, h):
        b = jnp.minimum(z + h, last)
        return remote(w.at[y, c, b, :, columns(j)], w.at[y, c, b, :, columns(j)], ls_sem.at[j, h], lr_sem.at[j, h], left)

    def to_y(j):
        return remote(w.at[y, c, :, :, columns(j)], w.at[y, c, :, :, columns(j)], ys_sem.at[j], yr_sem.at[j], across)

    def block_to_y(j, b):
        return remote(w.at[y, c, b, :, columns(j)], w.at[y, c, b, :, columns(j)], ys_sem.at[j], yr_sem.at[j], across)

    def to_core(j):
        return remote(w.at[:, c, :, :, columns(j)], w.at[:, c, :, :, columns(j)], cs_sem.at[j], cr_sem.at[j], near)

    def write_back(j):
        return pltpu.make_async_copy(w.at[:, :, :, :, columns(j)], w_out.at[:, :, :, :, columns(j)], back_sem.at[j])

    def stage(r, lag, body):
        @pl.when(jnp.logical_and(r >= lag, r - lag < parts))
        def _():
            body(r - lag)

    def send_own(j):
        @pl.when(z < last)
        def _():
            go_right(j, 0).start()

        @pl.when(z > 0)
        def _():
            go_left(j, 0).start()

        block_to_y(j, z).start()

    def hop(h, j):
        @pl.when(z >= h)
        def _():
            go_right(j, h - 1).wait_recv()
            block_to_y(j, z - h).start()

        @pl.when(z + h <= last)
        def _():
            go_left(j, h - 1).wait_recv()
            block_to_y(j, z + h).start()

        if h < last:

            @pl.when(jnp.logical_and(z >= h, z < last))
            def _():
                go_right(j, h).start()

            @pl.when(jnp.logical_and(z + h <= last, z > 0))
            def _():
                go_left(j, h).start()

    def over_core(j):
        to_y(j).wait_recv()
        to_core(j).start()

    def complete(j):
        to_core(j).wait_recv()
        write_back(j).start()

    def round_(r):
        stage(r, 0, send_own)
        stage(r, 1, functools.partial(hop, 1))
        stage(r, 2, functools.partial(hop, 2))
        stage(r, 3, functools.partial(hop, 3))
        stage(r, 5, over_core)
        stage(r, LAG, complete)

    def rounds(first, end):
        lax.fori_loop(first, end, lambda r, t: (round_(r), t)[1], 0)

    lead_parts = width // WIDE
    start = 17
    token_rows = xin.shape[1] // 16
    for i in range(2):

        @pl.when(at_home(i))
        def _():
            token_home(i).start()

    def early(r, carry):
        round_(r)
        part = pl.ds(pl.multiple_of(r * token_rows, token_rows), token_rows)
        for i in range(2):

            @pl.when(jnp.logical_not(at_home(i)))
            def _():
                token_copy(i, part).start()

        return carry

    lax.fori_loop(0, 3, early, 0)
    small(0).wait()
    small(1).wait()
    small(2).start()

    mine = jnp.where(side == 0, lens[0], lens[1])
    mine = jnp.where(z % 2 == 0, mine[0:1], mine[1:2])
    at_q = c * rows + lax.broadcasted_iota(jnp.int32, (1, rows), 1)
    at_k = lax.broadcasted_iota(jnp.int32, (2 * rows, 1), 0)
    at_k = jnp.where(at_k < rows, c * rows + at_k, (1 - c) * rows + at_k - rows)
    seg_q, seg_k = jnp.zeros((1, rows), jnp.int32), jnp.zeros((2 * rows, 1), jnp.int32)
    end = jnp.zeros((1, 1), jnp.int32)
    for n in range(8):
        end = end + mine[:, n : n + 1]
        seg_q = seg_q + jnp.where(end <= at_q, 1, 0)
        seg_k = seg_k + jnp.where(end <= at_k, 1, 0)
    mask_out[...] = jnp.where(seg_k == seg_q, 0.0, neg_fill).astype(F32)
    lax.fori_loop(3, 16, early, 0)
    rounds(16, start)

    small(2).wait()
    halves = [ext[i // 2, i % 2].astype(F32) for i in range(4)]
    for k in range(2):
        for half in range(2):
            pieces = [halves[2 * half + i][3 * k + m : 3 * k + m + 1] for i in range(2) for m in range(3)]
            norm_out[2 * k + half : 2 * k + half + 1] = jnp.concatenate(pieces, axis=1)

    for i in range(2):

        @pl.when(at_home(i))
        def _():
            token_home(i).wait()

        @pl.when(jnp.logical_not(at_home(i)))
        def _():
            token_copy(i, pl.ds(0, xin.shape[1])).wait_send()
            remote(tok_ref.at[i], xin.at[i], tok_send.at[i], tok_recv.at[i], target(i)).wait_recv()

    x = xin[...].reshape(rows, width)
    x_out[...] = x
    cos, sin = cos_ref[pl.ds(c * rows, rows)], sin_ref[pl.ds(c * rows, rows)]
    low = low_lanes((rows, 128))
    for p in range(2):
        r = [dg(x, w[:, :, 2 * p + e, :, :640].reshape(width, 640), NN) for e in range(2)]
        t = [[v[:, 128 * i : 128 * i + 128] for i in range(5)] for v in r]
        qs = [t[0][0], jnp.where(low, t[0][3], swap64(t[1][3])), t[1][0]]
        ks = [t[0][1], jnp.where(low, swap64(t[0][3]), t[1][3]), t[1][1]]
        vs = [t[0][2], jnp.where(low, t[0][4], swap64(t[1][4])), t[1][2]]
        for i in range(3):
            q[3 * p + i] = (rope_fwd(qs[i], cos, sin) * HD**-0.5).astype(BF)
            kv[0, 3 * p + i] = rope_fwd(ks[i], cos, sin).astype(BF)
            kv[1, 3 * p + i] = vs[i].astype(BF)
    share = remote(kv, land_kv, kv_send, kv_recv, near)
    share.start()
    rounds(start, start + 1)
    share.wait()

    def pair(p, carry):
        k = jnp.concatenate([kv[0, p], land_kv[0, p]], axis=0)
        v = jnp.concatenate([kv[1, p], land_kv[1, p]], axis=0)
        vt = v.astype(F32).T.astype(BF)
        outs = []
        for h in range(2):
            qm = jnp.where(low if h == 0 else jnp.logical_not(low), q[p], jnp.zeros((rows, 128), BF))
            s = dg(k, qm, NT) + mask_out[...]
            e = jnp.exp(s - jnp.max(s, axis=0, keepdims=True))
            inv = 1.0 / jnp.sum(e, axis=0, keepdims=True)
            outs.append(dg(vt[HD * h : HD * h + HD], e.astype(BF), NN) * inv)
        o[p] = jnp.concatenate(outs, axis=0).T.astype(BF)
        round_(start + 1 + p)
        return carry

    lax.fori_loop(0, 6, pair, 0)
    r = x.astype(F32)
    for p in range(2):
        wo = []
        for e in range(2):
            wo.append([w[:, :, 2 * p + e, :, 512 + 128 * i : 640 + 128 * i].reshape(width, 128) for i in range(2)])
        mid = jnp.where(low_lanes((width, 128)), swap64(wo[0][0].astype(F32)), wo[1][0].astype(F32)).astype(BF)
        r = r + dg(
            jnp.concatenate([o[3 * p + i] for i in range(3)], axis=1),
            jnp.concatenate([wo[0][1], mid, wo[1][1]], axis=1),
            NT,
        )
    n, inv = norm_parts(r)
    h = n * norm_out[0:1] + norm_out[2:3]
    hb[...] = h.astype(BF)
    acc[...] = h
    rounds(start + 7, start + 8)

    def units(k, carry):
        @pl.when(k != 4)
        def _():
            round_(start + 8 + k - k // 5)

        wg, wu, wd = unit_weights(
            lambda t, m: w[:, :, t, :, pl.ds(pl.multiple_of(width + GROUP * k + 128 * m, 128), 128)].reshape(width, 128)
        )
        gate = dg(hb[...], wg, NN)
        up = dg(hb[...], wu, NN)
        act = (gate / (1.0 + jnp.exp(-gate)) * up).astype(BF)
        acc[...] += dg(act, wd, NT)
        return carry

    lax.fori_loop(0, 6, units, 0)
    n, inv = norm_parts(acc[...])
    y_out[...] = (n * norm_out[1:2] + norm_out[3:4]).astype(BF)

    def finish(j, carry):
        write_back(j).wait()
        to_y(j).wait_send()
        to_core(j).wait_send()
        for h in range(last):

            @pl.when(jnp.logical_and(z >= h, z < last))
            def _():
                go_right(j, h).wait_send()

            @pl.when(jnp.logical_and(z + h <= last, z > 0))
            def _():
                go_left(j, h).wait_send()

        return carry

    lax.fori_loop(0, parts, finish, 0)


def first_layer(tokens, shard, extra, lengths, cos, sin):
    micro, own, width = tokens.shape
    depth, columns = shard.shape
    rows = 2 * own
    parts = columns // WIDE
    heads = width // 128
    dma = pltpu.SemaphoreType.DMA
    hbm = pl.BlockSpec(memory_space=pl.ANY)
    vm = pl.BlockSpec(memory_space=VM)
    return pl.pallas_call(
        functools.partial(first_kernel, parts),
        in_specs=[hbm, hbm, vm, vm, vm, vm],
        out_specs=[hbm, vm, vm, vm, vm],
        out_shape=[
            sds((2, 2, 4, depth, columns), BF),
            sds((rows, width), BF),
            sds((rows, width), BF),
            sds((2 * rows, rows), F32),
            sds((4, width), F32),
        ],
        scratch_shapes=[
            VM((2, 2, 4, depth, columns), BF),
            VM((2, own, width), BF),
            VM((heads, rows, 128), BF),
            VM((2, heads, rows, 128), BF),
            VM((2, heads, rows, 128), BF),
            VM((heads, rows, 128), BF),
            VM((8, 128), F32),
            VM((rows, width), BF),
            VM((rows, width), F32),
            VM((2, 2) + extra.shape, BF),
            VM((2,) + lengths.shape, jnp.int32),
            dma, dma((2,)), dma((2,)), dma, dma((parts,)), dma, dma,
            dma((3,)), dma((3,)),
            dma((parts, 3)), dma((parts, 3)), dma((parts, 3)), dma((parts, 3)),
            dma((parts,)), dma((parts,)), dma((parts,)), dma((parts,)),
        ],
        compiler_params=pltpu.CompilerParams(collective_id=1, has_side_effects=True, vmem_limit_bytes=60 << 20),
        name="first",
    )(tokens, shard, extra, lengths, cos, sin)


def swap_pairs(tp, step, dp_axes):
    pairs = []
    half = tp // 2
    for core in range(2):
        for at in range(tp):
            source = core * tp + at
            target = (at // half) * tp + half * core + (at + step) % half
            pairs.append((source, target))
    return pairs


def to_sequences(rows, tp):
    half = tp // 2
    at = lax.axis_index("tensor")
    pieces = [None] * half
    got = []
    for step in range(half):
        piece = lax.dynamic_index_in_dim(rows, (at + step) % half, 0, keepdims=False)
        got.append(lax.ppermute(piece, ("core", "tensor"), swap_pairs(tp, step, None)))
    stacked = jnp.stack(got)
    order = (at - jnp.arange(half)) % half
    return jnp.take(stacked, order, axis=0).reshape(-1, rows.shape[-1])


def to_positions(rows, tp):
    half = tp // 2
    at = lax.axis_index("tensor")
    parts = rows.reshape(half, -1, rows.shape[-1])
    got = []
    for step in range(half):
        piece = lax.dynamic_index_in_dim(parts, (at - step) % half, 0, keepdims=False)
        back = [(target, source) for source, target in swap_pairs(tp, step, None)]
        got.append(lax.ppermute(piece, ("core", "tensor"), back))
    stacked = jnp.stack(got)
    order = (at + jnp.arange(half)) % half
    return jnp.take(stacked, (jnp.arange(half) - at) % half, axis=0)


def rope_tables(positions):
    halfway = HD // 2
    freqs = 1000.0 ** (-jnp.arange(halfway, dtype=F32) / halfway)
    angles = positions.astype(F32)[:, None] * freqs[None, :]
    cos, sin = jnp.cos(angles), jnp.sin(angles)
    wide = jnp.concatenate([cos] * 4, axis=1)
    signed = jnp.concatenate([-sin, sin] * 2, axis=1)
    return wide, signed, cos.T, sin.T


def pack_shard(w_qkv, w_out, w_gate_up, w_down):
    rows = w_qkv.shape[0]
    odd = lax.axis_index("tensor") % 2 == 1
    heads = w_qkv.reshape(rows, 3, 3, HD)
    mine = w_out.T.reshape(rows, 3, HD)
    heads = jnp.where(odd, jnp.roll(heads, -1, axis=2), heads)
    mine = jnp.where(odd, jnp.roll(mine, -1, axis=1), mine)
    first = jnp.concatenate(
        [heads[:, :, :2].reshape(rows, -1), heads[:, :, 2].reshape(rows, -1), mine[:, 2], mine[:, :2].reshape(rows, -1)], axis=1
    )
    units = jnp.concatenate([w_gate_up, w_down.T[:, None]], axis=1)
    units = units.reshape(rows, 3, -1, 128).transpose(0, 2, 1, 3)
    return jnp.concatenate([first, units.reshape(rows, -1)], axis=1)


def unpack_first(first):
    rows = first.shape[0]
    odd = lax.axis_index("tensor") % 2 == 1
    both = first[:, :384].reshape(rows, 3, 2, HD)
    single = first[:, 384:576].reshape(rows, 3, 1, HD)
    heads = jnp.concatenate([both, single], axis=2)
    mine = jnp.concatenate([first[:, 640:].reshape(rows, 2, HD), first[:, 576:640].reshape(rows, 1, HD)], axis=1)
    heads = jnp.where(odd, jnp.roll(heads, 1, axis=2), heads)
    mine = jnp.where(odd, jnp.roll(mine, 1, axis=1), mine)
    return heads.reshape(rows, 3, -1), mine.reshape(rows, -1).T


def host_tables(length):
    halfway = HD // 2
    freqs = np.float32(1000.0) ** (-np.arange(halfway, dtype=np.float32) / np.float32(halfway))
    angles = np.arange(length, dtype=np.float32)[:, None] * freqs[None, :]
    cos, sin = np.cos(angles), np.sin(angles)
    return np.concatenate([cos] * 4, axis=1), np.concatenate([-sin, sin] * 2, axis=1)


BLOCKS = 4


def gather_shard(shard, dp, tp):
    rows, columns = shard.shape
    got = lax.all_gather(shard, ALL, axis=0, tiled=False)
    got = got.reshape(BLOCKS, dp // BLOCKS, tp, rows, columns)
    return got.transpose(0, 2, 1, 3, 4).reshape(BLOCKS, tp, -1, columns)


def scatter_sum(whole, dp, tp):
    columns = whole.shape[3]
    parts = whole.reshape(BLOCKS, tp, dp // BLOCKS, -1, columns).transpose(0, 2, 1, 3, 4)
    parts = parts.reshape(dp * tp, -1, columns)
    return lax.psum_scatter(parts, ALL, scatter_dimension=0, tiled=False).astype(F32)


def on_device(dp, tp, tokens, cotangent, lengths, w_qkv, w_out, w_gate_up, w_down, norm_gains, norm_biases):
    section = lax.axis_index("section")
    core = lax.axis_index("core")
    at = lax.axis_index("tensor")
    micro, own, width = tokens.shape
    assert micro * 2 == tp
    length = own * tp
    rows = length // 2
    shard = pack_shard(w_qkv[0], w_out[0], w_gate_up[0], w_down[0])
    near = core * rows + jnp.arange(rows, dtype=jnp.int32)
    far = (1 - core) * rows + jnp.arange(rows, dtype=jnp.int32)
    tabs = rope_tables(near)
    if dp == 4 and tp == 4:
        extra = jnp.concatenate([norm_gains.reshape(-1, 128), norm_biases.reshape(-1, 128)])
        extra = jnp.pad(extra, ((0, 16 - extra.shape[0]), (0, 0)))
        padded = jnp.pad(lengths, ((0, 8 - lengths.shape[0]), (0, 128 - lengths.shape[1])))
        wide, signed = host_tables(length)
        rows_in = jnp.where(section == 0, tokens, cotangent)
        weights, y, tokens, mask, small = first_layer(rows_in, shard, extra, padded, wide, signed)
        grad_top = tokens
        weights = weights.reshape((BLOCKS,) + weights.shape[2:])
        norms = (small[:2], small[2:])
    else:
        weights = gather_shard(shard, dp, tp)
        norms = jnp.concatenate([norm_gains, norm_biases])
        norms = lax.all_gather(norms, ("y", "core"), axis=1, tiled=True).astype(F32)
        norms = (norms[0].reshape(2, width), norms[1].reshape(2, width))
        grad_top = to_sequences(cotangent, tp)
        tokens = to_sequences(tokens, tp)
        chip_lengths = lax.all_gather(lengths, "core", axis=0, tiled=True)
        my_lengths = lax.dynamic_index_in_dim(chip_lengths, at, 0, keepdims=False)
        ends_at = jnp.cumsum(my_lengths)

        def segment(positions):
            return jnp.sum((ends_at[None, :] <= positions[:, None]).astype(jnp.int32), axis=-1)

        seg_near = segment(near)
        seg_all = jnp.concatenate([seg_near, segment(far)])
        mask = jnp.where(seg_all[:, None] == seg_near[None, :], 0.0, neg_fill).astype(F32)
        y, unused = forward(tokens, weights, norms, mask, tabs)
    received = lax.ppermute(y, "section", [(0, 1)])
    inputs = jnp.where(section == 0, tokens, received)
    y, kept = forward(inputs, weights, norms, mask, tabs)
    dr1, da = ffn_backward(grad_top, kept, weights, norms, False)
    unused, dz = attn_backward(inputs, da, dr1, None, kept, weights, tabs)
    received = lax.ppermute(dz, "section", [(1, 0)])
    dy = jnp.where(section == 0, received, grad_top)
    g, dr1, da, ng = ffn_backward(dy, kept, weights, norms, True)
    if dp == 4 and tp == 4:
        first, pair, down, ends, total = last_back(inputs, y, da, dr1, g, ng, kept, weights, tabs)
        small = lax.dynamic_slice_in_dim(total[:4].reshape(2, dp * tp, -1), lax.axis_index(ALL), 1, 1)
        gains, biases = small[0, 0], small[1, 0]
    else:
        g, dz = attn_backward(inputs, da, dr1, g, kept, weights, tabs)
        ends = to_positions(jnp.where(section == 0, dz.astype(BF), y), tp)
        mine = scatter_sum(g, dp, tp)
        first = mine[:, :width]
        units = mine[:, width:].reshape(first.shape[0], -1, 3, 128).transpose(0, 2, 1, 3).reshape(first.shape[0], 3, -1)
        pair, down = units[:, :2], units[:, 2].T
        gains = lax.psum_scatter(ng[0:2].reshape(-1), ALL, scatter_dimension=0, tiled=True)
        biases = lax.psum_scatter(ng[2:4].reshape(-1), ALL, scatter_dimension=0, tiled=True)
    joint, mix = unpack_first(first)
    outs = (joint, mix, pair.reshape(pair.shape[0], 2, -1), down, gains, biases)
    return (ends[None],) + tuple(t[None] for t in outs)


def solution(mesh):
    sections, dp, tp = mesh.devices.shape
    fine = Mesh(mesh.devices.reshape(sections, dp // 2, 2, tp), ("section", "y", "core", "tensor"))
    both = ("y", "core")
    in_specs = (
        P(both, "tensor", None),
        P(both, "tensor", None),
        P(both, None),
        P("section", both, None, "tensor"),
        P("section", "tensor", both),
        P("section", both, None, "tensor"),
        P("section", "tensor", both),
        P("section", both),
        P("section", both),
    )
    out_specs = (
        P("section", both, "tensor", None),
        P("section", both, None, "tensor"),
        P("section", "tensor", both),
        P("section", both, None, "tensor"),
        P("section", "tensor", both),
        P("section", ALL),
        P("section", ALL),
    )
    return jax.shard_map(
        functools.partial(on_device, dp, tp), mesh=fine, in_specs=in_specs, out_specs=out_specs, check_vma=False
    )
```

```python
import functools

import jax
import jax.numpy as jnp
import numpy as np
from jax import lax
from jax.experimental import pallas as pl
from jax.experimental.pallas import tpu as pltpu
from jax.sharding import Mesh, PartitionSpec as P

HD = 64
eps = 1e-05
neg_fill = -1e30
ALL = ("y", "core", "tensor")
BF = jnp.bfloat16
F32 = jnp.float32
MESH = pl.DeviceIdType.MESH


def dg(a, b, dims):
    return lax.dot_general(a, b, (dims, ((), ())), preferred_element_type=F32)


NN = ((1,), (0,))
NT = ((1,), (1,))
TN = ((0,), (0,))


def low_lanes(shape):
    return lax.broadcasted_iota(jnp.int32, shape, 1) < HD


def swap64(v):
    return pltpu.roll(v, HD, axis=1)


def rope_fwd(t, cos, sin):
    lane = lax.broadcasted_iota(jnp.int32, t.shape, 1) % HD
    other = jnp.where(lane < HD // 2, pltpu.roll(t, 128 - HD // 2, axis=1), pltpu.roll(t, HD // 2, axis=1))
    return t * cos + other * sin


def qkv_kernel(x_ref, w_ref, cos_ref, sin_ref, q_ref, k_ref, v_ref):
    x = x_ref[...]
    width = x.shape[1]
    r = [dg(x, w_ref[:, e, :, :640].reshape(width, 640), NN) for e in range(2)]
    c = [[t[:, 128 * i : 128 * i + 128] for i in range(5)] for t in r]
    low = low_lanes(c[0][0].shape)
    qs = [c[0][0], jnp.where(low, c[0][3], swap64(c[1][3])), c[1][0]]
    ks = [c[0][1], jnp.where(low, swap64(c[0][3]), c[1][3]), c[1][1]]
    vs = [c[0][2], jnp.where(low, c[0][4], swap64(c[1][4])), c[1][2]]
    cos, sin = cos_ref[...], sin_ref[...]
    for i in range(3):
        q_ref[i] = (rope_fwd(qs[i], cos, sin) * HD**-0.5).astype(BF)
        k_ref[i] = rope_fwd(ks[i], cos, sin).astype(BF)
        v_ref[i] = vs[i].astype(BF)


def attn_kernel(q_ref, k_ref, v_ref, ko_ref, vo_ref, m_ref, o_ref, e_ref, l_ref):
    q = q_ref[0]
    k = jnp.concatenate([k_ref[0], ko_ref[0]], axis=0)
    v = jnp.concatenate([v_ref[0], vo_ref[0]], axis=0)
    vt = v.astype(F32).T.astype(BF)
    outs = []
    for h in range(2):
        low = low_lanes(q.shape)
        qm = jnp.where(low if h == 0 else jnp.logical_not(low), q, jnp.zeros_like(q))
        s = dg(k, qm, NT) + m_ref[...]
        e = jnp.exp(s - jnp.max(s, axis=0, keepdims=True))
        inv = 1.0 / jnp.sum(e, axis=0, keepdims=True)
        eb = e.astype(BF)
        e_ref[0, h] = eb
        l_ref[0, h] = jnp.broadcast_to(inv, l_ref.shape[2:])
        outs.append(dg(vt[HD * h : HD * h + HD], eb, NN) * inv)
    o_ref[0] = jnp.concatenate(outs, axis=0).T.astype(BF)


def norm_parts(r):
    center = r - jnp.mean(r, axis=-1, keepdims=True)
    inv = lax.rsqrt(jnp.mean(center * center, axis=-1, keepdims=True) + eps)
    return center * inv, inv


def norm_back(dn, n, inv):
    return inv * (dn - jnp.mean(dn, axis=-1, keepdims=True) - n * jnp.mean(dn * n, axis=-1, keepdims=True))


def out_weight(w_ref):
    c = [[w_ref[:, e, :, 128 * i : 128 * i + 128].reshape(-1, 128) for i in range(2)] for e in range(2)]
    low = low_lanes(c[0][0].shape)
    mid = jnp.where(low, swap64(c[0][0].astype(F32)), c[1][0].astype(F32)).astype(BF)
    return [c[0][1], mid, c[1][1]]


GROUP = 384
WIDE = 128


def unit_weights(load):
    return [jnp.concatenate([load(t, m) for t in range(4)], axis=1) for m in range(3)]


def ffn_kernel(x_ref, o_ref, wo_ref, w_ref, g_ref, b_ref, y_ref, gu_ref, n1_ref, i1_ref, n2_ref, i2_ref, h_ref, hb_ref, acc_ref):
    z = pl.program_id(0)
    width = x_ref.shape[1]

    @pl.when(z == 0)
    def _():
        r = x_ref[...].astype(F32)
        for p in range(2):
            w = jnp.concatenate(out_weight(wo_ref.at[:, 2 * p : 2 * p + 2]), axis=1)
            o = jnp.concatenate([o_ref[3 * p + i] for i in range(3)], axis=1)
            r = r + dg(o, w, NT)
        n, inv = norm_parts(r)
        n1_ref[...] = n.astype(BF)
        i1_ref[...] = jnp.broadcast_to(inv, i1_ref.shape)
        h = n * g_ref[0:1] + b_ref[0:1]
        h_ref[...] = h
        hb_ref[...] = h.astype(BF)

    hb = hb_ref[...]
    wg, wu, wd = unit_weights(lambda t, m: w_ref[:, t, :, 128 * m : 128 * m + 128].reshape(width, 128))
    gate = dg(hb, wg, NN)
    up = dg(hb, wu, NN)
    gu_ref[0, 0] = gate.astype(BF)
    gu_ref[0, 1] = up.astype(BF)
    act = (gate / (1.0 + jnp.exp(-gate)) * up).astype(BF)
    part = dg(act, wd, NT)

    @pl.when(z == 0)
    def _():
        acc_ref[...] = h_ref[...] + part

    @pl.when(z > 0)
    def _():
        acc_ref[...] += part

    @pl.when(z == pl.num_programs(0) - 1)
    def _():
        n, inv = norm_parts(acc_ref[...])
        n2_ref[...] = n.astype(BF)
        i2_ref[...] = jnp.broadcast_to(inv, i2_ref.shape)
        y_ref[...] = (n * g_ref[1:2] + b_ref[1:2]).astype(BF)


def ffn_back_kernel(grads, dy_ref, n1_ref, i1_ref, n2_ref, i2_ref, gu_ref, w_ref, g_ref, b_ref, *refs):
    if grads:
        g_out, dr1_ref, da_ref, ng_ref, hb_ref, df_ref, acc_ref = refs
    else:
        dr1_ref, da_ref, df_ref, acc_ref = refs
    z = pl.program_id(0)
    width = dy_ref.shape[1]

    @pl.when(z == 0)
    def _():
        dy = dy_ref[...].astype(F32)
        n = n2_ref[...].astype(F32)
        if grads:
            ng_ref[1:2] = jnp.sum(dy * n, axis=0, keepdims=True)
            ng_ref[3:4] = jnp.sum(dy, axis=0, keepdims=True)
            hb_ref[...] = (n1_ref[...].astype(F32) * g_ref[0:1] + b_ref[0:1]).astype(BF)
        dr2 = norm_back(dy * g_ref[1:2], n, i2_ref[:, :1])
        acc_ref[...] = dr2
        df_ref[...] = dr2.astype(BF)

    df = df_ref[...]
    gate = gu_ref[0, 0].astype(F32)
    up = gu_ref[0, 1].astype(F32)
    s = 1.0 / (1.0 + jnp.exp(-gate))
    silu = gate * s
    wg, wu, wd = unit_weights(lambda t, m: w_ref[:, t, :, 128 * m : 128 * m + 128].reshape(width, 128))

    def keep(m, grad):
        for t in range(g_out.shape[1]):
            g_out[:, t, :, 128 * m : 128 * m + 128] = grad[:, 128 * t : 128 * t + 128].astype(BF).reshape(g_out.shape[0], -1, 128)

    if grads:
        keep(2, dg(df, (silu * up).astype(BF), TN))
    d_act = dg(df, wd, NN)
    d_gate = (d_act * up * (s * (1.0 + gate * (1.0 - s)))).astype(BF)
    d_up = (d_act * silu).astype(BF)
    if grads:
        hb = hb_ref[...]
        keep(0, dg(hb, d_gate, TN))
        keep(1, dg(hb, d_up, TN))
    acc_ref[...] += dg(d_gate, wg, NT) + dg(d_up, wu, NT)

    @pl.when(z == pl.num_programs(0) - 1)
    def _():
        dh = acc_ref[...]
        n = n1_ref[...].astype(F32)
        if grads:
            ng_ref[0:1] = jnp.sum(dh * n, axis=0, keepdims=True)
            ng_ref[2:3] = jnp.sum(dh, axis=0, keepdims=True)
        dr1 = norm_back(dh * g_ref[0:1], n, i1_ref[:, :1])
        dr1_ref[...] = dr1
        da_ref[...] = dr1.astype(BF)


def pair_back(do, o, q, k, v, ko, vo, e, l, cos, sin):
    dot = do.astype(F32).T
    ot = o.astype(F32).T
    k = jnp.concatenate([k, ko], axis=0)
    v = jnp.concatenate([v, vo], axis=0)
    kt = k.astype(F32).T.astype(BF)
    qt = q.astype(F32).T.astype(BF)
    dqs, dks, dvs = [], [], []
    for h in range(2):
        span = slice(HD * h, HD * h + HD)
        scaled = dot[span] * l[h]
        inner = jnp.sum(scaled * ot[span], axis=0, keepdims=True)
        sb = scaled.astype(BF)
        zero = jnp.zeros_like(sb)
        padded = jnp.concatenate([sb, zero] if h == 0 else [zero, sb], axis=0)
        dp = dg(v, padded, NN)
        et = e[h][...]
        ds = (et.astype(F32) * (dp - inner)).astype(BF)
        dvs.append(dg(sb, et, NT))
        dks.append(dg(qt[span], ds, NT))
        dqt = dg(kt[span], ds, NN) * HD**-0.5
        d1, d2 = dqt[: HD // 2], dqt[HD // 2 :]
        dqs.append(d1 * cos + d2 * sin)
        dqs.append(d2 * cos - d1 * sin)
    return [jnp.concatenate(t, axis=0) for t in (dqs, dks, dvs)]


def joint_parts(dq, dkt, dvt, cos, sin):
    dk = []
    for t in dkt:
        parts = []
        for h in range(2):
            d1 = t[HD * h : HD * h + HD // 2]
            d2 = t[HD * h + HD // 2 : HD * h + HD]
            parts += [d1 * cos + d2 * sin, d2 * cos - d1 * sin]
        dk.append(jnp.concatenate(parts, axis=0).T)
    dv = [t.T for t in dvt]
    low = low_lanes(dq[0].shape)
    zero = jnp.zeros_like(dv[1])
    d = [
        [dq[0], dk[0], dv[0], jnp.where(low, dq[1], swap64(dk[1])), jnp.where(low, dv[1], zero)],
        [dq[2], dk[2], dv[2], jnp.where(low, swap64(dq[1]), dk[1]), jnp.where(low, swap64(dv[1]), zero)],
    ]
    return [jnp.concatenate(t, axis=1).astype(BF) for t in d]


def attn_back_kernel(grads, da_ref, wo_ref, o_ref, q_ref, k_ref, v_ref, ko_ref, vo_ref, e_ref, l_ref, cos_ref, sin_ref, dq_ref, own_ref, oth_ref, *dwo_ref):
    da = da_ref[...]
    rows = da.shape[0]
    w = jnp.concatenate(out_weight(wo_ref), axis=1)
    do3 = dg(da, w, NN).astype(BF)
    if grads:
        o3 = jnp.concatenate([o_ref[i] for i in range(3)], axis=1)
        dwo_ref[0][0] = dg(da, o3, TN).astype(BF)
    cos, sin = cos_ref[...], sin_ref[...]
    for i in range(3):
        dqt, dk, dv = pair_back(
            do3[:, 128 * i : 128 * i + 128], o_ref[i], q_ref[i], k_ref[i], v_ref[i], ko_ref[i], vo_ref[i],
            [e_ref[i, h] for h in range(2)], [l_ref[i, h, 0:1] for h in range(2)], cos, sin,
        )
        dq_ref[i] = dqt.T.astype(BF)
        own_ref[i, 0] = dk[:, :rows]
        own_ref[i, 1] = dv[:, :rows]
        oth_ref[i, 0] = dk[:, rows:].astype(BF)
        oth_ref[i, 1] = dv[:, rows:].astype(BF)


def joint_back_kernel(grads, *refs):
    if grads:
        old_ref, x_ref, w_ref, dr1_ref, dq_ref, own_ref, got_ref, dwo_ref, cos_ref, sin_ref, g_ref, dz_ref = refs
    else:
        w_ref, dr1_ref, dq_ref, own_ref, got_ref, cos_ref, sin_ref, dz_ref, dzb_ref = refs
    p = pl.program_id(0)
    width = dr1_ref.shape[1]
    d = joint_parts(
        [dq_ref[i].astype(F32) for i in range(3)],
        [own_ref[i, 0] + got_ref[i, 0].astype(F32) for i in range(3)],
        [own_ref[i, 1] + got_ref[i, 1].astype(F32) for i in range(3)],
        cos_ref[...],
        sin_ref[...],
    )
    acc = None
    for e in range(2):
        t = dg(d[e], w_ref[:, e, :, :640].reshape(width, 640), NT)
        acc = t if acc is None else acc + t
    if grads:
        x = x_ref[...]
        wlow = low_lanes((width, 128))
        mid = dwo_ref[0, :, 128:256].astype(F32)
        sides = [dwo_ref[0, :, 0:128], dwo_ref[0, :, 256:384]]
        mids = [swap64(mid), mid]
        for e in range(2):
            g = dg(x, d[e], TN)
            blocks = g_ref.shape[0]
            g_ref[:, e, :, :512] = g[:, :512].astype(BF).reshape(blocks, -1, 512)
            g_ref[:, e, :, 512:640] = jnp.where(wlow, g[:, 512:], mids[e]).astype(BF).reshape(blocks, -1, 128)
            g_ref[:, e, :, 640:] = sides[e].reshape(blocks, -1, 128)

    @pl.when(p == 0)
    def _():
        dz_ref[...] = dr1_ref[...] + acc

    @pl.when(p > 0)
    def _():
        total = dz_ref[...] + acc
        dz_ref[...] = total
        if not grads:
            dzb_ref[...] = total.astype(BF)


BIG = pltpu.CompilerParams(vmem_limit_bytes=58 << 20)
VM = pltpu.VMEM


def full(shape):
    return pl.BlockSpec(shape, lambda i: (0,) * len(shape))


def lead(shape, at=0):
    return pl.BlockSpec(shape, lambda i: tuple(i if j == at else 0 for j in range(len(shape))))


def joint_block(w):
    return pl.BlockSpec((w.shape[0], 2, w.shape[2], 768), lambda i: (0, i, 0, 0))


def group_block(w):
    return pl.BlockSpec((w.shape[0], w.shape[1], w.shape[2], GROUP), lambda i: (0, 0, 0, 2 + i))


def sds(shape, kind):
    return jax.ShapeDtypeStruct(shape, kind)


def forward(x, weights, norms, mask, tabs):
    w = weights
    rows, width = x.shape
    heads = width // 128
    blocks, tp, depth, columns = w.shape
    steps = tp // 2
    cos, sin, cost, sint = tabs
    q, k, v = pl.pallas_call(
        qkv_kernel,
        grid=(steps,),
        in_specs=[full((rows, width)), joint_block(w), full((rows, 128)), full((rows, 128))],
        out_specs=[lead((3, rows, 128))] * 3,
        out_shape=[sds((heads, rows, 128), BF)] * 3,
        compiler_params=BIG,
        name="qkv",
    )(x, w, cos, sin)
    ko, vo = lax.ppermute((k, v), "core", [(0, 1), (1, 0)])
    return attend(x, (q, k, v, ko, vo), w, norms, mask)


def attend(x, joint, w, norms, mask):
    gains, biases = norms
    q, k, v, ko, vo = joint
    rows, width = x.shape
    heads = width // 128
    blocks, tp, depth, columns = w.shape
    pair = lead((1, rows, 128))
    o, e, l = pl.pallas_call(
        attn_kernel,
        grid=(heads,),
        in_specs=[pair] * 5 + [full((2 * rows, rows))],
        out_specs=[pair, lead((1, 2, 2 * rows, rows)), lead((1, 2, 8, rows))],
        out_shape=[sds((heads, rows, 128), BF), sds((heads, 2, 2 * rows, rows), BF), sds((heads, 2, 8, rows), F32)],
        compiler_params=BIG,
        name="attn",
    )(q, k, v, ko, vo, mask)
    groups = (columns - width) // GROUP
    units = tp * 128
    y, gu, n1, i1, n2, i2 = pl.pallas_call(
        ffn_kernel,
        grid=(groups,),
        in_specs=[
            full((rows, width)),
            full((heads, rows, 128)),
            pl.BlockSpec((blocks, tp, depth, 256), lambda i: (0, 0, 0, 2)),
            group_block(w),
            full((2, width)),
            full((2, width)),
        ],
        out_specs=[full((rows, width)), lead((1, 2, rows, units))] + [full((rows, width)), full((rows, 128))] * 2,
        out_shape=[sds((rows, width), BF), sds((groups, 2, rows, units), BF)] + [sds((rows, width), BF), sds((rows, 128), F32)] * 2,
        scratch_shapes=[VM((rows, width), F32), VM((rows, width), BF), VM((rows, width), F32)],
        compiler_params=BIG,
        name="ffn",
    )(x, o, w, w, gains, biases)
    return y, (q, k, v, ko, vo, o, e, l, gu, n1, i1, n2, i2)


def ffn_backward(dy, kept, w, norms, grads):
    gains, biases = norms
    gu, n1, i1, n2, i2 = kept[8:]
    rows, width = dy.shape
    blocks, tp, depth, columns = w.shape
    groups = (columns - width) // GROUP
    whole, stat = full((rows, width)), full((rows, 128))
    outs = [whole, whole]
    shapes = [sds((rows, width), F32), sds((rows, width), BF)]
    scratch = [VM((rows, width), BF), VM((rows, width), F32)]
    if grads:
        outs = [group_block(w)] + outs + [full((8, width))]
        shapes = [sds(w.shape, BF)] + shapes + [sds((8, width), F32)]
        scratch = [VM((rows, width), BF)] + scratch
    return pl.pallas_call(
        functools.partial(ffn_back_kernel, grads),
        grid=(groups,),
        in_specs=[
            whole, whole, stat, whole, stat,
            lead((1, 2, rows, tp * 128)),
            group_block(w),
            full((2, width)), full((2, width)),
        ],
        out_specs=outs,
        out_shape=shapes,
        scratch_shapes=scratch,
        compiler_params=BIG,
        name="ffn_back" if grads else "ffn_back_light",
    )(dy, n1, i1, n2, i2, gu, w, gains, biases)


def attn_backward(x, da, dr1, g, kept, w, tabs):
    grads = g is not None
    q, k, v, ko, vo, o, e, l = kept[:8]
    rows, width = da.shape
    heads = width // 128
    blocks, tp, depth, columns = w.shape
    steps = tp // 2
    cos, sin, cost, sint = tabs
    whole = full((rows, width))
    three = lead((3, rows, 128))
    side = lead((3, 2, 128, rows))
    table = full((HD // 2, rows))
    extra = [lead((1, width, 384))] if grads else []
    dq, own, oth, *dwo = pl.pallas_call(
        functools.partial(attn_back_kernel, grads),
        grid=(steps,),
        in_specs=[
            whole,
            pl.BlockSpec((blocks, 2, depth, 256), lambda i: (0, i, 0, 2)),
            three, three, three, three, three, three,
            lead((3, 2, 2 * rows, rows)),
            lead((3, 2, 8, rows)),
            table, table,
        ],
        out_specs=[three, side, side] + extra,
        out_shape=[
            sds((heads, rows, 128), BF),
            sds((heads, 2, 128, rows), F32),
            sds((heads, 2, 128, rows), BF),
        ]
        + ([sds((steps, width, 384), BF)] if grads else []),
        compiler_params=BIG,
        name="attn_back",
    )(da, w, o, q, k, v, ko, vo, e, l, cost, sint)
    got = lax.ppermute(oth, "core", [(0, 1), (1, 0)])
    if grads:
        specs = [pl.BlockSpec(memory_space=pl.ANY), whole, joint_block(w), whole, three, side, side] + extra
        args = (g, x, w, dr1, dq, own, got, *dwo)
        outs, shapes = [joint_block(w), whole], [sds(w.shape, BF), sds((rows, width), F32)]
    else:
        specs = [joint_block(w), whole, three, side, side]
        args = (w, dr1, dq, own, got)
        outs, shapes = [whole, whole], [sds((rows, width), F32), sds((rows, width), BF)]
    return pl.pallas_call(
        functools.partial(joint_back_kernel, grads),
        grid=(steps,),
        in_specs=specs + [table, table],
        out_specs=outs,
        out_shape=shapes,
        input_output_aliases={0: 0} if grads else {},
        compiler_params=BIG,
        name="joint_back",
    )(*args, cost, sint)


PAIRS = 6
FIRST_PAIR = 6
FIRST_JOINT = 12
LAST_STEP = 13


def last_kernel(
    parts, n1_ref, i1_ref, n2_ref, i2_ref, gu_ref, wa_ref, wb_ref, gain_ref, bias_ref,
    o_ref, q_ref, k_ref, v_ref, ko_ref, vo_ref, l_ref, cos_ref, sin_ref, dy_hbm, x_hbm, y_hbm, e_hbm,
    first_out, pair_out, down_out, ends_out, norm_out,
    acc, df, hb, ring, do3, dwo, dq, keep, oth, got, eb, e_send, e_land, tmp, land_c, land_y, land_r, land_l, land_n,
    dy_sem, x_sem, y_sem, e_sem, oth_send, oth_recv, end_sem, end_send, end_recv,
    cs_sem, cr_sem, ys_sem, yr_sem, rs_sem, rr_sem, ls_sem, lr_sem, ns_sem, nr_sem,
):
    step = pl.program_id(0)
    section = lax.axis_index("section")
    y, c, z = lax.axis_index("y"), lax.axis_index("core"), lax.axis_index("tensor")
    last = 3
    rows, width = acc.shape
    early = parts - width // WIDE
    near, across = {"core": 1 - c}, {"y": 1 - y}
    right, left = {"tensor": jnp.minimum(z + 1, last)}, {"tensor": jnp.maximum(z - 1, 0)}
    pair = {"tensor": z + 1 - 2 * lax.rem(z, 2)}
    far = {"tensor": lax.rem(z + 2, 4)}
    side = z // 2
    barrier = pltpu.get_barrier_semaphore()

    def greet(device):
        pl.semaphore_signal(barrier, inc=1, device_id=device, device_id_type=MESH)

    def remote(src, dst, send, recv, device):
        return pltpu.make_async_remote_copy(src, dst, send, recv, device_id=device, device_id_type=MESH)

    def target(i):
        return {"core": side, "tensor": 2 * c + i}

    def at_home(i):
        return jnp.logical_and(side == c, 2 * c + i == z)

    def end_copy(i, part):
        return remote(e_send.at[i, part], e_land.at[z % 2, part], end_send.at[i], end_recv.at[z % 2], target(i))

    def end_home(i):
        return pltpu.make_async_copy(e_send.at[i], e_land.at[z % 2], end_sem)

    def oth_copy(p):
        return remote(oth.at[p], got.at[p], oth_send.at[p], oth_recv.at[p], near)

    dy_copy = pltpu.make_async_copy(dy_hbm, e_send, dy_sem)
    x_copy = pltpu.make_async_copy(x_hbm, hb, x_sem)
    y_copy = pltpu.make_async_copy(y_hbm, e_send, y_sem)

    def probs_copy(p):
        return pltpu.make_async_copy(e_hbm.at[p], eb, e_sem)

    def columns(j):
        return pl.ds(pl.multiple_of(j * WIDE, WIDE), WIDE)

    def slot(j):
        return (j // 3) % 2, columns(j % 3)

    def to_core(j):
        r, cols = slot(j)
        return remote(ring.at[r, :, 1 - c, :, :, cols], land_c.at[j], cs_sem.at[j], cr_sem.at[j], near)

    def to_y(j):
        return remote(land_c.at[j, 1 - y], land_y.at[j], ys_sem.at[j], yr_sem.at[j], across)

    def norm_copy(k):
        return remote(land_n.at[2 * k], land_n.at[2 * k + 1], ns_sem.at[k], nr_sem.at[k], (near, across, pair, far)[k])

    def go_right(j, first, src):
        return remote(src, land_r.at[j, pl.ds(first - 1, 4 - first)], rs_sem.at[j], rr_sem.at[j], right)

    def go_left(j, count, src):
        return remote(src, land_l.at[j, pl.ds(0, count)], ls_sem.at[j], lr_sem.at[j], left)

    def stage(i, lag, body):
        @pl.when(jnp.logical_and(i >= lag, i - lag < parts))
        def _():
            body(i - lag)

    def add_cores(group):
        def one(m, carry):
            j = 3 * group + m
            r, cols = slot(j)
            to_core(j).wait()
            land_c[j] = land_c[j] + ring[r, :, c, :, :, cols]
            return carry

        lax.fori_loop(0, 3, one, 0)

    def send_cores(group):
        lax.fori_loop(0, 3, lambda m, t: (to_core(3 * group + m).start(), t)[1], 0)

    def last_hop(j):
        @pl.when(z == 1)
        def _():
            go_left(j, 2, land_l.at[j, pl.ds(0, 2)]).wait_recv()
            land_l[j, 0] = land_l[j, 0] + land_c[j, y, 0]
            go_left(j, 1, land_l.at[j, pl.ds(0, 1)]).start()

        @pl.when(z == 2)
        def _():
            go_right(j, 2, land_r.at[j, pl.ds(1, 2)]).wait_recv()
            land_r[j, 2] = land_r[j, 2] + land_c[j, y, 3]
            go_right(j, 3, land_r.at[j, pl.ds(2, 1)]).start()

    def next_hop(j):
        @pl.when(z == 1)
        def _():
            go_right(j, 1, land_r.at[j]).wait_recv()
            for k in (2, 3):
                land_r[j, k - 1] = land_r[j, k - 1] + land_c[j, y, k]
            go_right(j, 2, land_r.at[j, pl.ds(1, 2)]).start()

        @pl.when(z == 2)
        def _():
            go_left(j, 3, land_l.at[j]).wait_recv()
            for k in (0, 1):
                land_l[j, k] = land_l[j, k] + land_c[j, y, k]
            go_left(j, 2, land_l.at[j, pl.ds(0, 2)]).start()

    def first_hop(j):
        to_y(j).wait_recv()
        land_c[j, y] = land_c[j, y] + land_y[j]

        @pl.when(z == 0)
        def _():
            go_right(j, 1, land_c.at[j, y, pl.ds(1, 3)]).start()

        @pl.when(z == last)
        def _():
            go_left(j, 3, land_c.at[j, y, pl.ds(0, 3)]).start()

    def result(j):
        mine = land_c[j, y, z].astype(F32)

        @pl.when(z == 0)
        def _():
            go_left(j, 1, land_l.at[j, pl.ds(0, 1)]).wait_recv()
            tmp[...] = mine + land_l[j, 0].astype(F32)

        @pl.when(z == 1)
        def _():
            tmp[...] = mine + land_r[j, 0].astype(F32) + land_l[j, 1].astype(F32)

        @pl.when(z == 2)
        def _():
            tmp[...] = mine + land_r[j, 1].astype(F32) + land_l[j, 2].astype(F32)

        @pl.when(z == last)
        def _():
            go_right(j, 3, land_r.at[j, pl.ds(2, 1)]).wait_recv()
            tmp[...] = mine + land_r[j, 2].astype(F32)

        group = j // 3

        @pl.when(j >= early)
        def _():
            first_out[:, columns(j - early)] = tmp[...]

        for m in range(2):

            @pl.when(jnp.logical_and(j < early, j % 3 == m))
            def _():
                pair_out[:, columns(group + m * (early // 3))] = tmp[...]

        @pl.when(jnp.logical_and(j < early, j % 3 == 2))
        def _():
            down_out[columns(group), :] = tmp[...].T

    def round_(i):
        stage(i, 0, lambda j: to_y(j).start())
        stage(i, 6, last_hop)
        stage(i, 4, next_hop)
        stage(i, 2, first_hop)
        stage(i, 8, result)
        for k in range(4):

            @pl.when(i == 3 * k + 8)
            def _():
                norm_copy(k).wait()
                total = land_n[2 * k] + land_n[2 * k + 1]
                if k < 3:
                    land_n[2 * k + 2] = total
                    norm_copy(k + 1).start()
                else:
                    norm_out[...] = total

    @pl.when(step == 0)
    def _():
        dy_copy.start()
        greet(near)
        greet(across)
        greet(far)

        @pl.when(z < last)
        def _():
            greet(right)

        @pl.when(z > 0)
        def _():
            greet(left)

        for i in range(2):

            @pl.when(jnp.logical_not(at_home(i)))
            def _():
                greet(target(i))

        count = 5 + jnp.where(z < last, 1, 0) + jnp.where(z > 0, 1, 0) - jnp.where(side == c, 1, 0)
        pl.semaphore_wait(barrier, count)
        dy_copy.wait()
        dy = e_send[...].reshape(rows, width).astype(F32)
        n = n2_ref[...].astype(F32)
        land_n[0] = jnp.zeros(land_n.shape[1:], F32)
        land_n[0, 1:2] = jnp.sum(dy * n, axis=0, keepdims=True)
        land_n[0, 3:4] = jnp.sum(dy, axis=0, keepdims=True)
        dr2 = norm_back(dy * gain_ref[1:2], n, i2_ref[:, :1])
        acc[...] = dr2
        df[...] = dr2.astype(BF)
        hb[...] = (n1_ref[...].astype(F32) * gain_ref[0:1] + bias_ref[0:1]).astype(BF)

    @pl.when(step < FIRST_PAIR)
    def _():
        gate = gu_ref[0, 0].astype(F32)
        up = gu_ref[0, 1].astype(F32)
        s = 1.0 / (1.0 + jnp.exp(-gate))
        silu = gate * s
        wg, wu, wd = unit_weights(lambda t, m: wa_ref[:, t, :, 128 * m : 128 * m + 128].reshape(width, 128))
        place = step % 2

        def put(m, grad):
            for t in range(4):
                ring[place, :, :, t, :, 128 * m : 128 * m + 128] = (
                    grad[:, 128 * t : 128 * t + 128].astype(BF).reshape(2, 2, -1, 128)
                )

        put(2, dg(df[...], (silu * up).astype(BF), TN))
        d_act = dg(df[...], wd, NN)
        d_gate = (d_act * up * (s * (1.0 + gate * (1.0 - s)))).astype(BF)
        d_up = (d_act * silu).astype(BF)
        put(0, dg(hb[...], d_gate, TN))
        put(1, dg(hb[...], d_up, TN))
        send_cores(step)
        acc[...] += dg(d_gate, wg, NT) + dg(d_up, wu, NT)

    @pl.when(step == FIRST_PAIR - 1)
    def _():
        dh = acc[...]
        n = n1_ref[...].astype(F32)
        land_n[0, 0:1] = jnp.sum(dh * n, axis=0, keepdims=True)
        land_n[0, 2:3] = jnp.sum(dh, axis=0, keepdims=True)
        dr1 = norm_back(dh * gain_ref[0:1], n, i1_ref[:, :1])
        acc[...] = dr1
        df[...] = dr1.astype(BF)
        x_copy.start()
        probs_copy(0).start()
        norm_copy(0).start()

    cos, sin = cos_ref[:, pl.ds(c * rows, rows)], sin_ref[:, pl.ds(c * rows, rows)]
    in_pairs = jnp.logical_and(step >= FIRST_PAIR, step < FIRST_JOINT)
    p = step - FIRST_PAIR

    @pl.when(jnp.logical_and(in_pairs, p % 3 == 0))
    def _():
        w = jnp.concatenate(out_weight(wb_ref.at[:, pl.ds(2 * (p // 3), 2), :, 128:384]), axis=1)
        t = dg(df[...], w, NN).astype(BF)
        for i in range(3):
            do3[i] = t[:, 128 * i : 128 * i + 128]
        o3 = jnp.concatenate([o_ref[p + i] for i in range(3)], axis=1)
        dwo[p // 3] = dg(df[...], o3, TN).astype(BF)

    @pl.when(in_pairs)
    def _():
        probs_copy(p).wait()
        dqt, dk, dv = pair_back(
            do3[p % 3], o_ref[p], q_ref[0], k_ref[0], v_ref[0], ko_ref[0], vo_ref[0],
            [eb.at[h] for h in range(2)], [l_ref[0, h, 0:1] for h in range(2)], cos, sin,
        )
        dq[p] = dqt.T.astype(BF)
        keep[p, 0] = dk[:, :rows].astype(BF)
        keep[p, 1] = dv[:, :rows].astype(BF)
        oth[p, 0] = dk[:, rows:].astype(BF)
        oth[p, 1] = dv[:, rows:].astype(BF)
        oth_copy(p).start()

        @pl.when(p + 1 < PAIRS)
        def _():
            probs_copy(p + 1).start()

    @pl.when(step >= FIRST_JOINT)
    def _():
        half = step - FIRST_JOINT

        @pl.when(half == 0)
        def _():
            x_copy.wait()

        for i in range(3):
            oth_copy(3 * half + i).wait()
        d = joint_parts(
            [dq[3 * half + i].astype(F32) for i in range(3)],
            [keep[3 * half + i, 0].astype(F32) + got[3 * half + i, 0].astype(F32) for i in range(3)],
            [keep[3 * half + i, 1].astype(F32) + got[3 * half + i, 1].astype(F32) for i in range(3)],
            cos, sin,
        )
        total = None
        wlow = low_lanes((width, 128))
        mid = dwo[half, :, 128:256].astype(F32)
        sides = [dwo[half, :, 0:128], dwo[half, :, 256:384]]
        mids = [swap64(mid), mid]
        shape = (2, 2, width // 4)
        for e in range(2):
            t = 2 * half + e
            w = jnp.concatenate([wa_ref[:, t].reshape(width, GROUP), wb_ref[:, t, :, :256].reshape(width, 256)], axis=1)
            part = dg(d[e], w, NT)
            total = part if total is None else total + part
            g = dg(hb[...], d[e], TN)
            ring[0, :, :, t] = g[:, :GROUP].astype(BF).reshape(shape + (GROUP,))
            ring[1, :, :, t, :, :128] = g[:, GROUP:512].astype(BF).reshape(shape + (128,))
            ring[1, :, :, t, :, 128:256] = jnp.where(wlow, g[:, 512:], mids[e]).astype(BF).reshape(shape + (128,))
            ring[1, :, :, t, :, 256:] = sides[e].reshape(shape + (128,))
        acc[...] += total

    @pl.when(step == LAST_STEP)
    def _():
        for k in range(2):
            send_cores(early // 3 + k)

        @pl.when(section == 0)
        def _():
            e_send[...] = acc[...].astype(BF).reshape(e_send.shape)

        @pl.when(section == 1)
        def _():
            y_copy.start()
            y_copy.wait()

        for i in range(2):

            @pl.when(at_home(i))
            def _():
                end_home(i).start()

    @pl.when(step < FIRST_PAIR)
    def _():
        add_cores(step)

    @pl.when(step == 0)
    def _():
        round_(0)

    round_(step + 1)

    @pl.when(step == LAST_STEP)
    def _():
        for k in range(2):
            add_cores(early // 3 + k)
        end_rows = e_send.shape[1] // 8

        def late(i, carry):
            part = pl.ds(pl.multiple_of((i - LAST_STEP - 2) * end_rows, end_rows), end_rows)
            for k in range(2):

                @pl.when(jnp.logical_not(at_home(k)))
                def _():
                    end_copy(k, part).start()

            round_(i)
            return carry

        lax.fori_loop(LAST_STEP + 2, LAST_STEP + 10, late, 0)
        lax.fori_loop(LAST_STEP + 10, parts + 8, lambda i, t: (round_(i), t)[1], 0)
        for i in range(2):

            @pl.when(at_home(i))
            def _():
                end_home(i).wait()

            @pl.when(jnp.logical_not(at_home(i)))
            def _():
                end_copy(i, pl.ds(0, e_send.shape[1])).wait_send()
                remote(e_send.at[i], e_land.at[i], end_send.at[i], end_recv.at[i], target(i)).wait_recv()

        ends_out[...] = e_land[...]

        def finish(j, carry):
            to_y(j).wait_send()

            @pl.when(z == 0)
            def _():
                go_right(j, 1, land_c.at[j, y, pl.ds(1, 3)]).wait_send()

            @pl.when(z == 1)
            def _():
                go_right(j, 2, land_r.at[j, pl.ds(1, 2)]).wait_send()
                go_left(j, 1, land_l.at[j, pl.ds(0, 1)]).wait_send()

            @pl.when(z == 2)
            def _():
                go_right(j, 3, land_r.at[j, pl.ds(2, 1)]).wait_send()
                go_left(j, 2, land_l.at[j, pl.ds(0, 2)]).wait_send()

            @pl.when(z == last)
            def _():
                go_left(j, 3, land_c.at[j, y, pl.ds(0, 3)]).wait_send()

            return carry

        lax.fori_loop(0, parts, finish, 0)


def last_back(x, y, dy, kept, w, norms, cost, sint):
    q, k, v, ko, vo, o, e, l, gu, n1, i1, n2, i2 = kept
    gains, biases = norms
    rows, width = x.shape
    heads = width // 128
    depth, columns = w.shape[2:]
    parts = columns // WIDE
    units = (columns - width) // 3
    dma = pltpu.SemaphoreType.DMA
    hbm = pl.BlockSpec(memory_space=pl.ANY)
    halves = (2, rows // 2, width)

    def once(shape, at=None):
        return pl.BlockSpec(shape, lambda i: at or (0,) * len(shape), pipeline_mode=pl.Buffered(1))

    def by_pair(shape):
        return pl.BlockSpec(shape, lambda i: (jnp.clip(i - FIRST_PAIR, 0, PAIRS - 1),) + (0,) * (len(shape) - 1))

    pair = by_pair((1, rows, 128))
    group = (4, 4, depth, GROUP)
    return pl.pallas_call(
        functools.partial(last_kernel, parts),
        grid=(LAST_STEP + 1,),
        in_specs=[
            once((rows, width)), once((rows, 128)), once((rows, width)), once((rows, 128)),
            pl.BlockSpec((1, 2, rows, 512), lambda i: (jnp.minimum(i, FIRST_PAIR - 1), 0, 0, 0)),
            pl.BlockSpec(group, lambda i: (0, 0, 0, jnp.where(i < FIRST_PAIR, 2 + i, 0))),
            once(group, (0, 0, 0, 1)),
            once((2, width)), once((2, width)),
            once((heads, rows, 128)),
            pair, pair, pair, pair, pair,
            by_pair((1, 2, 8, rows)),
            once(cost.shape), once(sint.shape),
            hbm, hbm, hbm, hbm,
        ],
        out_specs=[once((depth, width)), once((depth, 2 * units)), once((units, depth)), once(halves), once((8, width))],
        out_shape=[
            sds((depth, width), F32), sds((depth, 2 * units), F32), sds((units, depth), F32),
            sds(halves, BF), sds((8, width), F32),
        ],
        scratch_shapes=[
            VM((rows, width), F32),
            VM((rows, width), BF),
            VM((rows, width), BF),
            VM((2, 2, 2, 4, depth, GROUP), BF),
            VM((3, rows, 128), BF),
            VM((2, width, 384), BF),
            VM((heads, rows, 128), BF),
            VM((heads, 2, 128, rows), BF),
            VM((heads, 2, 128, rows), BF),
            VM((heads, 2, 128, rows), BF),
            VM((2, 2 * rows, rows), BF),
            VM(halves, BF),
            VM(halves, BF),
            VM((depth, WIDE), F32),
            VM((parts, 2, 4, depth, WIDE), BF),
            VM((parts, 4, depth, WIDE), BF),
            VM((parts, 3, depth, WIDE), BF),
            VM((parts, 3, depth, WIDE), BF),
            VM((8, 8, width), F32),
            dma, dma, dma, dma,
            dma((6,)), dma((6,)), dma, dma((2,)), dma((2,)),
        ]
        + [dma((parts,))] * 8
        + [dma((4,))] * 2,
        compiler_params=pltpu.CompilerParams(collective_id=0, has_side_effects=True, vmem_limit_bytes=63 << 20),
        name="last",
    )(n1, i1, n2, i2, gu, w, w, gains, biases, o, q, k, v, ko, vo, l, cost, sint, dy.reshape(halves), x, y.reshape(halves), e)


def mid_kernel(
    da_ref, dr1_ref, w_ref, o_ref, q_ref, k_ref, v_ref, ko_ref, vo_ref, e_ref, l_ref, cos_ref, sin_ref, top_ref,
    dy_out,
    do3, dq, keep, oth, got, d, send, land,
    oth_send, oth_recv, row_send, row_recv,
):
    step = pl.program_id(0)
    section, c = lax.axis_index("section"), lax.axis_index("core")
    rows, width = da_ref.shape
    pieces = send.shape[0]
    near, other = {"core": 1 - c}, {"section": 1 - section}

    def remote(src, dst, send, recv, device):
        return pltpu.make_async_remote_copy(src, dst, send, recv, device_id=device, device_id_type=MESH)

    def oth_copy(p):
        return remote(oth.at[p], got.at[p], oth_send.at[p], oth_recv.at[p], near)

    def row_copy(b):
        return remote(send.at[b], land.at[b], row_send.at[b], row_recv.at[b], other)

    @pl.when(step == 0)
    def _():
        barrier = pltpu.get_barrier_semaphore()
        for device in (near, other):
            pl.semaphore_signal(barrier, inc=1, device_id=device, device_id_type=MESH)
        pl.semaphore_wait(barrier, 2)

    cos, sin = cos_ref[:, pl.ds(c * rows, rows)], sin_ref[:, pl.ds(c * rows, rows)]

    @pl.when(jnp.logical_and(step < PAIRS, step % 3 == 0))
    def _():
        w = jnp.concatenate(out_weight(w_ref.at[:, pl.ds(2 * (step // 3), 2), :, 512:768]), axis=1)
        t = dg(da_ref[...], w, NN).astype(BF)
        for i in range(3):
            do3[i] = t[:, 128 * i : 128 * i + 128]

    @pl.when(step < PAIRS)
    def _():
        dqt, dk, dv = pair_back(
            do3[step % 3], o_ref[step], q_ref[0], k_ref[0], v_ref[0], ko_ref[0], vo_ref[0],
            [e_ref.at[0, h] for h in range(2)], [l_ref[0, h, 0:1] for h in range(2)], cos, sin,
        )
        dq[step] = dqt.T.astype(BF)
        keep[step, 0] = dk[:, :rows]
        keep[step, 1] = dv[:, :rows]
        oth[step, 0] = dk[:, rows:].astype(BF)
        oth[step, 1] = dv[:, rows:].astype(BF)
        oth_copy(step).start()

    def joint(half):
        for i in range(3):
            oth_copy(3 * half + i).wait()
        parts = joint_parts(
            [dq[3 * half + i].astype(F32) for i in range(3)],
            [keep[3 * half + i, 0] + got[3 * half + i, 0].astype(F32) for i in range(3)],
            [keep[3 * half + i, 1] + got[3 * half + i, 1].astype(F32) for i in range(3)],
            cos, sin,
        )
        for e in range(2):
            d[2 * half + e] = parts[e]

    @pl.when(step == PAIRS - 1)
    def _():
        joint(0)

    @pl.when(step == PAIRS)
    def _():
        joint(1)

        def rows_of(b, carry):
            part = pl.ds(pl.multiple_of(b * (rows // pieces), rows // pieces), rows // pieces)
            total = dr1_ref[part]
            for t in range(4):
                total += dg(d[t, part], w_ref[:, t, :, :640].reshape(width, 640), NT)
            send[b] = total.astype(BF)

            @pl.when(section == 1)
            def _():
                row_copy(b).start()

            return carry

        lax.fori_loop(0, pieces, rows_of, 0)

        @pl.when(section == 1)
        def _():
            lax.fori_loop(0, pieces, lambda b, t: (row_copy(b).wait_send(), t)[1], 0)
            dy_out[...] = top_ref[...]

        @pl.when(section == 0)
        def _():
            lax.fori_loop(0, pieces, lambda b, t: (row_copy(b).wait_recv(), t)[1], 0)
            dy_out[...] = land[...].reshape(rows, width)


def mid_back(top, da, dr1, kept, w, cost, sint):
    q, k, v, ko, vo, o, e, l = kept[:8]
    rows, width = da.shape
    heads = width // 128
    depth = w.shape[2]
    pieces = 4
    dma = pltpu.SemaphoreType.DMA

    def once(shape):
        return pl.BlockSpec(shape, lambda i: (0,) * len(shape), pipeline_mode=pl.Buffered(1))

    def by_pair(shape):
        return pl.BlockSpec(shape, lambda i: (jnp.minimum(i, PAIRS - 1),) + (0,) * (len(shape) - 1))

    pair = by_pair((1, rows, 128))
    return pl.pallas_call(
        mid_kernel,
        grid=(PAIRS + 1,),
        in_specs=[
            once((rows, width)), once((rows, width)), once((4, 4, depth, width)), once((heads, rows, 128)),
            pair, pair, pair, pair, pair,
            by_pair((1, 2, 2 * rows, rows)),
            by_pair((1, 2, 8, rows)),
            once(cost.shape), once(sint.shape), once((rows, width)),
        ],
        out_specs=once((rows, width)),
        out_shape=sds((rows, width), BF),
        scratch_shapes=[
            VM((3, rows, 128), BF),
            VM((heads, rows, 128), BF),
            VM((heads, 2, 128, rows), F32),
            VM((heads, 2, 128, rows), BF),
            VM((heads, 2, 128, rows), BF),
            VM((4, rows, 640), BF),
            VM((pieces, rows // pieces, width), BF),
            VM((pieces, rows // pieces, width), BF),
            dma((PAIRS,)), dma((PAIRS,)), dma((pieces,)), dma((pieces,)),
        ],
        compiler_params=pltpu.CompilerParams(collective_id=2, has_side_effects=True, vmem_limit_bytes=58 << 20),
        name="mid",
    )(da, dr1, w, o, q, k, v, ko, vo, e, l, cost, sint, top)


LAG = 6


def first_kernel(
    parts, tok_ref, shard_ref, extra_ref, len_ref, cos_ref, sin_ref,
    w_out, q_out, k_out, v_out, ko_out, vo_out, x_out, top_out, mask_out, norm_out,
    w, xin, q, kv, land_kv, late_kv, o, hb, acc, relay, land_rows, ext, lens,
    tok_sem, tok_send, tok_recv, shard_sem, back_sem, kv_send, kv_recv, out_sem, row_send, row_recv,
    small_send, small_recv, rs_sem, rr_sem, ls_sem, lr_sem, ys_sem, yr_sem, cs_sem, cr_sem,
):
    section = lax.axis_index("section")
    y, c, z = lax.axis_index("y"), lax.axis_index("core"), lax.axis_index("tensor")
    last = 3
    rows, width = xin.shape[0] * xin.shape[1], xin.shape[2]
    near, across, other = {"core": 1 - c}, {"y": 1 - y}, {"section": 1 - section}
    right, left = {"tensor": jnp.minimum(z + 1, last)}, {"tensor": jnp.maximum(z - 1, 0)}
    side = z // 2
    barrier = pltpu.get_barrier_semaphore()

    def greet(device):
        pl.semaphore_signal(barrier, inc=1, device_id=device, device_id_type=MESH)

    def remote(src, dst, send, recv, device):
        return pltpu.make_async_remote_copy(src, dst, send, recv, device_id=device, device_id_type=MESH)

    def target(i):
        return {"core": side, "tensor": 2 * c + i}

    def at_home(i):
        return jnp.logical_and(side == c, 2 * c + i == z)

    def token_copy(i, part):
        return remote(tok_ref.at[i, part], xin.at[z % 2, part], tok_send.at[i], tok_recv.at[z % 2], target(i))

    def token_home(i):
        return pltpu.make_async_copy(tok_ref.at[i], xin.at[z % 2], tok_sem)

    load = pltpu.make_async_copy(shard_ref, w.at[y, c, z], shard_sem)
    load.start()
    greet(near)
    greet(across)
    greet(other)

    @pl.when(z < last)
    def _():
        greet(right)

    @pl.when(z > 0)
    def _():
        greet(left)

    for i in range(2):

        @pl.when(jnp.logical_not(at_home(i)))
        def _():
            greet(target(i))

    count = 5 + jnp.where(z < last, 1, 0) + jnp.where(z > 0, 1, 0) - jnp.where(side == c, 1, 0)
    pl.semaphore_wait(barrier, count)

    ext[y, c] = extra_ref[...]
    lens[c] = len_ref[...]

    def small(k):
        if k == 0:
            return remote(lens.at[c], lens.at[c], small_send.at[0], small_recv.at[0], near)
        if k == 1:
            return remote(ext.at[y, c], ext.at[y, c], small_send.at[1], small_recv.at[1], across)
        return remote(ext.at[:, c], ext.at[:, c], small_send.at[2], small_recv.at[2], near)

    small(0).start()
    small(1).start()
    load.wait()

    def columns(j):
        return pl.ds(pl.multiple_of(j * WIDE, WIDE), WIDE)

    def go_right(j, h):
        b = jnp.maximum(z - h, 0)
        return remote(w.at[y, c, b, :, columns(j)], w.at[y, c, b, :, columns(j)], rs_sem.at[j, h], rr_sem.at[j, h], right)

    def go_left(j, h):
        b = jnp.minimum(z + h, last)
        return remote(w.at[y, c, b, :, columns(j)], w.at[y, c, b, :, columns(j)], ls_sem.at[j, h], lr_sem.at[j, h], left)

    def to_y(j):
        return remote(w.at[y, c, :, :, columns(j)], w.at[y, c, :, :, columns(j)], ys_sem.at[j], yr_sem.at[j], across)

    def block_to_y(j, b):
        return remote(w.at[y, c, b, :, columns(j)], w.at[y, c, b, :, columns(j)], ys_sem.at[j], yr_sem.at[j], across)

    def to_core(j):
        return remote(w.at[:, c, :, :, columns(j)], w.at[:, c, :, :, columns(j)], cs_sem.at[j], cr_sem.at[j], near)

    def write_back(j):
        return pltpu.make_async_copy(w.at[:, :, :, :, columns(j)], w_out.at[:, :, :, :, columns(j)], back_sem.at[j])

    def stage(r, lag, body):
        @pl.when(jnp.logical_and(r >= lag, r - lag < parts))
        def _():
            body(r - lag)

    def send_own(j):
        @pl.when(z < last)
        def _():
            go_right(j, 0).start()

        @pl.when(z > 0)
        def _():
            go_left(j, 0).start()

        block_to_y(j, z).start()

    def hop(h, j):
        @pl.when(z >= h)
        def _():
            go_right(j, h - 1).wait_recv()
            block_to_y(j, z - h).start()

        @pl.when(z + h <= last)
        def _():
            go_left(j, h - 1).wait_recv()
            block_to_y(j, z + h).start()

        if h < last:

            @pl.when(jnp.logical_and(z >= h, z < last))
            def _():
                go_right(j, h).start()

            @pl.when(jnp.logical_and(z + h <= last, z > 0))
            def _():
                go_left(j, h).start()

    def over_core(j):
        to_y(j).wait_recv()
        to_core(j).start()

    def complete(j):
        to_core(j).wait_recv()
        write_back(j).start()

    def round_(r):
        stage(r, 0, send_own)
        stage(r, 1, functools.partial(hop, 1))
        stage(r, 2, functools.partial(hop, 2))
        stage(r, 3, functools.partial(hop, 3))
        stage(r, 5, over_core)
        stage(r, LAG, complete)

    def rounds(first, end):
        lax.fori_loop(first, end, lambda r, t: (round_(r), t)[1], 0)

    lead_parts = width // WIDE
    start = 17
    token_rows = xin.shape[1] // 16
    for i in range(2):

        @pl.when(at_home(i))
        def _():
            token_home(i).start()

    def early(r, carry):
        round_(r)
        part = pl.ds(pl.multiple_of(r * token_rows, token_rows), token_rows)
        for i in range(2):

            @pl.when(jnp.logical_not(at_home(i)))
            def _():
                token_copy(i, part).start()

        return carry

    lax.fori_loop(0, 3, early, 0)
    small(0).wait()
    small(1).wait()
    small(2).start()

    mine = jnp.where(side == 0, lens[0], lens[1])
    mine = jnp.where(z % 2 == 0, mine[0:1], mine[1:2])
    at_q = c * rows + lax.broadcasted_iota(jnp.int32, (1, rows), 1)
    at_k = lax.broadcasted_iota(jnp.int32, (2 * rows, 1), 0)
    at_k = jnp.where(at_k < rows, c * rows + at_k, (1 - c) * rows + at_k - rows)
    seg_q, seg_k = jnp.zeros((1, rows), jnp.int32), jnp.zeros((2 * rows, 1), jnp.int32)
    end = jnp.zeros((1, 1), jnp.int32)
    for n in range(8):
        end = end + mine[:, n : n + 1]
        seg_q = seg_q + jnp.where(end <= at_q, 1, 0)
        seg_k = seg_k + jnp.where(end <= at_k, 1, 0)
    mask_out[...] = jnp.where(seg_k == seg_q, 0.0, neg_fill).astype(F32)
    lax.fori_loop(3, 16, early, 0)
    rounds(16, start)

    small(2).wait()
    halves = [ext[i // 2, i % 2].astype(F32) for i in range(4)]
    for k in range(2):
        for half in range(2):
            pieces = [halves[2 * half + i][3 * k + m : 3 * k + m + 1] for i in range(2) for m in range(3)]
            norm_out[2 * k + half : 2 * k + half + 1] = jnp.concatenate(pieces, axis=1)

    for i in range(2):

        @pl.when(at_home(i))
        def _():
            token_home(i).wait()

        @pl.when(jnp.logical_not(at_home(i)))
        def _():
            token_copy(i, pl.ds(0, xin.shape[1])).wait_send()
            remote(tok_ref.at[i], xin.at[i], tok_send.at[i], tok_recv.at[i], target(i)).wait_recv()

    def project(at, count, x):
        here = pl.ds(at, count)
        cos, sin = cos_ref[pl.ds(c * rows + at, count)], sin_ref[pl.ds(c * rows + at, count)]
        low = low_lanes((count, 128))
        for p in range(2):
            r = [dg(x, w[:, :, 2 * p + e, :, :640].reshape(width, 640), NN) for e in range(2)]
            t = [[v[:, 128 * i : 128 * i + 128] for i in range(5)] for v in r]
            qs = [t[0][0], jnp.where(low, t[0][3], swap64(t[1][3])), t[1][0]]
            ks = [t[0][1], jnp.where(low, swap64(t[0][3]), t[1][3]), t[1][1]]
            vs = [t[0][2], jnp.where(low, t[0][4], swap64(t[1][4])), t[1][2]]
            for i in range(3):
                q[3 * p + i, here] = (rope_fwd(qs[i], cos, sin) * HD**-0.5).astype(BF)
                kv[0, 3 * p + i, here] = rope_fwd(ks[i], cos, sin).astype(BF)
                kv[1, 3 * p + i, here] = vs[i].astype(BF)

    x = xin[...].reshape(rows, width)
    x_out[...] = x
    top_out[...] = x
    project(0, rows, x)
    low = low_lanes((rows, 128))
    share = remote(kv, land_kv, kv_send.at[0], kv_recv.at[0], near)
    share.start()
    rounds(start, start + 1)
    share.wait()

    def pair(p, carry):
        k = jnp.concatenate([kv[0, p], land_kv[0, p]], axis=0)
        v = jnp.concatenate([kv[1, p], land_kv[1, p]], axis=0)
        vt = v.astype(F32).T.astype(BF)
        outs = []
        for h in range(2):
            qm = jnp.where(low if h == 0 else jnp.logical_not(low), q[p], jnp.zeros((rows, 128), BF))
            s = dg(k, qm, NT) + mask_out[...]
            e = jnp.exp(s - jnp.max(s, axis=0, keepdims=True))
            inv = 1.0 / jnp.sum(e, axis=0, keepdims=True)
            outs.append(dg(vt[HD * h : HD * h + HD], e.astype(BF), NN) * inv)
        o[p] = jnp.concatenate(outs, axis=0).T.astype(BF)
        round_(start + 1 + p)
        return carry

    lax.fori_loop(0, 6, pair, 0)
    r = x.astype(F32)
    for p in range(2):
        wo = []
        for e in range(2):
            wo.append([w[:, :, 2 * p + e, :, 512 + 128 * i : 640 + 128 * i].reshape(width, 128) for i in range(2)])
        mid = jnp.where(low_lanes((width, 128)), swap64(wo[0][0].astype(F32)), wo[1][0].astype(F32)).astype(BF)
        r = r + dg(
            jnp.concatenate([o[3 * p + i] for i in range(3)], axis=1),
            jnp.concatenate([wo[0][1], mid, wo[1][1]], axis=1),
            NT,
        )
    n, inv = norm_parts(r)
    h = n * norm_out[0:1] + norm_out[2:3]
    hb[...] = h.astype(BF)
    acc[...] = h
    rounds(start + 7, start + 8)

    def units(k, carry):
        @pl.when(k != 4)
        def _():
            round_(start + 8 + k - k // 5)

        wg, wu, wd = unit_weights(
            lambda t, m: w[:, :, t, :, pl.ds(pl.multiple_of(width + GROUP * k + 128 * m, 128), 128)].reshape(width, 128)
        )
        gate = dg(hb[...], wg, NN)
        up = dg(hb[...], wu, NN)
        act = (gate / (1.0 + jnp.exp(-gate)) * up).astype(BF)
        acc[...] += dg(act, wd, NT)
        return carry

    lax.fori_loop(0, 6, units, 0)
    pieces = relay.shape[0]
    piece_rows = rows // pieces

    def row_copy(b):
        return remote(relay.at[b], land_rows.at[b], row_send.at[b], row_recv.at[b], other)

    def keep(arrays):
        outs = (q_out, k_out, v_out, ko_out, vo_out)
        copies = [pltpu.make_async_copy(t, out, out_sem.at[i]) for i, (t, out) in enumerate(zip(arrays, outs))]
        for t in copies:
            t.start()
        for t in copies:
            t.wait()

    @pl.when(section == 0)
    def _():
        def send_rows(b, carry):
            part = pl.ds(pl.multiple_of(b * piece_rows, piece_rows), piece_rows)
            n, inv = norm_parts(acc[part])
            relay[b] = (n * norm_out[1:2] + norm_out[3:4]).astype(BF)
            row_copy(b).start()
            return carry

        lax.fori_loop(0, pieces, send_rows, 0)
        keep((q, kv.at[0], kv.at[1], land_kv.at[0], land_kv.at[1]))
        lax.fori_loop(0, pieces, lambda b, t: (row_copy(b).wait_send(), t)[1], 0)

    @pl.when(section == 1)
    def _():
        def project_rows(b, carry):
            at = pl.multiple_of(b * piece_rows, piece_rows)
            row_copy(b).wait_recv()
            x_out[pl.ds(at, piece_rows)] = land_rows[b]
            project(at, piece_rows, land_rows[b])
            return carry

        lax.fori_loop(0, pieces, project_rows, 0)
        again = remote(kv, late_kv, kv_send.at[1], kv_recv.at[1], near)
        again.start()
        again.wait()
        keep((q, kv.at[0], kv.at[1], late_kv.at[0], late_kv.at[1]))

    def finish(j, carry):
        write_back(j).wait()
        to_y(j).wait_send()
        to_core(j).wait_send()
        for h in range(last):

            @pl.when(jnp.logical_and(z >= h, z < last))
            def _():
                go_right(j, h).wait_send()

            @pl.when(jnp.logical_and(z + h <= last, z > 0))
            def _():
                go_left(j, h).wait_send()

        return carry

    lax.fori_loop(0, parts, finish, 0)


def first_layer(tokens, shard, extra, lengths, cos, sin):
    micro, own, width = tokens.shape
    depth, columns = shard.shape
    rows = 2 * own
    parts = columns // WIDE
    heads = width // 128
    dma = pltpu.SemaphoreType.DMA
    hbm = pl.BlockSpec(memory_space=pl.ANY)
    vm = pl.BlockSpec(memory_space=VM)
    return pl.pallas_call(
        functools.partial(first_kernel, parts),
        in_specs=[hbm, hbm, vm, vm, vm, vm],
        out_specs=[hbm] * 6 + [vm] * 4,
        out_shape=[sds((2, 2, 4, depth, columns), BF)]
        + [sds((heads, rows, 128), BF)] * 5
        + [
            sds((rows, width), BF),
            sds((rows, width), BF),
            sds((2 * rows, rows), F32),
            sds((4, width), F32),
        ],
        scratch_shapes=[
            VM((2, 2, 4, depth, columns), BF),
            VM((2, own, width), BF),
            VM((heads, rows, 128), BF),
            VM((2, heads, rows, 128), BF),
            VM((2, heads, rows, 128), BF),
            VM((2, heads, rows, 128), BF),
            VM((heads, rows, 128), BF),
            VM((rows, width), BF),
            VM((rows, width), F32),
            VM((4, rows // 4, width), BF),
            VM((4, rows // 4, width), BF),
            VM((2, 2) + extra.shape, BF),
            VM((2,) + lengths.shape, jnp.int32),
            dma, dma((2,)), dma((2,)), dma, dma((parts,)), dma((2,)), dma((2,)), dma((5,)), dma((4,)), dma((4,)),
            dma((3,)), dma((3,)),
            dma((parts, 3)), dma((parts, 3)), dma((parts, 3)), dma((parts, 3)),
            dma((parts,)), dma((parts,)), dma((parts,)), dma((parts,)),
        ],
        compiler_params=pltpu.CompilerParams(collective_id=1, has_side_effects=True, vmem_limit_bytes=60 << 20),
        name="first",
    )(tokens, shard, extra, lengths, cos, sin)


def swap_pairs(tp, step, dp_axes):
    pairs = []
    half = tp // 2
    for core in range(2):
        for at in range(tp):
            source = core * tp + at
            target = (at // half) * tp + half * core + (at + step) % half
            pairs.append((source, target))
    return pairs


def to_sequences(rows, tp):
    half = tp // 2
    at = lax.axis_index("tensor")
    pieces = [None] * half
    got = []
    for step in range(half):
        piece = lax.dynamic_index_in_dim(rows, (at + step) % half, 0, keepdims=False)
        got.append(lax.ppermute(piece, ("core", "tensor"), swap_pairs(tp, step, None)))
    stacked = jnp.stack(got)
    order = (at - jnp.arange(half)) % half
    return jnp.take(stacked, order, axis=0).reshape(-1, rows.shape[-1])


def to_positions(rows, tp):
    half = tp // 2
    at = lax.axis_index("tensor")
    parts = rows.reshape(half, -1, rows.shape[-1])
    got = []
    for step in range(half):
        piece = lax.dynamic_index_in_dim(parts, (at - step) % half, 0, keepdims=False)
        back = [(target, source) for source, target in swap_pairs(tp, step, None)]
        got.append(lax.ppermute(piece, ("core", "tensor"), back))
    stacked = jnp.stack(got)
    order = (at + jnp.arange(half)) % half
    return jnp.take(stacked, (jnp.arange(half) - at) % half, axis=0)


def rope_tables(positions):
    halfway = HD // 2
    freqs = 1000.0 ** (-jnp.arange(halfway, dtype=F32) / halfway)
    angles = positions.astype(F32)[:, None] * freqs[None, :]
    cos, sin = jnp.cos(angles), jnp.sin(angles)
    wide = jnp.concatenate([cos] * 4, axis=1)
    signed = jnp.concatenate([-sin, sin] * 2, axis=1)
    return wide, signed, cos.T, sin.T


def pack_shard(w_qkv, w_out, w_gate_up, w_down):
    rows = w_qkv.shape[0]
    odd = lax.axis_index("tensor") % 2 == 1
    heads = w_qkv.reshape(rows, 3, 3, HD)
    mine = w_out.T.reshape(rows, 3, HD)
    heads = jnp.where(odd, jnp.roll(heads, -1, axis=2), heads)
    mine = jnp.where(odd, jnp.roll(mine, -1, axis=1), mine)
    first = jnp.concatenate(
        [heads[:, :, :2].reshape(rows, -1), heads[:, :, 2].reshape(rows, -1), mine[:, 2], mine[:, :2].reshape(rows, -1)], axis=1
    )
    units = jnp.concatenate([w_gate_up, w_down.T[:, None]], axis=1)
    units = units.reshape(rows, 3, -1, 128).transpose(0, 2, 1, 3)
    return jnp.concatenate([first, units.reshape(rows, -1)], axis=1)


def unpack_first(first):
    rows = first.shape[0]
    odd = lax.axis_index("tensor") % 2 == 1
    both = first[:, :384].reshape(rows, 3, 2, HD)
    single = first[:, 384:576].reshape(rows, 3, 1, HD)
    heads = jnp.concatenate([both, single], axis=2)
    mine = jnp.concatenate([first[:, 640:].reshape(rows, 2, HD), first[:, 576:640].reshape(rows, 1, HD)], axis=1)
    heads = jnp.where(odd, jnp.roll(heads, 1, axis=2), heads)
    mine = jnp.where(odd, jnp.roll(mine, 1, axis=1), mine)
    return heads.reshape(rows, 3, -1), mine.reshape(rows, -1).T


def host_tables(length):
    halfway = HD // 2
    freqs = np.float32(1000.0) ** (-np.arange(halfway, dtype=np.float32) / np.float32(halfway))
    angles = np.arange(length, dtype=np.float32)[:, None] * freqs[None, :]
    cos, sin = np.cos(angles), np.sin(angles)
    return np.concatenate([cos] * 4, axis=1), np.concatenate([-sin, sin] * 2, axis=1), cos.T.copy(), sin.T.copy()


BLOCKS = 4


def gather_shard(shard, dp, tp):
    rows, columns = shard.shape
    got = lax.all_gather(shard, ALL, axis=0, tiled=False)
    got = got.reshape(BLOCKS, dp // BLOCKS, tp, rows, columns)
    return got.transpose(0, 2, 1, 3, 4).reshape(BLOCKS, tp, -1, columns)


def scatter_sum(whole, dp, tp):
    columns = whole.shape[3]
    parts = whole.reshape(BLOCKS, tp, dp // BLOCKS, -1, columns).transpose(0, 2, 1, 3, 4)
    parts = parts.reshape(dp * tp, -1, columns)
    return lax.psum_scatter(parts, ALL, scatter_dimension=0, tiled=False).astype(F32)


def on_device(dp, tp, tokens, cotangent, lengths, w_qkv, w_out, w_gate_up, w_down, norm_gains, norm_biases):
    section = lax.axis_index("section")
    core = lax.axis_index("core")
    at = lax.axis_index("tensor")
    micro, own, width = tokens.shape
    assert micro * 2 == tp
    length = own * tp
    rows = length // 2
    shard = pack_shard(w_qkv[0], w_out[0], w_gate_up[0], w_down[0])
    if dp == 4 and tp == 4:
        extra = jnp.concatenate([norm_gains.reshape(-1, 128), norm_biases.reshape(-1, 128)])
        extra = jnp.pad(extra, ((0, 16 - extra.shape[0]), (0, 0)))
        padded = jnp.pad(lengths, ((0, 8 - lengths.shape[0]), (0, 128 - lengths.shape[1])))
        wide, signed, cost, sint = host_tables(length)
        rows_in = jnp.where(section == 0, tokens, cotangent)
        weights, *joint, inputs, grad_top, mask, small = first_layer(rows_in, shard, extra, padded, wide, signed)
        weights = weights.reshape((BLOCKS,) + weights.shape[2:])
        norms = (small[:2], small[2:])
        y, kept = attend(inputs, tuple(joint), weights, norms, mask)
        dr1, da = ffn_backward(grad_top, kept, weights, norms, False)
        dy = mid_back(grad_top, da, dr1, kept, weights, cost, sint)
        first, pair, down, ends, total = last_back(inputs, y, dy, kept, weights, norms, cost, sint)
        small = lax.dynamic_slice_in_dim(total[:4].reshape(2, dp * tp, -1), lax.axis_index(ALL), 1, 1)
        gains, biases = small[0, 0], small[1, 0]
    else:
        near = core * rows + jnp.arange(rows, dtype=jnp.int32)
        far = (1 - core) * rows + jnp.arange(rows, dtype=jnp.int32)
        tabs = rope_tables(near)
        weights = gather_shard(shard, dp, tp)
        norms = jnp.concatenate([norm_gains, norm_biases])
        norms = lax.all_gather(norms, ("y", "core"), axis=1, tiled=True).astype(F32)
        norms = (norms[0].reshape(2, width), norms[1].reshape(2, width))
        grad_top = to_sequences(cotangent, tp)
        tokens = to_sequences(tokens, tp)
        chip_lengths = lax.all_gather(lengths, "core", axis=0, tiled=True)
        my_lengths = lax.dynamic_index_in_dim(chip_lengths, at, 0, keepdims=False)
        ends_at = jnp.cumsum(my_lengths)

        def segment(positions):
            return jnp.sum((ends_at[None, :] <= positions[:, None]).astype(jnp.int32), axis=-1)

        seg_near = segment(near)
        seg_all = jnp.concatenate([seg_near, segment(far)])
        mask = jnp.where(seg_all[:, None] == seg_near[None, :], 0.0, neg_fill).astype(F32)
        y, unused = forward(tokens, weights, norms, mask, tabs)
        received = lax.ppermute(y, "section", [(0, 1)])
        inputs = jnp.where(section == 0, tokens, received)
        y, kept = forward(inputs, weights, norms, mask, tabs)
        dr1, da = ffn_backward(grad_top, kept, weights, norms, False)
        unused, dz = attn_backward(inputs, da, dr1, None, kept, weights, tabs)
        received = lax.ppermute(dz, "section", [(1, 0)])
        dy = jnp.where(section == 0, received, grad_top)
        g, dr1, da, ng = ffn_backward(dy, kept, weights, norms, True)
        g, dz = attn_backward(inputs, da, dr1, g, kept, weights, tabs)
        ends = to_positions(jnp.where(section == 0, dz.astype(BF), y), tp)
        mine = scatter_sum(g, dp, tp)
        first = mine[:, :width]
        units = mine[:, width:].reshape(first.shape[0], -1, 3, 128).transpose(0, 2, 1, 3).reshape(first.shape[0], 3, -1)
        pair, down = units[:, :2], units[:, 2].T
        gains = lax.psum_scatter(ng[0:2].reshape(-1), ALL, scatter_dimension=0, tiled=True)
        biases = lax.psum_scatter(ng[2:4].reshape(-1), ALL, scatter_dimension=0, tiled=True)
    joint, mix = unpack_first(first)
    outs = (joint, mix, pair.reshape(pair.shape[0], 2, -1), down, gains, biases)
    return (ends[None],) + tuple(t[None] for t in outs)


def solution(mesh):
    sections, dp, tp = mesh.devices.shape
    fine = Mesh(mesh.devices.reshape(sections, dp // 2, 2, tp), ("section", "y", "core", "tensor"))
    both = ("y", "core")
    in_specs = (
        P(both, "tensor", None),
        P(both, "tensor", None),
        P(both, None),
        P("section", both, None, "tensor"),
        P("section", "tensor", both),
        P("section", both, None, "tensor"),
        P("section", "tensor", both),
        P("section", both),
        P("section", both),
    )
    out_specs = (
        P("section", both, "tensor", None),
        P("section", both, None, "tensor"),
        P("section", "tensor", both),
        P("section", both, None, "tensor"),
        P("section", "tensor", both),
        P("section", ALL),
        P("section", ALL),
    )
    return jax.shard_map(
        functools.partial(on_device, dp, tp), mesh=fine, in_specs=in_specs, out_specs=out_specs, check_vma=False
    )
```

```python
import functools

import jax
import jax.numpy as jnp
import numpy as np
from jax import lax
from jax.experimental import pallas as pl
from jax.experimental.pallas import tpu as pltpu
from jax.sharding import Mesh, PartitionSpec as P

HD = 64
eps = 1e-05
neg_fill = -1e30
ALL = ("y", "core", "tensor")
BF = jnp.bfloat16
F32 = jnp.float32
MESH = pl.DeviceIdType.MESH


def dg(a, b, dims):
    return lax.dot_general(a, b, (dims, ((), ())), preferred_element_type=F32)


NN = ((1,), (0,))
NT = ((1,), (1,))
TN = ((0,), (0,))


def low_lanes(shape):
    return lax.broadcasted_iota(jnp.int32, shape, 1) < HD


def swap64(v):
    return pltpu.roll(v, HD, axis=1)


def rope_fwd(t, cos, sin):
    lane = lax.broadcasted_iota(jnp.int32, t.shape, 1) % HD
    other = jnp.where(lane < HD // 2, pltpu.roll(t, 128 - HD // 2, axis=1), pltpu.roll(t, HD // 2, axis=1))
    return t * cos + other * sin


def qkv_kernel(x_ref, w_ref, cos_ref, sin_ref, q_ref, k_ref, v_ref):
    x = x_ref[...]
    width = x.shape[1]
    r = [dg(x, w_ref[:, e, :, :640].reshape(width, 640), NN) for e in range(2)]
    c = [[t[:, 128 * i : 128 * i + 128] for i in range(5)] for t in r]
    low = low_lanes(c[0][0].shape)
    qs = [c[0][0], jnp.where(low, c[0][3], swap64(c[1][3])), c[1][0]]
    ks = [c[0][1], jnp.where(low, swap64(c[0][3]), c[1][3]), c[1][1]]
    vs = [c[0][2], jnp.where(low, c[0][4], swap64(c[1][4])), c[1][2]]
    cos, sin = cos_ref[...], sin_ref[...]
    for i in range(3):
        q_ref[i] = (rope_fwd(qs[i], cos, sin) * HD**-0.5).astype(BF)
        k_ref[i] = rope_fwd(ks[i], cos, sin).astype(BF)
        v_ref[i] = vs[i].astype(BF)


def attn_kernel(q_ref, k_ref, v_ref, ko_ref, vo_ref, m_ref, o_ref, e_ref, l_ref):
    q = q_ref[0]
    k = jnp.concatenate([k_ref[0], ko_ref[0]], axis=0)
    v = jnp.concatenate([v_ref[0], vo_ref[0]], axis=0)
    vt = v.astype(F32).T.astype(BF)
    outs = []
    for h in range(2):
        low = low_lanes(q.shape)
        qm = jnp.where(low if h == 0 else jnp.logical_not(low), q, jnp.zeros_like(q))
        s = dg(k, qm, NT) + m_ref[...]
        e = jnp.exp(s - jnp.max(s, axis=0, keepdims=True))
        inv = 1.0 / jnp.sum(e, axis=0, keepdims=True)
        eb = e.astype(BF)
        e_ref[0, h] = eb
        l_ref[0, h] = jnp.broadcast_to(inv, l_ref.shape[2:])
        outs.append(dg(vt[HD * h : HD * h + HD], eb, NN) * inv)
    o_ref[0] = jnp.concatenate(outs, axis=0).T.astype(BF)


def norm_parts(r):
    center = r - jnp.mean(r, axis=-1, keepdims=True)
    inv = lax.rsqrt(jnp.mean(center * center, axis=-1, keepdims=True) + eps)
    return center * inv, inv


def norm_back(dn, n, inv):
    return inv * (dn - jnp.mean(dn, axis=-1, keepdims=True) - n * jnp.mean(dn * n, axis=-1, keepdims=True))


def out_weight(w_ref):
    c = [[w_ref[:, e, :, 128 * i : 128 * i + 128].reshape(-1, 128) for i in range(2)] for e in range(2)]
    low = low_lanes(c[0][0].shape)
    mid = jnp.where(low, swap64(c[0][0].astype(F32)), c[1][0].astype(F32)).astype(BF)
    return [c[0][1], mid, c[1][1]]


GROUP = 384
WIDE = 128


def unit_weights(load):
    return [jnp.concatenate([load(t, m) for t in range(4)], axis=1) for m in range(3)]


def ffn_kernel(x_ref, o_ref, wo_ref, w_ref, g_ref, b_ref, y_ref, gu_ref, n1_ref, i1_ref, n2_ref, i2_ref, h_ref, hb_ref, acc_ref):
    z = pl.program_id(0)
    width = x_ref.shape[1]

    @pl.when(z == 0)
    def _():
        r = x_ref[...].astype(F32)
        for p in range(2):
            w = jnp.concatenate(out_weight(wo_ref.at[:, 2 * p : 2 * p + 2]), axis=1)
            o = jnp.concatenate([o_ref[3 * p + i] for i in range(3)], axis=1)
            r = r + dg(o, w, NT)
        n, inv = norm_parts(r)
        n1_ref[...] = n.astype(BF)
        i1_ref[...] = jnp.broadcast_to(inv, i1_ref.shape)
        h = n * g_ref[0:1] + b_ref[0:1]
        h_ref[...] = h
        hb_ref[...] = h.astype(BF)

    hb = hb_ref[...]
    wg, wu, wd = unit_weights(lambda t, m: w_ref[:, t, :, 128 * m : 128 * m + 128].reshape(width, 128))
    gate = dg(hb, wg, NN)
    up = dg(hb, wu, NN)
    gu_ref[0, 0] = gate.astype(BF)
    gu_ref[0, 1] = up.astype(BF)
    act = (gate / (1.0 + jnp.exp(-gate)) * up).astype(BF)
    part = dg(act, wd, NT)

    @pl.when(z == 0)
    def _():
        acc_ref[...] = h_ref[...] + part

    @pl.when(z > 0)
    def _():
        acc_ref[...] += part

    @pl.when(z == pl.num_programs(0) - 1)
    def _():
        n, inv = norm_parts(acc_ref[...])
        n2_ref[...] = n.astype(BF)
        i2_ref[...] = jnp.broadcast_to(inv, i2_ref.shape)
        y_ref[...] = (n * g_ref[1:2] + b_ref[1:2]).astype(BF)


def ffn_back_kernel(grads, dy_ref, n1_ref, i1_ref, n2_ref, i2_ref, gu_ref, w_ref, g_ref, b_ref, *refs):
    if grads:
        g_out, dr1_ref, da_ref, ng_ref, hb_ref, df_ref, acc_ref = refs
    else:
        dr1_ref, da_ref, df_ref, acc_ref = refs
    z = pl.program_id(0)
    width = dy_ref.shape[1]

    @pl.when(z == 0)
    def _():
        dy = dy_ref[...].astype(F32)
        n = n2_ref[...].astype(F32)
        if grads:
            ng_ref[1:2] = jnp.sum(dy * n, axis=0, keepdims=True)
            ng_ref[3:4] = jnp.sum(dy, axis=0, keepdims=True)
            hb_ref[...] = (n1_ref[...].astype(F32) * g_ref[0:1] + b_ref[0:1]).astype(BF)
        dr2 = norm_back(dy * g_ref[1:2], n, i2_ref[:, :1])
        acc_ref[...] = dr2
        df_ref[...] = dr2.astype(BF)

    df = df_ref[...]
    gate = gu_ref[0, 0].astype(F32)
    up = gu_ref[0, 1].astype(F32)
    s = 1.0 / (1.0 + jnp.exp(-gate))
    silu = gate * s
    wg, wu, wd = unit_weights(lambda t, m: w_ref[:, t, :, 128 * m : 128 * m + 128].reshape(width, 128))

    def keep(m, grad):
        for t in range(g_out.shape[1]):
            g_out[:, t, :, 128 * m : 128 * m + 128] = grad[:, 128 * t : 128 * t + 128].astype(BF).reshape(g_out.shape[0], -1, 128)

    if grads:
        keep(2, dg(df, (silu * up).astype(BF), TN))
    d_act = dg(df, wd, NN)
    d_gate = (d_act * up * (s * (1.0 + gate * (1.0 - s)))).astype(BF)
    d_up = (d_act * silu).astype(BF)
    if grads:
        hb = hb_ref[...]
        keep(0, dg(hb, d_gate, TN))
        keep(1, dg(hb, d_up, TN))
    acc_ref[...] += dg(d_gate, wg, NT) + dg(d_up, wu, NT)

    @pl.when(z == pl.num_programs(0) - 1)
    def _():
        dh = acc_ref[...]
        n = n1_ref[...].astype(F32)
        if grads:
            ng_ref[0:1] = jnp.sum(dh * n, axis=0, keepdims=True)
            ng_ref[2:3] = jnp.sum(dh, axis=0, keepdims=True)
        dr1 = norm_back(dh * g_ref[0:1], n, i1_ref[:, :1])
        dr1_ref[...] = dr1
        da_ref[...] = dr1.astype(BF)


def pair_back(do, o, q, k, v, ko, vo, e, l, cos, sin):
    dot = do.astype(F32).T
    ot = o.astype(F32).T
    k = jnp.concatenate([k, ko], axis=0)
    v = jnp.concatenate([v, vo], axis=0)
    kt = k.astype(F32).T.astype(BF)
    qt = q.astype(F32).T.astype(BF)
    dqs, dks, dvs = [], [], []
    for h in range(2):
        span = slice(HD * h, HD * h + HD)
        scaled = dot[span] * l[h]
        inner = jnp.sum(scaled * ot[span], axis=0, keepdims=True)
        sb = scaled.astype(BF)
        zero = jnp.zeros_like(sb)
        padded = jnp.concatenate([sb, zero] if h == 0 else [zero, sb], axis=0)
        dp = dg(v, padded, NN)
        et = e[h][...]
        ds = (et.astype(F32) * (dp - inner)).astype(BF)
        dvs.append(dg(sb, et, NT))
        dks.append(dg(qt[span], ds, NT))
        dqt = dg(kt[span], ds, NN) * HD**-0.5
        d1, d2 = dqt[: HD // 2], dqt[HD // 2 :]
        dqs.append(d1 * cos + d2 * sin)
        dqs.append(d2 * cos - d1 * sin)
    return [jnp.concatenate(t, axis=0) for t in (dqs, dks, dvs)]


def joint_parts(dq, dkt, dvt, cos, sin):
    dk = []
    for t in dkt:
        parts = []
        for h in range(2):
            d1 = t[HD * h : HD * h + HD // 2]
            d2 = t[HD * h + HD // 2 : HD * h + HD]
            parts += [d1 * cos + d2 * sin, d2 * cos - d1 * sin]
        dk.append(jnp.concatenate(parts, axis=0).T)
    dv = [t.T for t in dvt]
    low = low_lanes(dq[0].shape)
    zero = jnp.zeros_like(dv[1])
    d = [
        [dq[0], dk[0], dv[0], jnp.where(low, dq[1], swap64(dk[1])), jnp.where(low, dv[1], zero)],
        [dq[2], dk[2], dv[2], jnp.where(low, swap64(dq[1]), dk[1]), jnp.where(low, swap64(dv[1]), zero)],
    ]
    return [jnp.concatenate(t, axis=1).astype(BF) for t in d]


def attn_back_kernel(grads, da_ref, wo_ref, o_ref, q_ref, k_ref, v_ref, ko_ref, vo_ref, e_ref, l_ref, cos_ref, sin_ref, dq_ref, own_ref, oth_ref, *dwo_ref):
    da = da_ref[...]
    rows = da.shape[0]
    w = jnp.concatenate(out_weight(wo_ref), axis=1)
    do3 = dg(da, w, NN).astype(BF)
    if grads:
        o3 = jnp.concatenate([o_ref[i] for i in range(3)], axis=1)
        dwo_ref[0][0] = dg(da, o3, TN).astype(BF)
    cos, sin = cos_ref[...], sin_ref[...]
    for i in range(3):
        dqt, dk, dv = pair_back(
            do3[:, 128 * i : 128 * i + 128], o_ref[i], q_ref[i], k_ref[i], v_ref[i], ko_ref[i], vo_ref[i],
            [e_ref[i, h] for h in range(2)], [l_ref[i, h, 0:1] for h in range(2)], cos, sin,
        )
        dq_ref[i] = dqt.T.astype(BF)
        own_ref[i, 0] = dk[:, :rows]
        own_ref[i, 1] = dv[:, :rows]
        oth_ref[i, 0] = dk[:, rows:].astype(BF)
        oth_ref[i, 1] = dv[:, rows:].astype(BF)


def joint_back_kernel(grads, *refs):
    if grads:
        old_ref, x_ref, w_ref, dr1_ref, dq_ref, own_ref, got_ref, dwo_ref, cos_ref, sin_ref, g_ref, dz_ref = refs
    else:
        w_ref, dr1_ref, dq_ref, own_ref, got_ref, cos_ref, sin_ref, dz_ref, dzb_ref = refs
    p = pl.program_id(0)
    width = dr1_ref.shape[1]
    d = joint_parts(
        [dq_ref[i].astype(F32) for i in range(3)],
        [own_ref[i, 0] + got_ref[i, 0].astype(F32) for i in range(3)],
        [own_ref[i, 1] + got_ref[i, 1].astype(F32) for i in range(3)],
        cos_ref[...],
        sin_ref[...],
    )
    acc = None
    for e in range(2):
        t = dg(d[e], w_ref[:, e, :, :640].reshape(width, 640), NT)
        acc = t if acc is None else acc + t
    if grads:
        x = x_ref[...]
        wlow = low_lanes((width, 128))
        mid = dwo_ref[0, :, 128:256].astype(F32)
        sides = [dwo_ref[0, :, 0:128], dwo_ref[0, :, 256:384]]
        mids = [swap64(mid), mid]
        for e in range(2):
            g = dg(x, d[e], TN)
            blocks = g_ref.shape[0]
            g_ref[:, e, :, :512] = g[:, :512].astype(BF).reshape(blocks, -1, 512)
            g_ref[:, e, :, 512:640] = jnp.where(wlow, g[:, 512:], mids[e]).astype(BF).reshape(blocks, -1, 128)
            g_ref[:, e, :, 640:] = sides[e].reshape(blocks, -1, 128)

    @pl.when(p == 0)
    def _():
        dz_ref[...] = dr1_ref[...] + acc

    @pl.when(p > 0)
    def _():
        total = dz_ref[...] + acc
        dz_ref[...] = total
        if not grads:
            dzb_ref[...] = total.astype(BF)


BIG = pltpu.CompilerParams(vmem_limit_bytes=58 << 20)
VM = pltpu.VMEM


def full(shape):
    return pl.BlockSpec(shape, lambda i: (0,) * len(shape))


def lead(shape, at=0):
    return pl.BlockSpec(shape, lambda i: tuple(i if j == at else 0 for j in range(len(shape))))


def joint_block(w):
    return pl.BlockSpec((w.shape[0], 2, w.shape[2], 768), lambda i: (0, i, 0, 0))


def group_block(w):
    return pl.BlockSpec((w.shape[0], w.shape[1], w.shape[2], GROUP), lambda i: (0, 0, 0, 2 + i))


def sds(shape, kind):
    return jax.ShapeDtypeStruct(shape, kind)


def forward(x, weights, norms, mask, tabs):
    w = weights
    rows, width = x.shape
    heads = width // 128
    blocks, tp, depth, columns = w.shape
    steps = tp // 2
    cos, sin, cost, sint = tabs
    q, k, v = pl.pallas_call(
        qkv_kernel,
        grid=(steps,),
        in_specs=[full((rows, width)), joint_block(w), full((rows, 128)), full((rows, 128))],
        out_specs=[lead((3, rows, 128))] * 3,
        out_shape=[sds((heads, rows, 128), BF)] * 3,
        compiler_params=BIG,
        name="qkv",
    )(x, w, cos, sin)
    ko, vo = lax.ppermute((k, v), "core", [(0, 1), (1, 0)])
    return attend(x, (q, k, v, ko, vo), w, norms, mask)


def attend(x, joint, w, norms, mask):
    gains, biases = norms
    q, k, v, ko, vo = joint
    rows, width = x.shape
    heads = width // 128
    blocks, tp, depth, columns = w.shape
    pair = lead((1, rows, 128))
    o, e, l = pl.pallas_call(
        attn_kernel,
        grid=(heads,),
        in_specs=[pair] * 5 + [full((2 * rows, rows))],
        out_specs=[pair, lead((1, 2, 2 * rows, rows)), lead((1, 2, 8, rows))],
        out_shape=[sds((heads, rows, 128), BF), sds((heads, 2, 2 * rows, rows), BF), sds((heads, 2, 8, rows), F32)],
        compiler_params=BIG,
        name="attn",
    )(q, k, v, ko, vo, mask)
    groups = (columns - width) // GROUP
    units = tp * 128
    y, gu, n1, i1, n2, i2 = pl.pallas_call(
        ffn_kernel,
        grid=(groups,),
        in_specs=[
            full((rows, width)),
            full((heads, rows, 128)),
            pl.BlockSpec((blocks, tp, depth, 256), lambda i: (0, 0, 0, 2)),
            group_block(w),
            full((2, width)),
            full((2, width)),
        ],
        out_specs=[full((rows, width)), lead((1, 2, rows, units))] + [full((rows, width)), full((rows, 128))] * 2,
        out_shape=[sds((rows, width), BF), sds((groups, 2, rows, units), BF)] + [sds((rows, width), BF), sds((rows, 128), F32)] * 2,
        scratch_shapes=[VM((rows, width), F32), VM((rows, width), BF), VM((rows, width), F32)],
        compiler_params=BIG,
        name="ffn",
    )(x, o, w, w, gains, biases)
    return y, (q, k, v, ko, vo, o, e, l, gu, n1, i1, n2, i2)


def ffn_backward(dy, kept, w, norms, grads):
    gains, biases = norms
    gu, n1, i1, n2, i2 = kept[8:]
    rows, width = dy.shape
    blocks, tp, depth, columns = w.shape
    groups = (columns - width) // GROUP
    whole, stat = full((rows, width)), full((rows, 128))
    outs = [whole, whole]
    shapes = [sds((rows, width), F32), sds((rows, width), BF)]
    scratch = [VM((rows, width), BF), VM((rows, width), F32)]
    if grads:
        outs = [group_block(w)] + outs + [full((8, width))]
        shapes = [sds(w.shape, BF)] + shapes + [sds((8, width), F32)]
        scratch = [VM((rows, width), BF)] + scratch
    return pl.pallas_call(
        functools.partial(ffn_back_kernel, grads),
        grid=(groups,),
        in_specs=[
            whole, whole, stat, whole, stat,
            lead((1, 2, rows, tp * 128)),
            group_block(w),
            full((2, width)), full((2, width)),
        ],
        out_specs=outs,
        out_shape=shapes,
        scratch_shapes=scratch,
        compiler_params=BIG,
        name="ffn_back" if grads else "ffn_back_light",
    )(dy, n1, i1, n2, i2, gu, w, gains, biases)


def attn_backward(x, da, dr1, g, kept, w, tabs):
    grads = g is not None
    q, k, v, ko, vo, o, e, l = kept[:8]
    rows, width = da.shape
    heads = width // 128
    blocks, tp, depth, columns = w.shape
    steps = tp // 2
    cos, sin, cost, sint = tabs
    whole = full((rows, width))
    three = lead((3, rows, 128))
    side = lead((3, 2, 128, rows))
    table = full((HD // 2, rows))
    extra = [lead((1, width, 384))] if grads else []
    dq, own, oth, *dwo = pl.pallas_call(
        functools.partial(attn_back_kernel, grads),
        grid=(steps,),
        in_specs=[
            whole,
            pl.BlockSpec((blocks, 2, depth, 256), lambda i: (0, i, 0, 2)),
            three, three, three, three, three, three,
            lead((3, 2, 2 * rows, rows)),
            lead((3, 2, 8, rows)),
            table, table,
        ],
        out_specs=[three, side, side] + extra,
        out_shape=[
            sds((heads, rows, 128), BF),
            sds((heads, 2, 128, rows), F32),
            sds((heads, 2, 128, rows), BF),
        ]
        + ([sds((steps, width, 384), BF)] if grads else []),
        compiler_params=BIG,
        name="attn_back",
    )(da, w, o, q, k, v, ko, vo, e, l, cost, sint)
    got = lax.ppermute(oth, "core", [(0, 1), (1, 0)])
    if grads:
        specs = [pl.BlockSpec(memory_space=pl.ANY), whole, joint_block(w), whole, three, side, side] + extra
        args = (g, x, w, dr1, dq, own, got, *dwo)
        outs, shapes = [joint_block(w), whole], [sds(w.shape, BF), sds((rows, width), F32)]
    else:
        specs = [joint_block(w), whole, three, side, side]
        args = (w, dr1, dq, own, got)
        outs, shapes = [whole, whole], [sds((rows, width), F32), sds((rows, width), BF)]
    return pl.pallas_call(
        functools.partial(joint_back_kernel, grads),
        grid=(steps,),
        in_specs=specs + [table, table],
        out_specs=outs,
        out_shape=shapes,
        input_output_aliases={0: 0} if grads else {},
        compiler_params=BIG,
        name="joint_back",
    )(*args, cost, sint)


PAIRS = 6
FIRST_PAIR = 6
FIRST_JOINT = 12
LAST_STEP = 13


def last_kernel(
    parts, n1_ref, i1_ref, n2_ref, i2_ref, gu_ref, wa_ref, wb_ref, gain_ref, bias_ref,
    o_ref, q_ref, k_ref, v_ref, ko_ref, vo_ref, l_ref, cos_ref, sin_ref, dy_hbm, x_hbm, y_hbm, e_hbm,
    first_out, pair_out, down_out, ends_out, norm_out,
    acc, df, hb, ring, do3, dwo, dq, keep, oth, got, eb, e_send, e_land, tmp, land_c, land_y, land_r, land_l, land_n,
    dy_sem, x_sem, y_sem, e_sem, oth_send, oth_recv, end_sem, end_send, end_recv,
    cs_sem, cr_sem, ys_sem, yr_sem, rs_sem, rr_sem, ls_sem, lr_sem, ns_sem, nr_sem,
):
    step = pl.program_id(0)
    section = lax.axis_index("section")
    y, c, z = lax.axis_index("y"), lax.axis_index("core"), lax.axis_index("tensor")
    last = 3
    rows, width = acc.shape
    early = parts - width // WIDE
    near, across = {"core": 1 - c}, {"y": 1 - y}
    right, left = {"tensor": jnp.minimum(z + 1, last)}, {"tensor": jnp.maximum(z - 1, 0)}
    pair = {"tensor": z + 1 - 2 * lax.rem(z, 2)}
    far = {"tensor": lax.rem(z + 2, 4)}
    side = z // 2
    barrier = pltpu.get_barrier_semaphore()

    def greet(device):
        pl.semaphore_signal(barrier, inc=1, device_id=device, device_id_type=MESH)

    def remote(src, dst, send, recv, device):
        return pltpu.make_async_remote_copy(src, dst, send, recv, device_id=device, device_id_type=MESH)

    def target(i):
        return {"core": side, "tensor": 2 * c + i}

    def at_home(i):
        return jnp.logical_and(side == c, 2 * c + i == z)

    def end_copy(i, part):
        return remote(e_send.at[i, part], e_land.at[z % 2, part], end_send.at[i], end_recv.at[z % 2], target(i))

    def end_home(i):
        return pltpu.make_async_copy(e_send.at[i], e_land.at[z % 2], end_sem)

    def oth_copy(p):
        return remote(oth.at[p], got.at[p], oth_send.at[p], oth_recv.at[p], near)

    dy_copy = pltpu.make_async_copy(dy_hbm, e_send, dy_sem)
    x_copy = pltpu.make_async_copy(x_hbm, hb, x_sem)
    y_copy = pltpu.make_async_copy(y_hbm, e_send, y_sem)

    def probs_copy(p):
        return pltpu.make_async_copy(e_hbm.at[p], eb, e_sem)

    def columns(j):
        return pl.ds(pl.multiple_of(j * WIDE, WIDE), WIDE)

    def slot(j):
        return (j // 3) % 2, columns(j % 3)

    def to_core(j):
        r, cols = slot(j)
        return remote(ring.at[r, :, 1 - c, :, :, cols], land_c.at[j], cs_sem.at[j], cr_sem.at[j], near)

    def to_y(j):
        return remote(land_c.at[j, 1 - y], land_y.at[j], ys_sem.at[j], yr_sem.at[j], across)

    def norm_copy(k):
        return remote(land_n.at[2 * k], land_n.at[2 * k + 1], ns_sem.at[k], nr_sem.at[k], (near, across, pair, far)[k])

    def go_right(j, first, src):
        return remote(src, land_r.at[j, pl.ds(first - 1, 4 - first)], rs_sem.at[j], rr_sem.at[j], right)

    def go_left(j, count, src):
        return remote(src, land_l.at[j, pl.ds(0, count)], ls_sem.at[j], lr_sem.at[j], left)

    def stage(i, lag, body):
        @pl.when(jnp.logical_and(i >= lag, i - lag < parts))
        def _():
            body(i - lag)

    def add_cores(group):
        def one(m, carry):
            j = 3 * group + m
            r, cols = slot(j)
            to_core(j).wait()
            land_c[j] = land_c[j] + ring[r, :, c, :, :, cols]
            return carry

        lax.fori_loop(0, 3, one, 0)

    def send_cores(group):
        lax.fori_loop(0, 3, lambda m, t: (to_core(3 * group + m).start(), t)[1], 0)

    def last_hop(j):
        @pl.when(z == 1)
        def _():
            go_left(j, 2, land_l.at[j, pl.ds(0, 2)]).wait_recv()
            land_l[j, 0] = land_l[j, 0] + land_c[j, y, 0]
            go_left(j, 1, land_l.at[j, pl.ds(0, 1)]).start()

        @pl.when(z == 2)
        def _():
            go_right(j, 2, land_r.at[j, pl.ds(1, 2)]).wait_recv()
            land_r[j, 2] = land_r[j, 2] + land_c[j, y, 3]
            go_right(j, 3, land_r.at[j, pl.ds(2, 1)]).start()

    def next_hop(j):
        @pl.when(z == 1)
        def _():
            go_right(j, 1, land_r.at[j]).wait_recv()
            for k in (2, 3):
                land_r[j, k - 1] = land_r[j, k - 1] + land_c[j, y, k]
            go_right(j, 2, land_r.at[j, pl.ds(1, 2)]).start()

        @pl.when(z == 2)
        def _():
            go_left(j, 3, land_l.at[j]).wait_recv()
            for k in (0, 1):
                land_l[j, k] = land_l[j, k] + land_c[j, y, k]
            go_left(j, 2, land_l.at[j, pl.ds(0, 2)]).start()

    def first_hop(j):
        to_y(j).wait_recv()
        land_c[j, y] = land_c[j, y] + land_y[j]

        @pl.when(z == 0)
        def _():
            go_right(j, 1, land_c.at[j, y, pl.ds(1, 3)]).start()

        @pl.when(z == last)
        def _():
            go_left(j, 3, land_c.at[j, y, pl.ds(0, 3)]).start()

    def result(j):
        mine = land_c[j, y, z].astype(F32)

        @pl.when(z == 0)
        def _():
            go_left(j, 1, land_l.at[j, pl.ds(0, 1)]).wait_recv()
            tmp[...] = mine + land_l[j, 0].astype(F32)

        @pl.when(z == 1)
        def _():
            tmp[...] = mine + land_r[j, 0].astype(F32) + land_l[j, 1].astype(F32)

        @pl.when(z == 2)
        def _():
            tmp[...] = mine + land_r[j, 1].astype(F32) + land_l[j, 2].astype(F32)

        @pl.when(z == last)
        def _():
            go_right(j, 3, land_r.at[j, pl.ds(2, 1)]).wait_recv()
            tmp[...] = mine + land_r[j, 2].astype(F32)

        group = j // 3

        @pl.when(j >= early)
        def _():
            first_out[:, columns(j - early)] = tmp[...]

        for m in range(2):

            @pl.when(jnp.logical_and(j < early, j % 3 == m))
            def _():
                pair_out[:, columns(group + m * (early // 3))] = tmp[...]

        @pl.when(jnp.logical_and(j < early, j % 3 == 2))
        def _():
            down_out[columns(group), :] = tmp[...].T

    def round_(i):
        stage(i, 0, lambda j: to_y(j).start())
        stage(i, 6, last_hop)
        stage(i, 4, next_hop)
        stage(i, 2, first_hop)
        stage(i, 8, result)
        for k in range(4):

            @pl.when(i == 3 * k + 8)
            def _():
                norm_copy(k).wait()
                total = land_n[2 * k] + land_n[2 * k + 1]
                if k < 3:
                    land_n[2 * k + 2] = total
                    norm_copy(k + 1).start()
                else:
                    norm_out[...] = total

    @pl.when(step == 0)
    def _():
        dy_copy.start()
        greet(near)
        greet(across)
        greet(far)

        @pl.when(z < last)
        def _():
            greet(right)

        @pl.when(z > 0)
        def _():
            greet(left)

        for i in range(2):

            @pl.when(jnp.logical_not(at_home(i)))
            def _():
                greet(target(i))

        count = 5 + jnp.where(z < last, 1, 0) + jnp.where(z > 0, 1, 0) - jnp.where(side == c, 1, 0)
        pl.semaphore_wait(barrier, count)
        dy_copy.wait()
        dy = e_send[...].reshape(rows, width).astype(F32)
        n = n2_ref[...].astype(F32)
        land_n[0] = jnp.zeros(land_n.shape[1:], F32)
        land_n[0, 1:2] = jnp.sum(dy * n, axis=0, keepdims=True)
        land_n[0, 3:4] = jnp.sum(dy, axis=0, keepdims=True)
        dr2 = norm_back(dy * gain_ref[1:2], n, i2_ref[:, :1])
        acc[...] = dr2
        df[...] = dr2.astype(BF)
        hb[...] = (n1_ref[...].astype(F32) * gain_ref[0:1] + bias_ref[0:1]).astype(BF)

    @pl.when(step < FIRST_PAIR)
    def _():
        gate = gu_ref[0, 0].astype(F32)
        up = gu_ref[0, 1].astype(F32)
        s = 1.0 / (1.0 + jnp.exp(-gate))
        silu = gate * s
        wg, wu, wd = unit_weights(lambda t, m: wa_ref[:, t, :, 128 * m : 128 * m + 128].reshape(width, 128))
        place = step % 2

        def put(m, grad):
            for t in range(4):
                ring[place, :, :, t, :, 128 * m : 128 * m + 128] = (
                    grad[:, 128 * t : 128 * t + 128].astype(BF).reshape(2, 2, -1, 128)
                )

        put(2, dg(df[...], (silu * up).astype(BF), TN))
        d_act = dg(df[...], wd, NN)
        d_gate = (d_act * up * (s * (1.0 + gate * (1.0 - s)))).astype(BF)
        d_up = (d_act * silu).astype(BF)
        put(0, dg(hb[...], d_gate, TN))
        put(1, dg(hb[...], d_up, TN))
        send_cores(step)
        acc[...] += dg(d_gate, wg, NT) + dg(d_up, wu, NT)

    @pl.when(step == FIRST_PAIR - 1)
    def _():
        dh = acc[...]
        n = n1_ref[...].astype(F32)
        land_n[0, 0:1] = jnp.sum(dh * n, axis=0, keepdims=True)
        land_n[0, 2:3] = jnp.sum(dh, axis=0, keepdims=True)
        dr1 = norm_back(dh * gain_ref[0:1], n, i1_ref[:, :1])
        acc[...] = dr1
        df[...] = dr1.astype(BF)
        x_copy.start()
        probs_copy(0).start()
        norm_copy(0).start()

    cos, sin = cos_ref[:, pl.ds(c * rows, rows)], sin_ref[:, pl.ds(c * rows, rows)]
    in_pairs = jnp.logical_and(step >= FIRST_PAIR, step < FIRST_JOINT)
    p = step - FIRST_PAIR

    @pl.when(jnp.logical_and(in_pairs, p % 3 == 0))
    def _():
        w = jnp.concatenate(out_weight(wb_ref.at[:, pl.ds(2 * (p // 3), 2), :, 128:384]), axis=1)
        t = dg(df[...], w, NN).astype(BF)
        for i in range(3):
            do3[i] = t[:, 128 * i : 128 * i + 128]
        o3 = jnp.concatenate([o_ref[p + i] for i in range(3)], axis=1)
        dwo[p // 3] = dg(df[...], o3, TN).astype(BF)

    @pl.when(in_pairs)
    def _():
        probs_copy(p).wait()
        dqt, dk, dv = pair_back(
            do3[p % 3], o_ref[p], q_ref[0], k_ref[0], v_ref[0], ko_ref[0], vo_ref[0],
            [eb.at[h] for h in range(2)], [l_ref[0, h, 0:1] for h in range(2)], cos, sin,
        )
        dq[p] = dqt.T.astype(BF)
        keep[p, 0] = dk[:, :rows].astype(BF)
        keep[p, 1] = dv[:, :rows].astype(BF)
        oth[p, 0] = dk[:, rows:].astype(BF)
        oth[p, 1] = dv[:, rows:].astype(BF)
        oth_copy(p).start()

        @pl.when(p + 1 < PAIRS)
        def _():
            probs_copy(p + 1).start()

    @pl.when(step >= FIRST_JOINT)
    def _():
        half = step - FIRST_JOINT

        @pl.when(half == 0)
        def _():
            x_copy.wait()

        for i in range(3):
            oth_copy(3 * half + i).wait()
        d = joint_parts(
            [dq[3 * half + i].astype(F32) for i in range(3)],
            [keep[3 * half + i, 0].astype(F32) + got[3 * half + i, 0].astype(F32) for i in range(3)],
            [keep[3 * half + i, 1].astype(F32) + got[3 * half + i, 1].astype(F32) for i in range(3)],
            cos, sin,
        )
        total = None
        wlow = low_lanes((width, 128))
        mid = dwo[half, :, 128:256].astype(F32)
        sides = [dwo[half, :, 0:128], dwo[half, :, 256:384]]
        mids = [swap64(mid), mid]
        shape = (2, 2, width // 4)
        for e in range(2):
            t = 2 * half + e
            w = jnp.concatenate([wa_ref[:, t].reshape(width, GROUP), wb_ref[:, t, :, :256].reshape(width, 256)], axis=1)
            part = dg(d[e], w, NT)
            total = part if total is None else total + part
            g = dg(hb[...], d[e], TN)
            ring[0, :, :, t] = g[:, :GROUP].astype(BF).reshape(shape + (GROUP,))
            ring[1, :, :, t, :, :128] = g[:, GROUP:512].astype(BF).reshape(shape + (128,))
            ring[1, :, :, t, :, 128:256] = jnp.where(wlow, g[:, 512:], mids[e]).astype(BF).reshape(shape + (128,))
            ring[1, :, :, t, :, 256:] = sides[e].reshape(shape + (128,))
        acc[...] += total

    @pl.when(step == LAST_STEP)
    def _():
        for k in range(2):
            send_cores(early // 3 + k)

        @pl.when(section == 0)
        def _():
            e_send[...] = acc[...].astype(BF).reshape(e_send.shape)

        @pl.when(section == 1)
        def _():
            y_copy.start()
            y_copy.wait()

        for i in range(2):

            @pl.when(at_home(i))
            def _():
                end_home(i).start()

    @pl.when(step < FIRST_PAIR)
    def _():
        add_cores(step)

    @pl.when(step == 0)
    def _():
        round_(0)

    round_(step + 1)

    @pl.when(step == LAST_STEP)
    def _():
        for k in range(2):
            add_cores(early // 3 + k)
        end_rows = e_send.shape[1] // 8

        def late(i, carry):
            part = pl.ds(pl.multiple_of((i - LAST_STEP - 2) * end_rows, end_rows), end_rows)
            for k in range(2):

                @pl.when(jnp.logical_not(at_home(k)))
                def _():
                    end_copy(k, part).start()

            round_(i)
            return carry

        lax.fori_loop(LAST_STEP + 2, LAST_STEP + 10, late, 0)
        lax.fori_loop(LAST_STEP + 10, parts + 8, lambda i, t: (round_(i), t)[1], 0)
        for i in range(2):

            @pl.when(at_home(i))
            def _():
                end_home(i).wait()

            @pl.when(jnp.logical_not(at_home(i)))
            def _():
                end_copy(i, pl.ds(0, e_send.shape[1])).wait_send()
                remote(e_send.at[i], e_land.at[i], end_send.at[i], end_recv.at[i], target(i)).wait_recv()

        ends_out[...] = e_land[...]

        def finish(j, carry):
            to_y(j).wait_send()

            @pl.when(z == 0)
            def _():
                go_right(j, 1, land_c.at[j, y, pl.ds(1, 3)]).wait_send()

            @pl.when(z == 1)
            def _():
                go_right(j, 2, land_r.at[j, pl.ds(1, 2)]).wait_send()
                go_left(j, 1, land_l.at[j, pl.ds(0, 1)]).wait_send()

            @pl.when(z == 2)
            def _():
                go_right(j, 3, land_r.at[j, pl.ds(2, 1)]).wait_send()
                go_left(j, 2, land_l.at[j, pl.ds(0, 2)]).wait_send()

            @pl.when(z == last)
            def _():
                go_left(j, 3, land_c.at[j, y, pl.ds(0, 3)]).wait_send()

            return carry

        lax.fori_loop(0, parts, finish, 0)


def last_back(x, y, dy, kept, w, norms, cost, sint):
    q, k, v, ko, vo, o, e, l, gu, n1, i1, n2, i2 = kept
    gains, biases = norms
    rows, width = x.shape
    heads = width // 128
    depth, columns = w.shape[2:]
    parts = columns // WIDE
    units = (columns - width) // 3
    dma = pltpu.SemaphoreType.DMA
    hbm = pl.BlockSpec(memory_space=pl.ANY)
    halves = (2, rows // 2, width)

    def once(shape, at=None):
        return pl.BlockSpec(shape, lambda i: at or (0,) * len(shape), pipeline_mode=pl.Buffered(1))

    def by_pair(shape):
        return pl.BlockSpec(shape, lambda i: (jnp.clip(i - FIRST_PAIR, 0, PAIRS - 1),) + (0,) * (len(shape) - 1))

    pair = by_pair((1, rows, 128))
    group = (4, 4, depth, GROUP)
    return pl.pallas_call(
        functools.partial(last_kernel, parts),
        grid=(LAST_STEP + 1,),
        in_specs=[
            once((rows, width)), once((rows, 128)), once((rows, width)), once((rows, 128)),
            pl.BlockSpec((1, 2, rows, 512), lambda i: (jnp.minimum(i, FIRST_PAIR - 1), 0, 0, 0)),
            pl.BlockSpec(group, lambda i: (0, 0, 0, jnp.where(i < FIRST_PAIR, 2 + i, 0))),
            once(group, (0, 0, 0, 1)),
            once((2, width)), once((2, width)),
            once((heads, rows, 128)),
            pair, pair, pair, pair, pair,
            by_pair((1, 2, 8, rows)),
            once(cost.shape), once(sint.shape),
            hbm, hbm, hbm, hbm,
        ],
        out_specs=[once((depth, width)), once((depth, 2 * units)), once((units, depth)), once(halves), once((8, width))],
        out_shape=[
            sds((depth, width), F32), sds((depth, 2 * units), F32), sds((units, depth), F32),
            sds(halves, BF), sds((8, width), F32),
        ],
        scratch_shapes=[
            VM((rows, width), F32),
            VM((rows, width), BF),
            VM((rows, width), BF),
            VM((2, 2, 2, 4, depth, GROUP), BF),
            VM((3, rows, 128), BF),
            VM((2, width, 384), BF),
            VM((heads, rows, 128), BF),
            VM((heads, 2, 128, rows), BF),
            VM((heads, 2, 128, rows), BF),
            VM((heads, 2, 128, rows), BF),
            VM((2, 2 * rows, rows), BF),
            VM(halves, BF),
            VM(halves, BF),
            VM((depth, WIDE), F32),
            VM((parts, 2, 4, depth, WIDE), BF),
            VM((parts, 4, depth, WIDE), BF),
            VM((parts, 3, depth, WIDE), BF),
            VM((parts, 3, depth, WIDE), BF),
            VM((8, 8, width), F32),
            dma, dma, dma, dma,
            dma((6,)), dma((6,)), dma, dma((2,)), dma((2,)),
        ]
        + [dma((parts,))] * 8
        + [dma((4,))] * 2,
        compiler_params=pltpu.CompilerParams(collective_id=0, has_side_effects=True, vmem_limit_bytes=63 << 20),
        name="last",
    )(n1, i1, n2, i2, gu, w, w, gains, biases, o, q, k, v, ko, vo, l, cost, sint, dy.reshape(halves), x, y.reshape(halves), e)


LAG = 6


def first_kernel(
    parts, tok_ref, shard_ref, extra_ref, len_ref, cos_ref, sin_ref, cost_ref, sint_ref,
    w_out, q_out, k_out, v_out, ko_out, vo_out, y_out, e_out, o_out, gu_out, n1_out, n2_out,
    x_out, dy_out, l_out, i1_out, i2_out, norm_out,
    w, xin, q, kv, land_kv, late_kv, o, hb, acc, relay, land_rows, ext, lens,
    mask, eb, gu, n1, n2, df, do3, dq, keep, oth, got, d,
    tok_sem, tok_send, tok_recv, shard_sem, back_sem, kv_send, kv_recv, out_sem, row_send, row_recv,
    e_sem, gu_sem, oth_send, oth_recv, dz_send, dz_recv,
    small_send, small_recv, rs_sem, rr_sem, ls_sem, lr_sem, ys_sem, yr_sem, cs_sem, cr_sem,
):
    section = lax.axis_index("section")
    y, c, z = lax.axis_index("y"), lax.axis_index("core"), lax.axis_index("tensor")
    last = 3
    rows, width = xin.shape[0] * xin.shape[1], xin.shape[2]
    near, across, other = {"core": 1 - c}, {"y": 1 - y}, {"section": 1 - section}
    right, left = {"tensor": jnp.minimum(z + 1, last)}, {"tensor": jnp.maximum(z - 1, 0)}
    side = z // 2
    barrier = pltpu.get_barrier_semaphore()

    def greet(device):
        pl.semaphore_signal(barrier, inc=1, device_id=device, device_id_type=MESH)

    def remote(src, dst, send, recv, device):
        return pltpu.make_async_remote_copy(src, dst, send, recv, device_id=device, device_id_type=MESH)

    def target(i):
        return {"core": side, "tensor": 2 * c + i}

    def at_home(i):
        return jnp.logical_and(side == c, 2 * c + i == z)

    def token_copy(i, part):
        return remote(tok_ref.at[i, part], xin.at[z % 2, part], tok_send.at[i], tok_recv.at[z % 2], target(i))

    def token_home(i):
        return pltpu.make_async_copy(tok_ref.at[i], xin.at[z % 2], tok_sem)

    load = pltpu.make_async_copy(shard_ref, w.at[y, c, z], shard_sem)
    load.start()
    greet(near)
    greet(across)
    greet(other)

    @pl.when(z < last)
    def _():
        greet(right)

    @pl.when(z > 0)
    def _():
        greet(left)

    for i in range(2):

        @pl.when(jnp.logical_not(at_home(i)))
        def _():
            greet(target(i))

    count = 5 + jnp.where(z < last, 1, 0) + jnp.where(z > 0, 1, 0) - jnp.where(side == c, 1, 0)
    pl.semaphore_wait(barrier, count)

    ext[y, c] = extra_ref[...]
    lens[c] = len_ref[...]

    def small(k):
        if k == 0:
            return remote(lens.at[c], lens.at[c], small_send.at[0], small_recv.at[0], near)
        if k == 1:
            return remote(ext.at[y, c], ext.at[y, c], small_send.at[1], small_recv.at[1], across)
        return remote(ext.at[:, c], ext.at[:, c], small_send.at[2], small_recv.at[2], near)

    small(0).start()
    small(1).start()
    load.wait()

    def columns(j):
        return pl.ds(pl.multiple_of(j * WIDE, WIDE), WIDE)

    def go_right(j, h):
        b = jnp.maximum(z - h, 0)
        return remote(w.at[y, c, b, :, columns(j)], w.at[y, c, b, :, columns(j)], rs_sem.at[j, h], rr_sem.at[j, h], right)

    def go_left(j, h):
        b = jnp.minimum(z + h, last)
        return remote(w.at[y, c, b, :, columns(j)], w.at[y, c, b, :, columns(j)], ls_sem.at[j, h], lr_sem.at[j, h], left)

    def to_y(j):
        return remote(w.at[y, c, :, :, columns(j)], w.at[y, c, :, :, columns(j)], ys_sem.at[j], yr_sem.at[j], across)

    def block_to_y(j, b):
        return remote(w.at[y, c, b, :, columns(j)], w.at[y, c, b, :, columns(j)], ys_sem.at[j], yr_sem.at[j], across)

    def to_core(j):
        return remote(w.at[:, c, :, :, columns(j)], w.at[:, c, :, :, columns(j)], cs_sem.at[j], cr_sem.at[j], near)

    def write_back(j):
        return pltpu.make_async_copy(w.at[:, :, :, :, columns(j)], w_out.at[:, :, :, :, columns(j)], back_sem.at[j])

    def stage(r, lag, body):
        @pl.when(jnp.logical_and(r >= lag, r - lag < parts))
        def _():
            body(r - lag)

    def send_own(j):
        @pl.when(z < last)
        def _():
            go_right(j, 0).start()

        @pl.when(z > 0)
        def _():
            go_left(j, 0).start()

        block_to_y(j, z).start()

    def hop(h, j):
        @pl.when(z >= h)
        def _():
            go_right(j, h - 1).wait_recv()
            block_to_y(j, z - h).start()

        @pl.when(z + h <= last)
        def _():
            go_left(j, h - 1).wait_recv()
            block_to_y(j, z + h).start()

        if h < last:

            @pl.when(jnp.logical_and(z >= h, z < last))
            def _():
                go_right(j, h).start()

            @pl.when(jnp.logical_and(z + h <= last, z > 0))
            def _():
                go_left(j, h).start()

    def over_core(j):
        to_y(j).wait_recv()
        to_core(j).start()

    def complete(j):
        to_core(j).wait_recv()
        write_back(j).start()

    def round_(r):
        stage(r, 0, send_own)
        stage(r, 1, functools.partial(hop, 1))
        stage(r, 2, functools.partial(hop, 2))
        stage(r, 3, functools.partial(hop, 3))
        stage(r, 5, over_core)
        stage(r, LAG, complete)

    def rounds(first, end):
        lax.fori_loop(first, end, lambda r, t: (round_(r), t)[1], 0)

    lead_parts = width // WIDE
    start = 17
    token_rows = xin.shape[1] // 16
    for i in range(2):

        @pl.when(at_home(i))
        def _():
            token_home(i).start()

    def early(r, carry):
        round_(r)
        part = pl.ds(pl.multiple_of(r * token_rows, token_rows), token_rows)
        for i in range(2):

            @pl.when(jnp.logical_not(at_home(i)))
            def _():
                token_copy(i, part).start()

        return carry

    lax.fori_loop(0, 3, early, 0)
    small(0).wait()
    small(1).wait()
    small(2).start()

    mine = jnp.where(side == 0, lens[0], lens[1])
    mine = jnp.where(z % 2 == 0, mine[0:1], mine[1:2])
    at_q = c * rows + lax.broadcasted_iota(jnp.int32, (1, rows), 1)
    at_k = lax.broadcasted_iota(jnp.int32, (2 * rows, 1), 0)
    at_k = jnp.where(at_k < rows, c * rows + at_k, (1 - c) * rows + at_k - rows)
    seg_q, seg_k = jnp.zeros((1, rows), jnp.int32), jnp.zeros((2 * rows, 1), jnp.int32)
    end = jnp.zeros((1, 1), jnp.int32)
    for n in range(8):
        end = end + mine[:, n : n + 1]
        seg_q = seg_q + jnp.where(end <= at_q, 1, 0)
        seg_k = seg_k + jnp.where(end <= at_k, 1, 0)
    mask[...] = jnp.where(seg_k == seg_q, 0.0, neg_fill).astype(F32)
    lax.fori_loop(3, 16, early, 0)
    rounds(16, start)

    small(2).wait()
    halves = [ext[i // 2, i % 2].astype(F32) for i in range(4)]
    for k in range(2):
        for half in range(2):
            pieces = [halves[2 * half + i][3 * k + m : 3 * k + m + 1] for i in range(2) for m in range(3)]
            norm_out[2 * k + half : 2 * k + half + 1] = jnp.concatenate(pieces, axis=1)

    for i in range(2):

        @pl.when(at_home(i))
        def _():
            token_home(i).wait()

        @pl.when(jnp.logical_not(at_home(i)))
        def _():
            token_copy(i, pl.ds(0, xin.shape[1])).wait_send()
            remote(tok_ref.at[i], xin.at[i], tok_send.at[i], tok_recv.at[i], target(i)).wait_recv()

    def project(at, count, x):
        here = pl.ds(at, count)
        cos, sin = cos_ref[pl.ds(c * rows + at, count)], sin_ref[pl.ds(c * rows + at, count)]
        low = low_lanes((count, 128))
        for p in range(2):
            r = [dg(x, w[:, :, 2 * p + e, :, :640].reshape(width, 640), NN) for e in range(2)]
            t = [[v[:, 128 * i : 128 * i + 128] for i in range(5)] for v in r]
            qs = [t[0][0], jnp.where(low, t[0][3], swap64(t[1][3])), t[1][0]]
            ks = [t[0][1], jnp.where(low, swap64(t[0][3]), t[1][3]), t[1][1]]
            vs = [t[0][2], jnp.where(low, t[0][4], swap64(t[1][4])), t[1][2]]
            for i in range(3):
                q[3 * p + i, here] = (rope_fwd(qs[i], cos, sin) * HD**-0.5).astype(BF)
                kv[0, 3 * p + i, here] = rope_fwd(ks[i], cos, sin).astype(BF)
                kv[1, 3 * p + i, here] = vs[i].astype(BF)

    x = xin[...].reshape(rows, width)
    x_out[...] = x
    project(0, rows, x)
    low = low_lanes((rows, 128))
    share = remote(kv, land_kv, kv_send.at[0], kv_recv.at[0], near)
    share.start()
    rounds(start, start + 1)
    share.wait()

    def heads_of(p, others, save):
        k = jnp.concatenate([kv[0, p], others[0, p]], axis=0)
        v = jnp.concatenate([kv[1, p], others[1, p]], axis=0)
        vt = v.astype(F32).T.astype(BF)
        ones = jnp.ones((16, 2 * rows), BF)
        outs = []
        for h in range(2):
            qm = jnp.where(low if h == 0 else jnp.logical_not(low), q[p], jnp.zeros((rows, 128), BF))
            s = dg(k, qm, NT) + mask[...]
            e = jnp.exp(s - jnp.max(s, axis=0, keepdims=True)).astype(BF)
            t = dg(jnp.concatenate([vt[HD * h : HD * h + HD], ones], axis=0), e, NN)
            inv = 1.0 / t[HD : HD + 1]
            save(h, e, inv)
            outs.append(t[:HD] * inv)
        o[p] = jnp.concatenate(outs, axis=0).T.astype(BF)

    def pair(p, carry):
        heads_of(p, land_kv, lambda h, e, inv: None)
        round_(start + 1 + p)
        return carry

    def out_part(p):
        wo = []
        for e in range(2):
            wo.append([w[:, :, 2 * p + e, :, 512 + 128 * i : 640 + 128 * i].reshape(width, 128) for i in range(2)])
        mid = jnp.where(low_lanes((width, 128)), swap64(wo[0][0].astype(F32)), wo[1][0].astype(F32)).astype(BF)
        return jnp.concatenate([wo[0][1], mid, wo[1][1]], axis=1)

    def mix(x):
        r = x.astype(F32)
        for p in range(2):
            r = r + dg(jnp.concatenate([o[3 * p + i] for i in range(3)], axis=1), out_part(p), NT)
        return norm_parts(r)

    def group_of(k):
        return unit_weights(
            lambda t, m: w[:, :, t, :, pl.ds(pl.multiple_of(width + GROUP * k + 128 * m, 128), 128)].reshape(width, 128)
        )

    def unit(k, save):
        wg, wu, wd = group_of(k)
        gate = dg(hb[...], wg, NN)
        up = dg(hb[...], wu, NN)
        save(gate, up)
        act = (gate / (1.0 + jnp.exp(-gate)) * up).astype(BF)
        acc[...] += dg(act, wd, NT)

    lax.fori_loop(0, 6, pair, 0)
    n, inv = mix(x)
    h = n * norm_out[0:1] + norm_out[2:3]
    hb[...] = h.astype(BF)
    acc[...] = h
    rounds(start + 7, start + 8)

    def units(k, carry):
        @pl.when(k != 4)
        def _():
            round_(start + 8 + k - k // 5)

        unit(k, lambda gate, up: None)
        return carry

    lax.fori_loop(0, 6, units, 0)
    pieces = relay.shape[0]
    piece_rows = rows // pieces

    def row_copy(b):
        return remote(relay.at[b], land_rows.at[b], row_send.at[b], row_recv.at[b], other)

    kept_out = []

    def keep_out(src, dst):
        copy = pltpu.make_async_copy(src, dst, out_sem.at[len(kept_out)])
        kept_out.append(copy)
        copy.start()

    @pl.when(section == 0)
    def _():
        def send_rows(b, carry):
            part = pl.ds(pl.multiple_of(b * piece_rows, piece_rows), piece_rows)
            n, inv = norm_parts(acc[part])
            relay[b] = (n * norm_out[1:2] + norm_out[3:4]).astype(BF)
            row_copy(b).start()
            return carry

        lax.fori_loop(0, pieces, send_rows, 0)
        same = pltpu.make_async_copy(land_kv, late_kv, kv_send.at[1])
        same.start()
        same.wait()

    @pl.when(section == 1)
    def _():
        def project_rows(b, carry):
            at = pl.multiple_of(b * piece_rows, piece_rows)
            row_copy(b).wait_recv()
            x_out[pl.ds(at, piece_rows)] = land_rows[b]
            project(at, piece_rows, land_rows[b])
            return carry

        lax.fori_loop(0, pieces, project_rows, 0)
        again = remote(kv, late_kv, kv_send.at[1], kv_recv.at[1], near)
        again.start()
        again.wait()

    for src, dst in ((q, q_out), (kv.at[0], k_out), (kv.at[1], v_out), (late_kv.at[0], ko_out), (late_kv.at[1], vo_out)):
        keep_out(src, dst)

    def probs_out(p):
        return pltpu.make_async_copy(eb.at[p % 2], e_out.at[p], e_sem.at[p % 2])

    def probs_in(p):
        return pltpu.make_async_copy(e_out.at[p], eb.at[p % 2], e_sem.at[p % 2])

    def pair_kept(p, carry):
        @pl.when(p >= 2)
        def _():
            probs_out(p - 2).wait()

        def save(h, e, inv):
            eb[p % 2, h] = e
            l_out[p, h] = jnp.broadcast_to(inv, l_out.shape[2:])

        heads_of(p, late_kv, save)
        probs_out(p).start()
        return carry

    lax.fori_loop(0, PAIRS, pair_kept, 0)
    keep_out(o, o_out)
    n, inv = mix(x_out[...])
    n1[...] = n.astype(BF)
    i1_out[...] = jnp.broadcast_to(inv, i1_out.shape)
    keep_out(n1, n1_out)
    h = n * norm_out[0:1] + norm_out[2:3]
    hb[...] = h.astype(BF)
    acc[...] = h

    def units_out(k):
        return pltpu.make_async_copy(gu.at[k % 2], gu_out.at[k], gu_sem.at[k % 2])

    def units_in(k):
        return pltpu.make_async_copy(gu_out.at[k], gu.at[k % 2], gu_sem.at[k % 2])

    def unit_kept(k, carry):
        @pl.when(k >= 2)
        def _():
            units_out(k - 2).wait()

        def save(gate, up):
            gu[k % 2, 0] = gate.astype(BF)
            gu[k % 2, 1] = up.astype(BF)

        unit(k, save)
        units_out(k).start()
        return carry

    lax.fori_loop(0, 6, unit_kept, 0)
    n, inv = norm_parts(acc[...])
    n2[...] = n.astype(BF)
    i2_out[...] = jnp.broadcast_to(inv, i2_out.shape)
    keep_out(n2, n2_out)
    hb[...] = (n * norm_out[1:2] + norm_out[3:4]).astype(BF)
    keep_out(hb, y_out)
    for p in (PAIRS - 2, PAIRS - 1):
        probs_out(p).wait()
        units_out(p).wait()

    def dz_copy(b):
        return remote(relay.at[b], land_rows.at[b], dz_send.at[b], dz_recv.at[b], other)

    def oth_copy(p):
        return remote(oth.at[p], got.at[p], oth_send.at[p], oth_recv.at[p], near)

    @pl.when(section == 1)
    def _():
        dr2 = norm_back(xin[...].reshape(rows, width).astype(F32) * norm_out[1:2], n, inv)
        acc[...] = dr2
        df[...] = dr2.astype(BF)
        for p in range(2):
            probs_in(p).start()
            units_in(p).start()

        def unit_back(k, carry):
            wg, wu, wd = group_of(k)
            units_in(k).wait()
            gate = gu[k % 2, 0].astype(F32)
            up = gu[k % 2, 1].astype(F32)
            s = 1.0 / (1.0 + jnp.exp(-gate))
            d_act = dg(df[...], wd, NN)
            d_gate = (d_act * up * (s * (1.0 + gate * (1.0 - s)))).astype(BF)
            d_up = (d_act * (gate * s)).astype(BF)
            acc[...] += dg(d_gate, wg, NT) + dg(d_up, wu, NT)

            @pl.when(k + 2 < 6)
            def _():
                units_in(k + 2).start()

            return carry

        lax.fori_loop(0, 6, unit_back, 0)
        dr1 = norm_back(acc[...] * norm_out[0:1], n1[...].astype(F32), i1_out[:, :1])
        acc[...] = dr1
        df[...] = dr1.astype(BF)
        cost, sint = cost_ref[:, pl.ds(c * rows, rows)], sint_ref[:, pl.ds(c * rows, rows)]

        def pair_of(p, carry):
            probs_in(p).wait()
            dqt, dk, dv = pair_back(
                do3[p % 3], o[p], q[p], kv[0, p], kv[1, p], late_kv[0, p], late_kv[1, p],
                [eb.at[p % 2, h] for h in range(2)], [l_out[p, h, 0:1] for h in range(2)], cost, sint,
            )

            @pl.when(p + 2 < PAIRS)
            def _():
                probs_in(p + 2).start()

            dq[p] = dqt.T.astype(BF)
            keep[p, 0] = dk[:, :rows].astype(BF)
            keep[p, 1] = dv[:, :rows].astype(BF)
            oth[p, 0] = dk[:, rows:].astype(BF)
            oth[p, 1] = dv[:, rows:].astype(BF)
            oth_copy(p).start()
            return carry

        def joint(half):
            def total(i, m):
                return keep[i, m].astype(F32) + got[i, m].astype(F32)

            three = range(3 * half, 3 * half + 3)
            for i in three:
                oth_copy(i).wait()
            parts = joint_parts(
                [dq[i].astype(F32) for i in three], [total(i, 0) for i in three], [total(i, 1) for i in three], cost, sint
            )
            for e in range(2):
                d[2 * half + e] = parts[e]

        for half in range(2):
            t = dg(df[...], out_part(half), NN).astype(BF)
            for i in range(3):
                do3[i] = t[:, 128 * i : 128 * i + 128]
            lax.fori_loop(3 * half, 3 * half + 3, pair_of, 0)
        for half in range(2):
            joint(half)

        def send_back(b, carry):
            part = pl.ds(pl.multiple_of(b * piece_rows, piece_rows), piece_rows)
            total = acc[part]
            for t in range(4):
                total += dg(d[t, part], w[:, :, t, :, :640].reshape(width, 640), NT)
            relay[b] = total.astype(BF)
            dz_copy(b).start()
            return carry

        lax.fori_loop(0, pieces, send_back, 0)
        dy_out[...] = xin[...].reshape(rows, width)
        lax.fori_loop(0, pieces, lambda b, t: (dz_copy(b).wait_send(), t)[1], 0)

    @pl.when(section == 0)
    def _():
        lax.fori_loop(0, pieces, lambda b, t: (row_copy(b).wait_send(), t)[1], 0)
        lax.fori_loop(0, pieces, lambda b, t: (dz_copy(b).wait_recv(), t)[1], 0)
        dy_out[...] = land_rows[...].reshape(rows, width)

    for copy in kept_out:
        copy.wait()

    def finish(j, carry):
        write_back(j).wait()
        to_y(j).wait_send()
        to_core(j).wait_send()
        for h in range(last):

            @pl.when(jnp.logical_and(z >= h, z < last))
            def _():
                go_right(j, h).wait_send()

            @pl.when(jnp.logical_and(z + h <= last, z > 0))
            def _():
                go_left(j, h).wait_send()

        return carry

    lax.fori_loop(0, parts, finish, 0)


def first_layer(tokens, shard, extra, lengths, cos, sin, cost, sint):
    micro, own, width = tokens.shape
    depth, columns = shard.shape
    rows = 2 * own
    parts = columns // WIDE
    heads = width // 128
    dma = pltpu.SemaphoreType.DMA
    hbm = pl.BlockSpec(memory_space=pl.ANY)
    vm = pl.BlockSpec(memory_space=VM)
    return pl.pallas_call(
        functools.partial(first_kernel, parts),
        in_specs=[hbm, hbm] + [vm] * 6,
        out_specs=[hbm] * 12 + [vm] * 6,
        out_shape=[sds((2, 2, 4, depth, columns), BF)]
        + [sds((heads, rows, 128), BF)] * 5
        + [
            sds((rows, width), BF),
            sds((heads, 2, 2 * rows, rows), BF),
            sds((heads, rows, 128), BF),
            sds((6, 2, rows, 512), BF),
            sds((rows, width), BF),
            sds((rows, width), BF),
            sds((rows, width), BF),
            sds((rows, width), BF),
            sds((heads, 2, 8, rows), F32),
            sds((rows, 128), F32),
            sds((rows, 128), F32),
            sds((4, width), F32),
        ],
        scratch_shapes=[
            VM((2, 2, 4, depth, columns), BF),
            VM((2, own, width), BF),
            VM((heads, rows, 128), BF),
            VM((2, heads, rows, 128), BF),
            VM((2, heads, rows, 128), BF),
            VM((2, heads, rows, 128), BF),
            VM((heads, rows, 128), BF),
            VM((rows, width), BF),
            VM((rows, width), F32),
            VM((4, rows // 4, width), BF),
            VM((4, rows // 4, width), BF),
            VM((2, 2) + extra.shape, BF),
            VM((2,) + lengths.shape, jnp.int32),
            VM((2 * rows, rows), F32),
            VM((2, 2, 2 * rows, rows), BF),
            VM((2, 2, rows, 512), BF),
            VM((rows, width), BF),
            VM((rows, width), BF),
            VM((rows, width), BF),
            VM((3, rows, 128), BF),
            VM((heads, rows, 128), BF),
            VM((heads, 2, 128, rows), BF),
            VM((heads, 2, 128, rows), BF),
            VM((heads, 2, 128, rows), BF),
            VM((4, rows, 640), BF),
            dma, dma((2,)), dma((2,)), dma, dma((parts,)), dma((2,)), dma((2,)), dma((9,)), dma((4,)), dma((4,)),
            dma((2,)), dma((2,)), dma((6,)), dma((6,)), dma((4,)), dma((4,)),
            dma((3,)), dma((3,)),
            dma((parts, 3)), dma((parts, 3)), dma((parts, 3)), dma((parts, 3)),
            dma((parts,)), dma((parts,)), dma((parts,)), dma((parts,)),
        ],
        compiler_params=pltpu.CompilerParams(collective_id=1, has_side_effects=True, vmem_limit_bytes=63 << 20),
        name="first",
    )(tokens, shard, extra, lengths, cos, sin, cost, sint)


def swap_pairs(tp, step, dp_axes):
    pairs = []
    half = tp // 2
    for core in range(2):
        for at in range(tp):
            source = core * tp + at
            target = (at // half) * tp + half * core + (at + step) % half
            pairs.append((source, target))
    return pairs


def to_sequences(rows, tp):
    half = tp // 2
    at = lax.axis_index("tensor")
    pieces = [None] * half
    got = []
    for step in range(half):
        piece = lax.dynamic_index_in_dim(rows, (at + step) % half, 0, keepdims=False)
        got.append(lax.ppermute(piece, ("core", "tensor"), swap_pairs(tp, step, None)))
    stacked = jnp.stack(got)
    order = (at - jnp.arange(half)) % half
    return jnp.take(stacked, order, axis=0).reshape(-1, rows.shape[-1])


def to_positions(rows, tp):
    half = tp // 2
    at = lax.axis_index("tensor")
    parts = rows.reshape(half, -1, rows.shape[-1])
    got = []
    for step in range(half):
        piece = lax.dynamic_index_in_dim(parts, (at - step) % half, 0, keepdims=False)
        back = [(target, source) for source, target in swap_pairs(tp, step, None)]
        got.append(lax.ppermute(piece, ("core", "tensor"), back))
    stacked = jnp.stack(got)
    order = (at + jnp.arange(half)) % half
    return jnp.take(stacked, (jnp.arange(half) - at) % half, axis=0)


def rope_tables(positions):
    halfway = HD // 2
    freqs = 1000.0 ** (-jnp.arange(halfway, dtype=F32) / halfway)
    angles = positions.astype(F32)[:, None] * freqs[None, :]
    cos, sin = jnp.cos(angles), jnp.sin(angles)
    wide = jnp.concatenate([cos] * 4, axis=1)
    signed = jnp.concatenate([-sin, sin] * 2, axis=1)
    return wide, signed, cos.T, sin.T


def pack_shard(w_qkv, w_out, w_gate_up, w_down):
    rows = w_qkv.shape[0]
    odd = lax.axis_index("tensor") % 2 == 1
    heads = w_qkv.reshape(rows, 3, 3, HD)
    mine = w_out.T.reshape(rows, 3, HD)
    heads = jnp.where(odd, jnp.roll(heads, -1, axis=2), heads)
    mine = jnp.where(odd, jnp.roll(mine, -1, axis=1), mine)
    first = jnp.concatenate(
        [heads[:, :, :2].reshape(rows, -1), heads[:, :, 2].reshape(rows, -1), mine[:, 2], mine[:, :2].reshape(rows, -1)], axis=1
    )
    units = jnp.concatenate([w_gate_up, w_down.T[:, None]], axis=1)
    units = units.reshape(rows, 3, -1, 128).transpose(0, 2, 1, 3)
    return jnp.concatenate([first, units.reshape(rows, -1)], axis=1)


def unpack_first(first):
    rows = first.shape[0]
    odd = lax.axis_index("tensor") % 2 == 1
    both = first[:, :384].reshape(rows, 3, 2, HD)
    single = first[:, 384:576].reshape(rows, 3, 1, HD)
    heads = jnp.concatenate([both, single], axis=2)
    mine = jnp.concatenate([first[:, 640:].reshape(rows, 2, HD), first[:, 576:640].reshape(rows, 1, HD)], axis=1)
    heads = jnp.where(odd, jnp.roll(heads, 1, axis=2), heads)
    mine = jnp.where(odd, jnp.roll(mine, 1, axis=1), mine)
    return heads.reshape(rows, 3, -1), mine.reshape(rows, -1).T


def host_tables(length):
    halfway = HD // 2
    freqs = np.float32(1000.0) ** (-np.arange(halfway, dtype=np.float32) / np.float32(halfway))
    angles = np.arange(length, dtype=np.float32)[:, None] * freqs[None, :]
    cos, sin = np.cos(angles), np.sin(angles)
    return np.concatenate([cos] * 4, axis=1), np.concatenate([-sin, sin] * 2, axis=1), cos.T.copy(), sin.T.copy()


BLOCKS = 4


def gather_shard(shard, dp, tp):
    rows, columns = shard.shape
    got = lax.all_gather(shard, ALL, axis=0, tiled=False)
    got = got.reshape(BLOCKS, dp // BLOCKS, tp, rows, columns)
    return got.transpose(0, 2, 1, 3, 4).reshape(BLOCKS, tp, -1, columns)


def scatter_sum(whole, dp, tp):
    columns = whole.shape[3]
    parts = whole.reshape(BLOCKS, tp, dp // BLOCKS, -1, columns).transpose(0, 2, 1, 3, 4)
    parts = parts.reshape(dp * tp, -1, columns)
    return lax.psum_scatter(parts, ALL, scatter_dimension=0, tiled=False).astype(F32)


def on_device(dp, tp, tokens, cotangent, lengths, w_qkv, w_out, w_gate_up, w_down, norm_gains, norm_biases):
    section = lax.axis_index("section")
    core = lax.axis_index("core")
    at = lax.axis_index("tensor")
    micro, own, width = tokens.shape
    assert micro * 2 == tp
    length = own * tp
    rows = length // 2
    shard = pack_shard(w_qkv[0], w_out[0], w_gate_up[0], w_down[0])
    if dp == 4 and tp == 4:
        extra = jnp.concatenate([norm_gains.reshape(-1, 128), norm_biases.reshape(-1, 128)])
        extra = jnp.pad(extra, ((0, 16 - extra.shape[0]), (0, 0)))
        padded = jnp.pad(lengths, ((0, 8 - lengths.shape[0]), (0, 128 - lengths.shape[1])))
        wide, signed, cost, sint = host_tables(length)
        rows_in = jnp.where(section == 0, tokens, cotangent)
        (
            weights, q, k, v, ko, vo, y, e, o, gu, n1, n2, inputs, dy, l, i1, i2, small,
        ) = first_layer(rows_in, shard, extra, padded, wide, signed, cost, sint)
        weights = weights.reshape((BLOCKS,) + weights.shape[2:])
        norms = (small[:2], small[2:])
        kept = (q, k, v, ko, vo, o, e, l, gu, n1, i1, n2, i2)
        first, pair, down, ends, total = last_back(inputs, y, dy, kept, weights, norms, cost, sint)
        small = lax.dynamic_slice_in_dim(total[:4].reshape(2, dp * tp, -1), lax.axis_index(ALL), 1, 1)
        gains, biases = small[0, 0], small[1, 0]
    else:
        near = core * rows + jnp.arange(rows, dtype=jnp.int32)
        far = (1 - core) * rows + jnp.arange(rows, dtype=jnp.int32)
        tabs = rope_tables(near)
        weights = gather_shard(shard, dp, tp)
        norms = jnp.concatenate([norm_gains, norm_biases])
        norms = lax.all_gather(norms, ("y", "core"), axis=1, tiled=True).astype(F32)
        norms = (norms[0].reshape(2, width), norms[1].reshape(2, width))
        grad_top = to_sequences(cotangent, tp)
        tokens = to_sequences(tokens, tp)
        chip_lengths = lax.all_gather(lengths, "core", axis=0, tiled=True)
        my_lengths = lax.dynamic_index_in_dim(chip_lengths, at, 0, keepdims=False)
        ends_at = jnp.cumsum(my_lengths)

        def segment(positions):
            return jnp.sum((ends_at[None, :] <= positions[:, None]).astype(jnp.int32), axis=-1)

        seg_near = segment(near)
        seg_all = jnp.concatenate([seg_near, segment(far)])
        mask = jnp.where(seg_all[:, None] == seg_near[None, :], 0.0, neg_fill).astype(F32)
        y, unused = forward(tokens, weights, norms, mask, tabs)
        received = lax.ppermute(y, "section", [(0, 1)])
        inputs = jnp.where(section == 0, tokens, received)
        y, kept = forward(inputs, weights, norms, mask, tabs)
        dr1, da = ffn_backward(grad_top, kept, weights, norms, False)
        unused, dz = attn_backward(inputs, da, dr1, None, kept, weights, tabs)
        received = lax.ppermute(dz, "section", [(1, 0)])
        dy = jnp.where(section == 0, received, grad_top)
        g, dr1, da, ng = ffn_backward(dy, kept, weights, norms, True)
        g, dz = attn_backward(inputs, da, dr1, g, kept, weights, tabs)
        ends = to_positions(jnp.where(section == 0, dz.astype(BF), y), tp)
        mine = scatter_sum(g, dp, tp)
        first = mine[:, :width]
        units = mine[:, width:].reshape(first.shape[0], -1, 3, 128).transpose(0, 2, 1, 3).reshape(first.shape[0], 3, -1)
        pair, down = units[:, :2], units[:, 2].T
        gains = lax.psum_scatter(ng[0:2].reshape(-1), ALL, scatter_dimension=0, tiled=True)
        biases = lax.psum_scatter(ng[2:4].reshape(-1), ALL, scatter_dimension=0, tiled=True)
    joint, mix = unpack_first(first)
    outs = (joint, mix, pair.reshape(pair.shape[0], 2, -1), down, gains, biases)
    return (ends[None],) + tuple(t[None] for t in outs)


def solution(mesh):
    sections, dp, tp = mesh.devices.shape
    fine = Mesh(mesh.devices.reshape(sections, dp // 2, 2, tp), ("section", "y", "core", "tensor"))
    both = ("y", "core")
    in_specs = (
        P(both, "tensor", None),
        P(both, "tensor", None),
        P(both, None),
        P("section", both, None, "tensor"),
        P("section", "tensor", both),
        P("section", both, None, "tensor"),
        P("section", "tensor", both),
        P("section", both),
        P("section", both),
    )
    out_specs = (
        P("section", both, "tensor", None),
        P("section", both, None, "tensor"),
        P("section", "tensor", both),
        P("section", both, None, "tensor"),
        P("section", "tensor", both),
        P("section", ALL),
        P("section", ALL),
    )
    return jax.shard_map(
        functools.partial(on_device, dp, tp), mesh=fine, in_specs=in_specs, out_specs=out_specs, check_vma=False
    )
```

```python
import functools

import jax
import jax.numpy as jnp
import numpy as np
from jax import lax
from jax.experimental import pallas as pl
from jax.experimental.pallas import tpu as pltpu
from jax.sharding import Mesh, PartitionSpec as P

HD = 64
eps = 1e-05
neg_fill = -1e30
ALL = ("y", "core", "tensor")
BF = jnp.bfloat16
F32 = jnp.float32
MESH = pl.DeviceIdType.MESH


def dg(a, b, dims):
    return lax.dot_general(a, b, (dims, ((), ())), preferred_element_type=F32)


NN = ((1,), (0,))
NT = ((1,), (1,))
TN = ((0,), (0,))


def low_lanes(shape):
    return lax.broadcasted_iota(jnp.int32, shape, 1) < HD


def swap64(v):
    return pltpu.roll(v, HD, axis=1)


def rope_fwd(t, cos, sin):
    lane = lax.broadcasted_iota(jnp.int32, t.shape, 1) % HD
    other = jnp.where(lane < HD // 2, pltpu.roll(t, 128 - HD // 2, axis=1), pltpu.roll(t, HD // 2, axis=1))
    return t * cos + other * sin


def qkv_kernel(x_ref, w_ref, cos_ref, sin_ref, q_ref, k_ref, v_ref):
    x = x_ref[...]
    width = x.shape[1]
    r = [dg(x, w_ref[:, e, :, :640].reshape(width, 640), NN) for e in range(2)]
    c = [[t[:, 128 * i : 128 * i + 128] for i in range(5)] for t in r]
    low = low_lanes(c[0][0].shape)
    qs = [c[0][0], jnp.where(low, c[0][3], swap64(c[1][3])), c[1][0]]
    ks = [c[0][1], jnp.where(low, swap64(c[0][3]), c[1][3]), c[1][1]]
    vs = [c[0][2], jnp.where(low, c[0][4], swap64(c[1][4])), c[1][2]]
    cos, sin = cos_ref[...], sin_ref[...]
    for i in range(3):
        q_ref[i] = (rope_fwd(qs[i], cos, sin) * HD**-0.5).astype(BF)
        k_ref[i] = rope_fwd(ks[i], cos, sin).astype(BF)
        v_ref[i] = vs[i].astype(BF)


def attn_kernel(q_ref, k_ref, v_ref, ko_ref, vo_ref, m_ref, o_ref, e_ref, l_ref):
    q = q_ref[0]
    k = jnp.concatenate([k_ref[0], ko_ref[0]], axis=0)
    v = jnp.concatenate([v_ref[0], vo_ref[0]], axis=0)
    vt = v.astype(F32).T.astype(BF)
    outs = []
    for h in range(2):
        low = low_lanes(q.shape)
        qm = jnp.where(low if h == 0 else jnp.logical_not(low), q, jnp.zeros_like(q))
        s = dg(k, qm, NT) + m_ref[...]
        e = jnp.exp(s - jnp.max(s, axis=0, keepdims=True))
        inv = 1.0 / jnp.sum(e, axis=0, keepdims=True)
        eb = e.astype(BF)
        e_ref[0, h] = eb
        l_ref[0, h] = jnp.broadcast_to(inv, l_ref.shape[2:])
        outs.append(dg(vt[HD * h : HD * h + HD], eb, NN) * inv)
    o_ref[0] = jnp.concatenate(outs, axis=0).T.astype(BF)


def norm_parts(r):
    center = r - jnp.mean(r, axis=-1, keepdims=True)
    inv = lax.rsqrt(jnp.mean(center * center, axis=-1, keepdims=True) + eps)
    return center * inv, inv


def norm_back(dn, n, inv):
    return inv * (dn - jnp.mean(dn, axis=-1, keepdims=True) - n * jnp.mean(dn * n, axis=-1, keepdims=True))


def out_weight(w_ref):
    c = [[w_ref[:, e, :, 128 * i : 128 * i + 128].reshape(-1, 128) for i in range(2)] for e in range(2)]
    low = low_lanes(c[0][0].shape)
    mid = jnp.where(low, swap64(c[0][0].astype(F32)), c[1][0].astype(F32)).astype(BF)
    return [c[0][1], mid, c[1][1]]


GROUP = 384
WIDE = 128


def unit_weights(load):
    return [jnp.concatenate([load(t, m) for t in range(4)], axis=1) for m in range(3)]


def ffn_kernel(x_ref, o_ref, wo_ref, w_ref, g_ref, b_ref, y_ref, gu_ref, n1_ref, i1_ref, n2_ref, i2_ref, h_ref, hb_ref, acc_ref):
    z = pl.program_id(0)
    width = x_ref.shape[1]

    @pl.when(z == 0)
    def _():
        r = x_ref[...].astype(F32)
        for p in range(2):
            w = jnp.concatenate(out_weight(wo_ref.at[:, 2 * p : 2 * p + 2]), axis=1)
            o = jnp.concatenate([o_ref[3 * p + i] for i in range(3)], axis=1)
            r = r + dg(o, w, NT)
        n, inv = norm_parts(r)
        n1_ref[...] = n.astype(BF)
        i1_ref[...] = jnp.broadcast_to(inv, i1_ref.shape)
        h = n * g_ref[0:1] + b_ref[0:1]
        h_ref[...] = h
        hb_ref[...] = h.astype(BF)

    hb = hb_ref[...]
    wd, wg, wu = unit_weights(lambda t, m: w_ref[:, t, :, 128 * m : 128 * m + 128].reshape(width, 128))
    gate = dg(hb, wg, NN)
    up = dg(hb, wu, NN)
    gu_ref[0, 0] = gate.astype(BF)
    gu_ref[0, 1] = up.astype(BF)
    act = (gate / (1.0 + jnp.exp(-gate)) * up).astype(BF)
    part = dg(act, wd, NT)

    @pl.when(z == 0)
    def _():
        acc_ref[...] = h_ref[...] + part

    @pl.when(z > 0)
    def _():
        acc_ref[...] += part

    @pl.when(z == pl.num_programs(0) - 1)
    def _():
        n, inv = norm_parts(acc_ref[...])
        n2_ref[...] = n.astype(BF)
        i2_ref[...] = jnp.broadcast_to(inv, i2_ref.shape)
        y_ref[...] = (n * g_ref[1:2] + b_ref[1:2]).astype(BF)


def ffn_back_kernel(grads, dy_ref, n1_ref, i1_ref, n2_ref, i2_ref, gu_ref, w_ref, g_ref, b_ref, *refs):
    if grads:
        g_out, dr1_ref, da_ref, ng_ref, hb_ref, df_ref, acc_ref = refs
    else:
        dr1_ref, da_ref, df_ref, acc_ref = refs
    z = pl.program_id(0)
    width = dy_ref.shape[1]

    @pl.when(z == 0)
    def _():
        dy = dy_ref[...].astype(F32)
        n = n2_ref[...].astype(F32)
        if grads:
            ng_ref[1:2] = jnp.sum(dy * n, axis=0, keepdims=True)
            ng_ref[3:4] = jnp.sum(dy, axis=0, keepdims=True)
            hb_ref[...] = (n1_ref[...].astype(F32) * g_ref[0:1] + b_ref[0:1]).astype(BF)
        dr2 = norm_back(dy * g_ref[1:2], n, i2_ref[:, :1])
        acc_ref[...] = dr2
        df_ref[...] = dr2.astype(BF)

    df = df_ref[...]
    gate = gu_ref[0, 0].astype(F32)
    up = gu_ref[0, 1].astype(F32)
    s = 1.0 / (1.0 + jnp.exp(-gate))
    silu = gate * s
    wd, wg, wu = unit_weights(lambda t, m: w_ref[:, t, :, 128 * m : 128 * m + 128].reshape(width, 128))

    def keep(m, grad):
        for t in range(g_out.shape[1]):
            g_out[:, t, :, 128 * m : 128 * m + 128] = grad[:, 128 * t : 128 * t + 128].astype(BF).reshape(g_out.shape[0], -1, 128)

    if grads:
        keep(0, dg(df, (silu * up).astype(BF), TN))
    d_act = dg(df, wd, NN)
    d_gate = (d_act * up * (s * (1.0 + gate * (1.0 - s)))).astype(BF)
    d_up = (d_act * silu).astype(BF)
    if grads:
        hb = hb_ref[...]
        keep(1, dg(hb, d_gate, TN))
        keep(2, dg(hb, d_up, TN))
    acc_ref[...] += dg(d_gate, wg, NT) + dg(d_up, wu, NT)

    @pl.when(z == pl.num_programs(0) - 1)
    def _():
        dh = acc_ref[...]
        n = n1_ref[...].astype(F32)
        if grads:
            ng_ref[0:1] = jnp.sum(dh * n, axis=0, keepdims=True)
            ng_ref[2:3] = jnp.sum(dh, axis=0, keepdims=True)
        dr1 = norm_back(dh * g_ref[0:1], n, i1_ref[:, :1])
        dr1_ref[...] = dr1
        da_ref[...] = dr1.astype(BF)


def pair_back(do, o, q, k, v, ko, vo, e, l, cos, sin):
    dot = do.astype(F32).T
    ot = o.astype(F32).T
    k = jnp.concatenate([k, ko], axis=0)
    v = jnp.concatenate([v, vo], axis=0)
    kt = k.astype(F32).T.astype(BF)
    qt = q.astype(F32).T.astype(BF)
    dqs, dks, dvs = [], [], []
    for h in range(2):
        span = slice(HD * h, HD * h + HD)
        scaled = dot[span] * l[h]
        inner = jnp.sum(scaled * ot[span], axis=0, keepdims=True)
        sb = scaled.astype(BF)
        zero = jnp.zeros_like(sb)
        padded = jnp.concatenate([sb, zero] if h == 0 else [zero, sb], axis=0)
        dp = dg(v, padded, NN)
        et = e[h][...]
        ds = (et.astype(F32) * (dp - inner)).astype(BF)
        dvs.append(dg(sb, et, NT))
        dks.append(dg(qt[span], ds, NT))
        dqt = dg(kt[span], ds, NN) * HD**-0.5
        d1, d2 = dqt[: HD // 2], dqt[HD // 2 :]
        dqs.append(d1 * cos + d2 * sin)
        dqs.append(d2 * cos - d1 * sin)
    return [jnp.concatenate(t, axis=0) for t in (dqs, dks, dvs)]


def joint_parts(dq, dkt, dvt, cos, sin):
    dk = []
    for t in dkt:
        parts = []
        for h in range(2):
            d1 = t[HD * h : HD * h + HD // 2]
            d2 = t[HD * h + HD // 2 : HD * h + HD]
            parts += [d1 * cos + d2 * sin, d2 * cos - d1 * sin]
        dk.append(jnp.concatenate(parts, axis=0).T)
    dv = [t.T for t in dvt]
    low = low_lanes(dq[0].shape)
    zero = jnp.zeros_like(dv[1])
    d = [
        [dq[0], dk[0], dv[0], jnp.where(low, dq[1], swap64(dk[1])), jnp.where(low, dv[1], zero)],
        [dq[2], dk[2], dv[2], jnp.where(low, swap64(dq[1]), dk[1]), jnp.where(low, swap64(dv[1]), zero)],
    ]
    return [jnp.concatenate(t, axis=1).astype(BF) for t in d]


def attn_back_kernel(grads, da_ref, wo_ref, o_ref, q_ref, k_ref, v_ref, ko_ref, vo_ref, e_ref, l_ref, cos_ref, sin_ref, dq_ref, own_ref, oth_ref, *dwo_ref):
    da = da_ref[...]
    rows = da.shape[0]
    w = jnp.concatenate(out_weight(wo_ref), axis=1)
    do3 = dg(da, w, NN).astype(BF)
    if grads:
        o3 = jnp.concatenate([o_ref[i] for i in range(3)], axis=1)
        dwo_ref[0][0] = dg(da, o3, TN).astype(BF)
    cos, sin = cos_ref[...], sin_ref[...]
    for i in range(3):
        dqt, dk, dv = pair_back(
            do3[:, 128 * i : 128 * i + 128], o_ref[i], q_ref[i], k_ref[i], v_ref[i], ko_ref[i], vo_ref[i],
            [e_ref[i, h] for h in range(2)], [l_ref[i, h, 0:1] for h in range(2)], cos, sin,
        )
        dq_ref[i] = dqt.T.astype(BF)
        own_ref[i, 0] = dk[:, :rows]
        own_ref[i, 1] = dv[:, :rows]
        oth_ref[i, 0] = dk[:, rows:].astype(BF)
        oth_ref[i, 1] = dv[:, rows:].astype(BF)


def joint_back_kernel(grads, *refs):
    if grads:
        old_ref, x_ref, w_ref, dr1_ref, dq_ref, own_ref, got_ref, dwo_ref, cos_ref, sin_ref, g_ref, dz_ref = refs
    else:
        w_ref, dr1_ref, dq_ref, own_ref, got_ref, cos_ref, sin_ref, dz_ref, dzb_ref = refs
    p = pl.program_id(0)
    width = dr1_ref.shape[1]
    d = joint_parts(
        [dq_ref[i].astype(F32) for i in range(3)],
        [own_ref[i, 0] + got_ref[i, 0].astype(F32) for i in range(3)],
        [own_ref[i, 1] + got_ref[i, 1].astype(F32) for i in range(3)],
        cos_ref[...],
        sin_ref[...],
    )
    acc = None
    for e in range(2):
        t = dg(d[e], w_ref[:, e, :, :640].reshape(width, 640), NT)
        acc = t if acc is None else acc + t
    if grads:
        x = x_ref[...]
        wlow = low_lanes((width, 128))
        mid = dwo_ref[0, :, 128:256].astype(F32)
        sides = [dwo_ref[0, :, 0:128], dwo_ref[0, :, 256:384]]
        mids = [swap64(mid), mid]
        for e in range(2):
            g = dg(x, d[e], TN)
            blocks = g_ref.shape[0]
            g_ref[:, e, :, :512] = g[:, :512].astype(BF).reshape(blocks, -1, 512)
            g_ref[:, e, :, 512:640] = jnp.where(wlow, g[:, 512:], mids[e]).astype(BF).reshape(blocks, -1, 128)
            g_ref[:, e, :, 640:] = sides[e].reshape(blocks, -1, 128)

    @pl.when(p == 0)
    def _():
        dz_ref[...] = dr1_ref[...] + acc

    @pl.when(p > 0)
    def _():
        total = dz_ref[...] + acc
        dz_ref[...] = total
        if not grads:
            dzb_ref[...] = total.astype(BF)


BIG = pltpu.CompilerParams(vmem_limit_bytes=58 << 20)
VM = pltpu.VMEM


def full(shape):
    return pl.BlockSpec(shape, lambda i: (0,) * len(shape))


def lead(shape, at=0):
    return pl.BlockSpec(shape, lambda i: tuple(i if j == at else 0 for j in range(len(shape))))


def joint_block(w):
    return pl.BlockSpec((w.shape[0], 2, w.shape[2], 768), lambda i: (0, i, 0, 0))


def group_block(w):
    return pl.BlockSpec((w.shape[0], w.shape[1], w.shape[2], GROUP), lambda i: (0, 0, 0, 2 + i))


def sds(shape, kind):
    return jax.ShapeDtypeStruct(shape, kind)


def forward(x, weights, norms, mask, tabs):
    w = weights
    rows, width = x.shape
    heads = width // 128
    blocks, tp, depth, columns = w.shape
    steps = tp // 2
    cos, sin, cost, sint = tabs
    q, k, v = pl.pallas_call(
        qkv_kernel,
        grid=(steps,),
        in_specs=[full((rows, width)), joint_block(w), full((rows, 128)), full((rows, 128))],
        out_specs=[lead((3, rows, 128))] * 3,
        out_shape=[sds((heads, rows, 128), BF)] * 3,
        compiler_params=BIG,
        name="qkv",
    )(x, w, cos, sin)
    ko, vo = lax.ppermute((k, v), "core", [(0, 1), (1, 0)])
    return attend(x, (q, k, v, ko, vo), w, norms, mask)


def attend(x, joint, w, norms, mask):
    gains, biases = norms
    q, k, v, ko, vo = joint
    rows, width = x.shape
    heads = width // 128
    blocks, tp, depth, columns = w.shape
    pair = lead((1, rows, 128))
    o, e, l = pl.pallas_call(
        attn_kernel,
        grid=(heads,),
        in_specs=[pair] * 5 + [full((2 * rows, rows))],
        out_specs=[pair, lead((1, 2, 2 * rows, rows)), lead((1, 2, 8, rows))],
        out_shape=[sds((heads, rows, 128), BF), sds((heads, 2, 2 * rows, rows), BF), sds((heads, 2, 8, rows), F32)],
        compiler_params=BIG,
        name="attn",
    )(q, k, v, ko, vo, mask)
    groups = (columns - width) // GROUP
    units = tp * 128
    y, gu, n1, i1, n2, i2 = pl.pallas_call(
        ffn_kernel,
        grid=(groups,),
        in_specs=[
            full((rows, width)),
            full((heads, rows, 128)),
            pl.BlockSpec((blocks, tp, depth, 256), lambda i: (0, 0, 0, 2)),
            group_block(w),
            full((2, width)),
            full((2, width)),
        ],
        out_specs=[full((rows, width)), lead((1, 2, rows, units))] + [full((rows, width)), full((rows, 128))] * 2,
        out_shape=[sds((rows, width), BF), sds((groups, 2, rows, units), BF)] + [sds((rows, width), BF), sds((rows, 128), F32)] * 2,
        scratch_shapes=[VM((rows, width), F32), VM((rows, width), BF), VM((rows, width), F32)],
        compiler_params=BIG,
        name="ffn",
    )(x, o, w, w, gains, biases)
    return y, (q, k, v, ko, vo, o, e, l, gu, n1, i1, n2, i2)


def ffn_backward(dy, kept, w, norms, grads):
    gains, biases = norms
    gu, n1, i1, n2, i2 = kept[8:]
    rows, width = dy.shape
    blocks, tp, depth, columns = w.shape
    groups = (columns - width) // GROUP
    whole, stat = full((rows, width)), full((rows, 128))
    outs = [whole, whole]
    shapes = [sds((rows, width), F32), sds((rows, width), BF)]
    scratch = [VM((rows, width), BF), VM((rows, width), F32)]
    if grads:
        outs = [group_block(w)] + outs + [full((8, width))]
        shapes = [sds(w.shape, BF)] + shapes + [sds((8, width), F32)]
        scratch = [VM((rows, width), BF)] + scratch
    return pl.pallas_call(
        functools.partial(ffn_back_kernel, grads),
        grid=(groups,),
        in_specs=[
            whole, whole, stat, whole, stat,
            lead((1, 2, rows, tp * 128)),
            group_block(w),
            full((2, width)), full((2, width)),
        ],
        out_specs=outs,
        out_shape=shapes,
        scratch_shapes=scratch,
        compiler_params=BIG,
        name="ffn_back" if grads else "ffn_back_light",
    )(dy, n1, i1, n2, i2, gu, w, gains, biases)


def attn_backward(x, da, dr1, g, kept, w, tabs):
    grads = g is not None
    q, k, v, ko, vo, o, e, l = kept[:8]
    rows, width = da.shape
    heads = width // 128
    blocks, tp, depth, columns = w.shape
    steps = tp // 2
    cos, sin, cost, sint = tabs
    whole = full((rows, width))
    three = lead((3, rows, 128))
    side = lead((3, 2, 128, rows))
    table = full((HD // 2, rows))
    extra = [lead((1, width, 384))] if grads else []
    dq, own, oth, *dwo = pl.pallas_call(
        functools.partial(attn_back_kernel, grads),
        grid=(steps,),
        in_specs=[
            whole,
            pl.BlockSpec((blocks, 2, depth, 256), lambda i: (0, i, 0, 2)),
            three, three, three, three, three, three,
            lead((3, 2, 2 * rows, rows)),
            lead((3, 2, 8, rows)),
            table, table,
        ],
        out_specs=[three, side, side] + extra,
        out_shape=[
            sds((heads, rows, 128), BF),
            sds((heads, 2, 128, rows), F32),
            sds((heads, 2, 128, rows), BF),
        ]
        + ([sds((steps, width, 384), BF)] if grads else []),
        compiler_params=BIG,
        name="attn_back",
    )(da, w, o, q, k, v, ko, vo, e, l, cost, sint)
    got = lax.ppermute(oth, "core", [(0, 1), (1, 0)])
    if grads:
        specs = [pl.BlockSpec(memory_space=pl.ANY), whole, joint_block(w), whole, three, side, side] + extra
        args = (g, x, w, dr1, dq, own, got, *dwo)
        outs, shapes = [joint_block(w), whole], [sds(w.shape, BF), sds((rows, width), F32)]
    else:
        specs = [joint_block(w), whole, three, side, side]
        args = (w, dr1, dq, own, got)
        outs, shapes = [whole, whole], [sds((rows, width), F32), sds((rows, width), BF)]
    return pl.pallas_call(
        functools.partial(joint_back_kernel, grads),
        grid=(steps,),
        in_specs=specs + [table, table],
        out_specs=outs,
        out_shape=shapes,
        input_output_aliases={0: 0} if grads else {},
        compiler_params=BIG,
        name="joint_back",
    )(*args, cost, sint)


PAIRS = 6
FIRST_PAIR = 6
FIRST_JOINT = 12
LAST_STEP = 13


FAR = 2
FAR_AT = 4
def last_kernel(
    parts, n1_ref, i1_ref, n2_ref, i2_ref, gu_ref, wa_ref, gain_ref, bias_ref,
    q_ref, k_ref, v_ref, ko_ref, vo_ref, l_ref, cos_ref, sin_ref, dy_hbm, x_hbm, y_hbm, e_hbm, o_hbm, w_hbm,
    joint_out, mix_out, pair_out, down_out, ends_out, norm_out,
    acc, df, hb, o_ref, wb_ref, ring, do3, dwo, dq, keep, oth, got, eb, e_send, e_land, tmp, land_c, land_y, land_r, land_l, land_n,
    z_sum, far_y, far_r, far_l,
    o_sem, wb_sem, dy_sem, x_sem, y_sem, e_sem, oth_send, oth_recv, end_sem, end_send, end_recv,
    cs_sem, cr_sem, ys_sem, yr_sem, rs_sem, rr_sem, ls_sem, lr_sem, ns_sem, nr_sem,
    fys_sem, fyr_sem, frs_sem, frr_sem, fls_sem, flr_sem,
):
    step = pl.program_id(0)
    section = lax.axis_index("section")
    y, c, z = lax.axis_index("y"), lax.axis_index("core"), lax.axis_index("tensor")
    last = 3
    rows, width = acc.shape
    early = parts - width // WIDE
    usual = parts - FAR
    near, across = {"core": 1 - c}, {"y": 1 - y}
    right, left = {"tensor": jnp.minimum(z + 1, last)}, {"tensor": jnp.maximum(z - 1, 0)}
    pair = {"tensor": z + 1 - 2 * lax.rem(z, 2)}
    far = {"tensor": lax.rem(z + 2, 4)}
    side = z // 2
    barrier = pltpu.get_barrier_semaphore()

    def greet(device):
        pl.semaphore_signal(barrier, inc=1, device_id=device, device_id_type=MESH)

    def remote(src, dst, send, recv, device):
        return pltpu.make_async_remote_copy(src, dst, send, recv, device_id=device, device_id_type=MESH)

    def target(i):
        return {"core": side, "tensor": 2 * c + i}

    def at_home(i):
        return jnp.logical_and(side == c, 2 * c + i == z)

    def end_copy(i, part):
        return remote(e_send.at[i, part], e_land.at[z % 2, part], end_send.at[i], end_recv.at[z % 2], target(i))

    def end_home(i):
        return pltpu.make_async_copy(e_send.at[i], e_land.at[z % 2], end_sem)

    def oth_copy(p):
        return remote(oth.at[p], got.at[p], oth_send.at[p], oth_recv.at[p], near)

    dy_copy = pltpu.make_async_copy(dy_hbm, e_send, dy_sem)
    x_copy = pltpu.make_async_copy(x_hbm, hb, x_sem)
    o_copy = pltpu.make_async_copy(o_hbm, o_ref, o_sem)
    wb_copy = pltpu.make_async_copy(w_hbm.at[:, :, :, pl.ds(GROUP, GROUP)], wb_ref, wb_sem)
    y_copy = pltpu.make_async_copy(y_hbm, e_send, y_sem)

    def probs_copy(p):
        return pltpu.make_async_copy(e_hbm.at[p], eb, e_sem)

    def columns(j):
        return pl.ds(pl.multiple_of(j * WIDE, WIDE), WIDE)

    def slot(j):
        return (j // 3) % 2, columns(j % 3)

    def chunk(j):
        return j + FAR * ((j + usual - FAR_AT) // usual)

    def to_core(j):
        r, cols = slot(j)
        return remote(ring.at[r, :, 1 - c, :, :, cols], land_c.at[j], cs_sem.at[j], cr_sem.at[j], near)

    def to_y(j):
        return remote(land_c.at[chunk(j), 1 - y], land_y.at[j], ys_sem.at[j], yr_sem.at[j], across)

    def norm_copy(k):
        return remote(land_n.at[2 * k], land_n.at[2 * k + 1], ns_sem.at[k], nr_sem.at[k], (near, across, pair, far)[k])

    def go_right(j, first, src):
        return remote(src, land_r.at[j, pl.ds(first - 1, 4 - first)], rs_sem.at[j], rr_sem.at[j], right)

    def go_left(j, count, src):
        return remote(src, land_l.at[j, pl.ds(0, count)], ls_sem.at[j], lr_sem.at[j], left)

    def stage(i, lag, body):
        @pl.when(jnp.logical_and(i >= lag, i - lag < usual))
        def _():
            body(i - lag)

    def add_core(j):
        r, cols = slot(j)
        to_core(j).wait()
        land_c[j] = land_c[j] + ring[r, :, c, :, :, cols]

    def far_right(b, first, src):
        return remote(src, far_r.at[b, :, pl.ds(first - 1, 4 - first)], frs_sem.at[b], frr_sem.at[b], right)

    def far_left(b, count, src):
        return remote(src, far_l.at[b, :, pl.ds(0, count)], fls_sem.at[b], flr_sem.at[b], left)

    def far_across(b):
        return remote(z_sum.at[b, 1 - y], far_y.at[b], fys_sem.at[b], fyr_sem.at[b], across)

    def far_first(b):
        j = FAR_AT + b

        @pl.when(z == 0)
        def _():
            far_right(b, 1, land_c.at[j, :, pl.ds(1, 3)]).start()

        @pl.when(z == last)
        def _():
            far_left(b, 3, land_c.at[j, :, pl.ds(0, 3)]).start()

    def far_next(b):
        j = FAR_AT + b

        @pl.when(z == 1)
        def _():
            far_right(b, 1, far_r.at[b]).wait_recv()
            for k in (2, 3):
                far_r[b, :, k - 1] = far_r[b, :, k - 1] + land_c[j, :, k]
            far_right(b, 2, far_r.at[b, :, pl.ds(1, 2)]).start()

        @pl.when(z == 2)
        def _():
            far_left(b, 3, far_l.at[b]).wait_recv()
            for k in (0, 1):
                far_l[b, :, k] = far_l[b, :, k] + land_c[j, :, k]
            far_left(b, 2, far_l.at[b, :, pl.ds(0, 2)]).start()

    def far_last(b):
        j = FAR_AT + b

        @pl.when(z == 1)
        def _():
            far_left(b, 2, far_l.at[b, :, pl.ds(0, 2)]).wait_recv()
            far_l[b, :, 0] = far_l[b, :, 0] + land_c[j, :, 0]
            far_left(b, 1, far_l.at[b, :, pl.ds(0, 1)]).start()

        @pl.when(z == 2)
        def _():
            far_right(b, 2, far_r.at[b, :, pl.ds(1, 2)]).wait_recv()
            far_r[b, :, 2] = far_r[b, :, 2] + land_c[j, :, 3]
            far_right(b, 3, far_r.at[b, :, pl.ds(2, 1)]).start()

    def far_sum(b):
        mine = land_c[FAR_AT + b, :, z]

        @pl.when(z == 0)
        def _():
            far_left(b, 1, far_l.at[b, :, pl.ds(0, 1)]).wait_recv()
            z_sum[b] = mine + far_l[b, :, 0]

        @pl.when(z == 1)
        def _():
            z_sum[b] = mine + far_r[b, :, 0] + far_l[b, :, 1]

        @pl.when(z == 2)
        def _():
            z_sum[b] = mine + far_r[b, :, 1] + far_l[b, :, 2]

        @pl.when(z == last)
        def _():
            far_right(b, 3, far_r.at[b, :, pl.ds(2, 1)]).wait_recv()
            z_sum[b] = mine + far_r[b, :, 2]

    def far_result(b):
        far_across(b).wait_recv()
        tmp[...] = z_sum[b, y].astype(F32) + far_y[b].astype(F32)
        emit(FAR_AT + b)

    def last_hop(j):
        @pl.when(z == 1)
        def _():
            go_left(j, 2, land_l.at[j, pl.ds(0, 2)]).wait_recv()
            land_l[j, 0] = land_l[j, 0] + land_c[chunk(j), y, 0]
            go_left(j, 1, land_l.at[j, pl.ds(0, 1)]).start()

        @pl.when(z == 2)
        def _():
            go_right(j, 2, land_r.at[j, pl.ds(1, 2)]).wait_recv()
            land_r[j, 2] = land_r[j, 2] + land_c[chunk(j), y, 3]
            go_right(j, 3, land_r.at[j, pl.ds(2, 1)]).start()

    def next_hop(j):
        @pl.when(z == 1)
        def _():
            go_right(j, 1, land_r.at[j]).wait_recv()
            for k in (2, 3):
                land_r[j, k - 1] = land_r[j, k - 1] + land_c[chunk(j), y, k]
            go_right(j, 2, land_r.at[j, pl.ds(1, 2)]).start()

        @pl.when(z == 2)
        def _():
            go_left(j, 3, land_l.at[j]).wait_recv()
            for k in (0, 1):
                land_l[j, k] = land_l[j, k] + land_c[chunk(j), y, k]
            go_left(j, 2, land_l.at[j, pl.ds(0, 2)]).start()

    def first_hop(j):
        to_y(j).wait_recv()
        land_c[chunk(j), y] = land_c[chunk(j), y] + land_y[j]

        @pl.when(z == 0)
        def _():
            go_right(j, 1, land_c.at[chunk(j), y, pl.ds(1, 3)]).start()

        @pl.when(z == last)
        def _():
            go_left(j, 3, land_c.at[chunk(j), y, pl.ds(0, 3)]).start()

    def result(j):
        mine = land_c[chunk(j), y, z].astype(F32)

        @pl.when(z == 0)
        def _():
            go_left(j, 1, land_l.at[j, pl.ds(0, 1)]).wait_recv()
            tmp[...] = mine + land_l[j, 0].astype(F32)

        @pl.when(z == 1)
        def _():
            tmp[...] = mine + land_r[j, 0].astype(F32) + land_l[j, 1].astype(F32)

        @pl.when(z == 2)
        def _():
            tmp[...] = mine + land_r[j, 1].astype(F32) + land_l[j, 2].astype(F32)

        @pl.when(z == last)
        def _():
            go_right(j, 3, land_r.at[j, pl.ds(2, 1)]).wait_recv()
            tmp[...] = mine + land_r[j, 2].astype(F32)

        emit(chunk(j))

    def emit(j):
        group = j // 3

        @pl.when(jnp.logical_and(j < early, j % 3 == 0))
        def _():
            down_out[columns(group), :] = tmp[...].T

        for m in (1, 2):

            @pl.when(jnp.logical_and(j < early, j % 3 == m))
            def _():
                pair_out[:, columns(group + (m - 1) * (early // 3))] = tmp[...]

        for odd in range(2):
            two = slice(HD, 3 * HD) if odd else slice(0, 2 * HD)
            one = slice(0, HD) if odd else slice(2 * HD, 3 * HD)

            def when(n, body, odd=odd):
                pl.when(jnp.logical_and(j == early + n, z % 2 == odd))(body)

            def store(out, place, part):
                def body():
                    out[:, place] = tmp[:, part]

                return body

            whole, low, high = slice(0, 128), slice(0, HD), slice(HD, 128)
            for n in range(3):
                when(n, store(joint_out.at[n], two, whole))
            when(3, store(joint_out.at[0], one, low))
            when(3, store(joint_out.at[1], one, high))
            when(4, store(joint_out.at[2], one, low))
            when(4, store(mix_out, one, high))
            when(5, store(mix_out, two, whole))

    def round_(i):
        stage(i, 0, lambda j: to_y(j).start())
        stage(i, 6, last_hop)
        stage(i, 4, next_hop)
        stage(i, 2, first_hop)
        stage(i, 8, result)
        for b in range(FAR):
            rounds = (4 + 3 * b, 7 + 3 * b, 10 + 3 * b, 13 + 3 * b, usual - 1 + b, usual + 3 + b)
            bodies = (far_first, far_next, far_last, far_sum, lambda b: far_across(b).start(), far_result)
            for at, body in zip(rounds, bodies):
                pl.when(i == at)(functools.partial(body, b))

        for k in range(4):

            @pl.when(i == 3 * k + 8)
            def _():
                norm_copy(k).wait()
                total = land_n[2 * k] + land_n[2 * k + 1]
                if k < 3:
                    land_n[2 * k + 2] = total
                    norm_copy(k + 1).start()
                else:
                    norm_out[...] = total

    @pl.when(step == 0)
    def _():
        dy_copy.start()
        o_copy.start()
        wb_copy.start()
        greet(near)
        greet(across)
        greet(far)

        @pl.when(z < last)
        def _():
            greet(right)

        @pl.when(z > 0)
        def _():
            greet(left)

        for i in range(2):

            @pl.when(jnp.logical_not(at_home(i)))
            def _():
                greet(target(i))

        count = 5 + jnp.where(z < last, 1, 0) + jnp.where(z > 0, 1, 0) - jnp.where(side == c, 1, 0)
        pl.semaphore_wait(barrier, count)
        dy_copy.wait()
        dy = e_send[...].reshape(rows, width).astype(F32)
        n = n2_ref[...].astype(F32)
        land_n[0] = jnp.zeros(land_n.shape[1:], F32)
        land_n[0, 1:2] = jnp.sum(dy * n, axis=0, keepdims=True)
        land_n[0, 3:4] = jnp.sum(dy, axis=0, keepdims=True)
        dr2 = norm_back(dy * gain_ref[1:2], n, i2_ref[:, :1])
        acc[...] = dr2
        df[...] = dr2.astype(BF)
        hb[...] = (n1_ref[...].astype(F32) * gain_ref[0:1] + bias_ref[0:1]).astype(BF)

    @pl.when(step < FIRST_PAIR)
    def _():
        gate = gu_ref[0, 0].astype(F32)
        up = gu_ref[0, 1].astype(F32)
        s = 1.0 / (1.0 + jnp.exp(-gate))
        silu = gate * s
        wd, wg, wu = unit_weights(lambda t, m: wa_ref[:, t, :, 128 * m : 128 * m + 128].reshape(width, 128))
        place = step % 2

        def put(m, grad):
            for t in range(4):
                ring[place, :, :, t, :, 128 * m : 128 * m + 128] = (
                    grad[:, 128 * t : 128 * t + 128].astype(BF).reshape(2, 2, -1, 128)
                )

        j = 3 * step

        def earlier(m):
            pl.when(step > (1 if m == 0 else 0))(lambda: add_core(j - 3 + m))

        put(0, dg(df[...], (silu * up).astype(BF), TN))
        to_core(j).start()
        earlier(0)
        d_act = dg(df[...], wd, NN)
        d_gate = (d_act * up * (s * (1.0 + gate * (1.0 - s)))).astype(BF)
        d_up = (d_act * silu).astype(BF)
        put(1, dg(hb[...], d_gate, TN))
        to_core(j + 1).start()
        earlier(1)

        @pl.when(step == 0)
        def _():
            add_core(0)
            round_(0)

        put(2, dg(hb[...], d_up, TN))
        to_core(j + 2).start()
        earlier(2)
        acc[...] += dg(d_gate, wg, NT) + dg(d_up, wu, NT)

    @pl.when(step == FIRST_PAIR - 1)
    def _():
        dh = acc[...]
        n = n1_ref[...].astype(F32)
        land_n[0, 0:1] = jnp.sum(dh * n, axis=0, keepdims=True)
        land_n[0, 2:3] = jnp.sum(dh, axis=0, keepdims=True)
        dr1 = norm_back(dh * gain_ref[0:1], n, i1_ref[:, :1])
        acc[...] = dr1
        df[...] = dr1.astype(BF)
        x_copy.start()
        probs_copy(0).start()
        norm_copy(0).start()

    cos, sin = cos_ref[:, pl.ds(c * rows, rows)], sin_ref[:, pl.ds(c * rows, rows)]
    in_pairs = jnp.logical_and(step >= FIRST_PAIR, step < FIRST_JOINT)
    p = step - FIRST_PAIR

    @pl.when(step == FIRST_PAIR)
    def _():
        for m in range(3):
            add_core(3 * FIRST_PAIR - 3 + m)
        o_copy.wait()
        wb_copy.wait()

    @pl.when(jnp.logical_and(in_pairs, p % 3 == 0))
    def _():
        w = jnp.concatenate(out_weight(wb_ref.at[:, pl.ds(2 * (p // 3), 2), :, 128:384]), axis=1)
        t = dg(df[...], w, NN).astype(BF)
        for i in range(3):
            do3[i] = t[:, 128 * i : 128 * i + 128]
        o3 = jnp.concatenate([o_ref[p + i] for i in range(3)], axis=1)
        dwo[p // 3] = dg(df[...], o3, TN).astype(BF)

    @pl.when(in_pairs)
    def _():
        probs_copy(p).wait()
        dqt, dk, dv = pair_back(
            do3[p % 3], o_ref[p], q_ref[0], k_ref[0], v_ref[0], ko_ref[0], vo_ref[0],
            [eb.at[h] for h in range(2)], [l_ref[0, h, 0:1] for h in range(2)], cos, sin,
        )
        dq[p] = dqt.T.astype(BF)
        keep[p, 0] = dk[:, :rows].astype(BF)
        keep[p, 1] = dv[:, :rows].astype(BF)
        oth[p, 0] = dk[:, rows:].astype(BF)
        oth[p, 1] = dv[:, rows:].astype(BF)
        oth_copy(p).start()

        @pl.when(p + 1 < PAIRS)
        def _():
            probs_copy(p + 1).start()

    @pl.when(step >= FIRST_JOINT)
    def _():
        half = step - FIRST_JOINT

        @pl.when(half == 0)
        def _():
            x_copy.wait()

        for i in range(3):
            oth_copy(3 * half + i).wait()
        d = joint_parts(
            [dq[3 * half + i].astype(F32) for i in range(3)],
            [keep[3 * half + i, 0].astype(F32) + got[3 * half + i, 0].astype(F32) for i in range(3)],
            [keep[3 * half + i, 1].astype(F32) + got[3 * half + i, 1].astype(F32) for i in range(3)],
            cos, sin,
        )
        total = None
        wlow = low_lanes((width, 128))
        mid = dwo[half, :, 128:256].astype(F32)
        sides = [dwo[half, :, 0:128], dwo[half, :, 256:384]]
        mids = [swap64(mid), mid]
        shape = (2, 2, width // 4)
        for e in range(2):
            t = 2 * half + e
            w = jnp.concatenate([wa_ref[:, t].reshape(width, GROUP), wb_ref[:, t, :, :256].reshape(width, 256)], axis=1)
            part = dg(d[e], w, NT)
            total = part if total is None else total + part
            g = dg(hb[...], d[e], TN)
            ring[0, :, :, t] = g[:, :GROUP].astype(BF).reshape(shape + (GROUP,))
            ring[1, :, :, t, :, :128] = g[:, GROUP:512].astype(BF).reshape(shape + (128,))
            ring[1, :, :, t, :, 128:256] = jnp.where(wlow, g[:, 512:], mids[e]).astype(BF).reshape(shape + (128,))
            ring[1, :, :, t, :, 256:] = sides[e].reshape(shape + (128,))
        acc[...] += total

    @pl.when(step == LAST_STEP)
    def _():
        lax.fori_loop(early, parts, lambda j, t: (to_core(j).start(), t)[1], 0)

        @pl.when(section == 0)
        def _():
            e_send[...] = acc[...].astype(BF).reshape(e_send.shape)

        @pl.when(section == 1)
        def _():
            y_copy.start()
            y_copy.wait()

        for i in range(2):

            @pl.when(at_home(i))
            def _():
                end_home(i).start()

    @pl.when(step == 1)
    def _():
        round_(1)

    @pl.when(step >= 1)
    def _():
        round_(step + 1)

    @pl.when(step == LAST_STEP)
    def _():
        lax.fori_loop(early, parts, lambda j, t: (add_core(j), t)[1], 0)
        end_rows = e_send.shape[1] // 8

        def late(i, carry):
            part = pl.ds(pl.multiple_of((i - LAST_STEP - 2) * end_rows, end_rows), end_rows)
            for k in range(2):

                @pl.when(jnp.logical_not(at_home(k)))
                def _():
                    end_copy(k, part).start()

            round_(i)
            return carry

        lax.fori_loop(LAST_STEP + 2, LAST_STEP + 10, late, 0)
        lax.fori_loop(LAST_STEP + 10, usual + 8, lambda i, t: (round_(i), t)[1], 0)
        for i in range(2):

            @pl.when(at_home(i))
            def _():
                end_home(i).wait()

            @pl.when(jnp.logical_not(at_home(i)))
            def _():
                end_copy(i, pl.ds(0, e_send.shape[1])).wait_send()
                remote(e_send.at[i], e_land.at[i], end_send.at[i], end_recv.at[i], target(i)).wait_recv()

        ends_out[...] = e_land[...]

        def finish(j, carry):
            to_y(j).wait_send()

            @pl.when(z == 0)
            def _():
                go_right(j, 1, land_c.at[chunk(j), y, pl.ds(1, 3)]).wait_send()

            @pl.when(z == 1)
            def _():
                go_right(j, 2, land_r.at[j, pl.ds(1, 2)]).wait_send()
                go_left(j, 1, land_l.at[j, pl.ds(0, 1)]).wait_send()

            @pl.when(z == 2)
            def _():
                go_right(j, 3, land_r.at[j, pl.ds(2, 1)]).wait_send()
                go_left(j, 2, land_l.at[j, pl.ds(0, 2)]).wait_send()

            @pl.when(z == last)
            def _():
                go_left(j, 3, land_c.at[chunk(j), y, pl.ds(0, 3)]).wait_send()

            return carry

        lax.fori_loop(0, usual, finish, 0)

        def finish_far(b, carry):
            j = FAR_AT + b
            far_across(b).wait_send()

            @pl.when(z == 0)
            def _():
                far_right(b, 1, land_c.at[j, :, pl.ds(1, 3)]).wait_send()

            @pl.when(z == 1)
            def _():
                far_right(b, 2, far_r.at[b, :, pl.ds(1, 2)]).wait_send()
                far_left(b, 1, far_l.at[b, :, pl.ds(0, 1)]).wait_send()

            @pl.when(z == 2)
            def _():
                far_right(b, 3, far_r.at[b, :, pl.ds(2, 1)]).wait_send()
                far_left(b, 2, far_l.at[b, :, pl.ds(0, 2)]).wait_send()

            @pl.when(z == last)
            def _():
                far_left(b, 3, land_c.at[j, :, pl.ds(0, 3)]).wait_send()

            return carry

        lax.fori_loop(0, FAR, finish_far, 0)


def last_back(x, y, dy, kept, w, norms, cost, sint):
    q, k, v, ko, vo, o, e, l, gu, n1, i1, n2, i2 = kept
    gains, biases = norms
    rows, width = x.shape
    heads = width // 128
    depth, columns = w.shape[2:]
    parts = columns // WIDE
    units = (columns - width) // 3
    dma = pltpu.SemaphoreType.DMA
    hbm = pl.BlockSpec(memory_space=pl.ANY)
    halves = (2, rows // 2, width)

    def once(shape, at=None):
        return pl.BlockSpec(shape, lambda i: at or (0,) * len(shape), pipeline_mode=pl.Buffered(1))

    def by_pair(shape):
        return pl.BlockSpec(shape, lambda i: (jnp.clip(i - FIRST_PAIR, 0, PAIRS - 1),) + (0,) * (len(shape) - 1))

    pair = by_pair((1, rows, 128))
    group = (4, 4, depth, GROUP)
    return pl.pallas_call(
        functools.partial(last_kernel, parts),
        grid=(LAST_STEP + 1,),
        in_specs=[
            once((rows, width)), once((rows, 128)), once((rows, width)), once((rows, 128)),
            pl.BlockSpec((1, 2, rows, 512), lambda i: (jnp.minimum(i, FIRST_PAIR - 1), 0, 0, 0)),
            pl.BlockSpec(group, lambda i: (0, 0, 0, jnp.where(i < FIRST_PAIR, 2 + i, 0))),
            once((2, width)), once((2, width)),
            pair, pair, pair, pair, pair,
            by_pair((1, 2, 8, rows)),
            once(cost.shape), once(sint.shape),
            hbm, hbm, hbm, hbm, hbm, hbm,
        ],
        out_specs=[
            once((3, depth, depth)), once((depth, depth)), once((depth, 2 * units)), once((units, depth)), once(halves), once((8, width)),
        ],
        out_shape=[
            sds((3, depth, depth), F32), sds((depth, depth), F32), sds((depth, 2 * units), F32), sds((units, depth), F32),
            sds(halves, BF), sds((8, width), F32),
        ],
        scratch_shapes=[
            VM((rows, width), F32),
            VM((rows, width), BF),
            VM((rows, width), BF),
            VM((heads, rows, 128), BF),
            VM(group, BF),
            VM((2, 2, 2, 4, depth, GROUP), BF),
            VM((3, rows, 128), BF),
            VM((2, width, 384), BF),
            VM((heads, rows, 128), BF),
            VM((heads, 2, 128, rows), BF),
            VM((heads, 2, 128, rows), BF),
            VM((heads, 2, 128, rows), BF),
            VM((2, 2 * rows, rows), BF),
            VM(halves, BF),
            VM(halves, BF),
            VM((depth, WIDE), F32),
            VM((parts, 2, 4, depth, WIDE), BF),
            VM((parts - FAR, 4, depth, WIDE), BF),
            VM((parts - FAR, 3, depth, WIDE), BF),
            VM((parts - FAR, 3, depth, WIDE), BF),
            VM((8, 8, width), F32),
            VM((FAR, 2, depth, WIDE), BF),
            VM((FAR, depth, WIDE), BF),
            VM((FAR, 2, 3, depth, WIDE), BF),
            VM((FAR, 2, 3, depth, WIDE), BF),
            dma, dma, dma, dma, dma, dma,
            dma((6,)), dma((6,)), dma, dma((2,)), dma((2,)),
        ]
        + [dma((parts,))] * 8
        + [dma((4,))] * 2
        + [dma((FAR,))] * 6,
        compiler_params=pltpu.CompilerParams(collective_id=0, has_side_effects=True, vmem_limit_bytes=63 << 20),
        name="last",
    )(n1, i1, n2, i2, gu, w, gains, biases, q, k, v, ko, vo, l, cost, sint, dy.reshape(halves), x, y.reshape(halves), e, o, w)


LAG = 6


def first_kernel(
    parts, tok_ref, top_ref, shard_ref, gain_ref, bias_ref, len_ref, cos_ref, sin_ref, cost_ref, sint_ref,
    w_out, q_out, k_out, v_out, ko_out, vo_out, y_out, e_out, o_out, gu_out, n1_out, n2_out,
    x_out, dy_out, l_out, i1_out, i2_out, norm_out,
    w, xin, q, kv, land_kv, late_kv, o, hb, acc, relay, land_rows, ext, lens,
    mask, eb, gu, n1, n2, df, do3, dq, keep, oth, got, d,
    tok_sem, tok_send, tok_recv, shard_sem, back_sem, kv_send, kv_recv, out_sem, row_send, row_recv,
    e_sem, gu_sem, oth_send, oth_recv, dz_send, dz_recv,
    small_send, small_recv, rs_sem, rr_sem, ls_sem, lr_sem, ys_sem, yr_sem, cs_sem, cr_sem,
):
    section = lax.axis_index("section")
    y, c, z = lax.axis_index("y"), lax.axis_index("core"), lax.axis_index("tensor")
    last = 3
    rows, width = xin.shape[0] * xin.shape[1], xin.shape[2]
    near, across, other = {"core": 1 - c}, {"y": 1 - y}, {"section": 1 - section}
    right, left = {"tensor": jnp.minimum(z + 1, last)}, {"tensor": jnp.maximum(z - 1, 0)}
    side = z // 2
    barrier = pltpu.get_barrier_semaphore()

    def greet(device):
        pl.semaphore_signal(barrier, inc=1, device_id=device, device_id_type=MESH)

    def remote(src, dst, send, recv, device):
        return pltpu.make_async_remote_copy(src, dst, send, recv, device_id=device, device_id_type=MESH)

    def target(i):
        return {"core": side, "tensor": 2 * c + i}

    def at_home(i):
        return jnp.logical_and(side == c, 2 * c + i == z)

    def token_copy(src, i, part):
        return remote(src.at[i, part], xin.at[z % 2, part], tok_send.at[i], tok_recv.at[z % 2], target(i))

    def token_home(src, i):
        return pltpu.make_async_copy(src.at[i], xin.at[z % 2], tok_sem)

    def by_section(body):
        for n, src in enumerate((tok_ref, top_ref)):
            pl.when(section == n)(functools.partial(body, src))

    load = pltpu.make_async_copy(shard_ref, w.at[y, c, z], shard_sem)
    load.start()
    greet(near)
    greet(across)
    greet(other)

    @pl.when(z < last)
    def _():
        greet(right)

    @pl.when(z > 0)
    def _():
        greet(left)

    for i in range(2):

        @pl.when(jnp.logical_not(at_home(i)))
        def _():
            greet(target(i))

    count = 5 + jnp.where(z < last, 1, 0) + jnp.where(z > 0, 1, 0) - jnp.where(side == c, 1, 0)
    pl.semaphore_wait(barrier, count)

    ext[y, c, 0:1] = gain_ref[...].astype(F32)
    ext[y, c, 1:2] = bias_ref[...].astype(F32)
    lens[c] = len_ref[...]

    def small(k):
        if k == 0:
            return remote(lens.at[c], lens.at[c], small_send.at[0], small_recv.at[0], near)
        if k == 1:
            return remote(ext.at[y, c], ext.at[y, c], small_send.at[1], small_recv.at[1], across)
        return remote(ext.at[:, c], ext.at[:, c], small_send.at[2], small_recv.at[2], near)

    small(0).start()
    small(1).start()
    load.wait()

    def columns(j):
        return pl.ds(pl.multiple_of(j * WIDE, WIDE), WIDE)

    def go_right(j, h):
        b = jnp.maximum(z - h, 0)
        return remote(w.at[y, c, b, :, columns(j)], w.at[y, c, b, :, columns(j)], rs_sem.at[j, h], rr_sem.at[j, h], right)

    def go_left(j, h):
        b = jnp.minimum(z + h, last)
        return remote(w.at[y, c, b, :, columns(j)], w.at[y, c, b, :, columns(j)], ls_sem.at[j, h], lr_sem.at[j, h], left)

    def to_y(j):
        return remote(w.at[y, c, :, :, columns(j)], w.at[y, c, :, :, columns(j)], ys_sem.at[j], yr_sem.at[j], across)

    def block_to_y(j, b):
        return remote(w.at[y, c, b, :, columns(j)], w.at[y, c, b, :, columns(j)], ys_sem.at[j], yr_sem.at[j], across)

    def to_core(j):
        return remote(w.at[:, c, :, :, columns(j)], w.at[:, c, :, :, columns(j)], cs_sem.at[j], cr_sem.at[j], near)

    def write_back(j):
        return pltpu.make_async_copy(w.at[:, :, :, :, columns(j)], w_out.at[:, :, :, :, columns(j)], back_sem.at[j])

    def stage(r, lag, body):
        @pl.when(jnp.logical_and(r >= lag, r - lag < parts))
        def _():
            body(r - lag)

    def send_own(j):
        @pl.when(z < last)
        def _():
            go_right(j, 0).start()

        @pl.when(z > 0)
        def _():
            go_left(j, 0).start()

        block_to_y(j, z).start()

    def hop(h, j):
        @pl.when(z >= h)
        def _():
            go_right(j, h - 1).wait_recv()
            block_to_y(j, z - h).start()

        @pl.when(z + h <= last)
        def _():
            go_left(j, h - 1).wait_recv()
            block_to_y(j, z + h).start()

        if h < last:

            @pl.when(jnp.logical_and(z >= h, z < last))
            def _():
                go_right(j, h).start()

            @pl.when(jnp.logical_and(z + h <= last, z > 0))
            def _():
                go_left(j, h).start()

    def over_core(j):
        to_y(j).wait_recv()
        to_core(j).start()

    def complete(j):
        to_core(j).wait_recv()
        write_back(j).start()

    def round_(r):
        stage(r, 0, send_own)
        stage(r, 1, functools.partial(hop, 1))
        stage(r, 2, functools.partial(hop, 2))
        stage(r, 3, functools.partial(hop, 3))
        stage(r, 5, over_core)
        stage(r, LAG, complete)

    def rounds(first, end):
        lax.fori_loop(first, end, lambda r, t: (round_(r), t)[1], 0)

    lead_parts = width // WIDE
    start = 17
    token_rows = xin.shape[1] // 16
    for i in range(2):

        @pl.when(at_home(i))
        def _():
            by_section(lambda src: token_home(src, i).start())

    def early(r, carry):
        round_(r)
        part = pl.ds(pl.multiple_of(r * token_rows, token_rows), token_rows)
        for i in range(2):

            @pl.when(jnp.logical_not(at_home(i)))
            def _():
                by_section(lambda src: token_copy(src, i, part).start())

        return carry

    lax.fori_loop(0, 3, early, 0)
    small(0).wait()
    small(1).wait()
    small(2).start()

    mine = jnp.where(side == 0, lens[0], lens[1])
    mine = jnp.where(z % 2 == 0, mine[0:1], mine[1:2])
    at_q = c * rows + lax.broadcasted_iota(jnp.int32, (1, rows), 1)
    at_k = lax.broadcasted_iota(jnp.int32, (2 * rows, 1), 0)
    at_k = jnp.where(at_k < rows, c * rows + at_k, (1 - c) * rows + at_k - rows)
    seg_q, seg_k = jnp.zeros((1, rows), jnp.int32), jnp.zeros((2 * rows, 1), jnp.int32)
    end = jnp.zeros((1, 1), jnp.int32)
    for n in range(8):
        end = end + mine[:, n : n + 1]
        seg_q = seg_q + jnp.where(end <= at_q, 1, 0)
        seg_k = seg_k + jnp.where(end <= at_k, 1, 0)
    mask[...] = jnp.where(seg_k == seg_q, 0.0, neg_fill).astype(F32)
    lax.fori_loop(3, 16, early, 0)
    rounds(16, start)

    small(2).wait()
    for k in range(2):
        for half in range(2):
            norm_out[2 * k + half : 2 * k + half + 1] = jnp.concatenate([ext[half, i, k : k + 1] for i in range(2)], axis=1)

    for i in range(2):

        @pl.when(at_home(i))
        def _():
            token_home(tok_ref, i).wait()

        @pl.when(jnp.logical_not(at_home(i)))
        def _():
            token_copy(tok_ref, i, pl.ds(0, xin.shape[1])).wait_send()
            remote(tok_ref.at[i], xin.at[i], tok_send.at[i], tok_recv.at[i], target(i)).wait_recv()

    def project(at, count, x):
        here = pl.ds(at, count)
        cos, sin = cos_ref[pl.ds(c * rows + at, count)], sin_ref[pl.ds(c * rows + at, count)]
        low = low_lanes((count, 128))
        for p in range(2):
            r = [dg(x, w[:, :, 2 * p + e, :, :640].reshape(width, 640), NN) for e in range(2)]
            t = [[v[:, 128 * i : 128 * i + 128] for i in range(5)] for v in r]
            qs = [t[0][0], jnp.where(low, t[0][3], swap64(t[1][3])), t[1][0]]
            ks = [t[0][1], jnp.where(low, swap64(t[0][3]), t[1][3]), t[1][1]]
            vs = [t[0][2], jnp.where(low, t[0][4], swap64(t[1][4])), t[1][2]]
            for i in range(3):
                q[3 * p + i, here] = (rope_fwd(qs[i], cos, sin) * HD**-0.5).astype(BF)
                kv[0, 3 * p + i, here] = rope_fwd(ks[i], cos, sin).astype(BF)
                kv[1, 3 * p + i, here] = vs[i].astype(BF)

    x = xin[...].reshape(rows, width)
    x_out[...] = x
    project(0, rows, x)
    low = low_lanes((rows, 128))
    share = remote(kv, land_kv, kv_send.at[0], kv_recv.at[0], near)
    share.start()
    rounds(start, start + 1)
    share.wait()

    def heads_of(p, others, save):
        k = jnp.concatenate([kv[0, p], others[0, p]], axis=0)
        v = jnp.concatenate([kv[1, p], others[1, p]], axis=0)
        vt = v.astype(F32).T.astype(BF)
        ones = jnp.ones((16, 2 * rows), BF)
        outs = []
        for h in range(2):
            qm = jnp.where(low if h == 0 else jnp.logical_not(low), q[p], jnp.zeros((rows, 128), BF))
            s = dg(k, qm, NT) + mask[...]
            e = jnp.exp(s - jnp.max(s, axis=0, keepdims=True)).astype(BF)
            t = dg(jnp.concatenate([vt[HD * h : HD * h + HD], ones], axis=0), e, NN)
            inv = 1.0 / t[HD : HD + 1]
            save(h, e, inv)
            outs.append(t[:HD] * inv)
        o[p] = jnp.concatenate(outs, axis=0).T.astype(BF)

    def pair(p, carry):
        heads_of(p, land_kv, lambda h, e, inv: None)
        round_(start + 1 + p)
        return carry

    def out_part(p):
        wo = []
        for e in range(2):
            wo.append([w[:, :, 2 * p + e, :, 512 + 128 * i : 640 + 128 * i].reshape(width, 128) for i in range(2)])
        mid = jnp.where(low_lanes((width, 128)), swap64(wo[0][0].astype(F32)), wo[1][0].astype(F32)).astype(BF)
        return jnp.concatenate([wo[0][1], mid, wo[1][1]], axis=1)

    def mix(x):
        r = x.astype(F32)
        for p in range(2):
            r = r + dg(jnp.concatenate([o[3 * p + i] for i in range(3)], axis=1), out_part(p), NT)
        return norm_parts(r)

    def group_of(k):
        return unit_weights(
            lambda t, m: w[:, :, t, :, pl.ds(pl.multiple_of(width + GROUP * k + 128 * m, 128), 128)].reshape(width, 128)
        )

    def unit(k, save):
        wd, wg, wu = group_of(k)
        gate = dg(hb[...], wg, NN)
        up = dg(hb[...], wu, NN)
        save(gate, up)
        act = (gate / (1.0 + jnp.exp(-gate)) * up).astype(BF)
        acc[...] += dg(act, wd, NT)

    lax.fori_loop(0, 6, pair, 0)
    n, inv = mix(x)
    h = n * norm_out[0:1] + norm_out[2:3]
    hb[...] = h.astype(BF)
    acc[...] = h
    rounds(start + 7, start + 8)

    def units(k, carry):
        @pl.when(k != 4)
        def _():
            round_(start + 8 + k - k // 5)

        unit(k, lambda gate, up: None)
        return carry

    lax.fori_loop(0, 6, units, 0)
    pieces = relay.shape[0]
    piece_rows = rows // pieces

    def row_copy(b):
        return remote(relay.at[b], land_rows.at[b], row_send.at[b], row_recv.at[b], other)

    kept_out = []

    def keep_out(src, dst):
        copy = pltpu.make_async_copy(src, dst, out_sem.at[len(kept_out)])
        kept_out.append(copy)
        copy.start()

    @pl.when(section == 0)
    def _():
        def send_rows(b, carry):
            part = pl.ds(pl.multiple_of(b * piece_rows, piece_rows), piece_rows)
            n, inv = norm_parts(acc[part])
            relay[b] = (n * norm_out[1:2] + norm_out[3:4]).astype(BF)
            row_copy(b).start()
            return carry

        lax.fori_loop(0, pieces, send_rows, 0)
        same = pltpu.make_async_copy(land_kv, late_kv, kv_send.at[1])
        same.start()
        same.wait()

    @pl.when(section == 1)
    def _():
        def project_rows(b, carry):
            at = pl.multiple_of(b * piece_rows, piece_rows)
            row_copy(b).wait_recv()
            x_out[pl.ds(at, piece_rows)] = land_rows[b]
            project(at, piece_rows, land_rows[b])
            return carry

        lax.fori_loop(0, pieces, project_rows, 0)
        again = remote(kv, late_kv, kv_send.at[1], kv_recv.at[1], near)
        again.start()
        again.wait()

    for src, dst in ((q, q_out), (kv.at[0], k_out), (kv.at[1], v_out), (late_kv.at[0], ko_out), (late_kv.at[1], vo_out)):
        keep_out(src, dst)

    def probs_out(p):
        return pltpu.make_async_copy(eb.at[p % 2], e_out.at[p], e_sem.at[p % 2])

    def probs_in(p):
        return pltpu.make_async_copy(e_out.at[p], eb.at[p % 2], e_sem.at[p % 2])

    def pair_kept(p, carry):
        @pl.when(p >= 2)
        def _():
            probs_out(p - 2).wait()

        def save(h, e, inv):
            eb[p % 2, h] = e
            l_out[p, h] = jnp.broadcast_to(inv, l_out.shape[2:])

        heads_of(p, late_kv, save)
        probs_out(p).start()
        return carry

    lax.fori_loop(0, PAIRS, pair_kept, 0)
    keep_out(o, o_out)
    n, inv = mix(x_out[...])
    n1[...] = n.astype(BF)
    i1_out[...] = jnp.broadcast_to(inv, i1_out.shape)
    keep_out(n1, n1_out)
    h = n * norm_out[0:1] + norm_out[2:3]
    hb[...] = h.astype(BF)
    acc[...] = h

    def units_out(k):
        return pltpu.make_async_copy(gu.at[k % 2], gu_out.at[k], gu_sem.at[k % 2])

    def units_in(k):
        return pltpu.make_async_copy(gu_out.at[k], gu.at[k % 2], gu_sem.at[k % 2])

    def unit_kept(k, carry):
        @pl.when(k >= 2)
        def _():
            units_out(k - 2).wait()

        def save(gate, up):
            gu[k % 2, 0] = gate.astype(BF)
            gu[k % 2, 1] = up.astype(BF)

        unit(k, save)
        units_out(k).start()
        return carry

    lax.fori_loop(0, 6, unit_kept, 0)
    n, inv = norm_parts(acc[...])
    n2[...] = n.astype(BF)
    i2_out[...] = jnp.broadcast_to(inv, i2_out.shape)
    keep_out(n2, n2_out)
    hb[...] = (n * norm_out[1:2] + norm_out[3:4]).astype(BF)
    keep_out(hb, y_out)
    for p in (PAIRS - 2, PAIRS - 1):
        probs_out(p).wait()
        units_out(p).wait()

    def dz_copy(b):
        return remote(relay.at[b], land_rows.at[b], dz_send.at[b], dz_recv.at[b], other)

    def oth_copy(p):
        return remote(oth.at[p], got.at[p], oth_send.at[p], oth_recv.at[p], near)

    @pl.when(section == 1)
    def _():
        dr2 = norm_back(xin[...].reshape(rows, width).astype(F32) * norm_out[1:2], n, inv)
        acc[...] = dr2
        df[...] = dr2.astype(BF)
        for p in range(2):
            probs_in(p).start()
            units_in(p).start()

        def unit_back(k, carry):
            wd, wg, wu = group_of(k)
            units_in(k).wait()
            gate = gu[k % 2, 0].astype(F32)
            up = gu[k % 2, 1].astype(F32)
            s = 1.0 / (1.0 + jnp.exp(-gate))
            d_act = dg(df[...], wd, NN)
            d_gate = (d_act * up * (s * (1.0 + gate * (1.0 - s)))).astype(BF)
            d_up = (d_act * (gate * s)).astype(BF)
            acc[...] += dg(d_gate, wg, NT) + dg(d_up, wu, NT)

            @pl.when(k + 2 < 6)
            def _():
                units_in(k + 2).start()

            return carry

        lax.fori_loop(0, 6, unit_back, 0)
        dr1 = norm_back(acc[...] * norm_out[0:1], n1[...].astype(F32), i1_out[:, :1])
        acc[...] = dr1
        df[...] = dr1.astype(BF)
        cost, sint = cost_ref[:, pl.ds(c * rows, rows)], sint_ref[:, pl.ds(c * rows, rows)]

        def pair_of(p, carry):
            probs_in(p).wait()
            dqt, dk, dv = pair_back(
                do3[p % 3], o[p], q[p], kv[0, p], kv[1, p], late_kv[0, p], late_kv[1, p],
                [eb.at[p % 2, h] for h in range(2)], [l_out[p, h, 0:1] for h in range(2)], cost, sint,
            )

            @pl.when(p + 2 < PAIRS)
            def _():
                probs_in(p + 2).start()

            dq[p] = dqt.T.astype(BF)
            keep[p, 0] = dk[:, :rows].astype(BF)
            keep[p, 1] = dv[:, :rows].astype(BF)
            oth[p, 0] = dk[:, rows:].astype(BF)
            oth[p, 1] = dv[:, rows:].astype(BF)
            oth_copy(p).start()
            return carry

        def joint(half):
            def total(i, m):
                return keep[i, m].astype(F32) + got[i, m].astype(F32)

            three = range(3 * half, 3 * half + 3)
            for i in three:
                oth_copy(i).wait()
            parts = joint_parts(
                [dq[i].astype(F32) for i in three], [total(i, 0) for i in three], [total(i, 1) for i in three], cost, sint
            )
            for e in range(2):
                d[2 * half + e] = parts[e]

        for half in range(2):
            t = dg(df[...], out_part(half), NN).astype(BF)
            for i in range(3):
                do3[i] = t[:, 128 * i : 128 * i + 128]
            lax.fori_loop(3 * half, 3 * half + 3, pair_of, 0)
        for half in range(2):
            joint(half)

        def send_back(b, carry):
            part = pl.ds(pl.multiple_of(b * piece_rows, piece_rows), piece_rows)
            total = acc[part]
            for t in range(4):
                total += dg(d[t, part], w[:, :, t, :, :640].reshape(width, 640), NT)
            relay[b] = total.astype(BF)
            dz_copy(b).start()
            return carry

        lax.fori_loop(0, pieces, send_back, 0)
        dy_out[...] = xin[...].reshape(rows, width)
        lax.fori_loop(0, pieces, lambda b, t: (dz_copy(b).wait_send(), t)[1], 0)

    @pl.when(section == 0)
    def _():
        lax.fori_loop(0, pieces, lambda b, t: (row_copy(b).wait_send(), t)[1], 0)
        lax.fori_loop(0, pieces, lambda b, t: (dz_copy(b).wait_recv(), t)[1], 0)
        dy_out[...] = land_rows[...].reshape(rows, width)

    for copy in kept_out:
        copy.wait()

    def finish(j, carry):
        write_back(j).wait()
        to_y(j).wait_send()
        to_core(j).wait_send()
        for h in range(last):

            @pl.when(jnp.logical_and(z >= h, z < last))
            def _():
                go_right(j, h).wait_send()

            @pl.when(jnp.logical_and(z + h <= last, z > 0))
            def _():
                go_left(j, h).wait_send()

        return carry

    lax.fori_loop(0, parts, finish, 0)


def first_layer(tokens, top, shard, gains, biases, lengths, cos, sin, cost, sint):
    micro, own, width = tokens.shape
    depth, columns = shard.shape
    rows = 2 * own
    parts = columns // WIDE
    heads = width // 128
    dma = pltpu.SemaphoreType.DMA
    hbm = pl.BlockSpec(memory_space=pl.ANY)
    vm = pl.BlockSpec(memory_space=VM)
    return pl.pallas_call(
        functools.partial(first_kernel, parts),
        in_specs=[hbm] * 3 + [vm] * 7,
        out_specs=[hbm] * 12 + [vm] * 6,
        out_shape=[sds((2, 2, 4, depth, columns), BF)]
        + [sds((heads, rows, 128), BF)] * 5
        + [
            sds((rows, width), BF),
            sds((heads, 2, 2 * rows, rows), BF),
            sds((heads, rows, 128), BF),
            sds((6, 2, rows, 512), BF),
            sds((rows, width), BF),
            sds((rows, width), BF),
            sds((rows, width), BF),
            sds((rows, width), BF),
            sds((heads, 2, 8, rows), F32),
            sds((rows, 128), F32),
            sds((rows, 128), F32),
            sds((4, width), F32),
        ],
        scratch_shapes=[
            VM((2, 2, 4, depth, columns), BF),
            VM((2, own, width), BF),
            VM((heads, rows, 128), BF),
            VM((2, heads, rows, 128), BF),
            VM((2, heads, rows, 128), BF),
            VM((2, heads, rows, 128), BF),
            VM((heads, rows, 128), BF),
            VM((rows, width), BF),
            VM((rows, width), F32),
            VM((4, rows // 4, width), BF),
            VM((4, rows // 4, width), BF),
            VM((2, 2, 8, gains.shape[1]), F32),
            VM((2,) + lengths.shape, jnp.int32),
            VM((2 * rows, rows), F32),
            VM((2, 2, 2 * rows, rows), BF),
            VM((2, 2, rows, 512), BF),
            VM((rows, width), BF),
            VM((rows, width), BF),
            VM((rows, width), BF),
            VM((3, rows, 128), BF),
            VM((heads, rows, 128), BF),
            VM((heads, 2, 128, rows), BF),
            VM((heads, 2, 128, rows), BF),
            VM((heads, 2, 128, rows), BF),
            VM((4, rows, 640), BF),
            dma, dma((2,)), dma((2,)), dma, dma((parts,)), dma((2,)), dma((2,)), dma((9,)), dma((4,)), dma((4,)),
            dma((2,)), dma((2,)), dma((6,)), dma((6,)), dma((4,)), dma((4,)),
            dma((3,)), dma((3,)),
            dma((parts, 3)), dma((parts, 3)), dma((parts, 3)), dma((parts, 3)),
            dma((parts,)), dma((parts,)), dma((parts,)), dma((parts,)),
        ],
        compiler_params=pltpu.CompilerParams(collective_id=1, has_side_effects=True, vmem_limit_bytes=63 << 20),
        name="first",
    )(tokens, top, shard, gains, biases, lengths, cos, sin, cost, sint)


def swap_pairs(tp, step, dp_axes):
    pairs = []
    half = tp // 2
    for core in range(2):
        for at in range(tp):
            source = core * tp + at
            target = (at // half) * tp + half * core + (at + step) % half
            pairs.append((source, target))
    return pairs


def to_sequences(rows, tp):
    half = tp // 2
    at = lax.axis_index("tensor")
    pieces = [None] * half
    got = []
    for step in range(half):
        piece = lax.dynamic_index_in_dim(rows, (at + step) % half, 0, keepdims=False)
        got.append(lax.ppermute(piece, ("core", "tensor"), swap_pairs(tp, step, None)))
    stacked = jnp.stack(got)
    order = (at - jnp.arange(half)) % half
    return jnp.take(stacked, order, axis=0).reshape(-1, rows.shape[-1])


def to_positions(rows, tp):
    half = tp // 2
    at = lax.axis_index("tensor")
    parts = rows.reshape(half, -1, rows.shape[-1])
    got = []
    for step in range(half):
        piece = lax.dynamic_index_in_dim(parts, (at - step) % half, 0, keepdims=False)
        back = [(target, source) for source, target in swap_pairs(tp, step, None)]
        got.append(lax.ppermute(piece, ("core", "tensor"), back))
    stacked = jnp.stack(got)
    order = (at + jnp.arange(half)) % half
    return jnp.take(stacked, (jnp.arange(half) - at) % half, axis=0)


def rope_tables(positions):
    halfway = HD // 2
    freqs = 1000.0 ** (-jnp.arange(halfway, dtype=F32) / halfway)
    angles = positions.astype(F32)[:, None] * freqs[None, :]
    cos, sin = jnp.cos(angles), jnp.sin(angles)
    wide = jnp.concatenate([cos] * 4, axis=1)
    signed = jnp.concatenate([-sin, sin] * 2, axis=1)
    return wide, signed, cos.T, sin.T


def pack_shard(w_qkv, w_out, w_gate_up, w_down):
    rows = w_qkv.shape[0]
    odd = lax.axis_index("tensor") % 2 == 1
    heads = w_qkv.reshape(rows, 3, 3, HD)
    mine = w_out.T.reshape(rows, 3, HD)
    heads = jnp.where(odd, jnp.roll(heads, -1, axis=2), heads)
    mine = jnp.where(odd, jnp.roll(mine, -1, axis=1), mine)
    first = jnp.concatenate(
        [heads[:, :, :2].reshape(rows, -1), heads[:, :, 2].reshape(rows, -1), mine[:, 2], mine[:, :2].reshape(rows, -1)], axis=1
    )
    units = jnp.concatenate([w_down.T[:, None], w_gate_up], axis=1)
    units = units.reshape(rows, 3, -1, 128).transpose(0, 2, 1, 3)
    return jnp.concatenate([first, units.reshape(rows, -1)], axis=1)


def unpack_first(first):
    rows = first.shape[0]
    odd = lax.axis_index("tensor") % 2 == 1
    both = first[:, :384].reshape(rows, 3, 2, HD)
    single = first[:, 384:576].reshape(rows, 3, 1, HD)
    heads = jnp.concatenate([both, single], axis=2)
    mine = jnp.concatenate([first[:, 640:].reshape(rows, 2, HD), first[:, 576:640].reshape(rows, 1, HD)], axis=1)
    heads = jnp.where(odd, jnp.roll(heads, 1, axis=2), heads)
    mine = jnp.where(odd, jnp.roll(mine, 1, axis=1), mine)
    return heads.reshape(rows, 3, -1), mine.reshape(rows, -1).T


def host_tables(length):
    halfway = HD // 2
    freqs = np.float32(1000.0) ** (-np.arange(halfway, dtype=np.float32) / np.float32(halfway))
    angles = np.arange(length, dtype=np.float32)[:, None] * freqs[None, :]
    cos, sin = np.cos(angles), np.sin(angles)
    return np.concatenate([cos] * 4, axis=1), np.concatenate([-sin, sin] * 2, axis=1), cos.T.copy(), sin.T.copy()


BLOCKS = 4


def gather_shard(shard, dp, tp):
    rows, columns = shard.shape
    got = lax.all_gather(shard, ALL, axis=0, tiled=False)
    got = got.reshape(BLOCKS, dp // BLOCKS, tp, rows, columns)
    return got.transpose(0, 2, 1, 3, 4).reshape(BLOCKS, tp, -1, columns)


def scatter_sum(whole, dp, tp):
    columns = whole.shape[3]
    parts = whole.reshape(BLOCKS, tp, dp // BLOCKS, -1, columns).transpose(0, 2, 1, 3, 4)
    parts = parts.reshape(dp * tp, -1, columns)
    return lax.psum_scatter(parts, ALL, scatter_dimension=0, tiled=False).astype(F32)


def on_device(dp, tp, tokens, cotangent, lengths, w_qkv, w_out, w_gate_up, w_down, norm_gains, norm_biases):
    section = lax.axis_index("section")
    core = lax.axis_index("core")
    at = lax.axis_index("tensor")
    micro, own, width = tokens.shape
    assert micro * 2 == tp
    length = own * tp
    rows = length // 2
    shard = pack_shard(w_qkv[0], w_out[0], w_gate_up[0], w_down[0])
    if dp == 4 and tp == 4:
        wide, signed, cost, sint = host_tables(length)
        (
            weights, q, k, v, ko, vo, y, e, o, gu, n1, n2, inputs, dy, l, i1, i2, small,
        ) = first_layer(tokens, cotangent, shard, norm_gains, norm_biases, lengths, wide, signed, cost, sint)
        weights = weights.reshape((BLOCKS,) + weights.shape[2:])
        norms = (small[:2], small[2:])
        kept = (q, k, v, ko, vo, o, e, l, gu, n1, i1, n2, i2)
        joint, mix, pair, down, ends, total = last_back(inputs, y, dy, kept, weights, norms, cost, sint)
        small = lax.dynamic_slice_in_dim(total[:4].reshape(2, dp * tp, -1), lax.axis_index(ALL), 1, 1)
        gains, biases = small[0, 0], small[1, 0]
        joint, mix = joint.transpose(1, 0, 2), mix.T
    else:
        near = core * rows + jnp.arange(rows, dtype=jnp.int32)
        far = (1 - core) * rows + jnp.arange(rows, dtype=jnp.int32)
        tabs = rope_tables(near)
        weights = gather_shard(shard, dp, tp)
        norms = jnp.concatenate([norm_gains, norm_biases])
        norms = lax.all_gather(norms, ("y", "core"), axis=1, tiled=True).astype(F32)
        norms = (norms[0].reshape(2, width), norms[1].reshape(2, width))
        grad_top = to_sequences(cotangent, tp)
        tokens = to_sequences(tokens, tp)
        chip_lengths = lax.all_gather(lengths, "core", axis=0, tiled=True)
        my_lengths = lax.dynamic_index_in_dim(chip_lengths, at, 0, keepdims=False)
        ends_at = jnp.cumsum(my_lengths)

        def segment(positions):
            return jnp.sum((ends_at[None, :] <= positions[:, None]).astype(jnp.int32), axis=-1)

        seg_near = segment(near)
        seg_all = jnp.concatenate([seg_near, segment(far)])
        mask = jnp.where(seg_all[:, None] == seg_near[None, :], 0.0, neg_fill).astype(F32)
        y, unused = forward(tokens, weights, norms, mask, tabs)
        received = lax.ppermute(y, "section", [(0, 1)])
        inputs = jnp.where(section == 0, tokens, received)
        y, kept = forward(inputs, weights, norms, mask, tabs)
        dr1, da = ffn_backward(grad_top, kept, weights, norms, False)
        unused, dz = attn_backward(inputs, da, dr1, None, kept, weights, tabs)
        received = lax.ppermute(dz, "section", [(1, 0)])
        dy = jnp.where(section == 0, received, grad_top)
        g, dr1, da, ng = ffn_backward(dy, kept, weights, norms, True)
        g, dz = attn_backward(inputs, da, dr1, g, kept, weights, tabs)
        ends = to_positions(jnp.where(section == 0, dz.astype(BF), y), tp)
        mine = scatter_sum(g, dp, tp)
        first = mine[:, :width]
        units = mine[:, width:].reshape(first.shape[0], -1, 3, 128).transpose(0, 2, 1, 3).reshape(first.shape[0], 3, -1)
        pair, down = units[:, 1:], units[:, 0].T
        joint, mix = unpack_first(first)
        gains = lax.psum_scatter(ng[0:2].reshape(-1), ALL, scatter_dimension=0, tiled=True)
        biases = lax.psum_scatter(ng[2:4].reshape(-1), ALL, scatter_dimension=0, tiled=True)
    outs = (joint, mix, pair.reshape(pair.shape[0], 2, -1), down, gains, biases)
    return (ends[None],) + tuple(t[None] for t in outs)


def solution(mesh):
    sections, dp, tp = mesh.devices.shape
    fine = Mesh(mesh.devices.reshape(sections, dp // 2, 2, tp), ("section", "y", "core", "tensor"))
    both = ("y", "core")
    in_specs = (
        P(both, "tensor", None),
        P(both, "tensor", None),
        P(both, None),
        P("section", both, None, "tensor"),
        P("section", "tensor", both),
        P("section", both, None, "tensor"),
        P("section", "tensor", both),
        P("section", both),
        P("section", both),
    )
    out_specs = (
        P("section", both, "tensor", None),
        P("section", both, None, "tensor"),
        P("section", "tensor", both),
        P("section", both, None, "tensor"),
        P("section", "tensor", both),
        P("section", ALL),
        P("section", ALL),
    )
    return jax.shard_map(
        functools.partial(on_device, dp, tp), mesh=fine, in_specs=in_specs, out_specs=out_specs, check_vma=False
    )
```

```python
import functools

import jax
import jax.numpy as jnp
import numpy as np
from jax import lax
from jax.experimental import pallas as pl
from jax.experimental.pallas import tpu as pltpu
from jax.sharding import Mesh, PartitionSpec as P

HD = 64
eps = 1e-05
neg_fill = -1e30
ALL = ("y", "core", "tensor")
BF = jnp.bfloat16
F32 = jnp.float32
MESH = pl.DeviceIdType.MESH


def dg(a, b, dims):
    return lax.dot_general(a, b, (dims, ((), ())), preferred_element_type=F32)


NN = ((1,), (0,))
NT = ((1,), (1,))
TN = ((0,), (0,))


def low_lanes(shape):
    return lax.broadcasted_iota(jnp.int32, shape, 1) < HD


def swap64(v):
    return pltpu.roll(v, HD, axis=1)


def rope_fwd(t, cos, sin):
    lane = lax.broadcasted_iota(jnp.int32, t.shape, 1) % HD
    other = jnp.where(lane < HD // 2, pltpu.roll(t, 128 - HD // 2, axis=1), pltpu.roll(t, HD // 2, axis=1))
    return t * cos + other * sin


def qkv_kernel(x_ref, w_ref, cos_ref, sin_ref, q_ref, k_ref, v_ref):
    x = x_ref[...]
    width = x.shape[1]
    r = [dg(x, w_ref[:, e, :, :640].reshape(width, 640), NN) for e in range(2)]
    c = [[t[:, 128 * i : 128 * i + 128] for i in range(5)] for t in r]
    low = low_lanes(c[0][0].shape)
    qs = [c[0][0], jnp.where(low, c[0][3], swap64(c[1][3])), c[1][0]]
    ks = [c[0][1], jnp.where(low, swap64(c[0][3]), c[1][3]), c[1][1]]
    vs = [c[0][2], jnp.where(low, c[0][4], swap64(c[1][4])), c[1][2]]
    cos, sin = cos_ref[...], sin_ref[...]
    for i in range(3):
        q_ref[i] = (rope_fwd(qs[i], cos, sin) * HD**-0.5).astype(BF)
        k_ref[i] = rope_fwd(ks[i], cos, sin).astype(BF)
        v_ref[i] = vs[i].astype(BF)


def attn_kernel(q_ref, k_ref, v_ref, ko_ref, vo_ref, m_ref, o_ref, e_ref, l_ref):
    q = q_ref[0]
    k = jnp.concatenate([k_ref[0], ko_ref[0]], axis=0)
    v = jnp.concatenate([v_ref[0], vo_ref[0]], axis=0)
    vt = v.astype(F32).T.astype(BF)
    outs = []
    for h in range(2):
        low = low_lanes(q.shape)
        qm = jnp.where(low if h == 0 else jnp.logical_not(low), q, jnp.zeros_like(q))
        s = dg(k, qm, NT) + m_ref[...]
        e = jnp.exp(s - jnp.max(s, axis=0, keepdims=True))
        inv = 1.0 / jnp.sum(e, axis=0, keepdims=True)
        eb = e.astype(BF)
        e_ref[0, h] = eb
        l_ref[0, h] = jnp.broadcast_to(inv, l_ref.shape[2:])
        outs.append(dg(vt[HD * h : HD * h + HD], eb, NN) * inv)
    o_ref[0] = jnp.concatenate(outs, axis=0).T.astype(BF)


def norm_parts(r):
    center = r - jnp.mean(r, axis=-1, keepdims=True)
    inv = lax.rsqrt(jnp.mean(center * center, axis=-1, keepdims=True) + eps)
    return center * inv, inv


def norm_back(dn, n, inv):
    return inv * (dn - jnp.mean(dn, axis=-1, keepdims=True) - n * jnp.mean(dn * n, axis=-1, keepdims=True))


def out_weight(w_ref):
    c = [[w_ref[:, e, :, 128 * i : 128 * i + 128].reshape(-1, 128) for i in range(2)] for e in range(2)]
    low = low_lanes(c[0][0].shape)
    mid = jnp.where(low, swap64(c[0][0].astype(F32)), c[1][0].astype(F32)).astype(BF)
    return [c[0][1], mid, c[1][1]]


GROUP = 384
WIDE = 128


def unit_weights(load):
    return [jnp.concatenate([load(t, m) for t in range(4)], axis=1) for m in range(3)]


def ffn_kernel(x_ref, o_ref, wo_ref, w_ref, g_ref, b_ref, y_ref, gu_ref, n1_ref, i1_ref, n2_ref, i2_ref, h_ref, hb_ref, acc_ref):
    z = pl.program_id(0)
    width = x_ref.shape[1]

    @pl.when(z == 0)
    def _():
        r = x_ref[...].astype(F32)
        for p in range(2):
            w = jnp.concatenate(out_weight(wo_ref.at[:, 2 * p : 2 * p + 2]), axis=1)
            o = jnp.concatenate([o_ref[3 * p + i] for i in range(3)], axis=1)
            r = r + dg(o, w, NT)
        n, inv = norm_parts(r)
        n1_ref[...] = n.astype(BF)
        i1_ref[...] = jnp.broadcast_to(inv, i1_ref.shape)
        h = n * g_ref[0:1] + b_ref[0:1]
        h_ref[...] = h
        hb_ref[...] = h.astype(BF)

    hb = hb_ref[...]
    wd, wg, wu = unit_weights(lambda t, m: w_ref[:, t, :, 128 * m : 128 * m + 128].reshape(width, 128))
    gate = dg(hb, wg, NN)
    up = dg(hb, wu, NN)
    gu_ref[0, 0] = gate.astype(BF)
    gu_ref[0, 1] = up.astype(BF)
    act = (gate / (1.0 + jnp.exp(-gate)) * up).astype(BF)
    part = dg(act, wd, NT)

    @pl.when(z == 0)
    def _():
        acc_ref[...] = h_ref[...] + part

    @pl.when(z > 0)
    def _():
        acc_ref[...] += part

    @pl.when(z == pl.num_programs(0) - 1)
    def _():
        n, inv = norm_parts(acc_ref[...])
        n2_ref[...] = n.astype(BF)
        i2_ref[...] = jnp.broadcast_to(inv, i2_ref.shape)
        y_ref[...] = (n * g_ref[1:2] + b_ref[1:2]).astype(BF)


def ffn_back_kernel(grads, dy_ref, n1_ref, i1_ref, n2_ref, i2_ref, gu_ref, w_ref, g_ref, b_ref, *refs):
    if grads:
        g_out, dr1_ref, da_ref, ng_ref, hb_ref, df_ref, acc_ref = refs
    else:
        dr1_ref, da_ref, df_ref, acc_ref = refs
    z = pl.program_id(0)
    width = dy_ref.shape[1]

    @pl.when(z == 0)
    def _():
        dy = dy_ref[...].astype(F32)
        n = n2_ref[...].astype(F32)
        if grads:
            ng_ref[1:2] = jnp.sum(dy * n, axis=0, keepdims=True)
            ng_ref[3:4] = jnp.sum(dy, axis=0, keepdims=True)
            hb_ref[...] = (n1_ref[...].astype(F32) * g_ref[0:1] + b_ref[0:1]).astype(BF)
        dr2 = norm_back(dy * g_ref[1:2], n, i2_ref[:, :1])
        acc_ref[...] = dr2
        df_ref[...] = dr2.astype(BF)

    df = df_ref[...]
    gate = gu_ref[0, 0].astype(F32)
    up = gu_ref[0, 1].astype(F32)
    s = 1.0 / (1.0 + jnp.exp(-gate))
    silu = gate * s
    wd, wg, wu = unit_weights(lambda t, m: w_ref[:, t, :, 128 * m : 128 * m + 128].reshape(width, 128))

    def keep(m, grad):
        for t in range(g_out.shape[1]):
            g_out[:, t, :, 128 * m : 128 * m + 128] = grad[:, 128 * t : 128 * t + 128].astype(BF).reshape(g_out.shape[0], -1, 128)

    if grads:
        keep(0, dg(df, (silu * up).astype(BF), TN))
    d_act = dg(df, wd, NN)
    d_gate = (d_act * up * (s * (1.0 + gate * (1.0 - s)))).astype(BF)
    d_up = (d_act * silu).astype(BF)
    if grads:
        hb = hb_ref[...]
        keep(1, dg(hb, d_gate, TN))
        keep(2, dg(hb, d_up, TN))
    acc_ref[...] += dg(d_gate, wg, NT) + dg(d_up, wu, NT)

    @pl.when(z == pl.num_programs(0) - 1)
    def _():
        dh = acc_ref[...]
        n = n1_ref[...].astype(F32)
        if grads:
            ng_ref[0:1] = jnp.sum(dh * n, axis=0, keepdims=True)
            ng_ref[2:3] = jnp.sum(dh, axis=0, keepdims=True)
        dr1 = norm_back(dh * g_ref[0:1], n, i1_ref[:, :1])
        dr1_ref[...] = dr1
        da_ref[...] = dr1.astype(BF)


def pair_back(do, o, q, k, v, ko, vo, e, l, cos, sin):
    dot = do.astype(F32).T
    ot = o.astype(F32).T
    k = jnp.concatenate([k, ko], axis=0)
    v = jnp.concatenate([v, vo], axis=0)
    kt = k.astype(F32).T.astype(BF)
    qt = q.astype(F32).T.astype(BF)
    dqs, dks, dvs = [], [], []
    for h in range(2):
        span = slice(HD * h, HD * h + HD)
        scaled = dot[span] * l[h]
        inner = jnp.sum(scaled * ot[span], axis=0, keepdims=True)
        sb = scaled.astype(BF)
        zero = jnp.zeros_like(sb)
        padded = jnp.concatenate([sb, zero] if h == 0 else [zero, sb], axis=0)
        dp = dg(v, padded, NN)
        et = e[h][...]
        ds = (et.astype(F32) * (dp - inner)).astype(BF)
        dvs.append(dg(sb, et, NT))
        dks.append(dg(qt[span], ds, NT))
        dqt = dg(kt[span], ds, NN) * HD**-0.5
        d1, d2 = dqt[: HD // 2], dqt[HD // 2 :]
        dqs.append(d1 * cos + d2 * sin)
        dqs.append(d2 * cos - d1 * sin)
    return [jnp.concatenate(t, axis=0) for t in (dqs, dks, dvs)]


def joint_parts(dq, dkt, dvt, cos, sin):
    dk = []
    for t in dkt:
        parts = []
        for h in range(2):
            d1 = t[HD * h : HD * h + HD // 2]
            d2 = t[HD * h + HD // 2 : HD * h + HD]
            parts += [d1 * cos + d2 * sin, d2 * cos - d1 * sin]
        dk.append(jnp.concatenate(parts, axis=0).T)
    dv = [t.T for t in dvt]
    low = low_lanes(dq[0].shape)
    zero = jnp.zeros_like(dv[1])
    d = [
        [dq[0], dk[0], dv[0], jnp.where(low, dq[1], swap64(dk[1])), jnp.where(low, dv[1], zero)],
        [dq[2], dk[2], dv[2], jnp.where(low, swap64(dq[1]), dk[1]), jnp.where(low, swap64(dv[1]), zero)],
    ]
    return [jnp.concatenate(t, axis=1).astype(BF) for t in d]


def attn_back_kernel(grads, da_ref, wo_ref, o_ref, q_ref, k_ref, v_ref, ko_ref, vo_ref, e_ref, l_ref, cos_ref, sin_ref, dq_ref, own_ref, oth_ref, *dwo_ref):
    da = da_ref[...]
    rows = da.shape[0]
    w = jnp.concatenate(out_weight(wo_ref), axis=1)
    do3 = dg(da, w, NN).astype(BF)
    if grads:
        o3 = jnp.concatenate([o_ref[i] for i in range(3)], axis=1)
        dwo_ref[0][0] = dg(da, o3, TN).astype(BF)
    cos, sin = cos_ref[...], sin_ref[...]
    for i in range(3):
        dqt, dk, dv = pair_back(
            do3[:, 128 * i : 128 * i + 128], o_ref[i], q_ref[i], k_ref[i], v_ref[i], ko_ref[i], vo_ref[i],
            [e_ref[i, h] for h in range(2)], [l_ref[i, h, 0:1] for h in range(2)], cos, sin,
        )
        dq_ref[i] = dqt.T.astype(BF)
        own_ref[i, 0] = dk[:, :rows]
        own_ref[i, 1] = dv[:, :rows]
        oth_ref[i, 0] = dk[:, rows:].astype(BF)
        oth_ref[i, 1] = dv[:, rows:].astype(BF)


def joint_back_kernel(grads, *refs):
    if grads:
        old_ref, x_ref, w_ref, dr1_ref, dq_ref, own_ref, got_ref, dwo_ref, cos_ref, sin_ref, g_ref, dz_ref = refs
    else:
        w_ref, dr1_ref, dq_ref, own_ref, got_ref, cos_ref, sin_ref, dz_ref, dzb_ref = refs
    p = pl.program_id(0)
    width = dr1_ref.shape[1]
    d = joint_parts(
        [dq_ref[i].astype(F32) for i in range(3)],
        [own_ref[i, 0] + got_ref[i, 0].astype(F32) for i in range(3)],
        [own_ref[i, 1] + got_ref[i, 1].astype(F32) for i in range(3)],
        cos_ref[...],
        sin_ref[...],
    )
    acc = None
    for e in range(2):
        t = dg(d[e], w_ref[:, e, :, :640].reshape(width, 640), NT)
        acc = t if acc is None else acc + t
    if grads:
        x = x_ref[...]
        wlow = low_lanes((width, 128))
        mid = dwo_ref[0, :, 128:256].astype(F32)
        sides = [dwo_ref[0, :, 0:128], dwo_ref[0, :, 256:384]]
        mids = [swap64(mid), mid]
        for e in range(2):
            g = dg(x, d[e], TN)
            blocks = g_ref.shape[0]
            g_ref[:, e, :, :512] = g[:, :512].astype(BF).reshape(blocks, -1, 512)
            g_ref[:, e, :, 512:640] = jnp.where(wlow, g[:, 512:], mids[e]).astype(BF).reshape(blocks, -1, 128)
            g_ref[:, e, :, 640:] = sides[e].reshape(blocks, -1, 128)

    @pl.when(p == 0)
    def _():
        dz_ref[...] = dr1_ref[...] + acc

    @pl.when(p > 0)
    def _():
        total = dz_ref[...] + acc
        dz_ref[...] = total
        if not grads:
            dzb_ref[...] = total.astype(BF)


BIG = pltpu.CompilerParams(vmem_limit_bytes=58 << 20)
VM = pltpu.VMEM


def full(shape):
    return pl.BlockSpec(shape, lambda i: (0,) * len(shape))


def lead(shape, at=0):
    return pl.BlockSpec(shape, lambda i: tuple(i if j == at else 0 for j in range(len(shape))))


def joint_block(w):
    return pl.BlockSpec((w.shape[0], 2, w.shape[2], 768), lambda i: (0, i, 0, 0))


def group_block(w):
    return pl.BlockSpec((w.shape[0], w.shape[1], w.shape[2], GROUP), lambda i: (0, 0, 0, 2 + i))


def sds(shape, kind):
    return jax.ShapeDtypeStruct(shape, kind)


def forward(x, weights, norms, mask, tabs):
    w = weights
    rows, width = x.shape
    heads = width // 128
    blocks, tp, depth, columns = w.shape
    steps = tp // 2
    cos, sin, cost, sint = tabs
    q, k, v = pl.pallas_call(
        qkv_kernel,
        grid=(steps,),
        in_specs=[full((rows, width)), joint_block(w), full((rows, 128)), full((rows, 128))],
        out_specs=[lead((3, rows, 128))] * 3,
        out_shape=[sds((heads, rows, 128), BF)] * 3,
        compiler_params=BIG,
        name="qkv",
    )(x, w, cos, sin)
    ko, vo = lax.ppermute((k, v), "core", [(0, 1), (1, 0)])
    return attend(x, (q, k, v, ko, vo), w, norms, mask)


def attend(x, joint, w, norms, mask):
    gains, biases = norms
    q, k, v, ko, vo = joint
    rows, width = x.shape
    heads = width // 128
    blocks, tp, depth, columns = w.shape
    pair = lead((1, rows, 128))
    o, e, l = pl.pallas_call(
        attn_kernel,
        grid=(heads,),
        in_specs=[pair] * 5 + [full((2 * rows, rows))],
        out_specs=[pair, lead((1, 2, 2 * rows, rows)), lead((1, 2, 8, rows))],
        out_shape=[sds((heads, rows, 128), BF), sds((heads, 2, 2 * rows, rows), BF), sds((heads, 2, 8, rows), F32)],
        compiler_params=BIG,
        name="attn",
    )(q, k, v, ko, vo, mask)
    groups = (columns - width) // GROUP
    units = tp * 128
    y, gu, n1, i1, n2, i2 = pl.pallas_call(
        ffn_kernel,
        grid=(groups,),
        in_specs=[
            full((rows, width)),
            full((heads, rows, 128)),
            pl.BlockSpec((blocks, tp, depth, 256), lambda i: (0, 0, 0, 2)),
            group_block(w),
            full((2, width)),
            full((2, width)),
        ],
        out_specs=[full((rows, width)), lead((1, 2, rows, units))] + [full((rows, width)), full((rows, 128))] * 2,
        out_shape=[sds((rows, width), BF), sds((groups, 2, rows, units), BF)] + [sds((rows, width), BF), sds((rows, 128), F32)] * 2,
        scratch_shapes=[VM((rows, width), F32), VM((rows, width), BF), VM((rows, width), F32)],
        compiler_params=BIG,
        name="ffn",
    )(x, o, w, w, gains, biases)
    return y, (q, k, v, ko, vo, o, e, l, gu, n1, i1, n2, i2)


def ffn_backward(dy, kept, w, norms, grads):
    gains, biases = norms
    gu, n1, i1, n2, i2 = kept[8:]
    rows, width = dy.shape
    blocks, tp, depth, columns = w.shape
    groups = (columns - width) // GROUP
    whole, stat = full((rows, width)), full((rows, 128))
    outs = [whole, whole]
    shapes = [sds((rows, width), F32), sds((rows, width), BF)]
    scratch = [VM((rows, width), BF), VM((rows, width), F32)]
    if grads:
        outs = [group_block(w)] + outs + [full((8, width))]
        shapes = [sds(w.shape, BF)] + shapes + [sds((8, width), F32)]
        scratch = [VM((rows, width), BF)] + scratch
    return pl.pallas_call(
        functools.partial(ffn_back_kernel, grads),
        grid=(groups,),
        in_specs=[
            whole, whole, stat, whole, stat,
            lead((1, 2, rows, tp * 128)),
            group_block(w),
            full((2, width)), full((2, width)),
        ],
        out_specs=outs,
        out_shape=shapes,
        scratch_shapes=scratch,
        compiler_params=BIG,
        name="ffn_back" if grads else "ffn_back_light",
    )(dy, n1, i1, n2, i2, gu, w, gains, biases)


def attn_backward(x, da, dr1, g, kept, w, tabs):
    grads = g is not None
    q, k, v, ko, vo, o, e, l = kept[:8]
    rows, width = da.shape
    heads = width // 128
    blocks, tp, depth, columns = w.shape
    steps = tp // 2
    cos, sin, cost, sint = tabs
    whole = full((rows, width))
    three = lead((3, rows, 128))
    side = lead((3, 2, 128, rows))
    table = full((HD // 2, rows))
    extra = [lead((1, width, 384))] if grads else []
    dq, own, oth, *dwo = pl.pallas_call(
        functools.partial(attn_back_kernel, grads),
        grid=(steps,),
        in_specs=[
            whole,
            pl.BlockSpec((blocks, 2, depth, 256), lambda i: (0, i, 0, 2)),
            three, three, three, three, three, three,
            lead((3, 2, 2 * rows, rows)),
            lead((3, 2, 8, rows)),
            table, table,
        ],
        out_specs=[three, side, side] + extra,
        out_shape=[
            sds((heads, rows, 128), BF),
            sds((heads, 2, 128, rows), F32),
            sds((heads, 2, 128, rows), BF),
        ]
        + ([sds((steps, width, 384), BF)] if grads else []),
        compiler_params=BIG,
        name="attn_back",
    )(da, w, o, q, k, v, ko, vo, e, l, cost, sint)
    got = lax.ppermute(oth, "core", [(0, 1), (1, 0)])
    if grads:
        specs = [pl.BlockSpec(memory_space=pl.ANY), whole, joint_block(w), whole, three, side, side] + extra
        args = (g, x, w, dr1, dq, own, got, *dwo)
        outs, shapes = [joint_block(w), whole], [sds(w.shape, BF), sds((rows, width), F32)]
    else:
        specs = [joint_block(w), whole, three, side, side]
        args = (w, dr1, dq, own, got)
        outs, shapes = [whole, whole], [sds((rows, width), F32), sds((rows, width), BF)]
    return pl.pallas_call(
        functools.partial(joint_back_kernel, grads),
        grid=(steps,),
        in_specs=specs + [table, table],
        out_specs=outs,
        out_shape=shapes,
        input_output_aliases={0: 0} if grads else {},
        compiler_params=BIG,
        name="joint_back",
    )(*args, cost, sint)


PAIRS = 6
FIRST_PAIR = 6
FIRST_JOINT = 12
LAST_STEP = 13


FAR = 2
FAR_AT = 4
def last_kernel(
    parts, n1_ref, i1_ref, n2_ref, i2_ref, gu_ref, wa_ref, norm_ref,
    q_ref, k_ref, v_ref, ko_ref, vo_ref, l_ref, cos_ref, sin_ref, dy_hbm, x_hbm, y_hbm, e_hbm, o_hbm, w_hbm,
    joint_out, mix_out, pair_out, down_out, ends_out, norm_out,
    acc, df, hb, o_ref, wb_ref, ring, do3, dwo, dq, keep, oth, got, eb, e_send, e_land, tmp, land_c, land_y, land_r, land_l, land_n,
    z_sum, far_y, far_r, far_l,
    o_sem, wb_sem, dy_sem, x_sem, y_sem, e_sem, oth_send, oth_recv, end_sem, end_send, end_recv,
    cs_sem, cr_sem, ys_sem, yr_sem, rs_sem, rr_sem, ls_sem, lr_sem, ns_sem, nr_sem,
    fys_sem, fyr_sem, frs_sem, frr_sem, fls_sem, flr_sem,
):
    step = pl.program_id(0)
    section = lax.axis_index("section")
    y, c, z = lax.axis_index("y"), lax.axis_index("core"), lax.axis_index("tensor")
    last = 3
    rows, width = acc.shape
    early = parts - width // WIDE
    usual = parts - FAR
    near, across = {"core": 1 - c}, {"y": 1 - y}
    right, left = {"tensor": jnp.minimum(z + 1, last)}, {"tensor": jnp.maximum(z - 1, 0)}
    pair = {"tensor": z + 1 - 2 * lax.rem(z, 2)}
    far = {"tensor": lax.rem(z + 2, 4)}
    side = z // 2
    barrier = pltpu.get_barrier_semaphore()

    def greet(device):
        pl.semaphore_signal(barrier, inc=1, device_id=device, device_id_type=MESH)

    def remote(src, dst, send, recv, device):
        return pltpu.make_async_remote_copy(src, dst, send, recv, device_id=device, device_id_type=MESH)

    def target(i):
        return {"core": side, "tensor": 2 * c + i}

    def at_home(i):
        return jnp.logical_and(side == c, 2 * c + i == z)

    def end_copy(i, part):
        return remote(e_send.at[i, part], e_land.at[z % 2, part], end_send.at[i], end_recv.at[z % 2], target(i))

    def end_home(i):
        return pltpu.make_async_copy(e_send.at[i], e_land.at[z % 2], end_sem)

    def oth_copy(p):
        return remote(oth.at[p], got.at[p], oth_send.at[p], oth_recv.at[p], near)

    dy_copy = pltpu.make_async_copy(dy_hbm, e_send, dy_sem)
    x_copy = pltpu.make_async_copy(x_hbm, hb, x_sem)
    o_copy = pltpu.make_async_copy(o_hbm, o_ref, o_sem)
    wb_copy = pltpu.make_async_copy(w_hbm.at[:, :, :, pl.ds(GROUP, GROUP)], wb_ref, wb_sem)
    y_copy = pltpu.make_async_copy(y_hbm, e_send, y_sem)

    def probs_copy(p):
        return pltpu.make_async_copy(e_hbm.at[p], eb, e_sem)

    def columns(j):
        return pl.ds(pl.multiple_of(j * WIDE, WIDE), WIDE)

    def slot(j):
        return (j // 3) % 2, columns(j % 3)

    def chunk(j):
        return j + FAR * ((j + usual - FAR_AT) // usual)

    def to_core(j):
        r, cols = slot(j)
        return remote(ring.at[r, :, 1 - c, :, :, cols], land_c.at[j], cs_sem.at[j], cr_sem.at[j], near)

    def to_y(j):
        return remote(land_c.at[chunk(j), 1 - y], land_y.at[j], ys_sem.at[j], yr_sem.at[j], across)

    def norm_copy(k):
        return remote(land_n.at[2 * k], land_n.at[2 * k + 1], ns_sem.at[k], nr_sem.at[k], (near, across, pair, far)[k])

    def go_right(j, first, src):
        return remote(src, land_r.at[j, pl.ds(first - 1, 4 - first)], rs_sem.at[j], rr_sem.at[j], right)

    def go_left(j, count, src):
        return remote(src, land_l.at[j, pl.ds(0, count)], ls_sem.at[j], lr_sem.at[j], left)

    def stage(i, lag, body):
        @pl.when(jnp.logical_and(i >= lag, i - lag < usual))
        def _():
            body(i - lag)

    def add_core(j):
        r, cols = slot(j)
        to_core(j).wait()
        land_c[j] = land_c[j] + ring[r, :, c, :, :, cols]

    def far_right(b, first, src):
        return remote(src, far_r.at[b, :, pl.ds(first - 1, 4 - first)], frs_sem.at[b], frr_sem.at[b], right)

    def far_left(b, count, src):
        return remote(src, far_l.at[b, :, pl.ds(0, count)], fls_sem.at[b], flr_sem.at[b], left)

    def far_across(b):
        return remote(z_sum.at[b, 1 - y], far_y.at[b], fys_sem.at[b], fyr_sem.at[b], across)

    def far_first(b):
        j = FAR_AT + b

        @pl.when(z == 0)
        def _():
            far_right(b, 1, land_c.at[j, :, pl.ds(1, 3)]).start()

        @pl.when(z == last)
        def _():
            far_left(b, 3, land_c.at[j, :, pl.ds(0, 3)]).start()

    def far_next(b):
        j = FAR_AT + b

        @pl.when(z == 1)
        def _():
            far_right(b, 1, far_r.at[b]).wait_recv()
            for k in (2, 3):
                far_r[b, :, k - 1] = far_r[b, :, k - 1] + land_c[j, :, k]
            far_right(b, 2, far_r.at[b, :, pl.ds(1, 2)]).start()

        @pl.when(z == 2)
        def _():
            far_left(b, 3, far_l.at[b]).wait_recv()
            for k in (0, 1):
                far_l[b, :, k] = far_l[b, :, k] + land_c[j, :, k]
            far_left(b, 2, far_l.at[b, :, pl.ds(0, 2)]).start()

    def far_last(b):
        j = FAR_AT + b

        @pl.when(z == 1)
        def _():
            far_left(b, 2, far_l.at[b, :, pl.ds(0, 2)]).wait_recv()
            far_l[b, :, 0] = far_l[b, :, 0] + land_c[j, :, 0]
            far_left(b, 1, far_l.at[b, :, pl.ds(0, 1)]).start()

        @pl.when(z == 2)
        def _():
            far_right(b, 2, far_r.at[b, :, pl.ds(1, 2)]).wait_recv()
            far_r[b, :, 2] = far_r[b, :, 2] + land_c[j, :, 3]
            far_right(b, 3, far_r.at[b, :, pl.ds(2, 1)]).start()

    def far_sum(b):
        mine = land_c[FAR_AT + b, :, z]

        @pl.when(z == 0)
        def _():
            far_left(b, 1, far_l.at[b, :, pl.ds(0, 1)]).wait_recv()
            z_sum[b] = mine + far_l[b, :, 0]

        @pl.when(z == 1)
        def _():
            z_sum[b] = mine + far_r[b, :, 0] + far_l[b, :, 1]

        @pl.when(z == 2)
        def _():
            z_sum[b] = mine + far_r[b, :, 1] + far_l[b, :, 2]

        @pl.when(z == last)
        def _():
            far_right(b, 3, far_r.at[b, :, pl.ds(2, 1)]).wait_recv()
            z_sum[b] = mine + far_r[b, :, 2]

    def far_result(b):
        far_across(b).wait_recv()
        tmp[...] = z_sum[b, y].astype(F32) + far_y[b].astype(F32)
        emit(FAR_AT + b)

    def last_hop(j):
        @pl.when(z == 1)
        def _():
            go_left(j, 2, land_l.at[j, pl.ds(0, 2)]).wait_recv()
            land_l[j, 0] = land_l[j, 0] + land_c[chunk(j), y, 0]
            go_left(j, 1, land_l.at[j, pl.ds(0, 1)]).start()

        @pl.when(z == 2)
        def _():
            go_right(j, 2, land_r.at[j, pl.ds(1, 2)]).wait_recv()
            land_r[j, 2] = land_r[j, 2] + land_c[chunk(j), y, 3]
            go_right(j, 3, land_r.at[j, pl.ds(2, 1)]).start()

    def next_hop(j):
        @pl.when(z == 1)
        def _():
            go_right(j, 1, land_r.at[j]).wait_recv()
            for k in (2, 3):
                land_r[j, k - 1] = land_r[j, k - 1] + land_c[chunk(j), y, k]
            go_right(j, 2, land_r.at[j, pl.ds(1, 2)]).start()

        @pl.when(z == 2)
        def _():
            go_left(j, 3, land_l.at[j]).wait_recv()
            for k in (0, 1):
                land_l[j, k] = land_l[j, k] + land_c[chunk(j), y, k]
            go_left(j, 2, land_l.at[j, pl.ds(0, 2)]).start()

    def first_hop(j):
        to_y(j).wait_recv()
        land_c[chunk(j), y] = land_c[chunk(j), y] + land_y[j]

        @pl.when(z == 0)
        def _():
            go_right(j, 1, land_c.at[chunk(j), y, pl.ds(1, 3)]).start()

        @pl.when(z == last)
        def _():
            go_left(j, 3, land_c.at[chunk(j), y, pl.ds(0, 3)]).start()

    def result(j):
        mine = land_c[chunk(j), y, z].astype(F32)

        @pl.when(z == 0)
        def _():
            go_left(j, 1, land_l.at[j, pl.ds(0, 1)]).wait_recv()
            tmp[...] = mine + land_l[j, 0].astype(F32)

        @pl.when(z == 1)
        def _():
            tmp[...] = mine + land_r[j, 0].astype(F32) + land_l[j, 1].astype(F32)

        @pl.when(z == 2)
        def _():
            tmp[...] = mine + land_r[j, 1].astype(F32) + land_l[j, 2].astype(F32)

        @pl.when(z == last)
        def _():
            go_right(j, 3, land_r.at[j, pl.ds(2, 1)]).wait_recv()
            tmp[...] = mine + land_r[j, 2].astype(F32)

        emit(chunk(j))

    def emit(j):
        group = j // 3

        @pl.when(jnp.logical_and(j < early, j % 3 == 0))
        def _():
            down_out[:, columns(group)] = tmp[...]

        for m in (1, 2):

            @pl.when(jnp.logical_and(j < early, j % 3 == m))
            def _():
                pair_out[:, columns(group + (m - 1) * (early // 3))] = tmp[...]

        for odd in range(2):
            two = slice(HD, 3 * HD) if odd else slice(0, 2 * HD)
            one = slice(0, HD) if odd else slice(2 * HD, 3 * HD)

            def when(n, body, odd=odd):
                pl.when(jnp.logical_and(j == early + n, z % 2 == odd))(body)

            def store(out, place, part):
                def body():
                    out[:, place] = tmp[:, part]

                return body

            def turn(place, part):
                def body():
                    mix_out[place, :] = tmp[...].T[part]

                return body

            whole, low, high = slice(0, 128), slice(0, HD), slice(HD, 128)
            for n in range(3):
                when(n, store(joint_out.at[n], two, whole))
            when(3, store(joint_out.at[0], one, low))
            when(3, store(joint_out.at[1], one, high))
            when(4, store(joint_out.at[2], one, low))
            when(4, turn(one, high))
            when(5, turn(two, whole))

    def round_(i):
        stage(i, 0, lambda j: to_y(j).start())
        stage(i, 6, last_hop)
        stage(i, 4, next_hop)
        stage(i, 2, first_hop)
        stage(i, 8, result)
        for b in range(FAR):
            rounds = (4 + 3 * b, 7 + 3 * b, 10 + 3 * b, 13 + 3 * b, usual - 1 + b, usual + 3 + b)
            bodies = (far_first, far_next, far_last, far_sum, lambda b: far_across(b).start(), far_result)
            for at, body in zip(rounds, bodies):
                pl.when(i == at)(functools.partial(body, b))

        for k in range(4):

            @pl.when(i == 3 * k + 8)
            def _():
                norm_copy(k).wait()
                total = land_n[2 * k] + land_n[2 * k + 1]
                if k < 3:
                    land_n[2 * k + 2] = total
                    norm_copy(k + 1).start()
                else:
                    norm_out[...] = total

    @pl.when(step == 0)
    def _():
        dy_copy.start()
        o_copy.start()
        wb_copy.start()
        greet(near)
        greet(across)
        greet(far)

        @pl.when(z < last)
        def _():
            greet(right)

        @pl.when(z > 0)
        def _():
            greet(left)

        for i in range(2):

            @pl.when(jnp.logical_not(at_home(i)))
            def _():
                greet(target(i))

        count = 5 + jnp.where(z < last, 1, 0) + jnp.where(z > 0, 1, 0) - jnp.where(side == c, 1, 0)
        pl.semaphore_wait(barrier, count)
        dy_copy.wait()
        dy = e_send[...].reshape(rows, width).astype(F32)
        n = n2_ref[...].astype(F32)
        land_n[0] = jnp.zeros(land_n.shape[1:], F32)
        land_n[0, 1:2] = jnp.sum(dy * n, axis=0, keepdims=True)
        land_n[0, 3:4] = jnp.sum(dy, axis=0, keepdims=True)
        dr2 = norm_back(dy * norm_ref[1:2], n, i2_ref[:, :1])
        acc[...] = dr2
        df[...] = dr2.astype(BF)
        hb[...] = (n1_ref[...].astype(F32) * norm_ref[0:1] + norm_ref[2:3]).astype(BF)

    @pl.when(step < FIRST_PAIR)
    def _():
        gate = gu_ref[0, 0].astype(F32)
        up = gu_ref[0, 1].astype(F32)
        s = 1.0 / (1.0 + jnp.exp(-gate))
        silu = gate * s
        wd, wg, wu = unit_weights(lambda t, m: wa_ref[:, t, :, 128 * m : 128 * m + 128].reshape(width, 128))
        place = step % 2

        def put(m, grad):
            for t in range(4):
                ring[place, :, :, t, :, 128 * m : 128 * m + 128] = (
                    grad[:, 128 * t : 128 * t + 128].astype(BF).reshape(2, 2, -1, 128)
                )

        j = 3 * step

        def earlier(m):
            pl.when(step > (1 if m == 0 else 0))(lambda: add_core(j - 3 + m))

        put(0, dg(df[...], (silu * up).astype(BF), TN))
        to_core(j).start()
        earlier(0)
        d_act = dg(df[...], wd, NN)
        d_gate = (d_act * up * (s * (1.0 + gate * (1.0 - s)))).astype(BF)
        d_up = (d_act * silu).astype(BF)
        put(1, dg(hb[...], d_gate, TN))
        to_core(j + 1).start()
        earlier(1)

        @pl.when(step == 0)
        def _():
            add_core(0)
            round_(0)

        put(2, dg(hb[...], d_up, TN))
        to_core(j + 2).start()
        earlier(2)
        acc[...] += dg(d_gate, wg, NT) + dg(d_up, wu, NT)

    @pl.when(step == FIRST_PAIR - 1)
    def _():
        dh = acc[...]
        n = n1_ref[...].astype(F32)
        land_n[0, 0:1] = jnp.sum(dh * n, axis=0, keepdims=True)
        land_n[0, 2:3] = jnp.sum(dh, axis=0, keepdims=True)
        dr1 = norm_back(dh * norm_ref[0:1], n, i1_ref[:, :1])
        acc[...] = dr1
        df[...] = dr1.astype(BF)
        x_copy.start()
        probs_copy(0).start()
        norm_copy(0).start()

    cos, sin = cos_ref[:, pl.ds(c * rows, rows)], sin_ref[:, pl.ds(c * rows, rows)]
    in_pairs = jnp.logical_and(step >= FIRST_PAIR, step < FIRST_JOINT)
    p = step - FIRST_PAIR

    @pl.when(step == FIRST_PAIR)
    def _():
        for m in range(3):
            add_core(3 * FIRST_PAIR - 3 + m)
        o_copy.wait()
        wb_copy.wait()

    @pl.when(jnp.logical_and(in_pairs, p % 3 == 0))
    def _():
        w = jnp.concatenate(out_weight(wb_ref.at[:, pl.ds(2 * (p // 3), 2), :, 128:384]), axis=1)
        t = dg(df[...], w, NN).astype(BF)
        for i in range(3):
            do3[i] = t[:, 128 * i : 128 * i + 128]
        o3 = jnp.concatenate([o_ref[p + i] for i in range(3)], axis=1)
        dwo[p // 3] = dg(df[...], o3, TN).astype(BF)

    @pl.when(in_pairs)
    def _():
        probs_copy(p).wait()
        dqt, dk, dv = pair_back(
            do3[p % 3], o_ref[p], q_ref[0], k_ref[0], v_ref[0], ko_ref[0], vo_ref[0],
            [eb.at[h] for h in range(2)], [l_ref[0, h, 0:1] for h in range(2)], cos, sin,
        )
        dq[p] = dqt.T.astype(BF)
        keep[p, 0] = dk[:, :rows].astype(BF)
        keep[p, 1] = dv[:, :rows].astype(BF)
        oth[p, 0] = dk[:, rows:].astype(BF)
        oth[p, 1] = dv[:, rows:].astype(BF)
        oth_copy(p).start()

        @pl.when(p + 1 < PAIRS)
        def _():
            probs_copy(p + 1).start()

    @pl.when(step >= FIRST_JOINT)
    def _():
        half = step - FIRST_JOINT

        @pl.when(half == 0)
        def _():
            x_copy.wait()

        for i in range(3):
            oth_copy(3 * half + i).wait()
        d = joint_parts(
            [dq[3 * half + i].astype(F32) for i in range(3)],
            [keep[3 * half + i, 0].astype(F32) + got[3 * half + i, 0].astype(F32) for i in range(3)],
            [keep[3 * half + i, 1].astype(F32) + got[3 * half + i, 1].astype(F32) for i in range(3)],
            cos, sin,
        )
        total = None
        wlow = low_lanes((width, 128))
        mid = dwo[half, :, 128:256].astype(F32)
        sides = [dwo[half, :, 0:128], dwo[half, :, 256:384]]
        mids = [swap64(mid), mid]
        shape = (2, 2, width // 4)
        for e in range(2):
            t = 2 * half + e
            w = jnp.concatenate([wa_ref[:, t].reshape(width, GROUP), wb_ref[:, t, :, :256].reshape(width, 256)], axis=1)
            part = dg(d[e], w, NT)
            total = part if total is None else total + part
            g = dg(hb[...], d[e], TN)
            ring[0, :, :, t] = g[:, :GROUP].astype(BF).reshape(shape + (GROUP,))
            ring[1, :, :, t, :, :128] = g[:, GROUP:512].astype(BF).reshape(shape + (128,))
            ring[1, :, :, t, :, 128:256] = jnp.where(wlow, g[:, 512:], mids[e]).astype(BF).reshape(shape + (128,))
            ring[1, :, :, t, :, 256:] = sides[e].reshape(shape + (128,))
        acc[...] += total

    @pl.when(step == LAST_STEP)
    def _():
        lax.fori_loop(early, parts, lambda j, t: (to_core(j).start(), t)[1], 0)

        @pl.when(section == 0)
        def _():
            e_send[...] = acc[...].astype(BF).reshape(e_send.shape)

        @pl.when(section == 1)
        def _():
            y_copy.start()
            y_copy.wait()

        for i in range(2):

            @pl.when(at_home(i))
            def _():
                end_home(i).start()

    @pl.when(step == 1)
    def _():
        round_(1)

    @pl.when(step >= 1)
    def _():
        round_(step + 1)

    @pl.when(step == LAST_STEP)
    def _():
        lax.fori_loop(early, parts, lambda j, t: (add_core(j), t)[1], 0)
        end_rows = e_send.shape[1] // 8

        def late(i, carry):
            part = pl.ds(pl.multiple_of((i - LAST_STEP - 2) * end_rows, end_rows), end_rows)
            for k in range(2):

                @pl.when(jnp.logical_not(at_home(k)))
                def _():
                    end_copy(k, part).start()

            round_(i)
            return carry

        lax.fori_loop(LAST_STEP + 2, LAST_STEP + 10, late, 0)
        lax.fori_loop(LAST_STEP + 10, usual + 8, lambda i, t: (round_(i), t)[1], 0)
        for i in range(2):

            @pl.when(at_home(i))
            def _():
                end_home(i).wait()

            @pl.when(jnp.logical_not(at_home(i)))
            def _():
                end_copy(i, pl.ds(0, e_send.shape[1])).wait_send()
                remote(e_send.at[i], e_land.at[i], end_send.at[i], end_recv.at[i], target(i)).wait_recv()

        ends_out[...] = e_land[...]

        def finish(j, carry):
            to_y(j).wait_send()

            @pl.when(z == 0)
            def _():
                go_right(j, 1, land_c.at[chunk(j), y, pl.ds(1, 3)]).wait_send()

            @pl.when(z == 1)
            def _():
                go_right(j, 2, land_r.at[j, pl.ds(1, 2)]).wait_send()
                go_left(j, 1, land_l.at[j, pl.ds(0, 1)]).wait_send()

            @pl.when(z == 2)
            def _():
                go_right(j, 3, land_r.at[j, pl.ds(2, 1)]).wait_send()
                go_left(j, 2, land_l.at[j, pl.ds(0, 2)]).wait_send()

            @pl.when(z == last)
            def _():
                go_left(j, 3, land_c.at[chunk(j), y, pl.ds(0, 3)]).wait_send()

            return carry

        lax.fori_loop(0, usual, finish, 0)

        def finish_far(b, carry):
            j = FAR_AT + b
            far_across(b).wait_send()

            @pl.when(z == 0)
            def _():
                far_right(b, 1, land_c.at[j, :, pl.ds(1, 3)]).wait_send()

            @pl.when(z == 1)
            def _():
                far_right(b, 2, far_r.at[b, :, pl.ds(1, 2)]).wait_send()
                far_left(b, 1, far_l.at[b, :, pl.ds(0, 1)]).wait_send()

            @pl.when(z == 2)
            def _():
                far_right(b, 3, far_r.at[b, :, pl.ds(2, 1)]).wait_send()
                far_left(b, 2, far_l.at[b, :, pl.ds(0, 2)]).wait_send()

            @pl.when(z == last)
            def _():
                far_left(b, 3, land_c.at[j, :, pl.ds(0, 3)]).wait_send()

            return carry

        lax.fori_loop(0, FAR, finish_far, 0)


def last_back(x, y, dy, kept, w, norms, cost, sint):
    q, k, v, ko, vo, o, e, l, gu, n1, i1, n2, i2 = kept
    rows, width = x.shape
    heads = width // 128
    depth, columns = w.shape[2:]
    parts = columns // WIDE
    units = (columns - width) // 3
    dma = pltpu.SemaphoreType.DMA
    hbm = pl.BlockSpec(memory_space=pl.ANY)
    halves = (2, rows // 2, width)

    def once(shape, at=None):
        return pl.BlockSpec(shape, lambda i: at or (0,) * len(shape), pipeline_mode=pl.Buffered(1))

    def by_pair(shape):
        return pl.BlockSpec(shape, lambda i: (jnp.clip(i - FIRST_PAIR, 0, PAIRS - 1),) + (0,) * (len(shape) - 1))

    pair = by_pair((1, rows, 128))
    group = (4, 4, depth, GROUP)
    return pl.pallas_call(
        functools.partial(last_kernel, parts),
        grid=(LAST_STEP + 1,),
        in_specs=[
            once((rows, width)), once((rows, 128)), once((rows, width)), once((rows, 128)),
            pl.BlockSpec((1, 2, rows, 512), lambda i: (jnp.minimum(i, FIRST_PAIR - 1), 0, 0, 0)),
            pl.BlockSpec(group, lambda i: (0, 0, 0, jnp.where(i < FIRST_PAIR, 2 + i, 0))),
            once((4, width)),
            pair, pair, pair, pair, pair,
            by_pair((1, 2, 8, rows)),
            once(cost.shape), once(sint.shape),
            hbm, hbm, hbm, hbm, hbm, hbm,
        ],
        out_specs=[
            once((3, depth, depth)), once((depth, depth)), once((depth, 2 * units)), once((depth, units)), once(halves), once((8, width)),
        ],
        out_shape=[
            sds((3, depth, depth), F32), sds((depth, depth), F32), sds((depth, 2 * units), F32), sds((depth, units), F32),
            sds(halves, BF), sds((8, width), F32),
        ],
        scratch_shapes=[
            VM((rows, width), F32),
            VM((rows, width), BF),
            VM((rows, width), BF),
            VM((heads, rows, 128), BF),
            VM(group, BF),
            VM((2, 2, 2, 4, depth, GROUP), BF),
            VM((3, rows, 128), BF),
            VM((2, width, 384), BF),
            VM((heads, rows, 128), BF),
            VM((heads, 2, 128, rows), BF),
            VM((heads, 2, 128, rows), BF),
            VM((heads, 2, 128, rows), BF),
            VM((2, 2 * rows, rows), BF),
            VM(halves, BF),
            VM(halves, BF),
            VM((depth, WIDE), F32),
            VM((parts, 2, 4, depth, WIDE), BF),
            VM((parts - FAR, 4, depth, WIDE), BF),
            VM((parts - FAR, 3, depth, WIDE), BF),
            VM((parts - FAR, 3, depth, WIDE), BF),
            VM((8, 8, width), F32),
            VM((FAR, 2, depth, WIDE), BF),
            VM((FAR, depth, WIDE), BF),
            VM((FAR, 2, 3, depth, WIDE), BF),
            VM((FAR, 2, 3, depth, WIDE), BF),
            dma, dma, dma, dma, dma, dma,
            dma((6,)), dma((6,)), dma, dma((2,)), dma((2,)),
        ]
        + [dma((parts,))] * 8
        + [dma((4,))] * 2
        + [dma((FAR,))] * 6,
        compiler_params=pltpu.CompilerParams(collective_id=0, has_side_effects=True, vmem_limit_bytes=63 << 20),
        name="last",
    )(n1, i1, n2, i2, gu, w, norms, q, k, v, ko, vo, l, cost, sint, dy.reshape(halves), x, y.reshape(halves), e, o, w)


LAG = 6
GATHER = 256


def first_kernel(
    parts, tok_ref, top_ref, lead_ref, down_ref, pair_ref, gain_ref, bias_ref, len_ref, cos_ref, sin_ref, cost_ref, sint_ref,
    w_out, q_out, k_out, v_out, ko_out, vo_out, y_out, e_out, o_out, gu_out, n1_out, n2_out,
    x_out, dy_out, l_out, i1_out, i2_out, norm_out,
    w, xin, q, kv, land_kv, late_kv, o, hb, acc, relay, land_rows, ext, lens,
    mask, eb, gu, n1, n2, df, do3, dq, keep, oth, got, d,
    tok_sem, tok_send, tok_recv, lead_sem, shard_sem, back_sem, kv_send, kv_recv, out_sem, row_send, row_recv, again_send, again_recv,
    e_sem, gu_sem, oth_send, oth_recv, dz_send, dz_recv,
    small_send, small_recv, rs_sem, rr_sem, ls_sem, lr_sem, ys_sem, yr_sem, cs_sem, cr_sem,
):
    section = lax.axis_index("section")
    y, c, z = lax.axis_index("y"), lax.axis_index("core"), lax.axis_index("tensor")
    last = 3
    rows, width = xin.shape[0] * xin.shape[1], xin.shape[2]
    near, across, other = {"core": 1 - c}, {"y": 1 - y}, {"section": 1 - section}
    right, left = {"tensor": jnp.minimum(z + 1, last)}, {"tensor": jnp.maximum(z - 1, 0)}
    side = z // 2
    barrier = pltpu.get_barrier_semaphore()

    def greet(device):
        pl.semaphore_signal(barrier, inc=1, device_id=device, device_id_type=MESH)

    def remote(src, dst, send, recv, device):
        return pltpu.make_async_remote_copy(src, dst, send, recv, device_id=device, device_id_type=MESH)

    def target(i):
        return {"core": side, "tensor": 2 * c + i}

    def at_home(i):
        return jnp.logical_and(side == c, 2 * c + i == z)

    def token_copy(src, i, part):
        return remote(src.at[i, part], xin.at[z % 2, part], tok_send.at[i], tok_recv.at[z % 2], target(i))

    def token_home(src, i):
        return pltpu.make_async_copy(src.at[i], xin.at[z % 2], tok_sem)

    def by_section(body):
        for n, src in enumerate((tok_ref, top_ref)):
            pl.when(section == n)(functools.partial(body, src))

    groups = down_ref.shape[1] // 128

    def load_group(k, m):
        src = down_ref if m == 0 else pair_ref
        cols = pl.ds(128 * (k + (m - 1) * groups if m else k), 128)
        return pltpu.make_async_copy(src.at[:, cols], w.at[y, c, z, :, pl.ds(width + GROUP * k + 128 * m, 128)], shard_sem.at[k, m])

    load_lead = pltpu.make_async_copy(lead_ref, w.at[y, c, z, :, pl.ds(0, width)], lead_sem)
    load_lead.start()
    loads = [load_group(k, m) for k in range(groups) for m in range(3)]
    for load in loads:
        load.start()
    greet(near)
    greet(across)
    greet(other)

    @pl.when(z < last)
    def _():
        greet(right)

    @pl.when(z > 0)
    def _():
        greet(left)

    for i in range(2):

        @pl.when(jnp.logical_not(at_home(i)))
        def _():
            greet(target(i))

    count = 5 + jnp.where(z < last, 1, 0) + jnp.where(z > 0, 1, 0) - jnp.where(side == c, 1, 0)
    pl.semaphore_wait(barrier, count)

    ext[y, c, 0:1] = gain_ref[...].astype(F32)
    ext[y, c, 1:2] = bias_ref[...].astype(F32)
    lens[c] = len_ref[...]

    def small(k):
        if k == 0:
            return remote(lens.at[c], lens.at[c], small_send.at[0], small_recv.at[0], near)
        if k == 1:
            return remote(ext.at[y, c], ext.at[y, c], small_send.at[1], small_recv.at[1], across)
        return remote(ext.at[:, c], ext.at[:, c], small_send.at[2], small_recv.at[2], near)

    small(0).start()
    small(1).start()
    load_lead.wait()
    for load in loads:
        load.wait()

    def columns(j):
        return pl.ds(pl.multiple_of(j * GATHER, GATHER), GATHER)

    def go_right(j, h):
        b = jnp.maximum(z - h, 0)
        return remote(w.at[y, c, b, :, columns(j)], w.at[y, c, b, :, columns(j)], rs_sem.at[j, h], rr_sem.at[j, h], right)

    def go_left(j, h):
        b = jnp.minimum(z + h, last)
        return remote(w.at[y, c, b, :, columns(j)], w.at[y, c, b, :, columns(j)], ls_sem.at[j, h], lr_sem.at[j, h], left)

    def to_y(j):
        return remote(w.at[y, c, :, :, columns(j)], w.at[y, c, :, :, columns(j)], ys_sem.at[j], yr_sem.at[j], across)

    def block_to_y(j, b):
        return remote(w.at[y, c, b, :, columns(j)], w.at[y, c, b, :, columns(j)], ys_sem.at[j], yr_sem.at[j], across)

    def to_core(j):
        return remote(w.at[:, c, :, :, columns(j)], w.at[:, c, :, :, columns(j)], cs_sem.at[j], cr_sem.at[j], near)

    def write_back(j):
        return pltpu.make_async_copy(w.at[:, :, :, :, columns(j)], w_out.at[:, :, :, :, columns(j)], back_sem.at[j])

    def stage(r, lag, body):
        @pl.when(jnp.logical_and(r >= lag, r - lag < parts))
        def _():
            body(r - lag)

    def send_own(j):
        @pl.when(z < last)
        def _():
            go_right(j, 0).start()

        @pl.when(z > 0)
        def _():
            go_left(j, 0).start()

        block_to_y(j, z).start()

    def hop(h, j):
        @pl.when(z >= h)
        def _():
            go_right(j, h - 1).wait_recv()
            block_to_y(j, z - h).start()

        @pl.when(z + h <= last)
        def _():
            go_left(j, h - 1).wait_recv()
            block_to_y(j, z + h).start()

        if h < last:

            @pl.when(jnp.logical_and(z >= h, z < last))
            def _():
                go_right(j, h).start()

            @pl.when(jnp.logical_and(z + h <= last, z > 0))
            def _():
                go_left(j, h).start()

    def over_core(j):
        to_y(j).wait_recv()
        to_core(j).start()

    def complete(j):
        to_core(j).wait_recv()
        write_back(j).start()

    def round_(r):
        stage(r, 0, send_own)
        stage(r, 1, functools.partial(hop, 1))
        stage(r, 2, functools.partial(hop, 2))
        stage(r, 3, functools.partial(hop, 3))
        stage(r, 5, over_core)
        stage(r, LAG, complete)

    def rounds(first, end):
        lax.fori_loop(first, end, lambda r, t: (round_(r), t)[1], 0)

    start = 9
    token_rows = xin.shape[1] // 8
    for i in range(2):

        @pl.when(at_home(i))
        def _():
            by_section(lambda src: token_home(src, i).start())

    def early(r, carry):
        round_(r)
        part = pl.ds(pl.multiple_of(r * token_rows, token_rows), token_rows)
        for i in range(2):

            @pl.when(jnp.logical_not(at_home(i)))
            def _():
                by_section(lambda src: token_copy(src, i, part).start())

        return carry

    lax.fori_loop(0, 3, early, 0)
    small(0).wait()
    small(1).wait()
    small(2).start()

    mine = jnp.where(side == 0, lens[0], lens[1])
    mine = jnp.where(z % 2 == 0, mine[0:1], mine[1:2])
    at_q = c * rows + lax.broadcasted_iota(jnp.int32, (1, rows), 1)
    at_k = lax.broadcasted_iota(jnp.int32, (2 * rows, 1), 0)
    at_k = jnp.where(at_k < rows, c * rows + at_k, (1 - c) * rows + at_k - rows)
    seg_q, seg_k = jnp.zeros((1, rows), jnp.int32), jnp.zeros((2 * rows, 1), jnp.int32)
    end = jnp.zeros((1, 1), jnp.int32)
    for n in range(8):
        end = end + mine[:, n : n + 1]
        seg_q = seg_q + jnp.where(end <= at_q, 1, 0)
        seg_k = seg_k + jnp.where(end <= at_k, 1, 0)
    mask[...] = jnp.where(seg_k == seg_q, 0.0, neg_fill).astype(F32)
    lax.fori_loop(3, 8, early, 0)
    rounds(8, start)

    small(2).wait()
    for k in range(2):
        for half in range(2):
            norm_out[2 * k + half : 2 * k + half + 1] = jnp.concatenate([ext[half, i, k : k + 1] for i in range(2)], axis=1)

    for i in range(2):

        @pl.when(at_home(i))
        def _():
            token_home(tok_ref, i).wait()

        @pl.when(jnp.logical_not(at_home(i)))
        def _():
            token_copy(tok_ref, i, pl.ds(0, xin.shape[1])).wait_send()
            remote(tok_ref.at[i], xin.at[i], tok_send.at[i], tok_recv.at[i], target(i)).wait_recv()

    def project(at, count, x):
        here = pl.ds(at, count)
        cos, sin = cos_ref[pl.ds(c * rows + at, count)], sin_ref[pl.ds(c * rows + at, count)]
        low = low_lanes((count, 128))
        for p in range(2):
            r = [dg(x, w[:, :, 2 * p + e, :, :640].reshape(width, 640), NN) for e in range(2)]
            t = [[v[:, 128 * i : 128 * i + 128] for i in range(5)] for v in r]
            qs = [t[0][0], jnp.where(low, t[0][3], swap64(t[1][3])), t[1][0]]
            ks = [t[0][1], jnp.where(low, swap64(t[0][3]), t[1][3]), t[1][1]]
            vs = [t[0][2], jnp.where(low, t[0][4], swap64(t[1][4])), t[1][2]]
            for i in range(3):
                q[3 * p + i, here] = (rope_fwd(qs[i], cos, sin) * HD**-0.5).astype(BF)
                kv[0, 3 * p + i, here] = rope_fwd(ks[i], cos, sin).astype(BF)
                kv[1, 3 * p + i, here] = vs[i].astype(BF)

    x = xin[...].reshape(rows, width)
    x_out[...] = x
    project(0, rows, x)
    low = low_lanes((rows, 128))
    share = remote(kv, land_kv, kv_send.at[0], kv_recv.at[0], near)
    share.start()
    rounds(start, start + 1)
    share.wait()

    def heads_of(p, others, save):
        k = jnp.concatenate([kv[0, p], others[0, p]], axis=0)
        v = jnp.concatenate([kv[1, p], others[1, p]], axis=0)
        vt = v.astype(F32).T.astype(BF)
        ones = jnp.ones((16, 2 * rows), BF)
        outs = []
        for h in range(2):
            qm = jnp.where(low if h == 0 else jnp.logical_not(low), q[p], jnp.zeros((rows, 128), BF))
            s = dg(k, qm, NT) + mask[...]
            e = jnp.exp(s - jnp.max(s, axis=0, keepdims=True)).astype(BF)
            t = dg(jnp.concatenate([vt[HD * h : HD * h + HD], ones], axis=0), e, NN)
            inv = 1.0 / t[HD : HD + 1]
            save(h, e, inv)
            outs.append(t[:HD] * inv)
        o[p] = jnp.concatenate(outs, axis=0).T.astype(BF)

    def pair(p, carry):
        heads_of(p, land_kv, lambda h, e, inv: None)
        pl.when(p % 2 == 1)(functools.partial(round_, start + 1 + p // 2))
        return carry

    def out_part(p):
        wo = []
        for e in range(2):
            wo.append([w[:, :, 2 * p + e, :, 512 + 128 * i : 640 + 128 * i].reshape(width, 128) for i in range(2)])
        mid = jnp.where(low_lanes((width, 128)), swap64(wo[0][0].astype(F32)), wo[1][0].astype(F32)).astype(BF)
        return jnp.concatenate([wo[0][1], mid, wo[1][1]], axis=1)

    def mix(x):
        r = x.astype(F32)
        for p in range(2):
            r = r + dg(jnp.concatenate([o[3 * p + i] for i in range(3)], axis=1), out_part(p), NT)
        return norm_parts(r)

    def group_of(k):
        return unit_weights(
            lambda t, m: w[:, :, t, :, pl.ds(pl.multiple_of(width + GROUP * k + 128 * m, 128), 128)].reshape(width, 128)
        )

    def unit(k, save):
        wd, wg, wu = group_of(k)
        gate = dg(hb[...], wg, NN)
        up = dg(hb[...], wu, NN)
        save(gate, up)
        act = (gate / (1.0 + jnp.exp(-gate)) * up).astype(BF)
        acc[...] += dg(act, wd, NT)

    lax.fori_loop(0, 6, pair, 0)
    n, inv = mix(x)
    h = n * norm_out[0:1] + norm_out[2:3]
    hb[...] = h.astype(BF)
    acc[...] = h
    rounds(start + 4, start + 5)

    def units(k, carry):
        for at, r in ((2, 5), (4, 6), (4, 7), (5, 8)):
            pl.when(k == at)(functools.partial(round_, start + r))

        unit(k, lambda gate, up: None)
        return carry

    lax.fori_loop(0, 6, units, 0)
    pieces = relay.shape[0]
    piece_rows = rows // pieces

    def row_copy(b):
        return remote(relay.at[b], land_rows.at[b], row_send.at[b], row_recv.at[b], other)

    def again(b):
        part = pl.ds(pl.multiple_of(b * piece_rows, piece_rows), piece_rows)
        return remote(kv.at[:, :, part], late_kv.at[:, :, part], again_send.at[b], again_recv.at[b], near)

    kept_out = []

    def keep_out(src, dst):
        copy = pltpu.make_async_copy(src, dst, out_sem.at[len(kept_out)])
        kept_out.append(copy)
        copy.start()

    @pl.when(section == 0)
    def _():
        def send_rows(b, carry):
            part = pl.ds(pl.multiple_of(b * piece_rows, piece_rows), piece_rows)
            n, inv = norm_parts(acc[part])
            relay[b] = (n * norm_out[1:2] + norm_out[3:4]).astype(BF)
            row_copy(b).start()
            return carry

        lax.fori_loop(0, pieces, send_rows, 0)
        same = pltpu.make_async_copy(land_kv, late_kv, kv_send.at[1])
        same.start()
        same.wait()

    @pl.when(section == 1)
    def _():
        def project_rows(b, carry):
            at = pl.multiple_of(b * piece_rows, piece_rows)
            row_copy(b).wait_recv()
            x_out[pl.ds(at, piece_rows)] = land_rows[b]
            project(at, piece_rows, land_rows[b])
            again(b).start()
            return carry

        lax.fori_loop(0, pieces, project_rows, 0)
        lax.fori_loop(0, pieces, lambda b, t: (again(b).wait(), t)[1], 0)

    for src, dst in ((q, q_out), (kv.at[0], k_out), (kv.at[1], v_out), (late_kv.at[0], ko_out), (late_kv.at[1], vo_out)):
        keep_out(src, dst)

    def probs_out(p):
        return pltpu.make_async_copy(eb.at[p % 2], e_out.at[p], e_sem.at[p % 2])

    def probs_in(p):
        return pltpu.make_async_copy(e_out.at[p], eb.at[p % 2], e_sem.at[p % 2])

    def pair_kept(p, carry):
        @pl.when(p >= 2)
        def _():
            probs_out(p - 2).wait()

        def save(h, e, inv):
            eb[p % 2, h] = e
            l_out[p, h] = jnp.broadcast_to(inv, l_out.shape[2:])

        heads_of(p, late_kv, save)
        probs_out(p).start()
        return carry

    lax.fori_loop(0, PAIRS, pair_kept, 0)
    keep_out(o, o_out)
    n, inv = mix(x_out[...])
    n1[...] = n.astype(BF)
    i1_out[...] = jnp.broadcast_to(inv, i1_out.shape)
    keep_out(n1, n1_out)
    h = n * norm_out[0:1] + norm_out[2:3]
    hb[...] = h.astype(BF)
    acc[...] = h

    def units_out(k):
        return pltpu.make_async_copy(gu.at[k % 2], gu_out.at[k], gu_sem.at[k % 2])

    def units_in(k):
        return pltpu.make_async_copy(gu_out.at[k], gu.at[k % 2], gu_sem.at[k % 2])

    def unit_kept(k, carry):
        @pl.when(k >= 2)
        def _():
            units_out(k - 2).wait()

        def save(gate, up):
            gu[k % 2, 0] = gate.astype(BF)
            gu[k % 2, 1] = up.astype(BF)

        unit(k, save)
        units_out(k).start()
        return carry

    lax.fori_loop(0, 6, unit_kept, 0)
    n, inv = norm_parts(acc[...])
    n2[...] = n.astype(BF)
    i2_out[...] = jnp.broadcast_to(inv, i2_out.shape)
    keep_out(n2, n2_out)
    hb[...] = (n * norm_out[1:2] + norm_out[3:4]).astype(BF)
    keep_out(hb, y_out)
    for p in (PAIRS - 2, PAIRS - 1):
        probs_out(p).wait()
        units_out(p).wait()

    def dz_copy(b):
        return remote(relay.at[b], land_rows.at[b], dz_send.at[b], dz_recv.at[b], other)

    def oth_copy(p):
        return remote(oth.at[p], got.at[p], oth_send.at[p], oth_recv.at[p], near)

    @pl.when(section == 1)
    def _():
        dr2 = norm_back(xin[...].reshape(rows, width).astype(F32) * norm_out[1:2], n, inv)
        acc[...] = dr2
        df[...] = dr2.astype(BF)
        for p in range(2):
            probs_in(p).start()
            units_in(p).start()

        def unit_back(k, carry):
            wd, wg, wu = group_of(k)
            units_in(k).wait()
            gate = gu[k % 2, 0].astype(F32)
            up = gu[k % 2, 1].astype(F32)
            s = 1.0 / (1.0 + jnp.exp(-gate))
            d_act = dg(df[...], wd, NN)
            d_gate = (d_act * up * (s * (1.0 + gate * (1.0 - s)))).astype(BF)
            d_up = (d_act * (gate * s)).astype(BF)
            acc[...] += dg(d_gate, wg, NT) + dg(d_up, wu, NT)

            @pl.when(k + 2 < 6)
            def _():
                units_in(k + 2).start()

            return carry

        lax.fori_loop(0, 6, unit_back, 0)
        dr1 = norm_back(acc[...] * norm_out[0:1], n1[...].astype(F32), i1_out[:, :1])
        acc[...] = dr1
        df[...] = dr1.astype(BF)
        cost, sint = cost_ref[:, pl.ds(c * rows, rows)], sint_ref[:, pl.ds(c * rows, rows)]

        def pair_of(p, carry):
            probs_in(p).wait()
            dqt, dk, dv = pair_back(
                do3[p % 3], o[p], q[p], kv[0, p], kv[1, p], late_kv[0, p], late_kv[1, p],
                [eb.at[p % 2, h] for h in range(2)], [l_out[p, h, 0:1] for h in range(2)], cost, sint,
            )

            @pl.when(p + 2 < PAIRS)
            def _():
                probs_in(p + 2).start()

            dq[p] = dqt.T.astype(BF)
            keep[p, 0] = dk[:, :rows].astype(BF)
            keep[p, 1] = dv[:, :rows].astype(BF)
            oth[p, 0] = dk[:, rows:].astype(BF)
            oth[p, 1] = dv[:, rows:].astype(BF)
            oth_copy(p).start()
            return carry

        def joint(half):
            def total(i, m):
                return keep[i, m].astype(F32) + got[i, m].astype(F32)

            three = range(3 * half, 3 * half + 3)
            for i in three:
                oth_copy(i).wait()
            parts = joint_parts(
                [dq[i].astype(F32) for i in three], [total(i, 0) for i in three], [total(i, 1) for i in three], cost, sint
            )
            for e in range(2):
                d[2 * half + e] = parts[e]

        for half in range(2):
            t = dg(df[...], out_part(half), NN).astype(BF)
            for i in range(3):
                do3[i] = t[:, 128 * i : 128 * i + 128]
            lax.fori_loop(3 * half, 3 * half + 3, pair_of, 0)
        for half in range(2):
            joint(half)

        def send_back(b, carry):
            part = pl.ds(pl.multiple_of(b * piece_rows, piece_rows), piece_rows)
            total = acc[part]
            for t in range(4):
                total += dg(d[t, part], w[:, :, t, :, :640].reshape(width, 640), NT)
            relay[b] = total.astype(BF)
            dz_copy(b).start()
            return carry

        lax.fori_loop(0, pieces, send_back, 0)
        dy_out[...] = xin[...].reshape(rows, width)
        lax.fori_loop(0, pieces, lambda b, t: (dz_copy(b).wait_send(), t)[1], 0)

    @pl.when(section == 0)
    def _():
        lax.fori_loop(0, pieces, lambda b, t: (row_copy(b).wait_send(), t)[1], 0)
        lax.fori_loop(0, pieces, lambda b, t: (dz_copy(b).wait_recv(), t)[1], 0)
        dy_out[...] = land_rows[...].reshape(rows, width)

    for copy in kept_out:
        copy.wait()

    def finish(j, carry):
        write_back(j).wait()
        to_y(j).wait_send()
        to_core(j).wait_send()
        for h in range(last):

            @pl.when(jnp.logical_and(z >= h, z < last))
            def _():
                go_right(j, h).wait_send()

            @pl.when(jnp.logical_and(z + h <= last, z > 0))
            def _():
                go_left(j, h).wait_send()

        return carry

    lax.fori_loop(0, parts, finish, 0)


def first_layer(tokens, top, shards, gains, biases, lengths, cos, sin, cost, sint):
    micro, own, width = tokens.shape
    lead_part, down, pair = shards
    depth = lead_part.shape[0]
    columns = lead_part.shape[1] + down.shape[1] + pair.shape[1]
    rows = 2 * own
    parts = columns // GATHER
    heads = width // 128
    dma = pltpu.SemaphoreType.DMA
    hbm = pl.BlockSpec(memory_space=pl.ANY)
    vm = pl.BlockSpec(memory_space=VM)
    return pl.pallas_call(
        functools.partial(first_kernel, parts),
        in_specs=[hbm] * 5 + [vm] * 7,
        out_specs=[hbm] * 12 + [vm] * 6,
        out_shape=[sds((2, 2, 4, depth, columns), BF)]
        + [sds((heads, rows, 128), BF)] * 5
        + [
            sds((rows, width), BF),
            sds((heads, 2, 2 * rows, rows), BF),
            sds((heads, rows, 128), BF),
            sds((6, 2, rows, 512), BF),
            sds((rows, width), BF),
            sds((rows, width), BF),
            sds((rows, width), BF),
            sds((rows, width), BF),
            sds((heads, 2, 8, rows), F32),
            sds((rows, 128), F32),
            sds((rows, 128), F32),
            sds((4, width), F32),
        ],
        scratch_shapes=[
            VM((2, 2, 4, depth, columns), BF),
            VM((2, own, width), BF),
            VM((heads, rows, 128), BF),
            VM((2, heads, rows, 128), BF),
            VM((2, heads, rows, 128), BF),
            VM((2, heads, rows, 128), BF),
            VM((heads, rows, 128), BF),
            VM((rows, width), BF),
            VM((rows, width), F32),
            VM((4, rows // 4, width), BF),
            VM((4, rows // 4, width), BF),
            VM((2, 2, 8, gains.shape[1]), F32),
            VM((2,) + lengths.shape, jnp.int32),
            VM((2 * rows, rows), F32),
            VM((2, 2, 2 * rows, rows), BF),
            VM((2, 2, rows, 512), BF),
            VM((rows, width), BF),
            VM((rows, width), BF),
            VM((rows, width), BF),
            VM((3, rows, 128), BF),
            VM((heads, rows, 128), BF),
            VM((heads, 2, 128, rows), BF),
            VM((heads, 2, 128, rows), BF),
            VM((heads, 2, 128, rows), BF),
            VM((4, rows, 640), BF),
            dma, dma((2,)), dma((2,)), dma, dma((6, 3)), dma((parts,)), dma((2,)), dma((2,)), dma((9,)), dma((4,)), dma((4,)), dma((4,)), dma((4,)),
            dma((2,)), dma((2,)), dma((6,)), dma((6,)), dma((4,)), dma((4,)),
            dma((3,)), dma((3,)),
            dma((parts, 3)), dma((parts, 3)), dma((parts, 3)), dma((parts, 3)),
            dma((parts,)), dma((parts,)), dma((parts,)), dma((parts,)),
        ],
        compiler_params=pltpu.CompilerParams(collective_id=1, has_side_effects=True, vmem_limit_bytes=63 << 20),
        name="first",
    )(tokens, top, *shards, gains, biases, lengths, cos, sin, cost, sint)


def swap_pairs(tp, step, dp_axes):
    pairs = []
    half = tp // 2
    for core in range(2):
        for at in range(tp):
            source = core * tp + at
            target = (at // half) * tp + half * core + (at + step) % half
            pairs.append((source, target))
    return pairs


def to_sequences(rows, tp):
    half = tp // 2
    at = lax.axis_index("tensor")
    pieces = [None] * half
    got = []
    for step in range(half):
        piece = lax.dynamic_index_in_dim(rows, (at + step) % half, 0, keepdims=False)
        got.append(lax.ppermute(piece, ("core", "tensor"), swap_pairs(tp, step, None)))
    stacked = jnp.stack(got)
    order = (at - jnp.arange(half)) % half
    return jnp.take(stacked, order, axis=0).reshape(-1, rows.shape[-1])


def to_positions(rows, tp):
    half = tp // 2
    at = lax.axis_index("tensor")
    parts = rows.reshape(half, -1, rows.shape[-1])
    got = []
    for step in range(half):
        piece = lax.dynamic_index_in_dim(parts, (at - step) % half, 0, keepdims=False)
        back = [(target, source) for source, target in swap_pairs(tp, step, None)]
        got.append(lax.ppermute(piece, ("core", "tensor"), back))
    stacked = jnp.stack(got)
    order = (at + jnp.arange(half)) % half
    return jnp.take(stacked, (jnp.arange(half) - at) % half, axis=0)


def rope_tables(positions):
    halfway = HD // 2
    freqs = 1000.0 ** (-jnp.arange(halfway, dtype=F32) / halfway)
    angles = positions.astype(F32)[:, None] * freqs[None, :]
    cos, sin = jnp.cos(angles), jnp.sin(angles)
    wide = jnp.concatenate([cos] * 4, axis=1)
    signed = jnp.concatenate([-sin, sin] * 2, axis=1)
    return wide, signed, cos.T, sin.T


def pack_shard(w_qkv, w_out, w_gate_up, w_down):
    rows = w_qkv.shape[0]
    odd = lax.axis_index("tensor") % 2 == 1
    heads = w_qkv.reshape(rows, 3, 3, HD)
    mine = w_out.T.reshape(rows, 3, HD)
    heads = jnp.where(odd, jnp.roll(heads, -1, axis=2), heads)
    mine = jnp.where(odd, jnp.roll(mine, -1, axis=1), mine)
    first = jnp.concatenate(
        [heads[:, :, :2].reshape(rows, -1), heads[:, :, 2].reshape(rows, -1), mine[:, 2], mine[:, :2].reshape(rows, -1)], axis=1
    )
    return first, w_down.T, w_gate_up.reshape(rows, -1)


def join_shard(first, down, pair):
    rows = first.shape[0]
    units = jnp.concatenate([down, pair], axis=1).reshape(rows, 3, -1, 128).transpose(0, 2, 1, 3)
    return jnp.concatenate([first, units.reshape(rows, -1)], axis=1)


def unpack_first(first):
    rows = first.shape[0]
    odd = lax.axis_index("tensor") % 2 == 1
    both = first[:, :384].reshape(rows, 3, 2, HD)
    single = first[:, 384:576].reshape(rows, 3, 1, HD)
    heads = jnp.concatenate([both, single], axis=2)
    mine = jnp.concatenate([first[:, 640:].reshape(rows, 2, HD), first[:, 576:640].reshape(rows, 1, HD)], axis=1)
    heads = jnp.where(odd, jnp.roll(heads, 1, axis=2), heads)
    mine = jnp.where(odd, jnp.roll(mine, 1, axis=1), mine)
    return heads.reshape(rows, 3, -1), mine.reshape(rows, -1).T


def host_tables(length):
    halfway = HD // 2
    freqs = np.float32(1000.0) ** (-np.arange(halfway, dtype=np.float32) / np.float32(halfway))
    angles = np.arange(length, dtype=np.float32)[:, None] * freqs[None, :]
    cos, sin = np.cos(angles), np.sin(angles)
    return np.concatenate([cos] * 4, axis=1), np.concatenate([-sin, sin] * 2, axis=1), cos.T.copy(), sin.T.copy()


BLOCKS = 4


def gather_shard(shard, dp, tp):
    rows, columns = shard.shape
    got = lax.all_gather(shard, ALL, axis=0, tiled=False)
    got = got.reshape(BLOCKS, dp // BLOCKS, tp, rows, columns)
    return got.transpose(0, 2, 1, 3, 4).reshape(BLOCKS, tp, -1, columns)


def scatter_sum(whole, dp, tp):
    columns = whole.shape[3]
    parts = whole.reshape(BLOCKS, tp, dp // BLOCKS, -1, columns).transpose(0, 2, 1, 3, 4)
    parts = parts.reshape(dp * tp, -1, columns)
    return lax.psum_scatter(parts, ALL, scatter_dimension=0, tiled=False).astype(F32)


def on_device(dp, tp, tokens, cotangent, lengths, w_qkv, w_out, w_gate_up, w_down, norm_gains, norm_biases):
    section = lax.axis_index("section")
    core = lax.axis_index("core")
    at = lax.axis_index("tensor")
    micro, own, width = tokens.shape
    assert micro * 2 == tp
    length = own * tp
    rows = length // 2
    shards = pack_shard(w_qkv[0], w_out[0], w_gate_up[0], w_down[0])
    if dp == 4 and tp == 4:
        wide, signed, cost, sint = host_tables(length)
        (
            weights, q, k, v, ko, vo, y, e, o, gu, n1, n2, inputs, dy, l, i1, i2, small,
        ) = first_layer(tokens, cotangent, shards, norm_gains, norm_biases, lengths, wide, signed, cost, sint)
        weights = weights.reshape((BLOCKS,) + weights.shape[2:])
        kept = (q, k, v, ko, vo, o, e, l, gu, n1, i1, n2, i2)
        joint, mix, pair, down, ends, total = last_back(inputs, y, dy, kept, weights, small, cost, sint)
        small = lax.dynamic_slice_in_dim(total[:4].reshape(2, dp * tp, -1), lax.axis_index(ALL), 1, 1)
        gains, biases = small[0, 0], small[1, 0]
        joint, down = joint.transpose(1, 0, 2), down.T
    else:
        near = core * rows + jnp.arange(rows, dtype=jnp.int32)
        far = (1 - core) * rows + jnp.arange(rows, dtype=jnp.int32)
        tabs = rope_tables(near)
        weights = gather_shard(join_shard(*shards), dp, tp)
        norms = jnp.concatenate([norm_gains, norm_biases])
        norms = lax.all_gather(norms, ("y", "core"), axis=1, tiled=True).astype(F32)
        norms = (norms[0].reshape(2, width), norms[1].reshape(2, width))
        grad_top = to_sequences(cotangent, tp)
        tokens = to_sequences(tokens, tp)
        chip_lengths = lax.all_gather(lengths, "core", axis=0, tiled=True)
        my_lengths = lax.dynamic_index_in_dim(chip_lengths, at, 0, keepdims=False)
        ends_at = jnp.cumsum(my_lengths)

        def segment(positions):
            return jnp.sum((ends_at[None, :] <= positions[:, None]).astype(jnp.int32), axis=-1)

        seg_near = segment(near)
        seg_all = jnp.concatenate([seg_near, segment(far)])
        mask = jnp.where(seg_all[:, None] == seg_near[None, :], 0.0, neg_fill).astype(F32)
        y, unused = forward(tokens, weights, norms, mask, tabs)
        received = lax.ppermute(y, "section", [(0, 1)])
        inputs = jnp.where(section == 0, tokens, received)
        y, kept = forward(inputs, weights, norms, mask, tabs)
        dr1, da = ffn_backward(grad_top, kept, weights, norms, False)
        unused, dz = attn_backward(inputs, da, dr1, None, kept, weights, tabs)
        received = lax.ppermute(dz, "section", [(1, 0)])
        dy = jnp.where(section == 0, received, grad_top)
        g, dr1, da, ng = ffn_backward(dy, kept, weights, norms, True)
        g, dz = attn_backward(inputs, da, dr1, g, kept, weights, tabs)
        ends = to_positions(jnp.where(section == 0, dz.astype(BF), y), tp)
        mine = scatter_sum(g, dp, tp)
        first = mine[:, :width]
        units = mine[:, width:].reshape(first.shape[0], -1, 3, 128).transpose(0, 2, 1, 3).reshape(first.shape[0], 3, -1)
        pair, down = units[:, 1:], units[:, 0].T
        joint, mix = unpack_first(first)
        gains = lax.psum_scatter(ng[0:2].reshape(-1), ALL, scatter_dimension=0, tiled=True)
        biases = lax.psum_scatter(ng[2:4].reshape(-1), ALL, scatter_dimension=0, tiled=True)
    outs = (joint, mix, pair.reshape(pair.shape[0], 2, -1), down, gains, biases)
    return (ends[None],) + tuple(t[None] for t in outs)


def solution(mesh):
    sections, dp, tp = mesh.devices.shape
    fine = Mesh(mesh.devices.reshape(sections, dp // 2, 2, tp), ("section", "y", "core", "tensor"))
    both = ("y", "core")
    in_specs = (
        P(both, "tensor", None),
        P(both, "tensor", None),
        P(both, None),
        P("section", both, None, "tensor"),
        P("section", "tensor", both),
        P("section", both, None, "tensor"),
        P("section", "tensor", both),
        P("section", both),
        P("section", both),
    )
    out_specs = (
        P("section", both, "tensor", None),
        P("section", both, None, "tensor"),
        P("section", "tensor", both),
        P("section", both, None, "tensor"),
        P("section", "tensor", both),
        P("section", ALL),
        P("section", ALL),
    )
    return jax.shard_map(
        functools.partial(on_device, dp, tp), mesh=fine, in_specs=in_specs, out_specs=out_specs, check_vma=False
    )
```

```python
import functools

import jax
import jax.numpy as jnp
import numpy as np
from jax import lax
from jax.experimental import pallas as pl
from jax.experimental.pallas import tpu as pltpu
from jax.sharding import Mesh, PartitionSpec as P

HD = 64
eps = 1e-05
neg_fill = -1e30
ALL = ("y", "core", "tensor")
BF = jnp.bfloat16
F32 = jnp.float32
MESH = pl.DeviceIdType.MESH


def dg(a, b, dims):
    return lax.dot_general(a, b, (dims, ((), ())), preferred_element_type=F32)


NN = ((1,), (0,))
NT = ((1,), (1,))
TN = ((0,), (0,))


def low_lanes(shape):
    return lax.broadcasted_iota(jnp.int32, shape, 1) < HD


def swap64(v):
    return pltpu.roll(v, HD, axis=1)


def rope_fwd(t, cos, sin):
    lane = lax.broadcasted_iota(jnp.int32, t.shape, 1) % HD
    other = jnp.where(lane < HD // 2, pltpu.roll(t, 128 - HD // 2, axis=1), pltpu.roll(t, HD // 2, axis=1))
    return t * cos + other * sin


def qkv_kernel(x_ref, w_ref, cos_ref, sin_ref, q_ref, k_ref, v_ref):
    x = x_ref[...]
    width = x.shape[1]
    r = [dg(x, w_ref[:, e, :, :640].reshape(width, 640), NN) for e in range(2)]
    c = [[t[:, 128 * i : 128 * i + 128] for i in range(5)] for t in r]
    low = low_lanes(c[0][0].shape)
    qs = [c[0][0], jnp.where(low, c[0][3], swap64(c[1][3])), c[1][0]]
    ks = [c[0][1], jnp.where(low, swap64(c[0][3]), c[1][3]), c[1][1]]
    vs = [c[0][2], jnp.where(low, c[0][4], swap64(c[1][4])), c[1][2]]
    cos, sin = cos_ref[...], sin_ref[...]
    for i in range(3):
        q_ref[i] = (rope_fwd(qs[i], cos, sin) * HD**-0.5).astype(BF)
        k_ref[i] = rope_fwd(ks[i], cos, sin).astype(BF)
        v_ref[i] = vs[i].astype(BF)


def attn_kernel(q_ref, k_ref, v_ref, ko_ref, vo_ref, m_ref, o_ref, e_ref, l_ref):
    q = q_ref[0]
    k = jnp.concatenate([k_ref[0], ko_ref[0]], axis=0)
    v = jnp.concatenate([v_ref[0], vo_ref[0]], axis=0)
    vt = v.astype(F32).T.astype(BF)
    outs = []
    for h in range(2):
        low = low_lanes(q.shape)
        qm = jnp.where(low if h == 0 else jnp.logical_not(low), q, jnp.zeros_like(q))
        s = dg(k, qm, NT) + m_ref[...]
        e = jnp.exp(s - jnp.max(s, axis=0, keepdims=True))
        inv = 1.0 / jnp.sum(e, axis=0, keepdims=True)
        eb = e.astype(BF)
        e_ref[0, h] = eb
        l_ref[0, h] = jnp.broadcast_to(inv, l_ref.shape[2:])
        outs.append(dg(vt[HD * h : HD * h + HD], eb, NN) * inv)
    o_ref[0] = jnp.concatenate(outs, axis=0).T.astype(BF)


def norm_parts(r):
    center = r - jnp.mean(r, axis=-1, keepdims=True)
    inv = lax.rsqrt(jnp.mean(center * center, axis=-1, keepdims=True) + eps)
    return center * inv, inv


def norm_back(dn, n, inv):
    return inv * (dn - jnp.mean(dn, axis=-1, keepdims=True) - n * jnp.mean(dn * n, axis=-1, keepdims=True))


def out_weight(w_ref):
    c = [[w_ref[:, e, :, 128 * i : 128 * i + 128].reshape(-1, 128) for i in range(2)] for e in range(2)]
    low = low_lanes(c[0][0].shape)
    mid = jnp.where(low, swap64(c[0][0].astype(F32)), c[1][0].astype(F32)).astype(BF)
    return [c[0][1], mid, c[1][1]]


GROUP = 384
WIDE = 128


def unit_weights(load):
    return [jnp.concatenate([load(t, m) for t in range(4)], axis=1) for m in range(3)]


def ffn_kernel(x_ref, o_ref, wo_ref, w_ref, g_ref, b_ref, y_ref, gu_ref, n1_ref, i1_ref, n2_ref, i2_ref, h_ref, hb_ref, acc_ref):
    z = pl.program_id(0)
    width = x_ref.shape[1]

    @pl.when(z == 0)
    def _():
        r = x_ref[...].astype(F32)
        for p in range(2):
            w = jnp.concatenate(out_weight(wo_ref.at[:, 2 * p : 2 * p + 2]), axis=1)
            o = jnp.concatenate([o_ref[3 * p + i] for i in range(3)], axis=1)
            r = r + dg(o, w, NT)
        n, inv = norm_parts(r)
        n1_ref[...] = n.astype(BF)
        i1_ref[...] = jnp.broadcast_to(inv, i1_ref.shape)
        h = n * g_ref[0:1] + b_ref[0:1]
        h_ref[...] = h
        hb_ref[...] = h.astype(BF)

    hb = hb_ref[...]
    wd, wg, wu = unit_weights(lambda t, m: w_ref[:, t, :, 128 * m : 128 * m + 128].reshape(width, 128))
    gate = dg(hb, wg, NN)
    up = dg(hb, wu, NN)
    gu_ref[0, 0] = gate.astype(BF)
    gu_ref[0, 1] = up.astype(BF)
    act = (gate / (1.0 + jnp.exp(-gate)) * up).astype(BF)
    part = dg(act, wd, NT)

    @pl.when(z == 0)
    def _():
        acc_ref[...] = h_ref[...] + part

    @pl.when(z > 0)
    def _():
        acc_ref[...] += part

    @pl.when(z == pl.num_programs(0) - 1)
    def _():
        n, inv = norm_parts(acc_ref[...])
        n2_ref[...] = n.astype(BF)
        i2_ref[...] = jnp.broadcast_to(inv, i2_ref.shape)
        y_ref[...] = (n * g_ref[1:2] + b_ref[1:2]).astype(BF)


def ffn_back_kernel(grads, dy_ref, n1_ref, i1_ref, n2_ref, i2_ref, gu_ref, w_ref, g_ref, b_ref, *refs):
    if grads:
        g_out, dr1_ref, da_ref, ng_ref, hb_ref, df_ref, acc_ref = refs
    else:
        dr1_ref, da_ref, df_ref, acc_ref = refs
    z = pl.program_id(0)
    width = dy_ref.shape[1]

    @pl.when(z == 0)
    def _():
        dy = dy_ref[...].astype(F32)
        n = n2_ref[...].astype(F32)
        if grads:
            ng_ref[1:2] = jnp.sum(dy * n, axis=0, keepdims=True)
            ng_ref[3:4] = jnp.sum(dy, axis=0, keepdims=True)
            hb_ref[...] = (n1_ref[...].astype(F32) * g_ref[0:1] + b_ref[0:1]).astype(BF)
        dr2 = norm_back(dy * g_ref[1:2], n, i2_ref[:, :1])
        acc_ref[...] = dr2
        df_ref[...] = dr2.astype(BF)

    df = df_ref[...]
    gate = gu_ref[0, 0].astype(F32)
    up = gu_ref[0, 1].astype(F32)
    s = 1.0 / (1.0 + jnp.exp(-gate))
    silu = gate * s
    wd, wg, wu = unit_weights(lambda t, m: w_ref[:, t, :, 128 * m : 128 * m + 128].reshape(width, 128))

    def keep(m, grad):
        for t in range(g_out.shape[1]):
            g_out[:, t, :, 128 * m : 128 * m + 128] = grad[:, 128 * t : 128 * t + 128].astype(BF).reshape(g_out.shape[0], -1, 128)

    if grads:
        keep(0, dg(df, (silu * up).astype(BF), TN))
    d_act = dg(df, wd, NN)
    d_gate = (d_act * up * (s * (1.0 + gate * (1.0 - s)))).astype(BF)
    d_up = (d_act * silu).astype(BF)
    if grads:
        hb = hb_ref[...]
        keep(1, dg(hb, d_gate, TN))
        keep(2, dg(hb, d_up, TN))
    acc_ref[...] += dg(d_gate, wg, NT) + dg(d_up, wu, NT)

    @pl.when(z == pl.num_programs(0) - 1)
    def _():
        dh = acc_ref[...]
        n = n1_ref[...].astype(F32)
        if grads:
            ng_ref[0:1] = jnp.sum(dh * n, axis=0, keepdims=True)
            ng_ref[2:3] = jnp.sum(dh, axis=0, keepdims=True)
        dr1 = norm_back(dh * g_ref[0:1], n, i1_ref[:, :1])
        dr1_ref[...] = dr1
        da_ref[...] = dr1.astype(BF)


def pair_back(do, o, q, k, v, ko, vo, e, l, cos, sin):
    dot = do.astype(F32).T
    ot = o.astype(F32).T
    k = jnp.concatenate([k, ko], axis=0)
    v = jnp.concatenate([v, vo], axis=0)
    kt = k.astype(F32).T.astype(BF)
    qt = q.astype(F32).T.astype(BF)
    dqs, dks, dvs = [], [], []
    for h in range(2):
        span = slice(HD * h, HD * h + HD)
        scaled = dot[span] * l[h]
        inner = jnp.sum(scaled * ot[span], axis=0, keepdims=True)
        sb = scaled.astype(BF)
        zero = jnp.zeros_like(sb)
        padded = jnp.concatenate([sb, zero] if h == 0 else [zero, sb], axis=0)
        dp = dg(v, padded, NN)
        et = e[h][...]
        ds = (et.astype(F32) * (dp - inner)).astype(BF)
        dvs.append(dg(sb, et, NT))
        dks.append(dg(qt[span], ds, NT))
        dqt = dg(kt[span], ds, NN) * HD**-0.5
        d1, d2 = dqt[: HD // 2], dqt[HD // 2 :]
        dqs.append(d1 * cos + d2 * sin)
        dqs.append(d2 * cos - d1 * sin)
    return [jnp.concatenate(t, axis=0) for t in (dqs, dks, dvs)]


def joint_parts(dq, dkt, dvt, cos, sin):
    dk = []
    for t in dkt:
        parts = []
        for h in range(2):
            d1 = t[HD * h : HD * h + HD // 2]
            d2 = t[HD * h + HD // 2 : HD * h + HD]
            parts += [d1 * cos + d2 * sin, d2 * cos - d1 * sin]
        dk.append(jnp.concatenate(parts, axis=0).T)
    dv = [t.T for t in dvt]
    low = low_lanes(dq[0].shape)
    zero = jnp.zeros_like(dv[1])
    d = [
        [dq[0], dk[0], dv[0], jnp.where(low, dq[1], swap64(dk[1])), jnp.where(low, dv[1], zero)],
        [dq[2], dk[2], dv[2], jnp.where(low, swap64(dq[1]), dk[1]), jnp.where(low, swap64(dv[1]), zero)],
    ]
    return [jnp.concatenate(t, axis=1).astype(BF) for t in d]


def attn_back_kernel(grads, da_ref, wo_ref, o_ref, q_ref, k_ref, v_ref, ko_ref, vo_ref, e_ref, l_ref, cos_ref, sin_ref, dq_ref, own_ref, oth_ref, *dwo_ref):
    da = da_ref[...]
    rows = da.shape[0]
    w = jnp.concatenate(out_weight(wo_ref), axis=1)
    do3 = dg(da, w, NN).astype(BF)
    if grads:
        o3 = jnp.concatenate([o_ref[i] for i in range(3)], axis=1)
        dwo_ref[0][0] = dg(da, o3, TN).astype(BF)
    cos, sin = cos_ref[...], sin_ref[...]
    for i in range(3):
        dqt, dk, dv = pair_back(
            do3[:, 128 * i : 128 * i + 128], o_ref[i], q_ref[i], k_ref[i], v_ref[i], ko_ref[i], vo_ref[i],
            [e_ref[i, h] for h in range(2)], [l_ref[i, h, 0:1] for h in range(2)], cos, sin,
        )
        dq_ref[i] = dqt.T.astype(BF)
        own_ref[i, 0] = dk[:, :rows]
        own_ref[i, 1] = dv[:, :rows]
        oth_ref[i, 0] = dk[:, rows:].astype(BF)
        oth_ref[i, 1] = dv[:, rows:].astype(BF)


def joint_back_kernel(grads, *refs):
    if grads:
        old_ref, x_ref, w_ref, dr1_ref, dq_ref, own_ref, got_ref, dwo_ref, cos_ref, sin_ref, g_ref, dz_ref = refs
    else:
        w_ref, dr1_ref, dq_ref, own_ref, got_ref, cos_ref, sin_ref, dz_ref, dzb_ref = refs
    p = pl.program_id(0)
    width = dr1_ref.shape[1]
    d = joint_parts(
        [dq_ref[i].astype(F32) for i in range(3)],
        [own_ref[i, 0] + got_ref[i, 0].astype(F32) for i in range(3)],
        [own_ref[i, 1] + got_ref[i, 1].astype(F32) for i in range(3)],
        cos_ref[...],
        sin_ref[...],
    )
    acc = None
    for e in range(2):
        t = dg(d[e], w_ref[:, e, :, :640].reshape(width, 640), NT)
        acc = t if acc is None else acc + t
    if grads:
        x = x_ref[...]
        wlow = low_lanes((width, 128))
        mid = dwo_ref[0, :, 128:256].astype(F32)
        sides = [dwo_ref[0, :, 0:128], dwo_ref[0, :, 256:384]]
        mids = [swap64(mid), mid]
        for e in range(2):
            g = dg(x, d[e], TN)
            blocks = g_ref.shape[0]
            g_ref[:, e, :, :512] = g[:, :512].astype(BF).reshape(blocks, -1, 512)
            g_ref[:, e, :, 512:640] = jnp.where(wlow, g[:, 512:], mids[e]).astype(BF).reshape(blocks, -1, 128)
            g_ref[:, e, :, 640:] = sides[e].reshape(blocks, -1, 128)

    @pl.when(p == 0)
    def _():
        dz_ref[...] = dr1_ref[...] + acc

    @pl.when(p > 0)
    def _():
        total = dz_ref[...] + acc
        dz_ref[...] = total
        if not grads:
            dzb_ref[...] = total.astype(BF)


BIG = pltpu.CompilerParams(vmem_limit_bytes=58 << 20)
VM = pltpu.VMEM


def full(shape):
    return pl.BlockSpec(shape, lambda i: (0,) * len(shape))


def lead(shape, at=0):
    return pl.BlockSpec(shape, lambda i: tuple(i if j == at else 0 for j in range(len(shape))))


def joint_block(w):
    return pl.BlockSpec((w.shape[0], 2, w.shape[2], 768), lambda i: (0, i, 0, 0))


def group_block(w):
    return pl.BlockSpec((w.shape[0], w.shape[1], w.shape[2], GROUP), lambda i: (0, 0, 0, 2 + i))


def sds(shape, kind):
    return jax.ShapeDtypeStruct(shape, kind)


def forward(x, weights, norms, mask, tabs):
    w = weights
    rows, width = x.shape
    heads = width // 128
    blocks, tp, depth, columns = w.shape
    steps = tp // 2
    cos, sin, cost, sint = tabs
    q, k, v = pl.pallas_call(
        qkv_kernel,
        grid=(steps,),
        in_specs=[full((rows, width)), joint_block(w), full((rows, 128)), full((rows, 128))],
        out_specs=[lead((3, rows, 128))] * 3,
        out_shape=[sds((heads, rows, 128), BF)] * 3,
        compiler_params=BIG,
        name="qkv",
    )(x, w, cos, sin)
    ko, vo = lax.ppermute((k, v), "core", [(0, 1), (1, 0)])
    return attend(x, (q, k, v, ko, vo), w, norms, mask)


def attend(x, joint, w, norms, mask):
    gains, biases = norms
    q, k, v, ko, vo = joint
    rows, width = x.shape
    heads = width // 128
    blocks, tp, depth, columns = w.shape
    pair = lead((1, rows, 128))
    o, e, l = pl.pallas_call(
        attn_kernel,
        grid=(heads,),
        in_specs=[pair] * 5 + [full((2 * rows, rows))],
        out_specs=[pair, lead((1, 2, 2 * rows, rows)), lead((1, 2, 8, rows))],
        out_shape=[sds((heads, rows, 128), BF), sds((heads, 2, 2 * rows, rows), BF), sds((heads, 2, 8, rows), F32)],
        compiler_params=BIG,
        name="attn",
    )(q, k, v, ko, vo, mask)
    groups = (columns - width) // GROUP
    units = tp * 128
    y, gu, n1, i1, n2, i2 = pl.pallas_call(
        ffn_kernel,
        grid=(groups,),
        in_specs=[
            full((rows, width)),
            full((heads, rows, 128)),
            pl.BlockSpec((blocks, tp, depth, 256), lambda i: (0, 0, 0, 2)),
            group_block(w),
            full((2, width)),
            full((2, width)),
        ],
        out_specs=[full((rows, width)), lead((1, 2, rows, units))] + [full((rows, width)), full((rows, 128))] * 2,
        out_shape=[sds((rows, width), BF), sds((groups, 2, rows, units), BF)] + [sds((rows, width), BF), sds((rows, 128), F32)] * 2,
        scratch_shapes=[VM((rows, width), F32), VM((rows, width), BF), VM((rows, width), F32)],
        compiler_params=BIG,
        name="ffn",
    )(x, o, w, w, gains, biases)
    return y, (q, k, v, ko, vo, o, e, l, gu, n1, i1, n2, i2)


def ffn_backward(dy, kept, w, norms, grads):
    gains, biases = norms
    gu, n1, i1, n2, i2 = kept[8:]
    rows, width = dy.shape
    blocks, tp, depth, columns = w.shape
    groups = (columns - width) // GROUP
    whole, stat = full((rows, width)), full((rows, 128))
    outs = [whole, whole]
    shapes = [sds((rows, width), F32), sds((rows, width), BF)]
    scratch = [VM((rows, width), BF), VM((rows, width), F32)]
    if grads:
        outs = [group_block(w)] + outs + [full((8, width))]
        shapes = [sds(w.shape, BF)] + shapes + [sds((8, width), F32)]
        scratch = [VM((rows, width), BF)] + scratch
    return pl.pallas_call(
        functools.partial(ffn_back_kernel, grads),
        grid=(groups,),
        in_specs=[
            whole, whole, stat, whole, stat,
            lead((1, 2, rows, tp * 128)),
            group_block(w),
            full((2, width)), full((2, width)),
        ],
        out_specs=outs,
        out_shape=shapes,
        scratch_shapes=scratch,
        compiler_params=BIG,
        name="ffn_back" if grads else "ffn_back_light",
    )(dy, n1, i1, n2, i2, gu, w, gains, biases)


def attn_backward(x, da, dr1, g, kept, w, tabs):
    grads = g is not None
    q, k, v, ko, vo, o, e, l = kept[:8]
    rows, width = da.shape
    heads = width // 128
    blocks, tp, depth, columns = w.shape
    steps = tp // 2
    cos, sin, cost, sint = tabs
    whole = full((rows, width))
    three = lead((3, rows, 128))
    side = lead((3, 2, 128, rows))
    table = full((HD // 2, rows))
    extra = [lead((1, width, 384))] if grads else []
    dq, own, oth, *dwo = pl.pallas_call(
        functools.partial(attn_back_kernel, grads),
        grid=(steps,),
        in_specs=[
            whole,
            pl.BlockSpec((blocks, 2, depth, 256), lambda i: (0, i, 0, 2)),
            three, three, three, three, three, three,
            lead((3, 2, 2 * rows, rows)),
            lead((3, 2, 8, rows)),
            table, table,
        ],
        out_specs=[three, side, side] + extra,
        out_shape=[
            sds((heads, rows, 128), BF),
            sds((heads, 2, 128, rows), F32),
            sds((heads, 2, 128, rows), BF),
        ]
        + ([sds((steps, width, 384), BF)] if grads else []),
        compiler_params=BIG,
        name="attn_back",
    )(da, w, o, q, k, v, ko, vo, e, l, cost, sint)
    got = lax.ppermute(oth, "core", [(0, 1), (1, 0)])
    if grads:
        specs = [pl.BlockSpec(memory_space=pl.ANY), whole, joint_block(w), whole, three, side, side] + extra
        args = (g, x, w, dr1, dq, own, got, *dwo)
        outs, shapes = [joint_block(w), whole], [sds(w.shape, BF), sds((rows, width), F32)]
    else:
        specs = [joint_block(w), whole, three, side, side]
        args = (w, dr1, dq, own, got)
        outs, shapes = [whole, whole], [sds((rows, width), F32), sds((rows, width), BF)]
    return pl.pallas_call(
        functools.partial(joint_back_kernel, grads),
        grid=(steps,),
        in_specs=specs + [table, table],
        out_specs=outs,
        out_shape=shapes,
        input_output_aliases={0: 0} if grads else {},
        compiler_params=BIG,
        name="joint_back",
    )(*args, cost, sint)


PAIRS = 6
FIRST_PAIR = 6
FIRST_JOINT = 12
LAST_STEP = 13


FAR = 2
FAR_AT = 4
def last_kernel(
    parts, n1_ref, i1_ref, n2_ref, i2_ref, gu_ref, wa_ref, norm_ref,
    q_ref, k_ref, v_ref, ko_ref, vo_ref, l_ref, cos_ref, sin_ref, dy_hbm, x_hbm, y_hbm, e_hbm, o_hbm, w_hbm,
    joint_out, mix_out, pair_out, down_out, ends_out, norm_out,
    acc, df, hb, o_ref, wb_ref, ring, do3, dwo, dq, keep, oth, got, eb, e_send, e_land, tmp, land_c, land_y, land_r, land_l, land_n,
    z_sum, far_y, far_r, far_l,
    o_sem, wb_sem, dy_sem, x_sem, y_sem, e_sem, oth_send, oth_recv, end_sem, end_send, end_recv,
    cs_sem, cr_sem, ys_sem, yr_sem, rs_sem, rr_sem, ls_sem, lr_sem, ns_sem, nr_sem,
    fys_sem, fyr_sem, frs_sem, frr_sem, fls_sem, flr_sem,
):
    step = pl.program_id(0)
    section = lax.axis_index("section")
    y, c, z = lax.axis_index("y"), lax.axis_index("core"), lax.axis_index("tensor")
    last = 3
    rows, width = acc.shape
    early = parts - width // WIDE
    usual = parts - FAR
    near, across = {"core": 1 - c}, {"y": 1 - y}
    right, left = {"tensor": jnp.minimum(z + 1, last)}, {"tensor": jnp.maximum(z - 1, 0)}
    pair = {"tensor": z + 1 - 2 * lax.rem(z, 2)}
    far = {"tensor": lax.rem(z + 2, 4)}
    side = z // 2
    barrier = pltpu.get_barrier_semaphore()

    def greet(device):
        pl.semaphore_signal(barrier, inc=1, device_id=device, device_id_type=MESH)

    def remote(src, dst, send, recv, device):
        return pltpu.make_async_remote_copy(src, dst, send, recv, device_id=device, device_id_type=MESH)

    def target(i):
        return {"core": side, "tensor": 2 * c + i}

    def at_home(i):
        return jnp.logical_and(side == c, 2 * c + i == z)

    def end_copy(i, part):
        return remote(e_send.at[i, part], e_land.at[z % 2, part], end_send.at[i], end_recv.at[z % 2], target(i))

    def end_home(i):
        return pltpu.make_async_copy(e_send.at[i], e_land.at[z % 2], end_sem)

    def oth_copy(p):
        return remote(oth.at[p], got.at[p], oth_send.at[p], oth_recv.at[p], near)

    dy_copy = pltpu.make_async_copy(dy_hbm, e_send, dy_sem)
    x_copy = pltpu.make_async_copy(x_hbm, hb, x_sem)
    o_copy = pltpu.make_async_copy(o_hbm, o_ref, o_sem)
    wb_copy = pltpu.make_async_copy(w_hbm.at[:, :, :, pl.ds(GROUP, GROUP)], wb_ref, wb_sem)
    y_copy = pltpu.make_async_copy(y_hbm, e_send, y_sem)

    def probs_copy(p):
        return pltpu.make_async_copy(e_hbm.at[p], eb, e_sem)

    def columns(j):
        return pl.ds(pl.multiple_of(j * WIDE, WIDE), WIDE)

    def slot(j):
        return (j // 3) % 2, columns(j % 3)

    def chunk(j):
        return j + FAR * ((j + usual - FAR_AT) // usual)

    def to_core(j):
        r, cols = slot(j)
        return remote(ring.at[r, :, 1 - c, :, :, cols], land_c.at[j], cs_sem.at[j], cr_sem.at[j], near)

    def to_y(j):
        return remote(land_c.at[chunk(j), 1 - y], land_y.at[j], ys_sem.at[j], yr_sem.at[j], across)

    def norm_copy(k):
        return remote(land_n.at[2 * k], land_n.at[2 * k + 1], ns_sem.at[k], nr_sem.at[k], (near, across, pair, far)[k])

    def go_right(j, first, src):
        return remote(src, land_r.at[j, pl.ds(first - 1, 4 - first)], rs_sem.at[j], rr_sem.at[j], right)

    def go_left(j, count, src):
        return remote(src, land_l.at[j, pl.ds(0, count)], ls_sem.at[j], lr_sem.at[j], left)

    def stage(i, lag, body):
        @pl.when(jnp.logical_and(i >= lag, i - lag < usual))
        def _():
            body(i - lag)

    def add_core(j):
        r, cols = slot(j)
        to_core(j).wait()
        land_c[j] = land_c[j] + ring[r, :, c, :, :, cols]

    def far_right(b, first, src):
        return remote(src, far_r.at[b, :, pl.ds(first - 1, 4 - first)], frs_sem.at[b], frr_sem.at[b], right)

    def far_left(b, count, src):
        return remote(src, far_l.at[b, :, pl.ds(0, count)], fls_sem.at[b], flr_sem.at[b], left)

    def far_across(b):
        return remote(z_sum.at[b, 1 - y], far_y.at[b], fys_sem.at[b], fyr_sem.at[b], across)

    def far_first(b):
        j = FAR_AT + b

        @pl.when(z == 0)
        def _():
            far_right(b, 1, land_c.at[j, :, pl.ds(1, 3)]).start()

        @pl.when(z == last)
        def _():
            far_left(b, 3, land_c.at[j, :, pl.ds(0, 3)]).start()

    def far_next(b):
        j = FAR_AT + b

        @pl.when(z == 1)
        def _():
            far_right(b, 1, far_r.at[b]).wait_recv()
            for k in (2, 3):
                far_r[b, :, k - 1] = far_r[b, :, k - 1] + land_c[j, :, k]
            far_right(b, 2, far_r.at[b, :, pl.ds(1, 2)]).start()

        @pl.when(z == 2)
        def _():
            far_left(b, 3, far_l.at[b]).wait_recv()
            for k in (0, 1):
                far_l[b, :, k] = far_l[b, :, k] + land_c[j, :, k]
            far_left(b, 2, far_l.at[b, :, pl.ds(0, 2)]).start()

    def far_last(b):
        j = FAR_AT + b

        @pl.when(z == 1)
        def _():
            far_left(b, 2, far_l.at[b, :, pl.ds(0, 2)]).wait_recv()
            far_l[b, :, 0] = far_l[b, :, 0] + land_c[j, :, 0]
            far_left(b, 1, far_l.at[b, :, pl.ds(0, 1)]).start()

        @pl.when(z == 2)
        def _():
            far_right(b, 2, far_r.at[b, :, pl.ds(1, 2)]).wait_recv()
            far_r[b, :, 2] = far_r[b, :, 2] + land_c[j, :, 3]
            far_right(b, 3, far_r.at[b, :, pl.ds(2, 1)]).start()

    def far_sum(b):
        mine = land_c[FAR_AT + b, :, z]

        @pl.when(z == 0)
        def _():
            far_left(b, 1, far_l.at[b, :, pl.ds(0, 1)]).wait_recv()
            z_sum[b] = mine + far_l[b, :, 0]

        @pl.when(z == 1)
        def _():
            z_sum[b] = mine + far_r[b, :, 0] + far_l[b, :, 1]

        @pl.when(z == 2)
        def _():
            z_sum[b] = mine + far_r[b, :, 1] + far_l[b, :, 2]

        @pl.when(z == last)
        def _():
            far_right(b, 3, far_r.at[b, :, pl.ds(2, 1)]).wait_recv()
            z_sum[b] = mine + far_r[b, :, 2]

    def far_result(b):
        far_across(b).wait_recv()
        tmp[...] = z_sum[b, y].astype(F32) + far_y[b].astype(F32)
        emit(FAR_AT + b)

    def last_hop(j):
        @pl.when(z == 1)
        def _():
            go_left(j, 2, land_l.at[j, pl.ds(0, 2)]).wait_recv()
            land_l[j, 0] = land_l[j, 0] + land_c[chunk(j), y, 0]
            go_left(j, 1, land_l.at[j, pl.ds(0, 1)]).start()

        @pl.when(z == 2)
        def _():
            go_right(j, 2, land_r.at[j, pl.ds(1, 2)]).wait_recv()
            land_r[j, 2] = land_r[j, 2] + land_c[chunk(j), y, 3]
            go_right(j, 3, land_r.at[j, pl.ds(2, 1)]).start()

    def next_hop(j):
        @pl.when(z == 1)
        def _():
            go_right(j, 1, land_r.at[j]).wait_recv()
            for k in (2, 3):
                land_r[j, k - 1] = land_r[j, k - 1] + land_c[chunk(j), y, k]
            go_right(j, 2, land_r.at[j, pl.ds(1, 2)]).start()

        @pl.when(z == 2)
        def _():
            go_left(j, 3, land_l.at[j]).wait_recv()
            for k in (0, 1):
                land_l[j, k] = land_l[j, k] + land_c[chunk(j), y, k]
            go_left(j, 2, land_l.at[j, pl.ds(0, 2)]).start()

    def first_hop(j):
        to_y(j).wait_recv()
        land_c[chunk(j), y] = land_c[chunk(j), y] + land_y[j]

        @pl.when(z == 0)
        def _():
            go_right(j, 1, land_c.at[chunk(j), y, pl.ds(1, 3)]).start()

        @pl.when(z == last)
        def _():
            go_left(j, 3, land_c.at[chunk(j), y, pl.ds(0, 3)]).start()

    def result(j):
        mine = land_c[chunk(j), y, z].astype(F32)

        @pl.when(z == 0)
        def _():
            go_left(j, 1, land_l.at[j, pl.ds(0, 1)]).wait_recv()
            tmp[...] = mine + land_l[j, 0].astype(F32)

        @pl.when(z == 1)
        def _():
            tmp[...] = mine + land_r[j, 0].astype(F32) + land_l[j, 1].astype(F32)

        @pl.when(z == 2)
        def _():
            tmp[...] = mine + land_r[j, 1].astype(F32) + land_l[j, 2].astype(F32)

        @pl.when(z == last)
        def _():
            go_right(j, 3, land_r.at[j, pl.ds(2, 1)]).wait_recv()
            tmp[...] = mine + land_r[j, 2].astype(F32)

        emit(chunk(j))

    def emit(j):
        group = j // 3

        @pl.when(jnp.logical_and(j < early, j % 3 == 0))
        def _():
            down_out[:, columns(group)] = tmp[...]

        for m in (1, 2):

            @pl.when(jnp.logical_and(j < early, j % 3 == m))
            def _():
                pair_out[:, columns(group + (m - 1) * (early // 3))] = tmp[...]

        for odd in range(2):
            two = slice(HD, 3 * HD) if odd else slice(0, 2 * HD)
            one = slice(0, HD) if odd else slice(2 * HD, 3 * HD)

            def when(n, body, odd=odd):
                pl.when(jnp.logical_and(j == early + n, z % 2 == odd))(body)

            def store(out, place, part):
                def body():
                    out[:, place] = tmp[:, part]

                return body

            def turn(place, part):
                def body():
                    mix_out[place, :] = tmp[...].T[part]

                return body

            whole, low, high = slice(0, 128), slice(0, HD), slice(HD, 128)
            for n in range(3):
                when(n, store(joint_out.at[n], two, whole))
            when(3, store(joint_out.at[0], one, low))
            when(3, store(joint_out.at[1], one, high))
            when(4, store(joint_out.at[2], one, low))
            when(4, turn(one, high))
            when(5, turn(two, whole))

    def round_(i):
        stage(i, 0, lambda j: to_y(j).start())
        stage(i, 6, last_hop)
        stage(i, 4, next_hop)
        stage(i, 2, first_hop)
        stage(i, 8, result)
        for b in range(FAR):
            rounds = (4 + 3 * b, 7 + 3 * b, 10 + 3 * b, 13 + 3 * b, usual - 1 + b, usual + 3 + b)
            bodies = (far_first, far_next, far_last, far_sum, lambda b: far_across(b).start(), far_result)
            for at, body in zip(rounds, bodies):
                pl.when(i == at)(functools.partial(body, b))

        for k in range(4):

            @pl.when(i == 3 * k + 8)
            def _():
                norm_copy(k).wait()
                total = land_n[2 * k] + land_n[2 * k + 1]
                if k < 3:
                    land_n[2 * k + 2] = total
                    norm_copy(k + 1).start()
                else:
                    norm_out[...] = total

    @pl.when(step == 0)
    def _():
        dy_copy.start()
        o_copy.start()
        wb_copy.start()
        greet(near)
        greet(across)
        greet(far)

        @pl.when(z < last)
        def _():
            greet(right)

        @pl.when(z > 0)
        def _():
            greet(left)

        for i in range(2):

            @pl.when(jnp.logical_not(at_home(i)))
            def _():
                greet(target(i))

        count = 5 + jnp.where(z < last, 1, 0) + jnp.where(z > 0, 1, 0) - jnp.where(side == c, 1, 0)
        pl.semaphore_wait(barrier, count)
        dy_copy.wait()
        dy = e_send[...].reshape(rows, width).astype(F32)
        n = n2_ref[...].astype(F32)
        land_n[0] = jnp.zeros(land_n.shape[1:], F32)
        land_n[0, 1:2] = jnp.sum(dy * n, axis=0, keepdims=True)
        land_n[0, 3:4] = jnp.sum(dy, axis=0, keepdims=True)
        dr2 = norm_back(dy * norm_ref[1:2], n, i2_ref[:, :1])
        acc[...] = dr2
        df[...] = dr2.astype(BF)
        hb[...] = (n1_ref[...].astype(F32) * norm_ref[0:1] + norm_ref[2:3]).astype(BF)

    @pl.when(step < FIRST_PAIR)
    def _():
        gate = gu_ref[0, 0].astype(F32)
        up = gu_ref[0, 1].astype(F32)
        s = 1.0 / (1.0 + jnp.exp(-gate))
        silu = gate * s
        wd, wg, wu = unit_weights(lambda t, m: wa_ref[:, t, :, 128 * m : 128 * m + 128].reshape(width, 128))
        place = step % 2

        def put(m, grad):
            for t in range(4):
                ring[place, :, :, t, :, 128 * m : 128 * m + 128] = (
                    grad[:, 128 * t : 128 * t + 128].astype(BF).reshape(2, 2, -1, 128)
                )

        j = 3 * step

        def earlier(m):
            pl.when(step > (1 if m == 0 else 0))(lambda: add_core(j - 3 + m))

        put(0, dg(df[...], (silu * up).astype(BF), TN))
        to_core(j).start()
        earlier(0)
        d_act = dg(df[...], wd, NN)
        d_gate = (d_act * up * (s * (1.0 + gate * (1.0 - s)))).astype(BF)
        d_up = (d_act * silu).astype(BF)
        put(1, dg(hb[...], d_gate, TN))
        to_core(j + 1).start()
        earlier(1)

        @pl.when(step == 0)
        def _():
            add_core(0)
            round_(0)

        put(2, dg(hb[...], d_up, TN))
        to_core(j + 2).start()
        earlier(2)
        acc[...] += dg(d_gate, wg, NT) + dg(d_up, wu, NT)

    @pl.when(step == FIRST_PAIR - 1)
    def _():
        dh = acc[...]
        n = n1_ref[...].astype(F32)
        land_n[0, 0:1] = jnp.sum(dh * n, axis=0, keepdims=True)
        land_n[0, 2:3] = jnp.sum(dh, axis=0, keepdims=True)
        dr1 = norm_back(dh * norm_ref[0:1], n, i1_ref[:, :1])
        acc[...] = dr1
        df[...] = dr1.astype(BF)
        x_copy.start()
        probs_copy(0).start()
        norm_copy(0).start()

    cos, sin = cos_ref[:, pl.ds(c * rows, rows)], sin_ref[:, pl.ds(c * rows, rows)]
    in_pairs = jnp.logical_and(step >= FIRST_PAIR, step < FIRST_JOINT)
    p = step - FIRST_PAIR

    @pl.when(step == FIRST_PAIR)
    def _():
        for m in range(3):
            add_core(3 * FIRST_PAIR - 3 + m)
        o_copy.wait()
        wb_copy.wait()

    @pl.when(jnp.logical_and(in_pairs, p % 3 == 0))
    def _():
        w = jnp.concatenate(out_weight(wb_ref.at[:, pl.ds(2 * (p // 3), 2), :, 128:384]), axis=1)
        t = dg(df[...], w, NN).astype(BF)
        for i in range(3):
            do3[i] = t[:, 128 * i : 128 * i + 128]
        o3 = jnp.concatenate([o_ref[p + i] for i in range(3)], axis=1)
        dwo[p // 3] = dg(df[...], o3, TN).astype(BF)

    @pl.when(in_pairs)
    def _():
        probs_copy(p).wait()
        dqt, dk, dv = pair_back(
            do3[p % 3], o_ref[p], q_ref[0], k_ref[0], v_ref[0], ko_ref[0], vo_ref[0],
            [eb.at[h] for h in range(2)], [l_ref[0, h, 0:1] for h in range(2)], cos, sin,
        )
        dq[p] = dqt.T.astype(BF)
        keep[p, 0] = dk[:, :rows].astype(BF)
        keep[p, 1] = dv[:, :rows].astype(BF)
        oth[p, 0] = dk[:, rows:].astype(BF)
        oth[p, 1] = dv[:, rows:].astype(BF)
        oth_copy(p).start()

        @pl.when(p + 1 < PAIRS)
        def _():
            probs_copy(p + 1).start()

    @pl.when(step >= FIRST_JOINT)
    def _():
        half = step - FIRST_JOINT

        @pl.when(half == 0)
        def _():
            x_copy.wait()

        for i in range(3):
            oth_copy(3 * half + i).wait()
        d = joint_parts(
            [dq[3 * half + i].astype(F32) for i in range(3)],
            [keep[3 * half + i, 0].astype(F32) + got[3 * half + i, 0].astype(F32) for i in range(3)],
            [keep[3 * half + i, 1].astype(F32) + got[3 * half + i, 1].astype(F32) for i in range(3)],
            cos, sin,
        )
        total = None
        wlow = low_lanes((width, 128))
        mid = dwo[half, :, 128:256].astype(F32)
        sides = [dwo[half, :, 0:128], dwo[half, :, 256:384]]
        mids = [swap64(mid), mid]
        shape = (2, 2, width // 4)
        for e in range(2):
            t = 2 * half + e
            w = jnp.concatenate([wa_ref[:, t].reshape(width, GROUP), wb_ref[:, t, :, :256].reshape(width, 256)], axis=1)
            part = dg(d[e], w, NT)
            total = part if total is None else total + part
            g = dg(hb[...], d[e], TN)
            ring[0, :, :, t] = g[:, :GROUP].astype(BF).reshape(shape + (GROUP,))
            ring[1, :, :, t, :, :128] = g[:, GROUP:512].astype(BF).reshape(shape + (128,))
            ring[1, :, :, t, :, 128:256] = jnp.where(wlow, g[:, 512:], mids[e]).astype(BF).reshape(shape + (128,))
            ring[1, :, :, t, :, 256:] = sides[e].reshape(shape + (128,))
        acc[...] += total

    @pl.when(step == LAST_STEP)
    def _():
        lax.fori_loop(early, parts, lambda j, t: (to_core(j).start(), t)[1], 0)

        @pl.when(section == 0)
        def _():
            e_send[...] = acc[...].astype(BF).reshape(e_send.shape)

        @pl.when(section == 1)
        def _():
            y_copy.start()
            y_copy.wait()

        for i in range(2):

            @pl.when(at_home(i))
            def _():
                end_home(i).start()

    @pl.when(step == 1)
    def _():
        round_(1)

    @pl.when(step >= 1)
    def _():
        round_(step + 1)

    @pl.when(step == LAST_STEP)
    def _():
        lax.fori_loop(early, parts, lambda j, t: (add_core(j), t)[1], 0)
        end_rows = e_send.shape[1] // 8

        def late(i, carry):
            part = pl.ds(pl.multiple_of((i - LAST_STEP - 2) * end_rows, end_rows), end_rows)
            for k in range(2):

                @pl.when(jnp.logical_not(at_home(k)))
                def _():
                    end_copy(k, part).start()

            round_(i)
            return carry

        lax.fori_loop(LAST_STEP + 2, LAST_STEP + 10, late, 0)
        lax.fori_loop(LAST_STEP + 10, usual + 8, lambda i, t: (round_(i), t)[1], 0)
        for i in range(2):

            @pl.when(at_home(i))
            def _():
                end_home(i).wait()

            @pl.when(jnp.logical_not(at_home(i)))
            def _():
                end_copy(i, pl.ds(0, e_send.shape[1])).wait_send()
                remote(e_send.at[i], e_land.at[i], end_send.at[i], end_recv.at[i], target(i)).wait_recv()

        ends_out[...] = e_land[...]

        def finish(j, carry):
            to_y(j).wait_send()

            @pl.when(z == 0)
            def _():
                go_right(j, 1, land_c.at[chunk(j), y, pl.ds(1, 3)]).wait_send()

            @pl.when(z == 1)
            def _():
                go_right(j, 2, land_r.at[j, pl.ds(1, 2)]).wait_send()
                go_left(j, 1, land_l.at[j, pl.ds(0, 1)]).wait_send()

            @pl.when(z == 2)
            def _():
                go_right(j, 3, land_r.at[j, pl.ds(2, 1)]).wait_send()
                go_left(j, 2, land_l.at[j, pl.ds(0, 2)]).wait_send()

            @pl.when(z == last)
            def _():
                go_left(j, 3, land_c.at[chunk(j), y, pl.ds(0, 3)]).wait_send()

            return carry

        lax.fori_loop(0, usual, finish, 0)

        def finish_far(b, carry):
            j = FAR_AT + b
            far_across(b).wait_send()

            @pl.when(z == 0)
            def _():
                far_right(b, 1, land_c.at[j, :, pl.ds(1, 3)]).wait_send()

            @pl.when(z == 1)
            def _():
                far_right(b, 2, far_r.at[b, :, pl.ds(1, 2)]).wait_send()
                far_left(b, 1, far_l.at[b, :, pl.ds(0, 1)]).wait_send()

            @pl.when(z == 2)
            def _():
                far_right(b, 3, far_r.at[b, :, pl.ds(2, 1)]).wait_send()
                far_left(b, 2, far_l.at[b, :, pl.ds(0, 2)]).wait_send()

            @pl.when(z == last)
            def _():
                far_left(b, 3, land_c.at[j, :, pl.ds(0, 3)]).wait_send()

            return carry

        lax.fori_loop(0, FAR, finish_far, 0)


def last_back(x, y, dy, kept, w, norms, cost, sint):
    q, k, v, ko, vo, o, e, l, gu, n1, i1, n2, i2 = kept
    rows, width = x.shape
    heads = width // 128
    depth, columns = w.shape[2:]
    parts = columns // WIDE
    units = (columns - width) // 3
    dma = pltpu.SemaphoreType.DMA
    hbm = pl.BlockSpec(memory_space=pl.ANY)
    halves = (2, rows // 2, width)

    def once(shape, at=None):
        return pl.BlockSpec(shape, lambda i: at or (0,) * len(shape), pipeline_mode=pl.Buffered(1))

    def by_pair(shape):
        return pl.BlockSpec(shape, lambda i: (jnp.clip(i - FIRST_PAIR, 0, PAIRS - 1),) + (0,) * (len(shape) - 1))

    pair = by_pair((1, rows, 128))
    group = (4, 4, depth, GROUP)
    return pl.pallas_call(
        functools.partial(last_kernel, parts),
        grid=(LAST_STEP + 1,),
        in_specs=[
            once((rows, width)), once((rows, 128)), once((rows, width)), once((rows, 128)),
            pl.BlockSpec((1, 2, rows, 512), lambda i: (jnp.minimum(i, FIRST_PAIR - 1), 0, 0, 0)),
            pl.BlockSpec(group, lambda i: (0, 0, 0, jnp.where(i < FIRST_PAIR, 2 + i, 0))),
            once((4, width)),
            pair, pair, pair, pair, pair,
            by_pair((1, 2, 8, rows)),
            once(cost.shape), once(sint.shape),
            hbm, hbm, hbm, hbm, hbm, hbm,
        ],
        out_specs=[
            once((3, depth, depth)), once((depth, depth)), once((depth, 2 * units)), once((depth, units)), once(halves), once((8, width)),
        ],
        out_shape=[
            sds((3, depth, depth), F32), sds((depth, depth), F32), sds((depth, 2 * units), F32), sds((depth, units), F32),
            sds(halves, BF), sds((8, width), F32),
        ],
        scratch_shapes=[
            VM((rows, width), F32),
            VM((rows, width), BF),
            VM((rows, width), BF),
            VM((heads, rows, 128), BF),
            VM(group, BF),
            VM((2, 2, 2, 4, depth, GROUP), BF),
            VM((3, rows, 128), BF),
            VM((2, width, 384), BF),
            VM((heads, rows, 128), BF),
            VM((heads, 2, 128, rows), BF),
            VM((heads, 2, 128, rows), BF),
            VM((heads, 2, 128, rows), BF),
            VM((2, 2 * rows, rows), BF),
            VM(halves, BF),
            VM(halves, BF),
            VM((depth, WIDE), F32),
            VM((parts, 2, 4, depth, WIDE), BF),
            VM((parts - FAR, 4, depth, WIDE), BF),
            VM((parts - FAR, 3, depth, WIDE), BF),
            VM((parts - FAR, 3, depth, WIDE), BF),
            VM((8, 8, width), F32),
            VM((FAR, 2, depth, WIDE), BF),
            VM((FAR, depth, WIDE), BF),
            VM((FAR, 2, 3, depth, WIDE), BF),
            VM((FAR, 2, 3, depth, WIDE), BF),
            dma, dma, dma, dma, dma, dma,
            dma((6,)), dma((6,)), dma, dma((2,)), dma((2,)),
        ]
        + [dma((parts,))] * 8
        + [dma((4,))] * 2
        + [dma((FAR,))] * 6,
        compiler_params=pltpu.CompilerParams(collective_id=0, has_side_effects=True, vmem_limit_bytes=63 << 20),
        name="last",
    )(n1, i1, n2, i2, gu, w, norms, q, k, v, ko, vo, l, cost, sint, dy.reshape(halves), x, y.reshape(halves), e, o, w)


LAG = 6
GATHER = 256


def first_kernel(
    parts, tok_ref, top_ref, lead_ref, down_ref, pair_ref, gain_ref, bias_ref, len_ref, cos_ref, sin_ref, cost_ref, sint_ref,
    w_out, q_out, k_out, v_out, ko_out, vo_out, y_out, e_out, o_out, gu_out, n1_out, n2_out,
    x_out, dy_out, l_out, i1_out, i2_out, norm_out,
    w, xin, q, kv, land_kv, late_kv, o, hb, acc, relay, land_rows, ext, lens,
    mask, eb, gu, n1, n2, df, do3, dq, keep, oth, got, d,
    tok_sem, tok_send, tok_recv, lead_sem, shard_sem, back_sem, kv_send, kv_recv, out_sem, row_send, row_recv, again_send, again_recv,
    e_sem, gu_sem, oth_send, oth_recv, dz_send, dz_recv,
    small_send, small_recv, rs_sem, rr_sem, ls_sem, lr_sem, ys_sem, yr_sem, cs_sem, cr_sem,
):
    section = lax.axis_index("section")
    y, c, z = lax.axis_index("y"), lax.axis_index("core"), lax.axis_index("tensor")
    last = 3
    rows, width = xin.shape[0] * xin.shape[1], xin.shape[2]
    near, across, other = {"core": 1 - c}, {"y": 1 - y}, {"section": 1 - section}
    right, left = {"tensor": jnp.minimum(z + 1, last)}, {"tensor": jnp.maximum(z - 1, 0)}
    side = z // 2
    barrier = pltpu.get_barrier_semaphore()

    def greet(device):
        pl.semaphore_signal(barrier, inc=1, device_id=device, device_id_type=MESH)

    def remote(src, dst, send, recv, device):
        return pltpu.make_async_remote_copy(src, dst, send, recv, device_id=device, device_id_type=MESH)

    def target(i):
        return {"core": side, "tensor": 2 * c + i}

    def at_home(i):
        return jnp.logical_and(side == c, 2 * c + i == z)

    def token_copy(src, i, part):
        return remote(src.at[i, part], xin.at[z % 2, part], tok_send.at[i], tok_recv.at[z % 2], target(i))

    def token_home(src, i):
        return pltpu.make_async_copy(src.at[i], xin.at[z % 2], tok_sem)

    def by_section(body):
        for n, src in enumerate((tok_ref, top_ref)):
            pl.when(section == n)(functools.partial(body, src))

    groups = down_ref.shape[1] // 128

    def load_group(k, m):
        src = down_ref if m == 0 else pair_ref
        cols = pl.ds(128 * (k + (m - 1) * groups if m else k), 128)
        return pltpu.make_async_copy(src.at[:, cols], w.at[y, c, z, :, pl.ds(width + GROUP * k + 128 * m, 128)], shard_sem.at[k, m])

    load_lead = pltpu.make_async_copy(lead_ref, w.at[y, c, z, :, pl.ds(0, width)], lead_sem)
    load_lead.start()
    loads = [load_group(k, m) for k in range(groups) for m in range(3)]
    for load in loads:
        load.start()
    greet(near)
    greet(across)
    greet(other)

    @pl.when(z < last)
    def _():
        greet(right)

    @pl.when(z > 0)
    def _():
        greet(left)

    for i in range(2):

        @pl.when(jnp.logical_not(at_home(i)))
        def _():
            greet(target(i))

    count = 5 + jnp.where(z < last, 1, 0) + jnp.where(z > 0, 1, 0) - jnp.where(side == c, 1, 0)
    pl.semaphore_wait(barrier, count)

    ext[y, c, 0:1] = gain_ref[...].astype(F32)
    ext[y, c, 1:2] = bias_ref[...].astype(F32)
    lens[c] = len_ref[...]

    def small(k):
        if k == 0:
            return remote(lens.at[c], lens.at[c], small_send.at[0], small_recv.at[0], near)
        if k == 1:
            return remote(ext.at[y, c], ext.at[y, c], small_send.at[1], small_recv.at[1], across)
        return remote(ext.at[:, c], ext.at[:, c], small_send.at[2], small_recv.at[2], near)

    small(0).start()
    small(1).start()
    load_lead.wait()
    for load in loads:
        load.wait()

    def columns(j):
        return pl.ds(pl.multiple_of(j * GATHER, GATHER), GATHER)

    def go_right(j, h):
        b = jnp.maximum(z - h, 0)
        return remote(w.at[y, c, b, :, columns(j)], w.at[y, c, b, :, columns(j)], rs_sem.at[j, h], rr_sem.at[j, h], right)

    def go_left(j, h):
        b = jnp.minimum(z + h, last)
        return remote(w.at[y, c, b, :, columns(j)], w.at[y, c, b, :, columns(j)], ls_sem.at[j, h], lr_sem.at[j, h], left)

    def to_y(j):
        return remote(w.at[y, c, :, :, columns(j)], w.at[y, c, :, :, columns(j)], ys_sem.at[j], yr_sem.at[j], across)

    def block_to_y(j, b):
        return remote(w.at[y, c, b, :, columns(j)], w.at[y, c, b, :, columns(j)], ys_sem.at[j], yr_sem.at[j], across)

    def to_core(j):
        return remote(w.at[:, c, :, :, columns(j)], w.at[:, c, :, :, columns(j)], cs_sem.at[j], cr_sem.at[j], near)

    def write_back(j):
        return pltpu.make_async_copy(w.at[:, :, :, :, columns(j)], w_out.at[:, :, :, :, columns(j)], back_sem.at[j])

    def stage(r, lag, body):
        @pl.when(jnp.logical_and(r >= lag, r - lag < parts))
        def _():
            body(r - lag)

    def send_own(j):
        @pl.when(z < last)
        def _():
            go_right(j, 0).start()

        @pl.when(z > 0)
        def _():
            go_left(j, 0).start()

        block_to_y(j, z).start()

    def hop(h, j):
        @pl.when(z >= h)
        def _():
            go_right(j, h - 1).wait_recv()
            block_to_y(j, z - h).start()

        @pl.when(z + h <= last)
        def _():
            go_left(j, h - 1).wait_recv()
            block_to_y(j, z + h).start()

        if h < last:

            @pl.when(jnp.logical_and(z >= h, z < last))
            def _():
                go_right(j, h).start()

            @pl.when(jnp.logical_and(z + h <= last, z > 0))
            def _():
                go_left(j, h).start()

    def over_core(j):
        to_y(j).wait_recv()
        to_core(j).start()

    def complete(j):
        to_core(j).wait_recv()
        write_back(j).start()

    def round_(r):
        stage(r, 0, send_own)
        stage(r, 1, functools.partial(hop, 1))
        stage(r, 2, functools.partial(hop, 2))
        stage(r, 3, functools.partial(hop, 3))
        stage(r, 5, over_core)
        stage(r, LAG, complete)

    def rounds(first, end):
        lax.fori_loop(first, end, lambda r, t: (round_(r), t)[1], 0)

    start = 9
    token_rows = xin.shape[1] // 8
    for i in range(2):

        @pl.when(at_home(i))
        def _():
            by_section(lambda src: token_home(src, i).start())

    def early(r, carry):
        round_(r)
        part = pl.ds(pl.multiple_of(r * token_rows, token_rows), token_rows)
        for i in range(2):

            @pl.when(jnp.logical_not(at_home(i)))
            def _():
                by_section(lambda src: token_copy(src, i, part).start())

        return carry

    lax.fori_loop(0, 3, early, 0)
    small(0).wait()
    small(1).wait()
    small(2).start()

    mine = jnp.where(side == 0, lens[0], lens[1])
    mine = jnp.where(z % 2 == 0, mine[0:1], mine[1:2])
    at_q = c * rows + lax.broadcasted_iota(jnp.int32, (1, rows), 1)
    at_k = lax.broadcasted_iota(jnp.int32, (2 * rows, 1), 0)
    at_k = jnp.where(at_k < rows, c * rows + at_k, (1 - c) * rows + at_k - rows)
    seg_q, seg_k = jnp.zeros((1, rows), jnp.int32), jnp.zeros((2 * rows, 1), jnp.int32)
    end = jnp.zeros((1, 1), jnp.int32)
    for n in range(8):
        end = end + mine[:, n : n + 1]
        seg_q = seg_q + jnp.where(end <= at_q, 1, 0)
        seg_k = seg_k + jnp.where(end <= at_k, 1, 0)
    mask[...] = jnp.where(seg_k == seg_q, 0.0, neg_fill).astype(F32)
    lax.fori_loop(3, 8, early, 0)
    rounds(8, start)

    small(2).wait()
    for k in range(2):
        for half in range(2):
            norm_out[2 * k + half : 2 * k + half + 1] = jnp.concatenate([ext[half, i, k : k + 1] for i in range(2)], axis=1)

    for i in range(2):

        @pl.when(at_home(i))
        def _():
            token_home(tok_ref, i).wait()

        @pl.when(jnp.logical_not(at_home(i)))
        def _():
            token_copy(tok_ref, i, pl.ds(0, xin.shape[1])).wait_send()
            remote(tok_ref.at[i], xin.at[i], tok_send.at[i], tok_recv.at[i], target(i)).wait_recv()

    def project(at, count, x):
        here = pl.ds(at, count)
        cos, sin = cos_ref[pl.ds(c * rows + at, count)], sin_ref[pl.ds(c * rows + at, count)]
        low = low_lanes((count, 128))
        for p in range(2):
            r = [dg(x, w[:, :, 2 * p + e, :, :640].reshape(width, 640), NN) for e in range(2)]
            t = [[v[:, 128 * i : 128 * i + 128] for i in range(5)] for v in r]
            qs = [t[0][0], jnp.where(low, t[0][3], swap64(t[1][3])), t[1][0]]
            ks = [t[0][1], jnp.where(low, swap64(t[0][3]), t[1][3]), t[1][1]]
            vs = [t[0][2], jnp.where(low, t[0][4], swap64(t[1][4])), t[1][2]]
            for i in range(3):
                q[3 * p + i, here] = (rope_fwd(qs[i], cos, sin) * HD**-0.5).astype(BF)
                kv[0, 3 * p + i, here] = rope_fwd(ks[i], cos, sin).astype(BF)
                kv[1, 3 * p + i, here] = vs[i].astype(BF)

    x = xin[...].reshape(rows, width)
    x_out[...] = x
    project(0, rows, x)
    low = low_lanes((rows, 128))
    share = remote(kv, land_kv, kv_send.at[0], kv_recv.at[0], near)
    share.start()
    rounds(start, start + 1)
    share.wait()

    def heads_of(p, others, save):
        k = jnp.concatenate([kv[0, p], others[0, p]], axis=0)
        v = jnp.concatenate([kv[1, p], others[1, p]], axis=0)
        vt = v.astype(F32).T.astype(BF)
        ones = jnp.ones((16, 2 * rows), BF)
        outs = []
        for h in range(2):
            qm = jnp.where(low if h == 0 else jnp.logical_not(low), q[p], jnp.zeros((rows, 128), BF))
            s = dg(k, qm, NT) + mask[...]
            e = jnp.exp(s - jnp.max(s, axis=0, keepdims=True)).astype(BF)
            t = dg(jnp.concatenate([vt[HD * h : HD * h + HD], ones], axis=0), e, NN)
            inv = 1.0 / t[HD : HD + 1]
            save(h, e, inv)
            outs.append(t[:HD] * inv)
        o[p] = jnp.concatenate(outs, axis=0).T.astype(BF)

    def pair(p, carry):
        heads_of(p, land_kv, lambda h, e, inv: None)
        pl.when(p % 2 == 1)(functools.partial(round_, start + 1 + p // 2))
        return carry

    def out_part(p):
        wo = []
        for e in range(2):
            wo.append([w[:, :, 2 * p + e, :, 512 + 128 * i : 640 + 128 * i].reshape(width, 128) for i in range(2)])
        mid = jnp.where(low_lanes((width, 128)), swap64(wo[0][0].astype(F32)), wo[1][0].astype(F32)).astype(BF)
        return jnp.concatenate([wo[0][1], mid, wo[1][1]], axis=1)

    def mix(x):
        r = x.astype(F32)
        for p in range(2):
            r = r + dg(jnp.concatenate([o[3 * p + i] for i in range(3)], axis=1), out_part(p), NT)
        return norm_parts(r)

    def group_of(k):
        return unit_weights(
            lambda t, m: w[:, :, t, :, pl.ds(pl.multiple_of(width + GROUP * k + 128 * m, 128), 128)].reshape(width, 128)
        )

    def unit(k, save):
        wd, wg, wu = group_of(k)
        gate = dg(hb[...], wg, NN)
        up = dg(hb[...], wu, NN)
        save(gate, up)
        act = (gate / (1.0 + jnp.exp(-gate)) * up).astype(BF)
        acc[...] += dg(act, wd, NT)

    lax.fori_loop(0, 6, pair, 0)
    n, inv = mix(x)
    h = n * norm_out[0:1] + norm_out[2:3]
    hb[...] = h.astype(BF)
    acc[...] = h
    rounds(start + 4, start + 5)

    def units(k, carry):
        for at, r in ((2, 5), (4, 6), (4, 7), (5, 8)):
            pl.when(k == at)(functools.partial(round_, start + r))

        unit(k, lambda gate, up: None)
        return carry

    lax.fori_loop(0, 6, units, 0)
    pieces = relay.shape[0]
    piece_rows = rows // pieces

    def row_copy(b):
        return remote(relay.at[b], land_rows.at[b], row_send.at[b], row_recv.at[b], other)

    def again(b):
        part = pl.ds(pl.multiple_of(b * piece_rows, piece_rows), piece_rows)
        return remote(kv.at[:, :, part], late_kv.at[:, :, part], again_send.at[b], again_recv.at[b], near)

    kept_out = []

    def keep_out(src, dst):
        copy = pltpu.make_async_copy(src, dst, out_sem.at[len(kept_out)])
        kept_out.append(copy)
        copy.start()

    @pl.when(section == 0)
    def _():
        def send_rows(b, carry):
            part = pl.ds(pl.multiple_of(b * piece_rows, piece_rows), piece_rows)
            n, inv = norm_parts(acc[part])
            relay[b] = (n * norm_out[1:2] + norm_out[3:4]).astype(BF)
            row_copy(b).start()
            return carry

        lax.fori_loop(0, pieces, send_rows, 0)
        same = pltpu.make_async_copy(land_kv, late_kv, kv_send.at[1])
        same.start()
        same.wait()

    @pl.when(section == 1)
    def _():
        def project_rows(b, carry):
            at = pl.multiple_of(b * piece_rows, piece_rows)
            row_copy(b).wait_recv()
            x_out[pl.ds(at, piece_rows)] = land_rows[b]
            project(at, piece_rows, land_rows[b])
            again(b).start()
            return carry

        lax.fori_loop(0, pieces, project_rows, 0)
        lax.fori_loop(0, pieces, lambda b, t: (again(b).wait(), t)[1], 0)

    for src, dst in ((q, q_out), (kv.at[0], k_out), (kv.at[1], v_out), (late_kv.at[0], ko_out), (late_kv.at[1], vo_out)):
        keep_out(src, dst)

    def probs_out(p):
        return pltpu.make_async_copy(eb.at[p % 2], e_out.at[p], e_sem.at[p % 2])

    def probs_in(p):
        return pltpu.make_async_copy(e_out.at[p], eb.at[p % 2], e_sem.at[p % 2])

    def pair_kept(p, carry):
        @pl.when(p >= 2)
        def _():
            probs_out(p - 2).wait()

        def save(h, e, inv):
            eb[p % 2, h] = e
            l_out[p, h] = jnp.broadcast_to(inv, l_out.shape[2:])

        heads_of(p, late_kv, save)
        probs_out(p).start()
        return carry

    lax.fori_loop(0, PAIRS, pair_kept, 0)
    keep_out(o, o_out)
    n, inv = mix(x_out[...])
    n1[...] = n.astype(BF)
    i1_out[...] = jnp.broadcast_to(inv, i1_out.shape)
    keep_out(n1, n1_out)
    h = n * norm_out[0:1] + norm_out[2:3]
    hb[...] = h.astype(BF)
    acc[...] = h

    def units_out(k):
        return pltpu.make_async_copy(gu.at[k % 2], gu_out.at[k], gu_sem.at[k % 2])

    def units_in(k):
        return pltpu.make_async_copy(gu_out.at[k], gu.at[k % 2], gu_sem.at[k % 2])

    def unit_kept(k, carry):
        @pl.when(k >= 2)
        def _():
            units_out(k - 2).wait()

        def save(gate, up):
            gu[k % 2, 0] = gate.astype(BF)
            gu[k % 2, 1] = up.astype(BF)

        unit(k, save)
        units_out(k).start()
        return carry

    lax.fori_loop(0, 6, unit_kept, 0)
    n, inv = norm_parts(acc[...])
    n2[...] = n.astype(BF)
    i2_out[...] = jnp.broadcast_to(inv, i2_out.shape)
    keep_out(n2, n2_out)
    hb[...] = (n * norm_out[1:2] + norm_out[3:4]).astype(BF)
    keep_out(hb, y_out)
    for p in (PAIRS - 2, PAIRS - 1):
        probs_out(p).wait()
        units_out(p).wait()

    def dz_copy(b):
        return remote(relay.at[b], land_rows.at[b], dz_send.at[b], dz_recv.at[b], other)

    def oth_copy(p):
        return remote(oth.at[p], got.at[p], oth_send.at[p], oth_recv.at[p], near)

    @pl.when(section == 1)
    def _():
        dr2 = norm_back(xin[...].reshape(rows, width).astype(F32) * norm_out[1:2], n, inv)
        acc[...] = dr2
        df[...] = dr2.astype(BF)
        for p in range(2):
            probs_in(p).start()
            units_in(p).start()

        def unit_back(k, carry):
            wd, wg, wu = group_of(k)
            units_in(k).wait()
            gate = gu[k % 2, 0].astype(F32)
            up = gu[k % 2, 1].astype(F32)
            s = 1.0 / (1.0 + jnp.exp(-gate))
            d_act = dg(df[...], wd, NN)
            d_gate = (d_act * up * (s * (1.0 + gate * (1.0 - s)))).astype(BF)
            d_up = (d_act * (gate * s)).astype(BF)
            acc[...] += dg(d_gate, wg, NT) + dg(d_up, wu, NT)

            @pl.when(k + 2 < 6)
            def _():
                units_in(k + 2).start()

            return carry

        lax.fori_loop(0, 6, unit_back, 0)
        dr1 = norm_back(acc[...] * norm_out[0:1], n1[...].astype(F32), i1_out[:, :1])
        acc[...] = dr1
        df[...] = dr1.astype(BF)
        cost, sint = cost_ref[:, pl.ds(c * rows, rows)], sint_ref[:, pl.ds(c * rows, rows)]

        def pair_of(p, carry):
            probs_in(p).wait()
            dqt, dk, dv = pair_back(
                do3[p % 3], o[p], q[p], kv[0, p], kv[1, p], late_kv[0, p], late_kv[1, p],
                [eb.at[p % 2, h] for h in range(2)], [l_out[p, h, 0:1] for h in range(2)], cost, sint,
            )

            @pl.when(p + 2 < PAIRS)
            def _():
                probs_in(p + 2).start()

            dq[p] = dqt.T.astype(BF)
            keep[p, 0] = dk[:, :rows].astype(BF)
            keep[p, 1] = dv[:, :rows].astype(BF)
            oth[p, 0] = dk[:, rows:].astype(BF)
            oth[p, 1] = dv[:, rows:].astype(BF)
            oth_copy(p).start()
            return carry

        def joint(half):
            def total(i, m):
                return keep[i, m].astype(F32) + got[i, m].astype(F32)

            three = range(3 * half, 3 * half + 3)
            for i in three:
                oth_copy(i).wait()
            parts = joint_parts(
                [dq[i].astype(F32) for i in three], [total(i, 0) for i in three], [total(i, 1) for i in three], cost, sint
            )
            for e in range(2):
                d[2 * half + e] = parts[e]

        for half in range(2):
            t = dg(df[...], out_part(half), NN).astype(BF)
            for i in range(3):
                do3[i] = t[:, 128 * i : 128 * i + 128]
            lax.fori_loop(3 * half, 3 * half + 3, pair_of, 0)
        for half in range(2):
            joint(half)

        def send_back(b, carry):
            part = pl.ds(pl.multiple_of(b * piece_rows, piece_rows), piece_rows)
            total = acc[part]
            for t in range(4):
                total += dg(d[t, part], w[:, :, t, :, :640].reshape(width, 640), NT)
            relay[b] = total.astype(BF)
            dz_copy(b).start()
            return carry

        lax.fori_loop(0, pieces, send_back, 0)
        dy_out[...] = xin[...].reshape(rows, width)
        lax.fori_loop(0, pieces, lambda b, t: (dz_copy(b).wait_send(), t)[1], 0)

    @pl.when(section == 0)
    def _():
        lax.fori_loop(0, pieces, lambda b, t: (row_copy(b).wait_send(), t)[1], 0)
        lax.fori_loop(0, pieces, lambda b, t: (dz_copy(b).wait_recv(), t)[1], 0)
        dy_out[...] = land_rows[...].reshape(rows, width)

    for copy in kept_out:
        copy.wait()

    def finish(j, carry):
        write_back(j).wait()
        to_y(j).wait_send()
        to_core(j).wait_send()
        for h in range(last):

            @pl.when(jnp.logical_and(z >= h, z < last))
            def _():
                go_right(j, h).wait_send()

            @pl.when(jnp.logical_and(z + h <= last, z > 0))
            def _():
                go_left(j, h).wait_send()

        return carry

    lax.fori_loop(0, parts, finish, 0)


def first_layer(tokens, top, shards, gains, biases, lengths, cos, sin, cost, sint):
    micro, own, width = tokens.shape
    lead_part, down, pair = shards
    depth = lead_part.shape[0]
    columns = lead_part.shape[1] + down.shape[1] + pair.shape[1]
    rows = 2 * own
    parts = columns // GATHER
    heads = width // 128
    dma = pltpu.SemaphoreType.DMA
    hbm = pl.BlockSpec(memory_space=pl.ANY)
    vm = pl.BlockSpec(memory_space=VM)
    return pl.pallas_call(
        functools.partial(first_kernel, parts),
        in_specs=[hbm] * 5 + [vm] * 7,
        out_specs=[hbm] * 12 + [vm] * 6,
        out_shape=[sds((2, 2, 4, depth, columns), BF)]
        + [sds((heads, rows, 128), BF)] * 5
        + [
            sds((rows, width), BF),
            sds((heads, 2, 2 * rows, rows), BF),
            sds((heads, rows, 128), BF),
            sds((6, 2, rows, 512), BF),
            sds((rows, width), BF),
            sds((rows, width), BF),
            sds((rows, width), BF),
            sds((rows, width), BF),
            sds((heads, 2, 8, rows), F32),
            sds((rows, 128), F32),
            sds((rows, 128), F32),
            sds((4, width), F32),
        ],
        scratch_shapes=[
            VM((2, 2, 4, depth, columns), BF),
            VM((2, own, width), BF),
            VM((heads, rows, 128), BF),
            VM((2, heads, rows, 128), BF),
            VM((2, heads, rows, 128), BF),
            VM((2, heads, rows, 128), BF),
            VM((heads, rows, 128), BF),
            VM((rows, width), BF),
            VM((rows, width), F32),
            VM((4, rows // 4, width), BF),
            VM((4, rows // 4, width), BF),
            VM((2, 2, 8, gains.shape[1]), F32),
            VM((2,) + lengths.shape, jnp.int32),
            VM((2 * rows, rows), F32),
            VM((2, 2, 2 * rows, rows), BF),
            VM((2, 2, rows, 512), BF),
            VM((rows, width), BF),
            VM((rows, width), BF),
            VM((rows, width), BF),
            VM((3, rows, 128), BF),
            VM((heads, rows, 128), BF),
            VM((heads, 2, 128, rows), BF),
            VM((heads, 2, 128, rows), BF),
            VM((heads, 2, 128, rows), BF),
            VM((4, rows, 640), BF),
            dma, dma((2,)), dma((2,)), dma, dma((6, 3)), dma((parts,)), dma((2,)), dma((2,)), dma((9,)), dma((4,)), dma((4,)), dma((4,)), dma((4,)),
            dma((2,)), dma((2,)), dma((6,)), dma((6,)), dma((4,)), dma((4,)),
            dma((3,)), dma((3,)),
            dma((parts, 3)), dma((parts, 3)), dma((parts, 3)), dma((parts, 3)),
            dma((parts,)), dma((parts,)), dma((parts,)), dma((parts,)),
        ],
        compiler_params=pltpu.CompilerParams(collective_id=1, has_side_effects=True, vmem_limit_bytes=63 << 20),
        name="first",
    )(tokens, top, *shards, gains, biases, lengths, cos, sin, cost, sint)


def swap_pairs(tp, step, dp_axes):
    pairs = []
    half = tp // 2
    for core in range(2):
        for at in range(tp):
            source = core * tp + at
            target = (at // half) * tp + half * core + (at + step) % half
            pairs.append((source, target))
    return pairs


def to_sequences(rows, tp):
    half = tp // 2
    at = lax.axis_index("tensor")
    pieces = [None] * half
    got = []
    for step in range(half):
        piece = lax.dynamic_index_in_dim(rows, (at + step) % half, 0, keepdims=False)
        got.append(lax.ppermute(piece, ("core", "tensor"), swap_pairs(tp, step, None)))
    stacked = jnp.stack(got)
    order = (at - jnp.arange(half)) % half
    return jnp.take(stacked, order, axis=0).reshape(-1, rows.shape[-1])


def to_positions(rows, tp):
    half = tp // 2
    at = lax.axis_index("tensor")
    parts = rows.reshape(half, -1, rows.shape[-1])
    got = []
    for step in range(half):
        piece = lax.dynamic_index_in_dim(parts, (at - step) % half, 0, keepdims=False)
        back = [(target, source) for source, target in swap_pairs(tp, step, None)]
        got.append(lax.ppermute(piece, ("core", "tensor"), back))
    stacked = jnp.stack(got)
    order = (at + jnp.arange(half)) % half
    return jnp.take(stacked, (jnp.arange(half) - at) % half, axis=0)


def rope_tables(positions):
    halfway = HD // 2
    freqs = 1000.0 ** (-jnp.arange(halfway, dtype=F32) / halfway)
    angles = positions.astype(F32)[:, None] * freqs[None, :]
    cos, sin = jnp.cos(angles), jnp.sin(angles)
    wide = jnp.concatenate([cos] * 4, axis=1)
    signed = jnp.concatenate([-sin, sin] * 2, axis=1)
    return wide, signed, cos.T, sin.T


def pack_shard(w_qkv, w_out, w_gate_up, w_down):
    rows = w_qkv.shape[0]
    odd = lax.axis_index("tensor") % 2 == 1
    heads = w_qkv.reshape(rows, 3, 3, HD)
    mine = w_out.T.reshape(rows, 3, HD)
    heads = jnp.where(odd, jnp.roll(heads, -1, axis=2), heads)
    mine = jnp.where(odd, jnp.roll(mine, -1, axis=1), mine)
    first = jnp.concatenate(
        [heads[:, :, :2].reshape(rows, -1), heads[:, :, 2].reshape(rows, -1), mine[:, 2], mine[:, :2].reshape(rows, -1)], axis=1
    )
    return first, w_down.T, w_gate_up.reshape(rows, -1)


def join_shard(first, down, pair):
    rows = first.shape[0]
    units = jnp.concatenate([down, pair], axis=1).reshape(rows, 3, -1, 128).transpose(0, 2, 1, 3)
    return jnp.concatenate([first, units.reshape(rows, -1)], axis=1)


def unpack_first(first):
    rows = first.shape[0]
    odd = lax.axis_index("tensor") % 2 == 1
    both = first[:, :384].reshape(rows, 3, 2, HD)
    single = first[:, 384:576].reshape(rows, 3, 1, HD)
    heads = jnp.concatenate([both, single], axis=2)
    mine = jnp.concatenate([first[:, 640:].reshape(rows, 2, HD), first[:, 576:640].reshape(rows, 1, HD)], axis=1)
    heads = jnp.where(odd, jnp.roll(heads, 1, axis=2), heads)
    mine = jnp.where(odd, jnp.roll(mine, 1, axis=1), mine)
    return heads.reshape(rows, 3, -1), mine.reshape(rows, -1).T


def host_tables(length):
    halfway = HD // 2
    freqs = np.float32(1000.0) ** (-np.arange(halfway, dtype=np.float32) / np.float32(halfway))
    angles = np.arange(length, dtype=np.float32)[:, None] * freqs[None, :]
    cos, sin = np.cos(angles), np.sin(angles)
    return np.concatenate([cos] * 4, axis=1), np.concatenate([-sin, sin] * 2, axis=1), cos.T.copy(), sin.T.copy()


BLOCKS = 4


def gather_shard(shard, dp, tp):
    rows, columns = shard.shape
    got = lax.all_gather(shard, ALL, axis=0, tiled=False)
    got = got.reshape(BLOCKS, dp // BLOCKS, tp, rows, columns)
    return got.transpose(0, 2, 1, 3, 4).reshape(BLOCKS, tp, -1, columns)


def scatter_sum(whole, dp, tp):
    columns = whole.shape[3]
    parts = whole.reshape(BLOCKS, tp, dp // BLOCKS, -1, columns).transpose(0, 2, 1, 3, 4)
    parts = parts.reshape(dp * tp, -1, columns)
    return lax.psum_scatter(parts, ALL, scatter_dimension=0, tiled=False).astype(F32)


def on_device(dp, tp, tokens, cotangent, lengths, w_qkv, w_out, w_gate_up, w_down, norm_gains, norm_biases):
    section = lax.axis_index("section")
    core = lax.axis_index("core")
    at = lax.axis_index("tensor")
    micro, own, width = tokens.shape
    assert micro * 2 == tp
    length = own * tp
    rows = length // 2
    shards = pack_shard(w_qkv[0], w_out[0], w_gate_up[0], w_down[0])
    if dp == 4 and tp == 4:
        wide, signed, cost, sint = host_tables(length)
        (
            weights, q, k, v, ko, vo, y, e, o, gu, n1, n2, inputs, dy, l, i1, i2, small,
        ) = first_layer(tokens, cotangent, shards, norm_gains, norm_biases, lengths, wide, signed, cost, sint)
        weights = weights.reshape((BLOCKS,) + weights.shape[2:])
        kept = (q, k, v, ko, vo, o, e, l, gu, n1, i1, n2, i2)
        joint, mix, pair, down, ends, total = last_back(inputs, y, dy, kept, weights, small, cost, sint)
        small = lax.dynamic_slice_in_dim(total[:4].reshape(2, dp * tp, -1), lax.axis_index(ALL), 1, 1)
        gains, biases = small[0, 0], small[1, 0]
        joint, down = joint.transpose(1, 0, 2), down.T
    else:
        near = core * rows + jnp.arange(rows, dtype=jnp.int32)
        far = (1 - core) * rows + jnp.arange(rows, dtype=jnp.int32)
        tabs = rope_tables(near)
        weights = gather_shard(join_shard(*shards), dp, tp)
        norms = jnp.concatenate([norm_gains, norm_biases])
        norms = lax.all_gather(norms, ("y", "core"), axis=1, tiled=True).astype(F32)
        norms = (norms[0].reshape(2, width), norms[1].reshape(2, width))
        grad_top = to_sequences(cotangent, tp)
        tokens = to_sequences(tokens, tp)
        chip_lengths = lax.all_gather(lengths, "core", axis=0, tiled=True)
        my_lengths = lax.dynamic_index_in_dim(chip_lengths, at, 0, keepdims=False)
        ends_at = jnp.cumsum(my_lengths)

        def segment(positions):
            return jnp.sum((ends_at[None, :] <= positions[:, None]).astype(jnp.int32), axis=-1)

        seg_near = segment(near)
        seg_all = jnp.concatenate([seg_near, segment(far)])
        mask = jnp.where(seg_all[:, None] == seg_near[None, :], 0.0, neg_fill).astype(F32)
        y, unused = forward(tokens, weights, norms, mask, tabs)
        received = lax.ppermute(y, "section", [(0, 1)])
        inputs = jnp.where(section == 0, tokens, received)
        y, kept = forward(inputs, weights, norms, mask, tabs)
        dr1, da = ffn_backward(grad_top, kept, weights, norms, False)
        unused, dz = attn_backward(inputs, da, dr1, None, kept, weights, tabs)
        received = lax.ppermute(dz, "section", [(1, 0)])
        dy = jnp.where(section == 0, received, grad_top)
        g, dr1, da, ng = ffn_backward(dy, kept, weights, norms, True)
        g, dz = attn_backward(inputs, da, dr1, g, kept, weights, tabs)
        ends = to_positions(jnp.where(section == 0, dz.astype(BF), y), tp)
        mine = scatter_sum(g, dp, tp)
        first = mine[:, :width]
        units = mine[:, width:].reshape(first.shape[0], -1, 3, 128).transpose(0, 2, 1, 3).reshape(first.shape[0], 3, -1)
        pair, down = units[:, 1:], units[:, 0].T
        joint, mix = unpack_first(first)
        gains = lax.psum_scatter(ng[0:2].reshape(-1), ALL, scatter_dimension=0, tiled=True)
        biases = lax.psum_scatter(ng[2:4].reshape(-1), ALL, scatter_dimension=0, tiled=True)
    outs = (joint, mix, pair.reshape(pair.shape[0], 2, -1), down, gains, biases)
    here = section >= 0
    return tuple(jnp.where(here, t, jnp.zeros_like(t))[None] for t in (ends,) + outs)


def solution(mesh):
    sections, dp, tp = mesh.devices.shape
    fine = Mesh(mesh.devices.reshape(sections, dp // 2, 2, tp), ("section", "y", "core", "tensor"))
    both = ("y", "core")
    in_specs = (
        P(both, "tensor", None),
        P(both, "tensor", None),
        P(both, None),
        P("section", both, None, "tensor"),
        P("section", "tensor", both),
        P("section", both, None, "tensor"),
        P("section", "tensor", both),
        P("section", both),
        P("section", both),
    )
    out_specs = (
        P("section", both, "tensor", None),
        P("section", both, None, "tensor"),
        P("section", "tensor", both),
        P("section", both, None, "tensor"),
        P("section", "tensor", both),
        P("section", ALL),
        P("section", ALL),
    )
    return jax.shard_map(
        functools.partial(on_device, dp, tp), mesh=fine, in_specs=in_specs, out_specs=out_specs, check_vma=False
    )
```

```python
import functools

import jax
import jax.numpy as jnp
import numpy as np
from jax import lax
from jax.experimental import pallas as pl
from jax.experimental.pallas import tpu as pltpu
from jax.sharding import Mesh, PartitionSpec as P

HD = 64
eps = 1e-05
neg_fill = -1e30
ALL = ("y", "core", "tensor")
BF = jnp.bfloat16
F32 = jnp.float32
MESH = pl.DeviceIdType.MESH


def dg(a, b, dims):
    return lax.dot_general(a, b, (dims, ((), ())), preferred_element_type=F32)


NN = ((1,), (0,))
NT = ((1,), (1,))
TN = ((0,), (0,))


def low_lanes(shape):
    return lax.broadcasted_iota(jnp.int32, shape, 1) < HD


def swap64(v):
    return pltpu.roll(v, HD, axis=1)


def rope_fwd(t, cos, sin):
    lane = lax.broadcasted_iota(jnp.int32, t.shape, 1) % HD
    other = jnp.where(lane < HD // 2, pltpu.roll(t, 128 - HD // 2, axis=1), pltpu.roll(t, HD // 2, axis=1))
    return t * cos + other * sin


def qkv_kernel(x_ref, w_ref, cos_ref, sin_ref, q_ref, k_ref, v_ref):
    x = x_ref[...]
    width = x.shape[1]
    r = [dg(x, w_ref[:, e, :, :640].reshape(width, 640), NN) for e in range(2)]
    c = [[t[:, 128 * i : 128 * i + 128] for i in range(5)] for t in r]
    low = low_lanes(c[0][0].shape)
    qs = [c[0][0], jnp.where(low, c[0][3], swap64(c[1][3])), c[1][0]]
    ks = [c[0][1], jnp.where(low, swap64(c[0][3]), c[1][3]), c[1][1]]
    vs = [c[0][2], jnp.where(low, c[0][4], swap64(c[1][4])), c[1][2]]
    cos, sin = cos_ref[...], sin_ref[...]
    for i in range(3):
        q_ref[i] = (rope_fwd(qs[i], cos, sin) * HD**-0.5).astype(BF)
        k_ref[i] = rope_fwd(ks[i], cos, sin).astype(BF)
        v_ref[i] = vs[i].astype(BF)


def attn_kernel(q_ref, k_ref, v_ref, ko_ref, vo_ref, m_ref, o_ref, e_ref, l_ref):
    q = q_ref[0]
    k = jnp.concatenate([k_ref[0], ko_ref[0]], axis=0)
    v = jnp.concatenate([v_ref[0], vo_ref[0]], axis=0)
    vt = v.astype(F32).T.astype(BF)
    outs = []
    for h in range(2):
        low = low_lanes(q.shape)
        qm = jnp.where(low if h == 0 else jnp.logical_not(low), q, jnp.zeros_like(q))
        s = dg(k, qm, NT) + m_ref[...]
        e = jnp.exp(s - jnp.max(s, axis=0, keepdims=True))
        inv = 1.0 / jnp.sum(e, axis=0, keepdims=True)
        eb = e.astype(BF)
        e_ref[0, h] = eb
        l_ref[0, h] = jnp.broadcast_to(inv, l_ref.shape[2:])
        outs.append(dg(vt[HD * h : HD * h + HD], eb, NN) * inv)
    o_ref[0] = jnp.concatenate(outs, axis=0).T.astype(BF)


def norm_parts(r):
    center = r - jnp.mean(r, axis=-1, keepdims=True)
    inv = lax.rsqrt(jnp.mean(center * center, axis=-1, keepdims=True) + eps)
    return center * inv, inv


def norm_back(dn, n, inv):
    return inv * (dn - jnp.mean(dn, axis=-1, keepdims=True) - n * jnp.mean(dn * n, axis=-1, keepdims=True))


def out_weight(w_ref):
    c = [[w_ref[:, e, :, 128 * i : 128 * i + 128].reshape(-1, 128) for i in range(2)] for e in range(2)]
    low = low_lanes(c[0][0].shape)
    mid = jnp.where(low, swap64(c[0][0].astype(F32)), c[1][0].astype(F32)).astype(BF)
    return [c[0][1], mid, c[1][1]]


GROUP = 384
WIDE = 128


def unit_weights(load):
    return [jnp.concatenate([load(t, m) for t in range(4)], axis=1) for m in range(3)]


def ffn_kernel(x_ref, o_ref, wo_ref, w_ref, g_ref, b_ref, y_ref, gu_ref, n1_ref, i1_ref, n2_ref, i2_ref, h_ref, hb_ref, acc_ref):
    z = pl.program_id(0)
    width = x_ref.shape[1]

    @pl.when(z == 0)
    def _():
        r = x_ref[...].astype(F32)
        for p in range(2):
            w = jnp.concatenate(out_weight(wo_ref.at[:, 2 * p : 2 * p + 2]), axis=1)
            o = jnp.concatenate([o_ref[3 * p + i] for i in range(3)], axis=1)
            r = r + dg(o, w, NT)
        n, inv = norm_parts(r)
        n1_ref[...] = n.astype(BF)
        i1_ref[...] = jnp.broadcast_to(inv, i1_ref.shape)
        h = n * g_ref[0:1] + b_ref[0:1]
        h_ref[...] = h
        hb_ref[...] = h.astype(BF)

    hb = hb_ref[...]
    wd, wg, wu = unit_weights(lambda t, m: w_ref[:, t, :, 128 * m : 128 * m + 128].reshape(width, 128))
    gate = dg(hb, wg, NN)
    up = dg(hb, wu, NN)
    gu_ref[0, 0] = gate.astype(BF)
    gu_ref[0, 1] = up.astype(BF)
    act = (gate / (1.0 + jnp.exp(-gate)) * up).astype(BF)
    part = dg(act, wd, NT)

    @pl.when(z == 0)
    def _():
        acc_ref[...] = h_ref[...] + part

    @pl.when(z > 0)
    def _():
        acc_ref[...] += part

    @pl.when(z == pl.num_programs(0) - 1)
    def _():
        n, inv = norm_parts(acc_ref[...])
        n2_ref[...] = n.astype(BF)
        i2_ref[...] = jnp.broadcast_to(inv, i2_ref.shape)
        y_ref[...] = (n * g_ref[1:2] + b_ref[1:2]).astype(BF)


def ffn_back_kernel(grads, dy_ref, n1_ref, i1_ref, n2_ref, i2_ref, gu_ref, w_ref, g_ref, b_ref, *refs):
    if grads:
        g_out, dr1_ref, da_ref, ng_ref, hb_ref, df_ref, acc_ref = refs
    else:
        dr1_ref, da_ref, df_ref, acc_ref = refs
    z = pl.program_id(0)
    width = dy_ref.shape[1]

    @pl.when(z == 0)
    def _():
        dy = dy_ref[...].astype(F32)
        n = n2_ref[...].astype(F32)
        if grads:
            ng_ref[1:2] = jnp.sum(dy * n, axis=0, keepdims=True)
            ng_ref[3:4] = jnp.sum(dy, axis=0, keepdims=True)
            hb_ref[...] = (n1_ref[...].astype(F32) * g_ref[0:1] + b_ref[0:1]).astype(BF)
        dr2 = norm_back(dy * g_ref[1:2], n, i2_ref[:, :1])
        acc_ref[...] = dr2
        df_ref[...] = dr2.astype(BF)

    df = df_ref[...]
    gate = gu_ref[0, 0].astype(F32)
    up = gu_ref[0, 1].astype(F32)
    s = 1.0 / (1.0 + jnp.exp(-gate))
    silu = gate * s
    wd, wg, wu = unit_weights(lambda t, m: w_ref[:, t, :, 128 * m : 128 * m + 128].reshape(width, 128))

    def keep(m, grad):
        for t in range(g_out.shape[1]):
            g_out[:, t, :, 128 * m : 128 * m + 128] = grad[:, 128 * t : 128 * t + 128].astype(BF).reshape(g_out.shape[0], -1, 128)

    if grads:
        keep(0, dg(df, (silu * up).astype(BF), TN))
    d_act = dg(df, wd, NN)
    d_gate = (d_act * up * (s * (1.0 + gate * (1.0 - s)))).astype(BF)
    d_up = (d_act * silu).astype(BF)
    if grads:
        hb = hb_ref[...]
        keep(1, dg(hb, d_gate, TN))
        keep(2, dg(hb, d_up, TN))
    acc_ref[...] += dg(d_gate, wg, NT) + dg(d_up, wu, NT)

    @pl.when(z == pl.num_programs(0) - 1)
    def _():
        dh = acc_ref[...]
        n = n1_ref[...].astype(F32)
        if grads:
            ng_ref[0:1] = jnp.sum(dh * n, axis=0, keepdims=True)
            ng_ref[2:3] = jnp.sum(dh, axis=0, keepdims=True)
        dr1 = norm_back(dh * g_ref[0:1], n, i1_ref[:, :1])
        dr1_ref[...] = dr1
        da_ref[...] = dr1.astype(BF)


def pair_back(do, o, q, k, v, ko, vo, e, l, cos, sin):
    dot = do.astype(F32).T
    ot = o.astype(F32).T
    k = jnp.concatenate([k, ko], axis=0)
    v = jnp.concatenate([v, vo], axis=0)
    kt = k.astype(F32).T.astype(BF)
    qt = q.astype(F32).T.astype(BF)
    dqs, dks, dvs = [], [], []
    for h in range(2):
        span = slice(HD * h, HD * h + HD)
        scaled = dot[span] * l[h]
        inner = jnp.sum(scaled * ot[span], axis=0, keepdims=True)
        sb = scaled.astype(BF)
        zero = jnp.zeros_like(sb)
        padded = jnp.concatenate([sb, zero] if h == 0 else [zero, sb], axis=0)
        dp = dg(v, padded, NN)
        et = e[h][...]
        ds = (et.astype(F32) * (dp - inner)).astype(BF)
        dvs.append(dg(sb, et, NT))
        dks.append(dg(qt[span], ds, NT))
        dqt = dg(kt[span], ds, NN) * HD**-0.5
        d1, d2 = dqt[: HD // 2], dqt[HD // 2 :]
        dqs.append(d1 * cos + d2 * sin)
        dqs.append(d2 * cos - d1 * sin)
    return [jnp.concatenate(t, axis=0) for t in (dqs, dks, dvs)]


def joint_parts(dq, dkt, dvt, cos, sin):
    dk = []
    for t in dkt:
        parts = []
        for h in range(2):
            d1 = t[HD * h : HD * h + HD // 2]
            d2 = t[HD * h + HD // 2 : HD * h + HD]
            parts += [d1 * cos + d2 * sin, d2 * cos - d1 * sin]
        dk.append(jnp.concatenate(parts, axis=0).T)
    dv = [t.T for t in dvt]
    low = low_lanes(dq[0].shape)
    zero = jnp.zeros_like(dv[1])
    d = [
        [dq[0], dk[0], dv[0], jnp.where(low, dq[1], swap64(dk[1])), jnp.where(low, dv[1], zero)],
        [dq[2], dk[2], dv[2], jnp.where(low, swap64(dq[1]), dk[1]), jnp.where(low, swap64(dv[1]), zero)],
    ]
    return [jnp.concatenate(t, axis=1).astype(BF) for t in d]


def attn_back_kernel(grads, da_ref, wo_ref, o_ref, q_ref, k_ref, v_ref, ko_ref, vo_ref, e_ref, l_ref, cos_ref, sin_ref, dq_ref, own_ref, oth_ref, *dwo_ref):
    da = da_ref[...]
    rows = da.shape[0]
    w = jnp.concatenate(out_weight(wo_ref), axis=1)
    do3 = dg(da, w, NN).astype(BF)
    if grads:
        o3 = jnp.concatenate([o_ref[i] for i in range(3)], axis=1)
        dwo_ref[0][0] = dg(da, o3, TN).astype(BF)
    cos, sin = cos_ref[...], sin_ref[...]
    for i in range(3):
        dqt, dk, dv = pair_back(
            do3[:, 128 * i : 128 * i + 128], o_ref[i], q_ref[i], k_ref[i], v_ref[i], ko_ref[i], vo_ref[i],
            [e_ref[i, h] for h in range(2)], [l_ref[i, h, 0:1] for h in range(2)], cos, sin,
        )
        dq_ref[i] = dqt.T.astype(BF)
        own_ref[i, 0] = dk[:, :rows]
        own_ref[i, 1] = dv[:, :rows]
        oth_ref[i, 0] = dk[:, rows:].astype(BF)
        oth_ref[i, 1] = dv[:, rows:].astype(BF)


def joint_back_kernel(grads, *refs):
    if grads:
        old_ref, x_ref, w_ref, dr1_ref, dq_ref, own_ref, got_ref, dwo_ref, cos_ref, sin_ref, g_ref, dz_ref = refs
    else:
        w_ref, dr1_ref, dq_ref, own_ref, got_ref, cos_ref, sin_ref, dz_ref, dzb_ref = refs
    p = pl.program_id(0)
    width = dr1_ref.shape[1]
    d = joint_parts(
        [dq_ref[i].astype(F32) for i in range(3)],
        [own_ref[i, 0] + got_ref[i, 0].astype(F32) for i in range(3)],
        [own_ref[i, 1] + got_ref[i, 1].astype(F32) for i in range(3)],
        cos_ref[...],
        sin_ref[...],
    )
    acc = None
    for e in range(2):
        t = dg(d[e], w_ref[:, e, :, :640].reshape(width, 640), NT)
        acc = t if acc is None else acc + t
    if grads:
        x = x_ref[...]
        wlow = low_lanes((width, 128))
        mid = dwo_ref[0, :, 128:256].astype(F32)
        sides = [dwo_ref[0, :, 0:128], dwo_ref[0, :, 256:384]]
        mids = [swap64(mid), mid]
        for e in range(2):
            g = dg(x, d[e], TN)
            blocks = g_ref.shape[0]
            g_ref[:, e, :, :512] = g[:, :512].astype(BF).reshape(blocks, -1, 512)
            g_ref[:, e, :, 512:640] = jnp.where(wlow, g[:, 512:], mids[e]).astype(BF).reshape(blocks, -1, 128)
            g_ref[:, e, :, 640:] = sides[e].reshape(blocks, -1, 128)

    @pl.when(p == 0)
    def _():
        dz_ref[...] = dr1_ref[...] + acc

    @pl.when(p > 0)
    def _():
        total = dz_ref[...] + acc
        dz_ref[...] = total
        if not grads:
            dzb_ref[...] = total.astype(BF)


BIG = pltpu.CompilerParams(vmem_limit_bytes=58 << 20)
VM = pltpu.VMEM


def full(shape):
    return pl.BlockSpec(shape, lambda i: (0,) * len(shape))


def lead(shape, at=0):
    return pl.BlockSpec(shape, lambda i: tuple(i if j == at else 0 for j in range(len(shape))))


def joint_block(w):
    return pl.BlockSpec((w.shape[0], 2, w.shape[2], 768), lambda i: (0, i, 0, 0))


def group_block(w):
    return pl.BlockSpec((w.shape[0], w.shape[1], w.shape[2], GROUP), lambda i: (0, 0, 0, 2 + i))


def sds(shape, kind):
    return jax.ShapeDtypeStruct(shape, kind)


def forward(x, weights, norms, mask, tabs):
    w = weights
    rows, width = x.shape
    heads = width // 128
    blocks, tp, depth, columns = w.shape
    steps = tp // 2
    cos, sin, cost, sint = tabs
    q, k, v = pl.pallas_call(
        qkv_kernel,
        grid=(steps,),
        in_specs=[full((rows, width)), joint_block(w), full((rows, 128)), full((rows, 128))],
        out_specs=[lead((3, rows, 128))] * 3,
        out_shape=[sds((heads, rows, 128), BF)] * 3,
        compiler_params=BIG,
        name="qkv",
    )(x, w, cos, sin)
    ko, vo = lax.ppermute((k, v), "core", [(0, 1), (1, 0)])
    return attend(x, (q, k, v, ko, vo), w, norms, mask)


def attend(x, joint, w, norms, mask):
    gains, biases = norms
    q, k, v, ko, vo = joint
    rows, width = x.shape
    heads = width // 128
    blocks, tp, depth, columns = w.shape
    pair = lead((1, rows, 128))
    o, e, l = pl.pallas_call(
        attn_kernel,
        grid=(heads,),
        in_specs=[pair] * 5 + [full((2 * rows, rows))],
        out_specs=[pair, lead((1, 2, 2 * rows, rows)), lead((1, 2, 8, rows))],
        out_shape=[sds((heads, rows, 128), BF), sds((heads, 2, 2 * rows, rows), BF), sds((heads, 2, 8, rows), F32)],
        compiler_params=BIG,
        name="attn",
    )(q, k, v, ko, vo, mask)
    groups = (columns - width) // GROUP
    units = tp * 128
    y, gu, n1, i1, n2, i2 = pl.pallas_call(
        ffn_kernel,
        grid=(groups,),
        in_specs=[
            full((rows, width)),
            full((heads, rows, 128)),
            pl.BlockSpec((blocks, tp, depth, 256), lambda i: (0, 0, 0, 2)),
            group_block(w),
            full((2, width)),
            full((2, width)),
        ],
        out_specs=[full((rows, width)), lead((1, 2, rows, units))] + [full((rows, width)), full((rows, 128))] * 2,
        out_shape=[sds((rows, width), BF), sds((groups, 2, rows, units), BF)] + [sds((rows, width), BF), sds((rows, 128), F32)] * 2,
        scratch_shapes=[VM((rows, width), F32), VM((rows, width), BF), VM((rows, width), F32)],
        compiler_params=BIG,
        name="ffn",
    )(x, o, w, w, gains, biases)
    return y, (q, k, v, ko, vo, o, e, l, gu, n1, i1, n2, i2)


def ffn_backward(dy, kept, w, norms, grads):
    gains, biases = norms
    gu, n1, i1, n2, i2 = kept[8:]
    rows, width = dy.shape
    blocks, tp, depth, columns = w.shape
    groups = (columns - width) // GROUP
    whole, stat = full((rows, width)), full((rows, 128))
    outs = [whole, whole]
    shapes = [sds((rows, width), F32), sds((rows, width), BF)]
    scratch = [VM((rows, width), BF), VM((rows, width), F32)]
    if grads:
        outs = [group_block(w)] + outs + [full((8, width))]
        shapes = [sds(w.shape, BF)] + shapes + [sds((8, width), F32)]
        scratch = [VM((rows, width), BF)] + scratch
    return pl.pallas_call(
        functools.partial(ffn_back_kernel, grads),
        grid=(groups,),
        in_specs=[
            whole, whole, stat, whole, stat,
            lead((1, 2, rows, tp * 128)),
            group_block(w),
            full((2, width)), full((2, width)),
        ],
        out_specs=outs,
        out_shape=shapes,
        scratch_shapes=scratch,
        compiler_params=BIG,
        name="ffn_back" if grads else "ffn_back_light",
    )(dy, n1, i1, n2, i2, gu, w, gains, biases)


def attn_backward(x, da, dr1, g, kept, w, tabs):
    grads = g is not None
    q, k, v, ko, vo, o, e, l = kept[:8]
    rows, width = da.shape
    heads = width // 128
    blocks, tp, depth, columns = w.shape
    steps = tp // 2
    cos, sin, cost, sint = tabs
    whole = full((rows, width))
    three = lead((3, rows, 128))
    side = lead((3, 2, 128, rows))
    table = full((HD // 2, rows))
    extra = [lead((1, width, 384))] if grads else []
    dq, own, oth, *dwo = pl.pallas_call(
        functools.partial(attn_back_kernel, grads),
        grid=(steps,),
        in_specs=[
            whole,
            pl.BlockSpec((blocks, 2, depth, 256), lambda i: (0, i, 0, 2)),
            three, three, three, three, three, three,
            lead((3, 2, 2 * rows, rows)),
            lead((3, 2, 8, rows)),
            table, table,
        ],
        out_specs=[three, side, side] + extra,
        out_shape=[
            sds((heads, rows, 128), BF),
            sds((heads, 2, 128, rows), F32),
            sds((heads, 2, 128, rows), BF),
        ]
        + ([sds((steps, width, 384), BF)] if grads else []),
        compiler_params=BIG,
        name="attn_back",
    )(da, w, o, q, k, v, ko, vo, e, l, cost, sint)
    got = lax.ppermute(oth, "core", [(0, 1), (1, 0)])
    if grads:
        specs = [pl.BlockSpec(memory_space=pl.ANY), whole, joint_block(w), whole, three, side, side] + extra
        args = (g, x, w, dr1, dq, own, got, *dwo)
        outs, shapes = [joint_block(w), whole], [sds(w.shape, BF), sds((rows, width), F32)]
    else:
        specs = [joint_block(w), whole, three, side, side]
        args = (w, dr1, dq, own, got)
        outs, shapes = [whole, whole], [sds((rows, width), F32), sds((rows, width), BF)]
    return pl.pallas_call(
        functools.partial(joint_back_kernel, grads),
        grid=(steps,),
        in_specs=specs + [table, table],
        out_specs=outs,
        out_shape=shapes,
        input_output_aliases={0: 0} if grads else {},
        compiler_params=BIG,
        name="joint_back",
    )(*args, cost, sint)


PAIRS = 6
FIRST_PAIR = 6
FIRST_JOINT = 12
LAST_STEP = 13


FAR = 2
FAR_AT = 4
def last_kernel(
    parts, n1_ref, i1_ref, n2_ref, i2_ref, gu_ref, wa_ref, norm_ref,
    q_ref, k_ref, v_ref, ko_ref, vo_ref, l_ref, cos_ref, sin_ref, dy_hbm, x_hbm, y_hbm, e_hbm, o_hbm, w_hbm,
    joint_out, mix_out, pair_out, down_out, ends_out, norm_out,
    acc, df, hb, o_ref, wb_ref, ring, do3, dwo, dq, keep, oth, got, eb, e_send, e_land, tmp, land_c, land_y, land_r, land_l, land_n,
    z_sum, far_y, far_r, far_l,
    o_sem, wb_sem, dy_sem, x_sem, y_sem, e_sem, oth_send, oth_recv, end_sem, end_send, end_recv,
    cs_sem, cr_sem, ys_sem, yr_sem, rs_sem, rr_sem, ls_sem, lr_sem, ns_sem, nr_sem,
    fys_sem, fyr_sem, frs_sem, frr_sem, fls_sem, flr_sem,
):
    step = pl.program_id(0)
    section = lax.axis_index("section")
    y, c, z = lax.axis_index("y"), lax.axis_index("core"), lax.axis_index("tensor")
    last = 3
    rows, width = acc.shape
    early = parts - width // WIDE
    usual = parts - FAR
    near, across = {"core": 1 - c}, {"y": 1 - y}
    right, left = {"tensor": jnp.minimum(z + 1, last)}, {"tensor": jnp.maximum(z - 1, 0)}
    pair = {"tensor": z + 1 - 2 * lax.rem(z, 2)}
    far = {"tensor": lax.rem(z + 2, 4)}
    side = z // 2
    barrier = pltpu.get_barrier_semaphore()

    def greet(device):
        pl.semaphore_signal(barrier, inc=1, device_id=device, device_id_type=MESH)

    def remote(src, dst, send, recv, device):
        return pltpu.make_async_remote_copy(src, dst, send, recv, device_id=device, device_id_type=MESH)

    def target(i):
        return {"core": side, "tensor": 2 * c + i}

    def at_home(i):
        return jnp.logical_and(side == c, 2 * c + i == z)

    def end_copy(i, part):
        return remote(e_send.at[i, part], e_land.at[z % 2, part], end_send.at[i], end_recv.at[z % 2], target(i))

    def end_home(i):
        return pltpu.make_async_copy(e_send.at[i], e_land.at[z % 2], end_sem)

    def oth_copy(p):
        return remote(oth.at[p], got.at[p], oth_send.at[p], oth_recv.at[p], near)

    dy_copy = pltpu.make_async_copy(dy_hbm, e_send, dy_sem)
    x_copy = pltpu.make_async_copy(x_hbm, hb, x_sem)
    o_copy = pltpu.make_async_copy(o_hbm, o_ref, o_sem)
    wb_copy = pltpu.make_async_copy(w_hbm.at[:, :, :, pl.ds(GROUP, GROUP)], wb_ref, wb_sem)
    y_copy = pltpu.make_async_copy(y_hbm, e_send, y_sem)

    def probs_copy(p):
        return pltpu.make_async_copy(e_hbm.at[p], eb, e_sem)

    def columns(j):
        return pl.ds(pl.multiple_of(j * WIDE, WIDE), WIDE)

    def slot(j):
        return (j // 3) % 2, columns(j % 3)

    def chunk(j):
        return j + FAR * ((j + usual - FAR_AT) // usual)

    def to_core(j):
        r, cols = slot(j)
        return remote(ring.at[r, :, 1 - c, :, :, cols], land_c.at[j], cs_sem.at[j], cr_sem.at[j], near)

    def to_y(j):
        return remote(land_c.at[chunk(j), 1 - y], land_y.at[j], ys_sem.at[j], yr_sem.at[j], across)

    def norm_copy(k):
        return remote(land_n.at[2 * k], land_n.at[2 * k + 1], ns_sem.at[k], nr_sem.at[k], (near, across, pair, far)[k])

    def go_right(j, first, src):
        return remote(src, land_r.at[j, pl.ds(first - 1, 4 - first)], rs_sem.at[j], rr_sem.at[j], right)

    def go_left(j, count, src):
        return remote(src, land_l.at[j, pl.ds(0, count)], ls_sem.at[j], lr_sem.at[j], left)

    def stage(i, lag, body):
        @pl.when(jnp.logical_and(i >= lag, i - lag < usual))
        def _():
            body(i - lag)

    def add_core(j):
        r, cols = slot(j)
        to_core(j).wait()
        land_c[j] = land_c[j] + ring[r, :, c, :, :, cols]

    def far_right(b, first, src):
        return remote(src, far_r.at[b, :, pl.ds(first - 1, 4 - first)], frs_sem.at[b], frr_sem.at[b], right)

    def far_left(b, count, src):
        return remote(src, far_l.at[b, :, pl.ds(0, count)], fls_sem.at[b], flr_sem.at[b], left)

    def far_across(b):
        return remote(z_sum.at[b, 1 - y], far_y.at[b], fys_sem.at[b], fyr_sem.at[b], across)

    def far_first(b):
        j = FAR_AT + b

        @pl.when(z == 0)
        def _():
            far_right(b, 1, land_c.at[j, :, pl.ds(1, 3)]).start()

        @pl.when(z == last)
        def _():
            far_left(b, 3, land_c.at[j, :, pl.ds(0, 3)]).start()

    def far_next(b):
        j = FAR_AT + b

        @pl.when(z == 1)
        def _():
            far_right(b, 1, far_r.at[b]).wait_recv()
            for k in (2, 3):
                far_r[b, :, k - 1] = far_r[b, :, k - 1] + land_c[j, :, k]
            far_right(b, 2, far_r.at[b, :, pl.ds(1, 2)]).start()

        @pl.when(z == 2)
        def _():
            far_left(b, 3, far_l.at[b]).wait_recv()
            for k in (0, 1):
                far_l[b, :, k] = far_l[b, :, k] + land_c[j, :, k]
            far_left(b, 2, far_l.at[b, :, pl.ds(0, 2)]).start()

    def far_last(b):
        j = FAR_AT + b

        @pl.when(z == 1)
        def _():
            far_left(b, 2, far_l.at[b, :, pl.ds(0, 2)]).wait_recv()
            far_l[b, :, 0] = far_l[b, :, 0] + land_c[j, :, 0]
            far_left(b, 1, far_l.at[b, :, pl.ds(0, 1)]).start()

        @pl.when(z == 2)
        def _():
            far_right(b, 2, far_r.at[b, :, pl.ds(1, 2)]).wait_recv()
            far_r[b, :, 2] = far_r[b, :, 2] + land_c[j, :, 3]
            far_right(b, 3, far_r.at[b, :, pl.ds(2, 1)]).start()

    def far_sum(b):
        mine = land_c[FAR_AT + b, :, z]

        @pl.when(z == 0)
        def _():
            far_left(b, 1, far_l.at[b, :, pl.ds(0, 1)]).wait_recv()
            z_sum[b] = mine + far_l[b, :, 0]

        @pl.when(z == 1)
        def _():
            z_sum[b] = mine + far_r[b, :, 0] + far_l[b, :, 1]

        @pl.when(z == 2)
        def _():
            z_sum[b] = mine + far_r[b, :, 1] + far_l[b, :, 2]

        @pl.when(z == last)
        def _():
            far_right(b, 3, far_r.at[b, :, pl.ds(2, 1)]).wait_recv()
            z_sum[b] = mine + far_r[b, :, 2]

    def far_result(b):
        far_across(b).wait_recv()
        tmp[...] = z_sum[b, y].astype(F32) + far_y[b].astype(F32)
        emit(FAR_AT + b)

    def last_hop(j):
        @pl.when(z == 1)
        def _():
            go_left(j, 2, land_l.at[j, pl.ds(0, 2)]).wait_recv()
            land_l[j, 0] = land_l[j, 0] + land_c[chunk(j), y, 0]
            go_left(j, 1, land_l.at[j, pl.ds(0, 1)]).start()

        @pl.when(z == 2)
        def _():
            go_right(j, 2, land_r.at[j, pl.ds(1, 2)]).wait_recv()
            land_r[j, 2] = land_r[j, 2] + land_c[chunk(j), y, 3]
            go_right(j, 3, land_r.at[j, pl.ds(2, 1)]).start()

    def next_hop(j):
        @pl.when(z == 1)
        def _():
            go_right(j, 1, land_r.at[j]).wait_recv()
            for k in (2, 3):
                land_r[j, k - 1] = land_r[j, k - 1] + land_c[chunk(j), y, k]
            go_right(j, 2, land_r.at[j, pl.ds(1, 2)]).start()

        @pl.when(z == 2)
        def _():
            go_left(j, 3, land_l.at[j]).wait_recv()
            for k in (0, 1):
                land_l[j, k] = land_l[j, k] + land_c[chunk(j), y, k]
            go_left(j, 2, land_l.at[j, pl.ds(0, 2)]).start()

    def first_hop(j):
        to_y(j).wait_recv()
        land_c[chunk(j), y] = land_c[chunk(j), y] + land_y[j]

        @pl.when(z == 0)
        def _():
            go_right(j, 1, land_c.at[chunk(j), y, pl.ds(1, 3)]).start()

        @pl.when(z == last)
        def _():
            go_left(j, 3, land_c.at[chunk(j), y, pl.ds(0, 3)]).start()

    def result(j):
        mine = land_c[chunk(j), y, z].astype(F32)

        @pl.when(z == 0)
        def _():
            go_left(j, 1, land_l.at[j, pl.ds(0, 1)]).wait_recv()
            tmp[...] = mine + land_l[j, 0].astype(F32)

        @pl.when(z == 1)
        def _():
            tmp[...] = mine + land_r[j, 0].astype(F32) + land_l[j, 1].astype(F32)

        @pl.when(z == 2)
        def _():
            tmp[...] = mine + land_r[j, 1].astype(F32) + land_l[j, 2].astype(F32)

        @pl.when(z == last)
        def _():
            go_right(j, 3, land_r.at[j, pl.ds(2, 1)]).wait_recv()
            tmp[...] = mine + land_r[j, 2].astype(F32)

        emit(chunk(j))

    def emit(j):
        group = j // 3

        @pl.when(jnp.logical_and(j < early, j % 3 == 0))
        def _():
            down_out[:, columns(group)] = tmp[...]

        for m in (1, 2):

            @pl.when(jnp.logical_and(j < early, j % 3 == m))
            def _():
                pair_out[:, columns(group + (m - 1) * (early // 3))] = tmp[...]

        for odd in range(2):
            two = slice(HD, 3 * HD) if odd else slice(0, 2 * HD)
            one = slice(0, HD) if odd else slice(2 * HD, 3 * HD)

            def when(n, body, odd=odd):
                pl.when(jnp.logical_and(j == early + n, z % 2 == odd))(body)

            def store(out, place, part):
                def body():
                    out[:, place] = tmp[:, part]

                return body

            def turn(place, part):
                def body():
                    mix_out[place, :] = tmp[...].T[part]

                return body

            whole, low, high = slice(0, 128), slice(0, HD), slice(HD, 128)
            for n in range(3):
                when(n, store(joint_out.at[n], two, whole))
            when(3, store(joint_out.at[0], one, low))
            when(3, store(joint_out.at[1], one, high))
            when(4, store(joint_out.at[2], one, low))
            when(4, turn(one, high))
            when(5, turn(two, whole))

    def round_(i):
        stage(i, 0, lambda j: to_y(j).start())
        stage(i, 6, last_hop)
        stage(i, 4, next_hop)
        stage(i, 2, first_hop)
        stage(i, 8, result)
        for b in range(FAR):
            rounds = (4 + 3 * b, 7 + 3 * b, 10 + 3 * b, 13 + 3 * b, usual - 1 + b, usual + 3 + b)
            bodies = (far_first, far_next, far_last, far_sum, lambda b: far_across(b).start(), far_result)
            for at, body in zip(rounds, bodies):
                pl.when(i == at)(functools.partial(body, b))

        for k in range(4):

            @pl.when(i == 3 * k + 8)
            def _():
                norm_copy(k).wait()
                total = land_n[2 * k] + land_n[2 * k + 1]
                if k < 3:
                    land_n[2 * k + 2] = total
                    norm_copy(k + 1).start()
                else:
                    norm_out[...] = total

    @pl.when(step == 0)
    def _():
        dy_copy.start()
        o_copy.start()
        wb_copy.start()
        greet(near)
        greet(across)
        greet(far)

        @pl.when(z < last)
        def _():
            greet(right)

        @pl.when(z > 0)
        def _():
            greet(left)

        for i in range(2):

            @pl.when(jnp.logical_not(at_home(i)))
            def _():
                greet(target(i))

        count = 5 + jnp.where(z < last, 1, 0) + jnp.where(z > 0, 1, 0) - jnp.where(side == c, 1, 0)
        pl.semaphore_wait(barrier, count)
        dy_copy.wait()
        dy = e_send[...].reshape(rows, width).astype(F32)
        n = n2_ref[...].astype(F32)
        land_n[0] = jnp.zeros(land_n.shape[1:], F32)
        land_n[0, 1:2] = jnp.sum(dy * n, axis=0, keepdims=True)
        land_n[0, 3:4] = jnp.sum(dy, axis=0, keepdims=True)
        dr2 = norm_back(dy * norm_ref[1:2], n, i2_ref[:, :1])
        acc[...] = dr2
        df[...] = dr2.astype(BF)
        hb[...] = (n1_ref[...].astype(F32) * norm_ref[0:1] + norm_ref[2:3]).astype(BF)

    @pl.when(step < FIRST_PAIR)
    def _():
        gate = gu_ref[0, 0].astype(F32)
        up = gu_ref[0, 1].astype(F32)
        s = 1.0 / (1.0 + jnp.exp(-gate))
        silu = gate * s
        wd, wg, wu = unit_weights(lambda t, m: wa_ref[:, t, :, 128 * m : 128 * m + 128].reshape(width, 128))
        place = step % 2

        def put(m, grad):
            for t in range(4):
                ring[place, :, :, t, :, 128 * m : 128 * m + 128] = (
                    grad[:, 128 * t : 128 * t + 128].astype(BF).reshape(2, 2, -1, 128)
                )

        j = 3 * step

        def earlier(m):
            pl.when(step > (1 if m == 0 else 0))(lambda: add_core(j - 3 + m))

        put(0, dg(df[...], (silu * up).astype(BF), TN))
        to_core(j).start()
        earlier(0)
        d_act = dg(df[...], wd, NN)
        d_gate = (d_act * up * (s * (1.0 + gate * (1.0 - s)))).astype(BF)
        d_up = (d_act * silu).astype(BF)
        put(1, dg(hb[...], d_gate, TN))
        to_core(j + 1).start()
        earlier(1)

        @pl.when(step == 0)
        def _():
            add_core(0)
            round_(0)

        put(2, dg(hb[...], d_up, TN))
        to_core(j + 2).start()
        earlier(2)
        acc[...] += dg(d_gate, wg, NT) + dg(d_up, wu, NT)

    @pl.when(step == FIRST_PAIR - 1)
    def _():
        dh = acc[...]
        n = n1_ref[...].astype(F32)
        land_n[0, 0:1] = jnp.sum(dh * n, axis=0, keepdims=True)
        land_n[0, 2:3] = jnp.sum(dh, axis=0, keepdims=True)
        dr1 = norm_back(dh * norm_ref[0:1], n, i1_ref[:, :1])
        acc[...] = dr1
        df[...] = dr1.astype(BF)
        x_copy.start()
        probs_copy(0).start()
        norm_copy(0).start()

    cos, sin = cos_ref[:, pl.ds(c * rows, rows)], sin_ref[:, pl.ds(c * rows, rows)]
    in_pairs = jnp.logical_and(step >= FIRST_PAIR, step < FIRST_JOINT)
    p = step - FIRST_PAIR

    @pl.when(step == FIRST_PAIR)
    def _():
        for m in range(3):
            add_core(3 * FIRST_PAIR - 3 + m)
        o_copy.wait()
        wb_copy.wait()

    @pl.when(jnp.logical_and(in_pairs, p % 3 == 0))
    def _():
        w = jnp.concatenate(out_weight(wb_ref.at[:, pl.ds(2 * (p // 3), 2), :, 128:384]), axis=1)
        t = dg(df[...], w, NN).astype(BF)
        for i in range(3):
            do3[i] = t[:, 128 * i : 128 * i + 128]
        o3 = jnp.concatenate([o_ref[p + i] for i in range(3)], axis=1)
        dwo[p // 3] = dg(df[...], o3, TN).astype(BF)

    @pl.when(in_pairs)
    def _():
        probs_copy(p).wait()
        dqt, dk, dv = pair_back(
            do3[p % 3], o_ref[p], q_ref[0], k_ref[0], v_ref[0], ko_ref[0], vo_ref[0],
            [eb.at[h] for h in range(2)], [l_ref[0, h, 0:1] for h in range(2)], cos, sin,
        )
        dq[p] = dqt.T.astype(BF)
        keep[p, 0] = dk[:, :rows].astype(BF)
        keep[p, 1] = dv[:, :rows].astype(BF)
        oth[p, 0] = dk[:, rows:].astype(BF)
        oth[p, 1] = dv[:, rows:].astype(BF)
        oth_copy(p).start()

        @pl.when(p + 1 < PAIRS)
        def _():
            probs_copy(p + 1).start()

    @pl.when(step >= FIRST_JOINT)
    def _():
        half = step - FIRST_JOINT

        @pl.when(half == 0)
        def _():
            x_copy.wait()

        for i in range(3):
            oth_copy(3 * half + i).wait()
        d = joint_parts(
            [dq[3 * half + i].astype(F32) for i in range(3)],
            [keep[3 * half + i, 0].astype(F32) + got[3 * half + i, 0].astype(F32) for i in range(3)],
            [keep[3 * half + i, 1].astype(F32) + got[3 * half + i, 1].astype(F32) for i in range(3)],
            cos, sin,
        )
        total = None
        wlow = low_lanes((width, 128))
        mid = dwo[half, :, 128:256].astype(F32)
        sides = [dwo[half, :, 0:128], dwo[half, :, 256:384]]
        mids = [swap64(mid), mid]
        shape = (2, 2, width // 4)
        for e in range(2):
            t = 2 * half + e
            w = jnp.concatenate([wa_ref[:, t].reshape(width, GROUP), wb_ref[:, t, :, :256].reshape(width, 256)], axis=1)
            part = dg(d[e], w, NT)
            total = part if total is None else total + part
            g = dg(hb[...], d[e], TN)
            ring[0, :, :, t] = g[:, :GROUP].astype(BF).reshape(shape + (GROUP,))
            ring[1, :, :, t, :, :128] = g[:, GROUP:512].astype(BF).reshape(shape + (128,))
            ring[1, :, :, t, :, 128:256] = jnp.where(wlow, g[:, 512:], mids[e]).astype(BF).reshape(shape + (128,))
            ring[1, :, :, t, :, 256:] = sides[e].reshape(shape + (128,))
        acc[...] += total

    @pl.when(step == LAST_STEP)
    def _():
        lax.fori_loop(early, parts, lambda j, t: (to_core(j).start(), t)[1], 0)

        @pl.when(section == 0)
        def _():
            e_send[...] = acc[...].astype(BF).reshape(e_send.shape)

        @pl.when(section == 1)
        def _():
            y_copy.start()
            y_copy.wait()

        for i in range(2):

            @pl.when(at_home(i))
            def _():
                end_home(i).start()

    @pl.when(step == 1)
    def _():
        round_(1)

    @pl.when(step >= 1)
    def _():
        round_(step + 1)

    @pl.when(step == LAST_STEP)
    def _():
        lax.fori_loop(early, parts, lambda j, t: (add_core(j), t)[1], 0)
        end_rows = e_send.shape[1] // 8

        def late(i, carry):
            part = pl.ds(pl.multiple_of((i - LAST_STEP - 2) * end_rows, end_rows), end_rows)
            for k in range(2):

                @pl.when(jnp.logical_not(at_home(k)))
                def _():
                    end_copy(k, part).start()

            round_(i)
            return carry

        lax.fori_loop(LAST_STEP + 2, LAST_STEP + 10, late, 0)
        lax.fori_loop(LAST_STEP + 10, usual + 8, lambda i, t: (round_(i), t)[1], 0)
        for i in range(2):

            @pl.when(at_home(i))
            def _():
                end_home(i).wait()

            @pl.when(jnp.logical_not(at_home(i)))
            def _():
                end_copy(i, pl.ds(0, e_send.shape[1])).wait_send()
                remote(e_send.at[i], e_land.at[i], end_send.at[i], end_recv.at[i], target(i)).wait_recv()

        ends_out[...] = e_land[...]

        def finish(j, carry):
            to_y(j).wait_send()

            @pl.when(z == 0)
            def _():
                go_right(j, 1, land_c.at[chunk(j), y, pl.ds(1, 3)]).wait_send()

            @pl.when(z == 1)
            def _():
                go_right(j, 2, land_r.at[j, pl.ds(1, 2)]).wait_send()
                go_left(j, 1, land_l.at[j, pl.ds(0, 1)]).wait_send()

            @pl.when(z == 2)
            def _():
                go_right(j, 3, land_r.at[j, pl.ds(2, 1)]).wait_send()
                go_left(j, 2, land_l.at[j, pl.ds(0, 2)]).wait_send()

            @pl.when(z == last)
            def _():
                go_left(j, 3, land_c.at[chunk(j), y, pl.ds(0, 3)]).wait_send()

            return carry

        lax.fori_loop(0, usual, finish, 0)

        def finish_far(b, carry):
            j = FAR_AT + b
            far_across(b).wait_send()

            @pl.when(z == 0)
            def _():
                far_right(b, 1, land_c.at[j, :, pl.ds(1, 3)]).wait_send()

            @pl.when(z == 1)
            def _():
                far_right(b, 2, far_r.at[b, :, pl.ds(1, 2)]).wait_send()
                far_left(b, 1, far_l.at[b, :, pl.ds(0, 1)]).wait_send()

            @pl.when(z == 2)
            def _():
                far_right(b, 3, far_r.at[b, :, pl.ds(2, 1)]).wait_send()
                far_left(b, 2, far_l.at[b, :, pl.ds(0, 2)]).wait_send()

            @pl.when(z == last)
            def _():
                far_left(b, 3, land_c.at[j, :, pl.ds(0, 3)]).wait_send()

            return carry

        lax.fori_loop(0, FAR, finish_far, 0)


def last_back(x, y, dy, kept, w, norms, cost, sint):
    q, k, v, ko, vo, o, e, l, gu, n1, i1, n2, i2 = kept
    rows, width = x.shape
    heads = width // 128
    depth, columns = w.shape[2:]
    parts = columns // WIDE
    units = (columns - width) // 3
    dma = pltpu.SemaphoreType.DMA
    hbm = pl.BlockSpec(memory_space=pl.ANY)
    halves = (2, rows // 2, width)

    def once(shape, at=None):
        return pl.BlockSpec(shape, lambda i: at or (0,) * len(shape), pipeline_mode=pl.Buffered(1))

    def by_pair(shape):
        return pl.BlockSpec(shape, lambda i: (jnp.clip(i - FIRST_PAIR, 0, PAIRS - 1),) + (0,) * (len(shape) - 1))

    pair = by_pair((1, rows, 128))
    group = (4, 4, depth, GROUP)
    return pl.pallas_call(
        functools.partial(last_kernel, parts),
        grid=(LAST_STEP + 1,),
        in_specs=[
            once((rows, width)), once((rows, 128)), once((rows, width)), once((rows, 128)),
            pl.BlockSpec((1, 2, rows, 512), lambda i: (jnp.minimum(i, FIRST_PAIR - 1), 0, 0, 0)),
            pl.BlockSpec(group, lambda i: (0, 0, 0, jnp.where(i < FIRST_PAIR, 2 + i, 0))),
            once((4, width)),
            pair, pair, pair, pair, pair,
            by_pair((1, 2, 8, rows)),
            once(cost.shape), once(sint.shape),
            hbm, hbm, hbm, hbm, hbm, hbm,
        ],
        out_specs=[
            once((3, depth, depth)), once((depth, depth)), once((depth, 2 * units)), once((depth, units)), once(halves), once((8, width)),
        ],
        out_shape=[
            sds((3, depth, depth), F32), sds((depth, depth), F32), sds((depth, 2 * units), F32), sds((depth, units), F32),
            sds(halves, BF), sds((8, width), F32),
        ],
        scratch_shapes=[
            VM((rows, width), F32),
            VM((rows, width), BF),
            VM((rows, width), BF),
            VM((heads, rows, 128), BF),
            VM(group, BF),
            VM((2, 2, 2, 4, depth, GROUP), BF),
            VM((3, rows, 128), BF),
            VM((2, width, 384), BF),
            VM((heads, rows, 128), BF),
            VM((heads, 2, 128, rows), BF),
            VM((heads, 2, 128, rows), BF),
            VM((heads, 2, 128, rows), BF),
            VM((2, 2 * rows, rows), BF),
            VM(halves, BF),
            VM(halves, BF),
            VM((depth, WIDE), F32),
            VM((parts, 2, 4, depth, WIDE), BF),
            VM((parts - FAR, 4, depth, WIDE), BF),
            VM((parts - FAR, 3, depth, WIDE), BF),
            VM((parts - FAR, 3, depth, WIDE), BF),
            VM((8, 8, width), F32),
            VM((FAR, 2, depth, WIDE), BF),
            VM((FAR, depth, WIDE), BF),
            VM((FAR, 2, 3, depth, WIDE), BF),
            VM((FAR, 2, 3, depth, WIDE), BF),
            dma, dma, dma, dma, dma, dma,
            dma((6,)), dma((6,)), dma, dma((2,)), dma((2,)),
        ]
        + [dma((parts,))] * 8
        + [dma((4,))] * 2
        + [dma((FAR,))] * 6,
        compiler_params=pltpu.CompilerParams(collective_id=0, has_side_effects=True, vmem_limit_bytes=63 << 20),
        name="last",
    )(n1, i1, n2, i2, gu, w, norms, q, k, v, ko, vo, l, cost, sint, dy.reshape(halves), x, y.reshape(halves), e, o, w)


LAG = 6
GATHER = 256


def first_kernel(
    parts, tok_ref, top_ref, lead_ref, down_ref, pair_ref, gain_ref, bias_ref, len_ref, cos_ref, sin_ref, cost_ref, sint_ref,
    w_out, q_out, k_out, v_out, ko_out, vo_out, y_out, e_out, o_out, gu_out, n1_out, n2_out,
    x_out, dy_out, l_out, i1_out, i2_out, norm_out,
    w, xin, q, kv, land_kv, late_kv, o, hb, acc, relay, land_rows, ext, lens,
    mask, eb, gu, n1, n2, df, do3, dq, keep, oth, got, d,
    tok_sem, tok_send, tok_recv, lead_sem, shard_sem, back_sem, kv_send, kv_recv, out_sem, row_send, row_recv, again_send, again_recv,
    e_sem, gu_sem, oth_send, oth_recv, dz_send, dz_recv,
    small_send, small_recv, rs_sem, rr_sem, ls_sem, lr_sem, ys_sem, yr_sem, cs_sem, cr_sem,
):
    section = lax.axis_index("section")
    y, c, z = lax.axis_index("y"), lax.axis_index("core"), lax.axis_index("tensor")
    last = 3
    rows, width = xin.shape[0] * xin.shape[1], xin.shape[2]
    near, across, other = {"core": 1 - c}, {"y": 1 - y}, {"section": 1 - section}
    right, left = {"tensor": jnp.minimum(z + 1, last)}, {"tensor": jnp.maximum(z - 1, 0)}
    side = z // 2
    barrier = pltpu.get_barrier_semaphore()

    def greet(device):
        pl.semaphore_signal(barrier, inc=1, device_id=device, device_id_type=MESH)

    def remote(src, dst, send, recv, device):
        return pltpu.make_async_remote_copy(src, dst, send, recv, device_id=device, device_id_type=MESH)

    def target(i):
        return {"core": side, "tensor": 2 * c + i}

    def at_home(i):
        return jnp.logical_and(side == c, 2 * c + i == z)

    def token_copy(src, i, part):
        return remote(src.at[i, part], xin.at[z % 2, part], tok_send.at[i], tok_recv.at[z % 2], target(i))

    def token_home(src, i):
        return pltpu.make_async_copy(src.at[i], xin.at[z % 2], tok_sem)

    def by_section(body):
        for n, src in enumerate((tok_ref, top_ref)):
            pl.when(section == n)(functools.partial(body, src))

    groups = down_ref.shape[1] // 128

    def load_group(k, m):
        src = down_ref if m == 0 else pair_ref
        cols = pl.ds(128 * (k + (m - 1) * groups if m else k), 128)
        return pltpu.make_async_copy(src.at[:, cols], w.at[y, c, z, :, pl.ds(width + GROUP * k + 128 * m, 128)], shard_sem.at[k, m])

    load_lead = pltpu.make_async_copy(lead_ref, w.at[y, c, z, :, pl.ds(0, width)], lead_sem)
    load_lead.start()
    loads = [load_group(k, m) for k in range(groups) for m in range(3)]
    for load in loads:
        load.start()
    greet(near)
    greet(across)
    greet(other)

    @pl.when(z < last)
    def _():
        greet(right)

    @pl.when(z > 0)
    def _():
        greet(left)

    for i in range(2):

        @pl.when(jnp.logical_not(at_home(i)))
        def _():
            greet(target(i))

    count = 5 + jnp.where(z < last, 1, 0) + jnp.where(z > 0, 1, 0) - jnp.where(side == c, 1, 0)
    pl.semaphore_wait(barrier, count)

    ext[y, c, 0:1] = gain_ref[...].astype(F32)
    ext[y, c, 1:2] = bias_ref[...].astype(F32)
    lens[c] = len_ref[...]

    def small(k):
        if k == 0:
            return remote(lens.at[c], lens.at[c], small_send.at[0], small_recv.at[0], near)
        if k == 1:
            return remote(ext.at[y, c], ext.at[y, c], small_send.at[1], small_recv.at[1], across)
        return remote(ext.at[:, c], ext.at[:, c], small_send.at[2], small_recv.at[2], near)

    small(0).start()
    small(1).start()
    load_lead.wait()
    for load in loads:
        load.wait()

    def columns(j):
        return pl.ds(pl.multiple_of(j * GATHER, GATHER), GATHER)

    def go_right(j, h):
        b = jnp.maximum(z - h, 0)
        return remote(w.at[y, c, b, :, columns(j)], w.at[y, c, b, :, columns(j)], rs_sem.at[j, h], rr_sem.at[j, h], right)

    def go_left(j, h):
        b = jnp.minimum(z + h, last)
        return remote(w.at[y, c, b, :, columns(j)], w.at[y, c, b, :, columns(j)], ls_sem.at[j, h], lr_sem.at[j, h], left)

    def to_y(j):
        return remote(w.at[y, c, :, :, columns(j)], w.at[y, c, :, :, columns(j)], ys_sem.at[j], yr_sem.at[j], across)

    def block_to_y(j, b):
        return remote(w.at[y, c, b, :, columns(j)], w.at[y, c, b, :, columns(j)], ys_sem.at[j], yr_sem.at[j], across)

    def to_core(j):
        return remote(w.at[:, c, :, :, columns(j)], w.at[:, c, :, :, columns(j)], cs_sem.at[j], cr_sem.at[j], near)

    def write_back(j):
        return pltpu.make_async_copy(w.at[:, :, :, :, columns(j)], w_out.at[:, :, :, :, columns(j)], back_sem.at[j])

    def stage(r, lag, body):
        @pl.when(jnp.logical_and(r >= lag, r - lag < parts))
        def _():
            body(r - lag)

    def send_own(j):
        @pl.when(z < last)
        def _():
            go_right(j, 0).start()

        @pl.when(z > 0)
        def _():
            go_left(j, 0).start()

        block_to_y(j, z).start()

    def hop(h, j):
        @pl.when(z >= h)
        def _():
            go_right(j, h - 1).wait_recv()
            block_to_y(j, z - h).start()

        @pl.when(z + h <= last)
        def _():
            go_left(j, h - 1).wait_recv()
            block_to_y(j, z + h).start()

        if h < last:

            @pl.when(jnp.logical_and(z >= h, z < last))
            def _():
                go_right(j, h).start()

            @pl.when(jnp.logical_and(z + h <= last, z > 0))
            def _():
                go_left(j, h).start()

    def over_core(j):
        to_y(j).wait_recv()
        to_core(j).start()

    def complete(j):
        to_core(j).wait_recv()
        write_back(j).start()

    def round_(r):
        stage(r, 0, send_own)
        stage(r, 1, functools.partial(hop, 1))
        stage(r, 2, functools.partial(hop, 2))
        stage(r, 3, functools.partial(hop, 3))
        stage(r, 5, over_core)
        stage(r, LAG, complete)

    def rounds(first, end):
        lax.fori_loop(first, end, lambda r, t: (round_(r), t)[1], 0)

    start = 9
    token_rows = xin.shape[1] // 8
    for i in range(2):

        @pl.when(at_home(i))
        def _():
            by_section(lambda src: token_home(src, i).start())

    def early(r, carry):
        round_(r)
        part = pl.ds(pl.multiple_of(r * token_rows, token_rows), token_rows)
        for i in range(2):

            @pl.when(jnp.logical_not(at_home(i)))
            def _():
                by_section(lambda src: token_copy(src, i, part).start())

        return carry

    lax.fori_loop(0, 3, early, 0)
    small(0).wait()
    small(1).wait()
    small(2).start()

    mine = jnp.where(side == 0, lens[0], lens[1])
    mine = jnp.where(z % 2 == 0, mine[0:1], mine[1:2])
    at_q = c * rows + lax.broadcasted_iota(jnp.int32, (1, rows), 1)
    at_k = lax.broadcasted_iota(jnp.int32, (2 * rows, 1), 0)
    at_k = jnp.where(at_k < rows, c * rows + at_k, (1 - c) * rows + at_k - rows)
    seg_q, seg_k = jnp.zeros((1, rows), jnp.int32), jnp.zeros((2 * rows, 1), jnp.int32)
    end = jnp.zeros((1, 1), jnp.int32)
    for n in range(8):
        end = end + mine[:, n : n + 1]
        seg_q = seg_q + jnp.where(end <= at_q, 1, 0)
        seg_k = seg_k + jnp.where(end <= at_k, 1, 0)
    mask[...] = jnp.where(seg_k == seg_q, 0.0, neg_fill).astype(F32)
    lax.fori_loop(3, 8, early, 0)
    rounds(8, start)

    small(2).wait()
    for k in range(2):
        for half in range(2):
            norm_out[2 * k + half : 2 * k + half + 1] = jnp.concatenate([ext[half, i, k : k + 1] for i in range(2)], axis=1)

    for i in range(2):

        @pl.when(at_home(i))
        def _():
            token_home(tok_ref, i).wait()

        @pl.when(jnp.logical_not(at_home(i)))
        def _():
            token_copy(tok_ref, i, pl.ds(0, xin.shape[1])).wait_send()
            remote(tok_ref.at[i], xin.at[i], tok_send.at[i], tok_recv.at[i], target(i)).wait_recv()

    def project(at, count, x):
        here = pl.ds(at, count)
        cos, sin = cos_ref[pl.ds(c * rows + at, count)], sin_ref[pl.ds(c * rows + at, count)]
        low = low_lanes((count, 128))
        for p in range(2):
            r = [dg(x, w[:, :, 2 * p + e, :, :640].reshape(width, 640), NN) for e in range(2)]
            t = [[v[:, 128 * i : 128 * i + 128] for i in range(5)] for v in r]
            qs = [t[0][0], jnp.where(low, t[0][3], swap64(t[1][3])), t[1][0]]
            ks = [t[0][1], jnp.where(low, swap64(t[0][3]), t[1][3]), t[1][1]]
            vs = [t[0][2], jnp.where(low, t[0][4], swap64(t[1][4])), t[1][2]]
            for i in range(3):
                q[3 * p + i, here] = (rope_fwd(qs[i], cos, sin) * HD**-0.5).astype(BF)
                kv[0, 3 * p + i, here] = rope_fwd(ks[i], cos, sin).astype(BF)
                kv[1, 3 * p + i, here] = vs[i].astype(BF)

    x = xin[...].reshape(rows, width)
    x_out[...] = x
    project(0, rows, x)
    low = low_lanes((rows, 128))
    share = remote(kv, land_kv, kv_send.at[0], kv_recv.at[0], near)
    share.start()
    rounds(start, start + 1)
    share.wait()

    def heads_of(p, others, save):
        k = jnp.concatenate([kv[0, p], others[0, p]], axis=0)
        v = jnp.concatenate([kv[1, p], others[1, p]], axis=0)
        vt = v.astype(F32).T.astype(BF)
        ones = jnp.ones((16, 2 * rows), BF)
        outs = []
        for h in range(2):
            qm = jnp.where(low if h == 0 else jnp.logical_not(low), q[p], jnp.zeros((rows, 128), BF))
            s = dg(k, qm, NT) + mask[...]
            e = jnp.exp(s - jnp.max(s, axis=0, keepdims=True)).astype(BF)
            t = dg(jnp.concatenate([vt[HD * h : HD * h + HD], ones], axis=0), e, NN)
            inv = 1.0 / t[HD : HD + 1]
            save(h, e, inv)
            outs.append(t[:HD] * inv)
        o[p] = jnp.concatenate(outs, axis=0).T.astype(BF)

    def pair(p, carry):
        heads_of(p, land_kv, lambda h, e, inv: None)
        pl.when(p % 2 == 1)(functools.partial(round_, start + 1 + p // 2))
        return carry

    def out_part(p):
        wo = []
        for e in range(2):
            wo.append([w[:, :, 2 * p + e, :, 512 + 128 * i : 640 + 128 * i].reshape(width, 128) for i in range(2)])
        mid = jnp.where(low_lanes((width, 128)), swap64(wo[0][0].astype(F32)), wo[1][0].astype(F32)).astype(BF)
        return jnp.concatenate([wo[0][1], mid, wo[1][1]], axis=1)

    def mix(x):
        r = x.astype(F32)
        for p in range(2):
            r = r + dg(jnp.concatenate([o[3 * p + i] for i in range(3)], axis=1), out_part(p), NT)
        return norm_parts(r)

    def group_of(k):
        return unit_weights(
            lambda t, m: w[:, :, t, :, pl.ds(pl.multiple_of(width + GROUP * k + 128 * m, 128), 128)].reshape(width, 128)
        )

    def unit(k, save):
        wd, wg, wu = group_of(k)
        gate = dg(hb[...], wg, NN)
        up = dg(hb[...], wu, NN)
        save(gate, up)
        act = (gate / (1.0 + jnp.exp(-gate)) * up).astype(BF)
        acc[...] += dg(act, wd, NT)

    lax.fori_loop(0, 6, pair, 0)
    n, inv = mix(x)
    h = n * norm_out[0:1] + norm_out[2:3]
    hb[...] = h.astype(BF)
    acc[...] = h
    rounds(start + 4, start + 5)

    def units(k, carry):
        for at, r in ((2, 5), (4, 6), (4, 7), (5, 8)):
            pl.when(k == at)(functools.partial(round_, start + r))

        unit(k, lambda gate, up: None)
        return carry

    lax.fori_loop(0, 6, units, 0)
    pieces = relay.shape[0]
    piece_rows = rows // pieces

    def row_copy(b):
        return remote(relay.at[b], land_rows.at[b], row_send.at[b], row_recv.at[b], other)

    def again(b):
        part = pl.ds(pl.multiple_of(b * piece_rows, piece_rows), piece_rows)
        return remote(kv.at[:, :, part], late_kv.at[:, :, part], again_send.at[b], again_recv.at[b], near)

    kept_out = []

    def keep_out(src, dst):
        copy = pltpu.make_async_copy(src, dst, out_sem.at[len(kept_out)])
        kept_out.append(copy)
        copy.start()

    @pl.when(section == 0)
    def _():
        def send_rows(b, carry):
            part = pl.ds(pl.multiple_of(b * piece_rows, piece_rows), piece_rows)
            n, inv = norm_parts(acc[part])
            relay[b] = (n * norm_out[1:2] + norm_out[3:4]).astype(BF)
            row_copy(b).start()
            return carry

        lax.fori_loop(0, pieces, send_rows, 0)
        same = pltpu.make_async_copy(land_kv, late_kv, kv_send.at[1])
        same.start()
        same.wait()

    @pl.when(section == 1)
    def _():
        def project_rows(b, carry):
            at = pl.multiple_of(b * piece_rows, piece_rows)
            row_copy(b).wait_recv()
            x_out[pl.ds(at, piece_rows)] = land_rows[b]
            project(at, piece_rows, land_rows[b])
            again(b).start()
            return carry

        lax.fori_loop(0, pieces, project_rows, 0)
        lax.fori_loop(0, pieces, lambda b, t: (again(b).wait(), t)[1], 0)

    for src, dst in ((q, q_out), (kv.at[0], k_out), (kv.at[1], v_out), (late_kv.at[0], ko_out), (late_kv.at[1], vo_out)):
        keep_out(src, dst)

    def probs_out(p):
        return pltpu.make_async_copy(eb.at[p % 2], e_out.at[p], e_sem.at[p % 2])

    def probs_in(p):
        return pltpu.make_async_copy(e_out.at[p], eb.at[p % 2], e_sem.at[p % 2])

    def pair_kept(p, carry):
        @pl.when(p >= 2)
        def _():
            probs_out(p - 2).wait()

        def save(h, e, inv):
            eb[p % 2, h] = e
            l_out[p, h] = jnp.broadcast_to(inv, l_out.shape[2:])

        heads_of(p, late_kv, save)
        probs_out(p).start()
        return carry

    lax.fori_loop(0, PAIRS, pair_kept, 0)
    keep_out(o, o_out)
    n, inv = mix(x_out[...])
    n1[...] = n.astype(BF)
    i1_out[...] = jnp.broadcast_to(inv, i1_out.shape)
    keep_out(n1, n1_out)
    h = n * norm_out[0:1] + norm_out[2:3]
    hb[...] = h.astype(BF)
    acc[...] = h

    def units_out(k):
        return pltpu.make_async_copy(gu.at[k % 2], gu_out.at[k], gu_sem.at[k % 2])

    def units_in(k):
        return pltpu.make_async_copy(gu_out.at[k], gu.at[k % 2], gu_sem.at[k % 2])

    def unit_kept(k, carry):
        @pl.when(k >= 2)
        def _():
            units_out(k - 2).wait()

        def save(gate, up):
            gu[k % 2, 0] = gate.astype(BF)
            gu[k % 2, 1] = up.astype(BF)

        unit(k, save)
        units_out(k).start()
        return carry

    lax.fori_loop(0, 6, unit_kept, 0)
    n, inv = norm_parts(acc[...])
    n2[...] = n.astype(BF)
    i2_out[...] = jnp.broadcast_to(inv, i2_out.shape)
    keep_out(n2, n2_out)
    hb[...] = (n * norm_out[1:2] + norm_out[3:4]).astype(BF)
    keep_out(hb, y_out)
    for p in (PAIRS - 2, PAIRS - 1):
        probs_out(p).wait()
        units_out(p).wait()

    def dz_copy(b):
        return remote(relay.at[b], land_rows.at[b], dz_send.at[b], dz_recv.at[b], other)

    def oth_copy(p):
        return remote(oth.at[p], got.at[p], oth_send.at[p], oth_recv.at[p], near)

    @pl.when(section == 1)
    def _():
        dr2 = norm_back(xin[...].reshape(rows, width).astype(F32) * norm_out[1:2], n, inv)
        acc[...] = dr2
        df[...] = dr2.astype(BF)
        for p in range(2):
            probs_in(p).start()
            units_in(p).start()

        def unit_back(k, carry):
            wd, wg, wu = group_of(k)
            units_in(k).wait()
            gate = gu[k % 2, 0].astype(F32)
            up = gu[k % 2, 1].astype(F32)
            s = 1.0 / (1.0 + jnp.exp(-gate))
            d_act = dg(df[...], wd, NN)
            d_gate = (d_act * up * (s * (1.0 + gate * (1.0 - s)))).astype(BF)
            d_up = (d_act * (gate * s)).astype(BF)
            acc[...] += dg(d_gate, wg, NT) + dg(d_up, wu, NT)

            @pl.when(k + 2 < 6)
            def _():
                units_in(k + 2).start()

            return carry

        lax.fori_loop(0, 6, unit_back, 0)
        dr1 = norm_back(acc[...] * norm_out[0:1], n1[...].astype(F32), i1_out[:, :1])
        acc[...] = dr1
        df[...] = dr1.astype(BF)
        cost, sint = cost_ref[:, pl.ds(c * rows, rows)], sint_ref[:, pl.ds(c * rows, rows)]

        def pair_of(p, carry):
            probs_in(p).wait()
            dqt, dk, dv = pair_back(
                do3[p % 3], o[p], q[p], kv[0, p], kv[1, p], late_kv[0, p], late_kv[1, p],
                [eb.at[p % 2, h] for h in range(2)], [l_out[p, h, 0:1] for h in range(2)], cost, sint,
            )

            @pl.when(p + 2 < PAIRS)
            def _():
                probs_in(p + 2).start()

            dq[p] = dqt.T.astype(BF)
            keep[p, 0] = dk[:, :rows].astype(BF)
            keep[p, 1] = dv[:, :rows].astype(BF)
            oth[p, 0] = dk[:, rows:].astype(BF)
            oth[p, 1] = dv[:, rows:].astype(BF)
            oth_copy(p).start()
            return carry

        def joint(half):
            def total(i, m):
                return keep[i, m].astype(F32) + got[i, m].astype(F32)

            three = range(3 * half, 3 * half + 3)
            for i in three:
                oth_copy(i).wait()
            parts = joint_parts(
                [dq[i].astype(F32) for i in three], [total(i, 0) for i in three], [total(i, 1) for i in three], cost, sint
            )
            for e in range(2):
                d[2 * half + e] = parts[e]

        for half in range(2):
            t = dg(df[...], out_part(half), NN).astype(BF)
            for i in range(3):
                do3[i] = t[:, 128 * i : 128 * i + 128]
            lax.fori_loop(3 * half, 3 * half + 3, pair_of, 0)
        for half in range(2):
            joint(half)

        def send_back(b, carry):
            part = pl.ds(pl.multiple_of(b * piece_rows, piece_rows), piece_rows)
            total = acc[part]
            for t in range(4):
                total += dg(d[t, part], w[:, :, t, :, :640].reshape(width, 640), NT)
            relay[b] = total.astype(BF)
            dz_copy(b).start()
            return carry

        lax.fori_loop(0, pieces, send_back, 0)
        dy_out[...] = xin[...].reshape(rows, width)
        lax.fori_loop(0, pieces, lambda b, t: (dz_copy(b).wait_send(), t)[1], 0)

    @pl.when(section == 0)
    def _():
        lax.fori_loop(0, pieces, lambda b, t: (row_copy(b).wait_send(), t)[1], 0)
        lax.fori_loop(0, pieces, lambda b, t: (dz_copy(b).wait_recv(), t)[1], 0)
        dy_out[...] = land_rows[...].reshape(rows, width)

    for copy in kept_out:
        copy.wait()

    def finish(j, carry):
        write_back(j).wait()
        to_y(j).wait_send()
        to_core(j).wait_send()
        for h in range(last):

            @pl.when(jnp.logical_and(z >= h, z < last))
            def _():
                go_right(j, h).wait_send()

            @pl.when(jnp.logical_and(z + h <= last, z > 0))
            def _():
                go_left(j, h).wait_send()

        return carry

    lax.fori_loop(0, parts, finish, 0)


def first_layer(tokens, top, shards, gains, biases, lengths, cos, sin, cost, sint):
    micro, own, width = tokens.shape
    lead_part, down, pair = shards
    depth = lead_part.shape[0]
    columns = lead_part.shape[1] + down.shape[1] + pair.shape[1]
    rows = 2 * own
    parts = columns // GATHER
    heads = width // 128
    dma = pltpu.SemaphoreType.DMA
    hbm = pl.BlockSpec(memory_space=pl.ANY)
    vm = pl.BlockSpec(memory_space=VM)
    return pl.pallas_call(
        functools.partial(first_kernel, parts),
        in_specs=[hbm] * 5 + [vm] * 7,
        out_specs=[hbm] * 12 + [vm] * 6,
        out_shape=[sds((2, 2, 4, depth, columns), BF)]
        + [sds((heads, rows, 128), BF)] * 5
        + [
            sds((rows, width), BF),
            sds((heads, 2, 2 * rows, rows), BF),
            sds((heads, rows, 128), BF),
            sds((6, 2, rows, 512), BF),
            sds((rows, width), BF),
            sds((rows, width), BF),
            sds((rows, width), BF),
            sds((rows, width), BF),
            sds((heads, 2, 8, rows), F32),
            sds((rows, 128), F32),
            sds((rows, 128), F32),
            sds((4, width), F32),
        ],
        scratch_shapes=[
            VM((2, 2, 4, depth, columns), BF),
            VM((2, own, width), BF),
            VM((heads, rows, 128), BF),
            VM((2, heads, rows, 128), BF),
            VM((2, heads, rows, 128), BF),
            VM((2, heads, rows, 128), BF),
            VM((heads, rows, 128), BF),
            VM((rows, width), BF),
            VM((rows, width), F32),
            VM((8, rows // 8, width), BF),
            VM((8, rows // 8, width), BF),
            VM((2, 2, 8, gains.shape[1]), F32),
            VM((2,) + lengths.shape, jnp.int32),
            VM((2 * rows, rows), F32),
            VM((2, 2, 2 * rows, rows), BF),
            VM((2, 2, rows, 512), BF),
            VM((rows, width), BF),
            VM((rows, width), BF),
            VM((rows, width), BF),
            VM((3, rows, 128), BF),
            VM((heads, rows, 128), BF),
            VM((heads, 2, 128, rows), BF),
            VM((heads, 2, 128, rows), BF),
            VM((heads, 2, 128, rows), BF),
            VM((4, rows, 640), BF),
            dma, dma((2,)), dma((2,)), dma, dma((6, 3)), dma((parts,)), dma((2,)), dma((2,)), dma((9,)), dma((8,)), dma((8,)), dma((8,)), dma((8,)),
            dma((2,)), dma((2,)), dma((6,)), dma((6,)), dma((8,)), dma((8,)),
            dma((3,)), dma((3,)),
            dma((parts, 3)), dma((parts, 3)), dma((parts, 3)), dma((parts, 3)),
            dma((parts,)), dma((parts,)), dma((parts,)), dma((parts,)),
        ],
        compiler_params=pltpu.CompilerParams(collective_id=1, has_side_effects=True, vmem_limit_bytes=63 << 20),
        name="first",
    )(tokens, top, *shards, gains, biases, lengths, cos, sin, cost, sint)


def swap_pairs(tp, step, dp_axes):
    pairs = []
    half = tp // 2
    for core in range(2):
        for at in range(tp):
            source = core * tp + at
            target = (at // half) * tp + half * core + (at + step) % half
            pairs.append((source, target))
    return pairs


def to_sequences(rows, tp):
    half = tp // 2
    at = lax.axis_index("tensor")
    pieces = [None] * half
    got = []
    for step in range(half):
        piece = lax.dynamic_index_in_dim(rows, (at + step) % half, 0, keepdims=False)
        got.append(lax.ppermute(piece, ("core", "tensor"), swap_pairs(tp, step, None)))
    stacked = jnp.stack(got)
    order = (at - jnp.arange(half)) % half
    return jnp.take(stacked, order, axis=0).reshape(-1, rows.shape[-1])


def to_positions(rows, tp):
    half = tp // 2
    at = lax.axis_index("tensor")
    parts = rows.reshape(half, -1, rows.shape[-1])
    got = []
    for step in range(half):
        piece = lax.dynamic_index_in_dim(parts, (at - step) % half, 0, keepdims=False)
        back = [(target, source) for source, target in swap_pairs(tp, step, None)]
        got.append(lax.ppermute(piece, ("core", "tensor"), back))
    stacked = jnp.stack(got)
    order = (at + jnp.arange(half)) % half
    return jnp.take(stacked, (jnp.arange(half) - at) % half, axis=0)


def rope_tables(positions):
    halfway = HD // 2
    freqs = 1000.0 ** (-jnp.arange(halfway, dtype=F32) / halfway)
    angles = positions.astype(F32)[:, None] * freqs[None, :]
    cos, sin = jnp.cos(angles), jnp.sin(angles)
    wide = jnp.concatenate([cos] * 4, axis=1)
    signed = jnp.concatenate([-sin, sin] * 2, axis=1)
    return wide, signed, cos.T, sin.T


def pack_shard(w_qkv, w_out, w_gate_up, w_down):
    rows = w_qkv.shape[0]
    odd = lax.axis_index("tensor") % 2 == 1
    heads = w_qkv.reshape(rows, 3, 3, HD)
    mine = w_out.T.reshape(rows, 3, HD)
    heads = jnp.where(odd, jnp.roll(heads, -1, axis=2), heads)
    mine = jnp.where(odd, jnp.roll(mine, -1, axis=1), mine)
    first = jnp.concatenate(
        [heads[:, :, :2].reshape(rows, -1), heads[:, :, 2].reshape(rows, -1), mine[:, 2], mine[:, :2].reshape(rows, -1)], axis=1
    )
    return first, w_down.T, w_gate_up.reshape(rows, -1)


def join_shard(first, down, pair):
    rows = first.shape[0]
    units = jnp.concatenate([down, pair], axis=1).reshape(rows, 3, -1, 128).transpose(0, 2, 1, 3)
    return jnp.concatenate([first, units.reshape(rows, -1)], axis=1)


def unpack_first(first):
    rows = first.shape[0]
    odd = lax.axis_index("tensor") % 2 == 1
    both = first[:, :384].reshape(rows, 3, 2, HD)
    single = first[:, 384:576].reshape(rows, 3, 1, HD)
    heads = jnp.concatenate([both, single], axis=2)
    mine = jnp.concatenate([first[:, 640:].reshape(rows, 2, HD), first[:, 576:640].reshape(rows, 1, HD)], axis=1)
    heads = jnp.where(odd, jnp.roll(heads, 1, axis=2), heads)
    mine = jnp.where(odd, jnp.roll(mine, 1, axis=1), mine)
    return heads.reshape(rows, 3, -1), mine.reshape(rows, -1).T


def host_tables(length):
    halfway = HD // 2
    freqs = np.float32(1000.0) ** (-np.arange(halfway, dtype=np.float32) / np.float32(halfway))
    angles = np.arange(length, dtype=np.float32)[:, None] * freqs[None, :]
    cos, sin = np.cos(angles), np.sin(angles)
    return np.concatenate([cos] * 4, axis=1), np.concatenate([-sin, sin] * 2, axis=1), cos.T.copy(), sin.T.copy()


BLOCKS = 4


def gather_shard(shard, dp, tp):
    rows, columns = shard.shape
    got = lax.all_gather(shard, ALL, axis=0, tiled=False)
    got = got.reshape(BLOCKS, dp // BLOCKS, tp, rows, columns)
    return got.transpose(0, 2, 1, 3, 4).reshape(BLOCKS, tp, -1, columns)


def scatter_sum(whole, dp, tp):
    columns = whole.shape[3]
    parts = whole.reshape(BLOCKS, tp, dp // BLOCKS, -1, columns).transpose(0, 2, 1, 3, 4)
    parts = parts.reshape(dp * tp, -1, columns)
    return lax.psum_scatter(parts, ALL, scatter_dimension=0, tiled=False).astype(F32)


def on_device(dp, tp, tokens, cotangent, lengths, w_qkv, w_out, w_gate_up, w_down, norm_gains, norm_biases):
    section = lax.axis_index("section")
    core = lax.axis_index("core")
    at = lax.axis_index("tensor")
    micro, own, width = tokens.shape
    assert micro * 2 == tp
    length = own * tp
    rows = length // 2
    shards = pack_shard(w_qkv[0], w_out[0], w_gate_up[0], w_down[0])
    if dp == 4 and tp == 4:
        wide, signed, cost, sint = host_tables(length)
        (
            weights, q, k, v, ko, vo, y, e, o, gu, n1, n2, inputs, dy, l, i1, i2, small,
        ) = first_layer(tokens, cotangent, shards, norm_gains, norm_biases, lengths, wide, signed, cost, sint)
        weights = weights.reshape((BLOCKS,) + weights.shape[2:])
        kept = (q, k, v, ko, vo, o, e, l, gu, n1, i1, n2, i2)
        joint, mix, pair, down, ends, total = last_back(inputs, y, dy, kept, weights, small, cost, sint)
        small = lax.dynamic_slice_in_dim(total[:4].reshape(2, dp * tp, -1), lax.axis_index(ALL), 1, 1)
        gains, biases = small[0, 0], small[1, 0]
        joint, down = joint.transpose(1, 0, 2), down.T
    else:
        near = core * rows + jnp.arange(rows, dtype=jnp.int32)
        far = (1 - core) * rows + jnp.arange(rows, dtype=jnp.int32)
        tabs = rope_tables(near)
        weights = gather_shard(join_shard(*shards), dp, tp)
        norms = jnp.concatenate([norm_gains, norm_biases])
        norms = lax.all_gather(norms, ("y", "core"), axis=1, tiled=True).astype(F32)
        norms = (norms[0].reshape(2, width), norms[1].reshape(2, width))
        grad_top = to_sequences(cotangent, tp)
        tokens = to_sequences(tokens, tp)
        chip_lengths = lax.all_gather(lengths, "core", axis=0, tiled=True)
        my_lengths = lax.dynamic_index_in_dim(chip_lengths, at, 0, keepdims=False)
        ends_at = jnp.cumsum(my_lengths)

        def segment(positions):
            return jnp.sum((ends_at[None, :] <= positions[:, None]).astype(jnp.int32), axis=-1)

        seg_near = segment(near)
        seg_all = jnp.concatenate([seg_near, segment(far)])
        mask = jnp.where(seg_all[:, None] == seg_near[None, :], 0.0, neg_fill).astype(F32)
        y, unused = forward(tokens, weights, norms, mask, tabs)
        received = lax.ppermute(y, "section", [(0, 1)])
        inputs = jnp.where(section == 0, tokens, received)
        y, kept = forward(inputs, weights, norms, mask, tabs)
        dr1, da = ffn_backward(grad_top, kept, weights, norms, False)
        unused, dz = attn_backward(inputs, da, dr1, None, kept, weights, tabs)
        received = lax.ppermute(dz, "section", [(1, 0)])
        dy = jnp.where(section == 0, received, grad_top)
        g, dr1, da, ng = ffn_backward(dy, kept, weights, norms, True)
        g, dz = attn_backward(inputs, da, dr1, g, kept, weights, tabs)
        ends = to_positions(jnp.where(section == 0, dz.astype(BF), y), tp)
        mine = scatter_sum(g, dp, tp)
        first = mine[:, :width]
        units = mine[:, width:].reshape(first.shape[0], -1, 3, 128).transpose(0, 2, 1, 3).reshape(first.shape[0], 3, -1)
        pair, down = units[:, 1:], units[:, 0].T
        joint, mix = unpack_first(first)
        gains = lax.psum_scatter(ng[0:2].reshape(-1), ALL, scatter_dimension=0, tiled=True)
        biases = lax.psum_scatter(ng[2:4].reshape(-1), ALL, scatter_dimension=0, tiled=True)
    outs = (joint, mix, pair.reshape(pair.shape[0], 2, -1), down, gains, biases)
    here = section >= 0
    return tuple(jnp.where(here, t, jnp.zeros_like(t))[None] for t in (ends,) + outs)


def solution(mesh):
    sections, dp, tp = mesh.devices.shape
    fine = Mesh(mesh.devices.reshape(sections, dp // 2, 2, tp), ("section", "y", "core", "tensor"))
    both = ("y", "core")
    in_specs = (
        P(both, "tensor", None),
        P(both, "tensor", None),
        P(both, None),
        P("section", both, None, "tensor"),
        P("section", "tensor", both),
        P("section", both, None, "tensor"),
        P("section", "tensor", both),
        P("section", both),
        P("section", both),
    )
    out_specs = (
        P("section", both, "tensor", None),
        P("section", both, None, "tensor"),
        P("section", "tensor", both),
        P("section", both, None, "tensor"),
        P("section", "tensor", both),
        P("section", ALL),
        P("section", ALL),
    )
    return jax.shard_map(
        functools.partial(on_device, dp, tp), mesh=fine, in_specs=in_specs, out_specs=out_specs, check_vma=False
    )
```
